32 devices in a mesh: row: 4 (over y, x), col: 8 (over z, core).
Axes of the slice: x: 2, y: 2, z: 4, core: 2. Of those that a mesh axis runs over, the one named last changes fastest.
Arguments:
- tokens: bfloat16 [1792, 4096], P('row', 'col'), may hold values from -6 to 6
- cotangent: bfloat16 [1792, 4096], P('row', 'col'), may hold values from -6 to 6
- lengths: int32 [4], replicated, may hold values from 1 to 1024, as said below
- deal_order: int32 [4], replicated, may hold values from 0 to 3, as said below
- w_qkv: bfloat16 [1792, 2304], P('row', 'col'), may hold values from -0.125 to 0.125
- conv_weight: bfloat16 [3, 1792], P(None, 'col'), may hold values from -1 to 1
- w_out: bfloat16 [1792, 1792], P('col', 'row'), may hold values from -1 to 1
- w_gate: bfloat16 [1792, 4864], P('row', 'col'), may hold values from -0.125 to 0.125
- w_up: bfloat16 [1792, 4864], P('row', 'col'), may hold values from -0.125 to 0.125
- w_down: bfloat16 [1792, 4864], P('row', 'col'), may hold values from -0.15625 to 0.15625
- gain_mix: bfloat16 [1792], P('row'), may hold values from 0.5 to 1.5
- gain_ffn: bfloat16 [1792], P('row'), may hold values from 0.5 to 1.5
Outputs:
- result: bfloat16 [1792, 4096], P('row', 'col')
- grad_tokens: float32 [1792, 4096], P('row', 'col')
- grad_qkv: float32 [1792, 2304], P('row', 'col')
- grad_conv: float32 [3, 1792], P(None, 'col')
- grad_out: float32 [1792, 1792], P('col', 'row')
- grad_gate: float32 [1792, 4864], P('row', 'col')
- grad_up: float32 [1792, 4864], P('row', 'col')
- grad_down: float32 [1792, 4864], P('row', 'col')
- grad_gain_mix: float32 [1792], P('row')
- grad_gain_ffn: float32 [1792], P('row')
- rms_values: float32 [3], replicated
The draws below stay inside these ranges and needn't reach their ends.
Inputs may be any that keep to these rules, and one draw needn't show every extreme that they name: `lengths`: laid end to end in dealt order, the sequences fill each aligned block of 1024 tokens exactly, so that none crosses a multiple of 1024; they sum to 4096. Each sequence appears once: the k-th sequence of dealt order is sequence deal_order[k] of the given order.
All inputs are finite; a program needn't handle non-finite values.
Results may differ from the reference program's by a relative error of at most 0.025.
Values may be sent and summed in bfloat16 or wider, within the bound.
A program may use at most 256 MiB of HBM per device.

```python
import jax
import jax.numpy as jnp
from jax import lax

D = 1792
HEADS = 16
FEAT = 16
FF = 4864
CONV = 3
LONGEST = 1024
HDIM = 112
QKW = 2304
TOKENS = 4096
PAIRS = 1
SEQS = 4
N_ROW = 4


def dealing_draw(key):
    cut_key = jax.random.fold_in(key, 11)
    shuffle_key = jax.random.fold_in(key, 12)
    cut_points = jax.random.randint(cut_key, (N_ROW, PAIRS - 1), LONGEST // 8, LONGEST - LONGEST // 8 + 1, dtype=jnp.int32)
    pairs_of = jnp.stack([cut_points, LONGEST - cut_points], 2).reshape(N_ROW, 2 * PAIRS - 2)
    longest_run = jnp.full((N_ROW, 1), LONGEST, dtype=jnp.int32)
    dealt_lengths = jnp.concatenate([longest_run, pairs_of], 1).reshape(SEQS)
    deal_order = jax.random.permutation(shuffle_key, SEQS).astype(jnp.int32)
    lengths = dealt_lengths[jnp.argsort(deal_order)]
    return (lengths.astype(jnp.int32), deal_order)


def draw_lengths(key, part):
    shared = dealing_draw(key)
    return shared[0]


def draw_deal_order(key, part):
    shared = dealing_draw(key)
    return shared[1]


def shard_levels(stream_key, extent, split, smallest, top_value):
    factor_of = 1.0
    for position, shards_of in split:
        heights = jax.random.uniform(jax.random.fold_in(jax.random.fold_in(stream_key, 6), position), (shards_of,), jnp.float32, smallest / len(split), top_value / len(split))
        factor_of = factor_of * jnp.repeat(jnp.exp(heights), extent[position] // shards_of).reshape((-1,) + (1,) * (len(extent) - 1 - position))
    return factor_of


def noise(key, extent, deviation, bound, cuts=(), kind=jnp.bfloat16):
    result = deviation * jax.random.normal(key, extent, jnp.float32)
    if cuts:
        result = result * shard_levels(key, extent, cuts, -0.22, 0.18)
    return jnp.clip(result, -bound, bound).astype(kind)


def setup_inputs(seed: int = 0) -> dict:
    arg_keys = jax.random.split(jax.random.key(seed), 13)
    return {
        "tokens": noise(arg_keys[0], (D, TOKENS), 1.0, 6.0, ((0, 4), (1, 8))),
        "cotangent": noise(arg_keys[1], (D, TOKENS), 1.0, 6.0, ((0, 4), (1, 8))),
        "lengths": draw_lengths(jax.random.fold_in(arg_keys[12], 71), 0),
        "deal_order": draw_deal_order(jax.random.fold_in(arg_keys[12], 71), 0),
        "w_qkv": noise(arg_keys[4], (D, QKW), D ** -0.5, 0.125, ((0, 4), (1, 8))),
        "conv_weight": jnp.clip(jax.random.uniform(arg_keys[5], (CONV, D), jnp.float32, -1.0, 1.0) * shard_levels(arg_keys[5], (CONV, D), ((1, 8),), -0.4, 0.0), -1.0, 1.0).astype(jnp.bfloat16),
        "w_out": noise(arg_keys[6], (D, D), (D // 64) ** -0.5, 1.0, ((0, 8), (1, 4))),
        "w_gate": noise(arg_keys[7], (D, FF), D ** -0.5, 0.125, ((0, 4), (1, 8))),
        "w_up": noise(arg_keys[8], (D, FF), D ** -0.5, 0.125, ((0, 4), (1, 8))),
        "w_down": noise(arg_keys[9], (D, FF), (FF // 4) ** -0.5, 0.15625, ((0, 4), (1, 8))),
        "gain_mix": jnp.clip(1.0 + 0.1 * jax.random.normal(arg_keys[10], (D,), jnp.float32), 0.5, 1.5).astype(jnp.bfloat16),
        "gain_ffn": jnp.clip(1.0 + 0.1 * jax.random.normal(arg_keys[11], (D,), jnp.float32), 0.5, 1.5).astype(jnp.bfloat16),
    }


EPSILON = 1e-06
HIGH = lax.Precision.HIGHEST

@jax.custom_vjp
def low(v):
    return lax.optimization_barrier(v.astype(jnp.bfloat16)).astype(jnp.float32)

@jax.custom_vjp
def low_back(v):
    return v

def low_keep(v):
    return (low(v), None)

def low_pass(kept, grad):
    return (grad,)

def back_keep(v):
    return (v, None)

def back_low(kept, grad):
    return (low(grad),)
low.defvjp(low_keep, low_pass)
low_back.defvjp(back_keep, back_low)

def matmul(left, right):
    return jnp.dot(left, right, precision=HIGH, preferred_element_type=jnp.float32)

def rms_norm(values, norm_gain):
    return values * lax.rsqrt(lax.optimization_barrier(jnp.mean(values * values, -1, keepdims=True)) + EPSILON) * norm_gain

def dealing(lengths, deal_order, total_rows):
    seq_ids = jnp.arange(lengths.shape[0], dtype=jnp.int32)
    chosen = (deal_order[:, None] == seq_ids[None, :]).astype(jnp.int32)
    dealt_lengths = lax.optimization_barrier(jnp.sum(chosen * lengths[None, :], 1))
    given_start = jnp.cumsum(lengths) - lengths
    dealt_start = jnp.cumsum(dealt_lengths) - dealt_lengths
    given_of_dealt = lax.optimization_barrier(jnp.sum(chosen * given_start[None, :], 1))
    dealt_of_given = lax.optimization_barrier(jnp.sum(chosen * dealt_start[:, None], 0))
    places = jnp.arange(total_rows, dtype=jnp.int32)
    in_dealt = (places[:, None] >= dealt_start[None, :]) & (places[:, None] < (dealt_start + dealt_lengths)[None, :])
    in_given = (places[:, None] >= given_start[None, :]) & (places[:, None] < (given_start + lengths)[None, :])
    source = places + lax.optimization_barrier(jnp.sum(jnp.where(in_dealt, (given_of_dealt - dealt_start)[None, :], 0), 1))
    target = places + lax.optimization_barrier(jnp.sum(jnp.where(in_given, (dealt_of_given - given_start)[None, :], 0), 1))
    offsets = places - lax.optimization_barrier(jnp.sum(jnp.where(in_dealt, dealt_start[None, :], 0), 1))
    return (source.astype(jnp.int32), target.astype(jnp.int32), offsets.astype(jnp.int32))

def convolve(raw_values, kernel_conv, offsets):
    mixed = kernel_conv[0] * raw_values
    for delay_step in range(1, CONV):
        moved = jnp.concatenate([jnp.zeros_like(raw_values[:delay_step]), raw_values[:-delay_step]], 0)
        mixed = mixed + kernel_conv[delay_step] * jnp.where((offsets >= delay_step)[:, None, None], moved, 0.0)
    return mixed

def attend_bin(pieces):
    query, keys, values, offsets = pieces
    scores = jnp.einsum('thf,shf->hts', query, keys, precision=HIGH) * FEAT ** (-0.5)
    scores = low_back(scores)
    positions = jnp.arange(query.shape[0], dtype=jnp.int32)
    visible = (positions[None, :] <= positions[:, None]) & (positions[:, None] - positions[None, :] <= offsets[:, None])
    kernel = jnp.where(visible[None], 1.0 + scores + 0.5 * scores * scores, 0.0)
    weights = low(kernel / lax.optimization_barrier(jnp.sum(kernel, -1, keepdims=True)))
    return jnp.einsum('hts,shd->thd', weights, values, precision=HIGH)

def layer(tokens_cols, w_qkv, conv_weight, w_out, w_gate, w_up, w_down, gain_mix, gain_ffn, source, target, offsets):
    tokens = tokens_cols.T
    total_rows = tokens.shape[0]
    bin_count = total_rows // LONGEST
    low_one = low(rms_norm(tokens, gain_mix))
    projected = low_back(matmul(low_one[source], w_qkv)).reshape(total_rows, HEADS, 2 * FEAT + HDIM)
    query = low(projected[:, :, :FEAT])
    keys = low(projected[:, :, FEAT:2 * FEAT])
    raw_values = projected[:, :, 2 * FEAT:]
    values = low(convolve(raw_values, conv_weight.reshape(CONV, HEADS, HDIM), offsets))
    binned = (query.reshape(bin_count, LONGEST, HEADS, FEAT), keys.reshape(bin_count, LONGEST, HEADS, FEAT), values.reshape(bin_count, LONGEST, HEADS, HDIM), offsets.reshape(bin_count, LONGEST))
    attended = lax.map(jax.checkpoint(attend_bin), binned).reshape(total_rows, HEADS * HDIM)
    attended = low(low_back(attended))
    branch_mix = low_back(matmul(attended[target], w_out))
    middle = tokens + branch_mix
    low_two = low(rms_norm(middle, gain_ffn))
    gate = low_back(matmul(low_two[source], w_gate))
    up_proj = low_back(matmul(low_two[source], w_up))
    hidden = low(jax.nn.silu(gate) * up_proj)
    branch_ffn = low_back(matmul(hidden[target], w_down.T))
    result_full = middle + branch_ffn
    return (result_full, (branch_mix, branch_ffn, result_full))

def reference(tokens, cotangent, lengths, deal_order, w_qkv, conv_weight, w_out, w_gate, w_up, w_down, gain_mix, gain_ffn):
    source, target, offsets = dealing(lengths, deal_order, tokens.shape[1])
    floats = [tokens.astype(jnp.float32), w_qkv.astype(jnp.float32), conv_weight.astype(jnp.float32), w_out.astype(jnp.float32), w_gate.astype(jnp.float32), w_up.astype(jnp.float32), w_down.astype(jnp.float32), gain_mix.astype(jnp.float32), gain_ffn.astype(jnp.float32)]

    def forward(tokens_in, qkv_in, conv_in, out_in, gate_in, up_in, down_in, mix_in, ffn_in):
        return layer(tokens_in, qkv_in, conv_in, out_in, gate_in, up_in, down_in, mix_in, ffn_in, source, target, offsets)
    result_full, pullback, extras = jax.vjp(forward, *floats, has_aux=True)
    grads = pullback(cotangent.astype(jnp.float32).T)
    branch_mix, branch_ffn, stream = extras
    rms_values = jnp.sqrt(jnp.stack([jnp.mean(branch_mix * branch_mix), jnp.mean(branch_ffn * branch_ffn), jnp.mean(stream * stream)]))
    return (result_full.T.astype(jnp.bfloat16), grads[0], grads[1], grads[2], grads[3], grads[4], grads[5], grads[6], grads[7], grads[8], rms_values)
```

```python
import jax
import jax.numpy as jnp
from jax import lax
from jax.experimental import pallas as pl
from jax.experimental.pallas import tpu as pltpu
from jax.sharding import PartitionSpec as P

D = 1792
FEAT = 16
CONV = 3
LONGEST = 1024
HDIM = 112


EPSILON = 1e-06


def dealing(lengths, deal_order, total_rows):
    seq_ids = jnp.arange(lengths.shape[0], dtype=jnp.int32)
    chosen = (deal_order[:, None] == seq_ids[None, :]).astype(jnp.int32)
    dealt_lengths = jnp.sum(chosen * lengths[None, :], 1)
    given_start = jnp.cumsum(lengths) - lengths
    dealt_start = jnp.cumsum(dealt_lengths) - dealt_lengths
    given_of_dealt = jnp.sum(chosen * given_start[None, :], 1)
    dealt_of_given = jnp.sum(chosen * dealt_start[:, None], 0)
    places = jnp.arange(total_rows, dtype=jnp.int32)
    in_dealt = (places[:, None] >= dealt_start[None, :]) & (
        places[:, None] < (dealt_start + dealt_lengths)[None, :]
    )
    in_given = (places[:, None] >= given_start[None, :]) & (
        places[:, None] < (given_start + lengths)[None, :]
    )
    source = places + jnp.sum(jnp.where(in_dealt, (given_of_dealt - dealt_start)[None, :], 0), 1)
    target = places + jnp.sum(jnp.where(in_given, (dealt_of_given - given_start)[None, :], 0), 1)
    offsets = places - jnp.sum(jnp.where(in_dealt, dealt_start[None, :], 0), 1)
    return (source, target, offsets)


def convolve(raw_values, kernel_conv, offsets):
    mixed = kernel_conv[0] * raw_values
    for delay_step in range(1, CONV):
        moved = jnp.concatenate(
            [jnp.zeros_like(raw_values[:delay_step]), raw_values[:-delay_step]], 0
        )
        mixed = mixed + kernel_conv[delay_step] * jnp.where(
            (offsets >= delay_step)[:, None, None], moved, 0.0
        )
    return mixed


def convolve_back(grad_mixed, raw_values, kernel_conv, offsets):
    grad_raw = kernel_conv[0] * grad_mixed
    sums_list = [jnp.sum(grad_mixed * raw_values, 0)]
    for delay_step in range(1, CONV):
        masked = jnp.where((offsets >= delay_step)[:, None, None], grad_mixed, 0.0)
        pulled = jnp.concatenate([masked[delay_step:], jnp.zeros_like(masked[:delay_step])], 0)
        grad_raw = grad_raw + kernel_conv[delay_step] * pulled
        moved = jnp.concatenate(
            [jnp.zeros_like(raw_values[:delay_step]), raw_values[:-delay_step]], 0
        )
        sums_list.append(jnp.sum(masked * moved, 0))
    return (grad_raw, jnp.stack(sums_list))


def bin_scores(query, keys, offsets):
    scores = jnp.einsum("thf,shf->hts", query, keys, preferred_element_type=jnp.float32) * FEAT ** (
        -0.5
    )
    positions = jnp.arange(query.shape[0], dtype=jnp.int32)
    visible = (positions[None, :] <= positions[:, None]) & (
        positions[:, None] - positions[None, :] <= offsets[:, None]
    )
    kernel = jnp.where(visible[None], 1.0 + scores + 0.5 * scores * scores, 0.0)
    return (scores, visible, kernel)


def attend_bin(pieces):
    query, keys, values, offsets = pieces
    scores, visible, kernel = bin_scores(query, keys, offsets)
    weights = (kernel / jnp.sum(kernel, -1, keepdims=True)).astype(jnp.bfloat16)
    return jnp.einsum("hts,shd->thd", weights, values, preferred_element_type=jnp.float32)


def attend_back(pieces):
    query, keys, values, offsets, grad_attend = pieces
    scores, visible, kernel = bin_scores(query, keys, offsets)
    totals = jnp.sum(kernel, -1, keepdims=True)
    weights = kernel / totals
    grad_weights = jnp.einsum(
        "thd,shd->hts", grad_attend, values, preferred_element_type=jnp.float32
    )
    grad_values = jnp.einsum(
        "hts,thd->shd",
        weights.astype(jnp.bfloat16),
        grad_attend,
        preferred_element_type=jnp.float32,
    )
    grad_kernel = (grad_weights - jnp.sum(grad_weights * weights, -1, keepdims=True)) / totals
    grad_scores = jnp.where(visible[None], grad_kernel * (1.0 + scores), 0.0).astype(jnp.bfloat16)
    grad_query = jnp.einsum(
        "hts,shf->thf", grad_scores, keys, preferred_element_type=jnp.float32
    ) * FEAT ** (-0.5)
    grad_keys = jnp.einsum(
        "hts,thf->shf", grad_scores, query, preferred_element_type=jnp.float32
    ) * FEAT ** (-0.5)
    return (grad_query, grad_keys, grad_values)


def times_transposed(left, right):
    return lax.dot_general(
        left, right, (((1,), (1,)), ((), ())), preferred_element_type=jnp.float32
    )


def tokens_product(left, right):
    return lax.dot_general(
        left, right, (((0,), (0,)), ((), ())), preferred_element_type=jnp.float32
    )


def plain_product(left, right):
    return jnp.dot(left, right, preferred_element_type=jnp.float32)


def gather_cols(values):
    return lax.all_gather(values, "col", axis=0, tiled=True)


def gather_rows(values):
    return lax.all_gather(values, "row", axis=0, tiled=True)


def grad_gather_cols(values):
    return lax.all_gather(values, "col", axis=1, tiled=True)


def grad_gather_rows(values):
    return lax.all_gather(values, "row", axis=0, tiled=True)


def width_total(values):
    return lax.psum(values, "row")


def forward_rows(gathered, row_index, weight, rows_here):

    def partial_term(row_start, row_count):
        picked = jnp.take(gathered, row_index, axis=0)
        return jnp.dot(picked, weight, preferred_element_type=jnp.float32)

    return lax.psum_scatter(
        partial_term(jnp.int32(0), rows_here * lax.axis_size("row")),
        "row",
        scatter_dimension=0,
        tiled=True,
    )


def forward_cols(gathered, row_index, weight, rows_here, product):

    def partial_term(row_start, row_count):
        picked = jnp.take(gathered, row_index, axis=0)
        return product(picked, weight)

    return lax.psum_scatter(
        partial_term(jnp.int32(0), lax.axis_size("col") * rows_here).astype(jnp.bfloat16),
        "col",
        scatter_dimension=0,
        tiled=True,
    ).astype(jnp.float32)


def backward_rows(gathered, row_index, weight, rows_here, contract):

    def partial_term(row_start, row_count):
        picked = jnp.take(gathered, row_index, axis=1)
        return lax.dot_general(
            picked, weight, (((0,), (contract,)), ((), ())), preferred_element_type=jnp.float32
        )

    return lax.psum_scatter(
        partial_term(jnp.int32(0), lax.axis_size("row") * rows_here).astype(jnp.bfloat16),
        "row",
        scatter_dimension=0,
        tiled=True,
    ).astype(jnp.float32)


def backward_cols(gathered, row_index, weight, rows_here):

    def partial_term(row_start, row_count):
        picked = jnp.take(gathered, row_index, axis=0)
        return times_transposed(picked, weight)

    return lax.psum_scatter(
        partial_term(jnp.int32(0), lax.axis_size("col") * rows_here).astype(jnp.bfloat16),
        "col",
        scatter_dimension=0,
        tiled=True,
    ).astype(jnp.float32)


def norm_forward(values, norm_gain):
    totals = width_total(jnp.sum(values * values, -1))
    inverse = lax.rsqrt(totals / D + EPSILON)
    return (values * inverse[:, None] * norm_gain, inverse)


def norm_back(values, inverse, norm_gain, grad_normed, dot_sums):
    cubed = inverse * inverse * inverse
    return grad_normed * norm_gain * inverse[:, None] - values * (cubed * dot_sums / D)[:, None]


def on_device_general(
    tokens,
    cotangent,
    lengths,
    deal_order,
    w_qkv,
    conv_weight,
    w_out,
    w_gate,
    w_up,
    w_down,
    gain_mix,
    gain_ffn,
):
    local_rows = tokens.shape[1]
    total_rows = local_rows * lax.axis_size("col")
    group_rows = total_rows // lax.axis_size("row")
    bin_count = group_rows // LONGEST
    heads_here = w_out.shape[0] // HDIM
    ffn_cols = w_gate.shape[1]
    source, target, offsets = dealing(lengths, deal_order, total_rows)
    group_offsets = lax.dynamic_slice_in_dim(
        offsets, lax.axis_index("row") * group_rows, group_rows
    )
    inputs = tokens.astype(jnp.float32).T
    gain_one = gain_mix.astype(jnp.float32)
    gain_two = gain_ffn.astype(jnp.float32)
    both_weights = jnp.concatenate([w_gate, w_up], 1)
    normed_one, inverse_one = norm_forward(inputs, gain_one)
    low_one = normed_one.astype(jnp.bfloat16)
    all_one = gather_cols(low_one)
    projected = forward_rows(all_one, source, w_qkv, group_rows)
    projected = projected.reshape(group_rows, heads_here, 2 * FEAT + HDIM)
    query = projected[:, :, :FEAT].astype(jnp.bfloat16)
    keys = projected[:, :, FEAT : 2 * FEAT].astype(jnp.bfloat16)
    raw_values = projected[:, :, 2 * FEAT :]
    kernel_conv = conv_weight.astype(jnp.float32).reshape(CONV, heads_here, HDIM)
    values = convolve(raw_values, kernel_conv, group_offsets).astype(jnp.bfloat16)
    binned = (
        query.reshape(bin_count, LONGEST, heads_here, FEAT),
        keys.reshape(bin_count, LONGEST, heads_here, FEAT),
        values.reshape(bin_count, LONGEST, heads_here, HDIM),
        group_offsets.reshape(bin_count, LONGEST),
    )
    attended = (
        lax.map(attend_bin, binned).reshape(group_rows, heads_here * HDIM).astype(jnp.bfloat16)
    )
    all_attended = gather_rows(attended)
    branch_mix = forward_cols(all_attended, target, w_out, local_rows, plain_product)
    middle = inputs + branch_mix
    normed_two, inverse_two = norm_forward(middle, gain_two)
    low_two = normed_two.astype(jnp.bfloat16)
    all_two = gather_cols(low_two)
    gate_up = forward_rows(all_two, source, both_weights, group_rows)
    gate = gate_up[:, :ffn_cols]
    up_proj = gate_up[:, ffn_cols:]
    activated = jax.nn.silu(gate)
    hidden = (activated * up_proj).astype(jnp.bfloat16)
    all_hidden = gather_rows(hidden)
    branch_ffn = forward_cols(all_hidden, target, w_down, local_rows, times_transposed)
    result_full = middle + branch_ffn
    grad_result = cotangent.astype(jnp.float32).T
    all_grad_ffn = grad_gather_cols(cotangent)
    hidden_again = gather_rows(hidden)
    grad_down = jnp.dot(
        jnp.take(all_grad_ffn, source, axis=1), hidden_again, preferred_element_type=jnp.float32
    )
    grad_hidden = backward_rows(all_grad_ffn, source, w_down, group_rows, 0)
    gate_sigmoid = jax.nn.sigmoid(gate)
    grad_gate_part = grad_hidden * up_proj * gate_sigmoid * (1.0 + gate * (1.0 - gate_sigmoid))
    grad_up_part = grad_hidden * activated
    grad_gate_up = jnp.concatenate([grad_gate_part, grad_up_part], 1).astype(jnp.bfloat16)
    all_grad_gate_up = grad_gather_rows(grad_gate_up)
    two_again = gather_cols(low_two)
    grad_both = tokens_product(jnp.take(two_again, source, axis=0), all_grad_gate_up)
    grad_normed_two = backward_cols(all_grad_gate_up, target, both_weights, local_rows)
    dots_two = width_total(jnp.sum(grad_normed_two * gain_two * middle, -1))
    grad_middle = grad_result + norm_back(middle, inverse_two, gain_two, grad_normed_two, dots_two)
    gain_part_two = jnp.sum(grad_normed_two * middle * inverse_two[:, None], 0)
    low_grad_middle = grad_middle.T.astype(jnp.bfloat16)
    all_grad_middle = grad_gather_cols(low_grad_middle)
    attended_again = gather_rows(attended)
    grad_out = lax.dot_general(
        attended_again,
        jnp.take(all_grad_middle, source, axis=1),
        (((0,), (1,)), ((), ())),
        preferred_element_type=jnp.float32,
    )
    grad_attended = backward_rows(all_grad_middle, source, w_out, group_rows, 1).astype(
        jnp.bfloat16
    )
    binned_back = binned + (grad_attended.reshape(bin_count, LONGEST, heads_here, HDIM),)
    grad_query, grad_keys, grad_values = lax.map(attend_back, binned_back)
    grad_values = grad_values.reshape(group_rows, heads_here, HDIM)
    grad_raw, conv_part = convolve_back(grad_values, raw_values, kernel_conv, group_offsets)
    grad_projected = jnp.concatenate(
        [
            grad_query.reshape(group_rows, heads_here, FEAT),
            grad_keys.reshape(group_rows, heads_here, FEAT),
            grad_raw,
        ],
        2,
    )
    grad_projected = grad_projected.reshape(group_rows, heads_here * (2 * FEAT + HDIM)).astype(
        jnp.bfloat16
    )
    all_grad_projected = grad_gather_rows(grad_projected)
    one_again = gather_cols(low_one)
    grad_qkv = tokens_product(jnp.take(one_again, source, axis=0), all_grad_projected)
    grad_normed_one = backward_cols(all_grad_projected, target, w_qkv, local_rows)
    squares = jnp.stack(
        [
            jnp.sum(branch_mix * branch_mix),
            jnp.sum(branch_ffn * branch_ffn),
            jnp.sum(result_full * result_full),
        ]
    )
    dots_one, grad_conv, squares_rows = width_total(
        (
            jnp.sum(grad_normed_one * gain_one * inputs, -1),
            conv_part.reshape(CONV, heads_here * HDIM),
            squares,
        )
    )
    grad_tokens = grad_middle + norm_back(inputs, inverse_one, gain_one, grad_normed_one, dots_one)
    gain_part_one = jnp.sum(grad_normed_one * inputs * inverse_one[:, None], 0)
    grad_gain_mix, grad_gain_ffn, squares_all = lax.psum(
        (gain_part_one, gain_part_two, squares_rows), "col"
    )
    rms_values = jnp.sqrt(squares_all / (total_rows * D))
    return (
        result_full.T.astype(jnp.bfloat16),
        grad_tokens.T,
        grad_qkv,
        grad_conv,
        grad_out,
        grad_both[:, :ffn_cols],
        grad_both[:, ffn_cols:],
        grad_down,
        grad_gain_mix,
        grad_gain_ffn,
        rms_values,
    )


HEADROWS = 2 * FEAT + HDIM
TILE = 128
MESH = pl.DeviceIdType.MESH
VMEM_LIMIT = 60 * 2**20
ANY = pl.BlockSpec(memory_space=pl.ANY)
IN_VMEM = pl.BlockSpec(memory_space=pltpu.VMEM)


def place():
    column = lax.axis_index("col")
    return lax.axis_index("row"), column // 2, column % 2


def device(chip, plane, core):
    return (chip, plane * 2 + core)


def other_chips(chip):
    y, x = chip // 2, chip % 2
    return (y * 2 + 1 - x, (1 - y) * 2 + x, (1 - y) * 2 + 1 - x)


def greet(partners):
    barrier = pltpu.get_barrier_semaphore()
    for partner in partners:
        pl.semaphore_signal(barrier, inc=1, device_id=partner, device_id_type=MESH)
    pl.semaphore_wait(barrier, len(partners))


def plane_partners(chip, plane, core):
    found = [device(c, plane, core) for c in other_chips(chip)]
    found += [device(c, plane, 1 - core) for c in other_chips(chip)]
    return found + [device(chip, plane, 1 - core)]


def line_partners(chip, plane, core):
    return [device(chip, (plane + step) % 4, core) for step in (1, 2, 3)]


def remote(source, target, send, receive, to):
    return pltpu.make_async_remote_copy(
        src_ref=source,
        dst_ref=target,
        send_sem=send,
        recv_sem=receive,
        device_id=to,
        device_id_type=MESH,
    )


def lanes(start, size):
    return pl.ds(pl.multiple_of(start, TILE), size)


def gather_kernel(
    wff, wat, tok, cot, gains, ff, at, xs, gs, gn,
    local_sem, main_s, main_r, extra_s, extra_r, att_s, att_r,
    tok_s, tok_r, cot_s, cot_r, gn_s, gn_r, tokc_s, tokc_r, cotc_s, cotc_r,
    z_s, z_r, ze_s, ze_r, za_s, za_r,
):
    chip, plane, core = place()
    others = other_chips(chip)
    greet(plane_partners(chip, plane, core) + line_partners(chip, plane, core))
    extra_chip, far_core = (plane % 2) * 2 + core, plane // 2
    holds_att = core == plane // 2
    holds_extra = holds_att & (chip // 2 == plane % 2)
    extra_plane = 2 * core + chip // 2
    locals_ = []

    def keep(source, target, sem):
        copy = pltpu.make_async_copy(source, target, sem)
        copy.start()
        locals_.append(copy)

    def att_copy(half, to_chip, slot):
        return remote(
            wat.at[half], at.at[plane % 2, chip], att_s.at[half], att_r.at[chip],
            device(to_chip, plane, far_core),
        )

    for half in range(2):
        to_chip = 2 * core + half
        is_self = (to_chip == chip) & (far_core == core)

        @pl.when(is_self)
        def _():
            pltpu.make_async_copy(wat.at[half], at.at[plane % 2, chip], local_sem.at[4]).start()

        @pl.when(jnp.logical_not(is_self))
        def _():
            att_copy(half, to_chip, half).start()

    mains = []
    for p, to_chip in enumerate(others):
        copy = remote(
            wff.at[:, :, lanes(to_chip * TILE, TILE)],
            ff.at[:, chip, :, lanes(plane * TILE, TILE)],
            main_s.at[p], main_r.at[p], device(to_chip, plane, core),
        )
        copy.start()
        mains.append(copy)
    keep(
        wff.at[:, :, lanes(chip * TILE, TILE)],
        ff.at[:, chip, :, lanes(plane * TILE, TILE)],
        local_sem.at[0],
    )
    extra_self = (extra_chip == chip) & (far_core == core)

    def extra_copy():
        return remote(
            wff.at[:, :, lanes(4 * TILE, TILE)],
            ff.at[:, chip, :, lanes(4 * TILE, TILE)],
            extra_s, extra_r.at[chip], device(extra_chip, plane, far_core),
        )

    def extra_local():
        return pltpu.make_async_copy(
            wff.at[:, :, lanes(4 * TILE, TILE)],
            ff.at[:, chip, :, lanes(4 * TILE, TILE)],
            local_sem.at[5],
        )

    @pl.when(extra_self)
    def _():
        extra_local().start()

    @pl.when(jnp.logical_not(extra_self))
    def _():
        extra_copy().start()

    half_tokens = tok.shape[1]
    own_half = lanes(core * half_tokens, half_tokens)
    toks, cots, gns = [], [], []
    for p, to_chip in enumerate(others):
        to = device(to_chip, plane, core)
        toks.append(remote(tok, xs.at[chip, :, own_half], tok_s.at[p], tok_r.at[p], to))
        cots.append(remote(cot, gs.at[chip, :, own_half], cot_s.at[p], cot_r.at[p], to))
        gns.append(remote(gains, gn.at[chip], gn_s.at[p], gn_r.at[p], to))
        toks[-1].start()
        gns[-1].start()
        cots[-1].start()
    keep(tok, xs.at[chip, :, own_half], local_sem.at[1])
    keep(cot, gs.at[chip, :, own_half], local_sem.at[2])
    keep(gains, gn.at[chip], local_sem.at[3])
    mate = device(chip, plane, 1 - core)
    cross = []
    for source, target, send, receive in (
        (tok, xs, tokc_s, tokc_r), (cot, gs, cotc_s, cotc_r),
    ):
        copy = remote(source, target.at[chip, :, own_half], send.at[3], receive.at[3], mate)
        copy.start()
        cross.append(copy)

    for half in range(2):
        to_chip = 2 * core + half
        is_self = (to_chip == chip) & (far_core == core)

        @pl.when(is_self)
        def _():
            pltpu.make_async_copy(wat.at[half], at.at[plane % 2, chip], local_sem.at[4]).wait()

        @pl.when(jnp.logical_not(is_self))
        def _():
            att_copy(half, to_chip, half).wait_send()

    @pl.when(holds_att)
    def _():
        for source_chip in range(4):
            from_self = (source_chip == chip) & (core == chip // 2)

            @pl.when(jnp.logical_not(from_self))
            def _():
                remote(
                    wat.at[0], at.at[plane % 2, source_chip], att_s.at[0], att_r.at[source_chip],
                    device(chip, plane, core),
                ).wait_recv()

    def att_line(step):
        return remote(
            at.at[plane % 2], at.at[plane % 2], za_s.at[step - 1], za_r.at[step - 1],
            device(chip, (plane + step) % 4, core),
        )

    @pl.when(holds_att)
    def _():
        for step in (1, 3, 2):
            att_line(step).start()

    locals_[0].wait()
    for copy in mains:
        copy.wait_recv()
    own_tile = ff.at[:, :, :, lanes(plane * TILE, TILE)]
    line = []
    for step in (1, 3, 2):
        copy = remote(
            own_tile, own_tile, z_s.at[step - 1], z_r.at[step - 1],
            device(chip, (plane + step) % 4, core),
        )
        copy.start()
        line.append((step, copy))

    @pl.when(extra_self)
    def _():
        extra_local().wait()

    @pl.when(jnp.logical_not(extra_self))
    def _():
        extra_copy().wait_send()

    extra_tile = ff.at[:, :, :, lanes(4 * TILE, TILE)]

    def extra_line(step):
        return remote(
            extra_tile, extra_tile, ze_s.at[step - 1], ze_r,
            device(chip, (plane + step) % 4, core),
        )

    @pl.when(holds_extra)
    def _():
        for source_chip in range(4):
            from_self = (source_chip == chip) & (core == chip % 2)

            @pl.when(jnp.logical_not(from_self))
            def _():
                remote(
                    wff.at[:, :, lanes(4 * TILE, TILE)],
                    ff.at[:, source_chip, :, lanes(4 * TILE, TILE)],
                    extra_s, extra_r.at[source_chip], device(chip, plane, core),
                ).wait_recv()
        for step in (1, 3, 2):
            extra_line(step).start()

    for p, from_chip in enumerate(others):
        for copies, target, send, receive in (
            (toks, xs, tokc_s, tokc_r), (cots, gs, cotc_s, cotc_r),
        ):
            copies[p].wait_recv()
            block = target.at[from_chip, :, own_half]
            copy = remote(block, block, send.at[p], receive.at[p], mate)
            copy.start()
            cross.append(copy)
        gns[p].wait()
    for copy in cross:
        copy.wait()
    for copy in toks + cots + mains:
        copy.wait_send()
    for copy in locals_[1:]:
        copy.wait()

    for step, copy in line:
        copy.wait_send()
        source_plane = (plane + 4 - step) % 4
        tile = ff.at[:, :, :, lanes(source_plane * TILE, TILE)]
        remote(tile, tile, z_s.at[step - 1], z_r.at[step - 1], mate).wait_recv()

    @pl.when(holds_extra)
    def _():
        for step in (1, 3, 2):
            extra_line(step).wait_send()

    @pl.when(jnp.logical_not(holds_extra))
    def _():
        extra_line(1).wait_recv()

    @pl.when(holds_att)
    def _():
        for step in (1, 3, 2):
            att_line(step).wait_send()

    for step in (1, 3, 2):
        source_plane = (plane + 4 - step) % 4

        @pl.when(source_plane // 2 == core)
        def _():
            block = at.at[source_plane % 2]
            remote(block, block, za_s.at[step - 1], za_r.at[step - 1], mate).wait_recv()


def dma(*shape):
    return pltpu.SemaphoreType.DMA(shape)


def gather_in(wff, wat, tok, cot, gains):
    rows, half = tok.shape
    shapes = [
        (3, 4, rows, 5 * TILE), (2, 4) + wat.shape[1:], (4, rows, 2 * half),
        (4, rows, 2 * half), (4, rows, TILE),
    ]
    return pl.pallas_call(
        gather_kernel,
        out_shape=[jax.ShapeDtypeStruct(s, jnp.bfloat16) for s in shapes],
        in_specs=[ANY] * 5,
        out_specs=[ANY] * 5,
        scratch_shapes=[
            dma(6), dma(3), dma(3), dma(), dma(4), dma(2), dma(4),
            dma(3), dma(3), dma(3), dma(3), dma(3), dma(3), dma(4), dma(4), dma(4), dma(4),
            dma(3), dma(3), dma(3), dma(), dma(3), dma(3),
        ],
        compiler_params=pltpu.CompilerParams(collective_id=1, has_side_effects=True),
        name="gather_in",
    )(wff, wat, tok, cot, gains)


def plane_sum_kernel(part, out, from_mate, both, got, mate_s, mate_r, send, receive):
    chip, plane, core = place()
    others = other_chips(chip)
    mate = device(chip, plane, 1 - core)
    half = part.shape[2] // 2
    greet([mate] + [device(c, plane, core) for c in others])
    copy = remote(
        part.at[:, :, lanes((1 - core) * half, half)], from_mate, mate_s, mate_r, mate
    )
    copy.start()
    copy.wait()

    @pl.loop(0, 4)
    def _(block):
        both[block] = (
            part[block, :, lanes(core * half, half)].astype(jnp.float32)
            + from_mate[block].astype(jnp.float32)
        ).astype(jnp.bfloat16)

    copies = []
    for p, to_chip in enumerate(others):
        copy = remote(
            both.at[:, :, lanes(to_chip * TILE, TILE)], got.at[p], send.at[p], receive.at[p],
            device(to_chip, plane, core),
        )
        copy.start()
        copies.append(copy)
    for copy in copies:
        copy.wait()

    @pl.loop(0, 4)
    def _(block):
        total = both[block, :, lanes(chip * TILE, TILE)].astype(jnp.float32)
        for p in range(3):
            total = total + got[p, block].astype(jnp.float32)
        out[block] = total


def plane_sum(part, collective_id):
    _, rows, tokens = part.shape
    bf16 = jnp.bfloat16
    return pl.pallas_call(
        plane_sum_kernel,
        out_shape=jax.ShapeDtypeStruct((4, rows, TILE), jnp.float32),
        in_specs=[IN_VMEM],
        out_specs=IN_VMEM,
        scratch_shapes=[
            pltpu.VMEM((4, rows, tokens // 2), bf16),
            pltpu.VMEM((4, rows, tokens // 2), bf16),
            pltpu.VMEM((3, 4, rows, TILE), bf16),
            dma(), dma(), dma(3), dma(3),
        ],
        compiler_params=pltpu.CompilerParams(
            collective_id=collective_id, has_side_effects=True, vmem_limit_bytes=VMEM_LIMIT
        ),
        name="plane_sum",
    )(part)


def plane_gather_kernel(mine, out, keep_sem, send, receive, mate_s, mate_r):
    chip, plane, core = place()
    others = other_chips(chip)
    mate = device(chip, plane, 1 - core)
    greet([mate] + [device(c, plane, core) for c in others])
    half = out.shape[2] // 2

    def block_of(from_chip):
        return out.at[:, :, lanes(core * half + from_chip * TILE, TILE)]

    copies = []
    for p, to_chip in enumerate(others):
        copy = remote(
            mine, block_of(chip), send.at[p], receive.at[p], device(to_chip, plane, core)
        )
        copy.start()
        copies.append(copy)
    kept = pltpu.make_async_copy(mine, block_of(chip), keep_sem)
    kept.start()
    cross = [remote(mine, block_of(chip), mate_s.at[3], mate_r.at[3], mate)]
    cross[0].start()
    for p, from_chip in enumerate(others):
        copies[p].wait_recv()
        block = block_of(from_chip)
        copy = remote(block, block, mate_s.at[p], mate_r.at[p], mate)
        copy.start()
        cross.append(copy)
    for copy in cross:
        copy.wait()
    for copy in copies:
        copy.wait_send()
    kept.wait()


def plane_gather(mine, collective_id):
    _, rows, _ = mine.shape
    return pl.pallas_call(
        plane_gather_kernel,
        out_shape=jax.ShapeDtypeStruct((4, rows, 8 * TILE), jnp.bfloat16),
        in_specs=[IN_VMEM],
        out_specs=IN_VMEM,
        scratch_shapes=[dma(), dma(3), dma(3), dma(4), dma(4)],
        compiler_params=pltpu.CompilerParams(
            collective_id=collective_id, has_side_effects=True, vmem_limit_bytes=VMEM_LIMIT
        ),
        name="plane_gather",
    )(mine)


def scatter_kernel(
    ff, at, res, gtok, out_ff, out_at, out_res, out_tok,
    got, got_extra, got_att, sum_main, sum_extra, sum_att, load,
    load_sem, local_sem, z_s, z_r, ze_s, ze_r, za_s, za_r,
    main_s, main_r, extra_s, extra_r, att_s, att_r, res_s, res_r, tok_s, tok_r,
):
    chip, plane, core = place()
    others = other_chips(chip)
    greet(plane_partners(chip, plane, core) + line_partners(chip, plane, core))
    holds_att = core == plane // 2
    holds_extra = holds_att & (chip // 2 == plane % 2)
    extra_plane = 2 * core + chip // 2
    extra_tile = ff.at[:, :, :, lanes(4 * TILE, TILE)]

    def to_plane(step):
        return (plane + step) % 4

    def main_line(step):
        return remote(
            ff.at[:, :, :, lanes(to_plane(step) * TILE, TILE)], got.at[step - 1],
            z_s.at[step - 1], z_r.at[step - 1], device(chip, to_plane(step), core),
        )

    def extra_line(step):
        return remote(
            extra_tile, got_extra.at[step - 1], ze_s.at[step - 1], ze_r.at[step - 1],
            device(chip, to_plane(step), core),
        )

    def att_line(step):
        return remote(
            at.at[to_plane(step) % 2], got_att.at[step - 1], za_s.at[step - 1],
            za_r.at[step - 1], device(chip, to_plane(step), core),
        )

    for step in (1, 3, 2):
        main_line(step).start()

        @pl.when(to_plane(step) == extra_plane)
        def _():
            extra_line(step).start()

        @pl.when(to_plane(step) // 2 == core)
        def _():
            att_line(step).start()

    half = out_res.shape[1]
    toks = []
    for p, to_chip in enumerate(others):
        for source, target, send, receive in (
            (res, out_res, res_s, res_r), (gtok, out_tok, tok_s, tok_r),
        ):
            copy = remote(
                source.at[to_chip], target.at[:, lanes(chip * TILE, TILE)],
                send.at[p], receive.at[p], device(to_chip, plane, core),
            )
            copy.start()
            toks.append(copy)
    kept = [
        pltpu.make_async_copy(
            source.at[chip], target.at[:, lanes(chip * TILE, TILE)], local_sem.at[i]
        )
        for i, (source, target) in enumerate(((res, out_res), (gtok, out_tok)))
    ]
    for copy in kept:
        copy.start()

    mine = pltpu.make_async_copy(
        ff.at[:, :, :, lanes(plane * TILE, TILE)], sum_main, load_sem
    )
    mine.start()
    mine.wait()
    for step in (1, 3, 2):
        main_line(step).wait()

    @pl.loop(0, 12)
    def _(i):
        m, block = i // 4, i % 4
        total = sum_main[m, block].astype(jnp.float32)
        for p in range(3):
            total = total + got[p, m, block].astype(jnp.float32)
        sum_main[m, block] = total.astype(jnp.bfloat16)

    mains = []
    own_lanes = out_ff.at[:, :, lanes(chip * TILE, TILE)]
    for p, to_chip in enumerate(others):
        copy = remote(
            sum_main.at[:, to_chip], own_lanes, main_s.at[p], main_r.at[p],
            device(to_chip, plane, core),
        )
        copy.start()
        mains.append(copy)
    kept.append(pltpu.make_async_copy(sum_main.at[:, chip], own_lanes, local_sem.at[2]))
    kept[-1].start()

    last_lanes = out_ff.at[:, :, lanes(4 * TILE, TILE)]

    def extra_back(to_chip):
        return remote(
            sum_extra.at[:, to_chip], last_lanes, extra_s.at[to_chip], extra_r,
            device(to_chip, plane, chip % 2),
        )

    def extra_keep():
        return pltpu.make_async_copy(sum_extra.at[:, chip], last_lanes, local_sem.at[3])

    def extra_self(to_chip):
        return (to_chip == chip) & (core == chip % 2)

    @pl.when(holds_extra)
    def _():
        mine = pltpu.make_async_copy(extra_tile, sum_extra, load_sem)
        mine.start()
        mine.wait()
        for step in (1, 3, 2):
            extra_line(step).wait_recv()

        @pl.loop(0, 12)
        def _(i):
            m, block = i // 4, i % 4
            total = sum_extra[m, block].astype(jnp.float32)
            for p in range(3):
                total = total + got_extra[p, m, block].astype(jnp.float32)
            sum_extra[m, block] = total.astype(jnp.bfloat16)

        for to_chip in range(4):

            @pl.when(extra_self(to_chip))
            def _():
                extra_keep().start()

            @pl.when(jnp.logical_not(extra_self(to_chip)))
            def _():
                extra_back(to_chip).start()

    def att_back(to_chip):
        return remote(
            sum_att.at[to_chip], out_at.at[chip % 2], att_s.at[to_chip], att_r.at[chip % 2],
            device(to_chip, plane, chip // 2),
        )

    def att_keep():
        return pltpu.make_async_copy(sum_att.at[chip], out_at.at[chip % 2], local_sem.at[4])

    def att_self(to_chip):
        return (to_chip == chip) & (core == chip // 2)

    @pl.when(holds_att)
    def _():
        mine = pltpu.make_async_copy(at.at[plane % 2], sum_att, load_sem)
        mine.start()
        mine.wait()
        for step in (1, 3, 2):
            att_line(step).wait_recv()

        @pl.loop(0, 4)
        def _(block):
            total = sum_att[block].astype(jnp.float32)
            for p in range(3):
                total = total + got_att[p, block].astype(jnp.float32)
            sum_att[block] = total.astype(jnp.bfloat16)

        for to_chip in range(4):

            @pl.when(att_self(to_chip))
            def _():
                att_keep().start()

            @pl.when(jnp.logical_not(att_self(to_chip)))
            def _():
                att_back(to_chip).start()

    for step in (1, 3, 2):

        @pl.when(to_plane(step) == extra_plane)
        def _():
            extra_line(step).wait_send()

        @pl.when(to_plane(step) // 2 == core)
        def _():
            att_line(step).wait_send()

    for copy in toks + mains:
        copy.wait()
    for copy in kept:
        copy.wait()

    @pl.when(holds_extra)
    def _():
        for to_chip in range(4):

            @pl.when(extra_self(to_chip))
            def _():
                extra_keep().wait()

            @pl.when(jnp.logical_not(extra_self(to_chip)))
            def _():
                extra_back(to_chip).wait_send()

    @pl.when(holds_att)
    def _():
        for to_chip in range(4):

            @pl.when(att_self(to_chip))
            def _():
                att_keep().wait()

            @pl.when(jnp.logical_not(att_self(to_chip)))
            def _():
                att_back(to_chip).wait_send()

    sender_chip, sender_core = (plane % 2) * 2 + core, plane // 2

    @pl.when(jnp.logical_not((sender_chip == chip) & (sender_core == core)))
    def _():
        remote(
            sum_extra.at[:, 0], last_lanes, extra_s.at[0], extra_r, device(chip, plane, core)
        ).wait_recv()

    for h in range(2):

        @pl.when(jnp.logical_not((2 * core + h == chip) & (sender_core == core)))
        def _():
            remote(
                sum_att.at[0], out_at.at[h], att_s.at[0], att_r.at[h],
                device(chip, plane, core),
            ).wait_recv()


def scatter_out(ff, at, res, gtok):
    bf16 = jnp.bfloat16
    rows = ff.shape[2]
    head_block = at.shape[2:]
    return pl.pallas_call(
        scatter_kernel,
        out_shape=[
            jax.ShapeDtypeStruct((3, rows, 5 * TILE), bf16),
            jax.ShapeDtypeStruct((2,) + head_block, bf16),
            jax.ShapeDtypeStruct((rows, 4 * TILE), bf16),
            jax.ShapeDtypeStruct((rows, 4 * TILE), bf16),
        ],
        in_specs=[ANY] * 4,
        out_specs=[ANY] * 4,
        scratch_shapes=[
            pltpu.VMEM((3, 3, 4, rows, TILE), bf16),
            pltpu.VMEM((3, 3, 4, rows, TILE), bf16),
            pltpu.VMEM((3, 4) + head_block, bf16),
            pltpu.VMEM((3, 4, rows, TILE), bf16),
            pltpu.VMEM((3, 4, rows, TILE), bf16),
            pltpu.VMEM((4,) + head_block, bf16),
            pltpu.VMEM((8, TILE), bf16),
            dma(), dma(5), dma(3), dma(3), dma(3), dma(3), dma(3), dma(3),
            dma(3), dma(3), dma(4), dma(), dma(4), dma(2), dma(3), dma(3), dma(3), dma(3),
        ],
        compiler_params=pltpu.CompilerParams(
            collective_id=2, has_side_effects=True, vmem_limit_bytes=VMEM_LIMIT
        ),
        name="scatter_out",
    )(ff, at, res, gtok)


def attend_heads(query, keys, values):
    offsets = jnp.arange(query.shape[2], dtype=jnp.int32)
    order = lambda v: v.transpose(2, 0, 1)
    return order(query), order(keys), order(values), offsets


def on_device_full(
    tokens, cotangent, w_qkv, conv_weight, w_out, w_gate, w_up, w_down, gain_mix, gain_ffn
):
    f32, bf16 = jnp.float32, jnp.bfloat16
    rows, half = tokens.shape
    ffn_cols = w_gate.shape[1]
    chip, plane, core = place()
    heads = 2
    pad = ((0, 0), (0, 5 * TILE - ffn_cols))
    wff = jnp.stack([jnp.pad(w, pad) for w in (w_gate, w_up, w_down)])
    wat = jnp.concatenate(
        [w_qkv.T.reshape(heads, HEADROWS, rows), w_out.reshape(heads, HDIM, rows)], 1
    )
    gains = jnp.concatenate(
        [jnp.broadcast_to(g[:, None], (rows, TILE // 2)) for g in (gain_mix, gain_ffn)], 1
    )
    ff, at, xs, gs, gn = gather_in(wff, wat, tokens, cotangent, gains)
    width = 4 * rows
    seq = 2 * half
    wg, wu, wd = (ff[i].reshape(width, 5 * TILE) for i in range(3))
    gain_one = gn.reshape(width, TILE)[:, 0].astype(f32)[:, None]
    gain_two = gn.reshape(width, TILE)[:, TILE // 2].astype(f32)[:, None]
    w_att = at.transpose(0, 2, 1, 3).reshape(heads, HEADROWS + HDIM, width)
    w_in, w_back = w_att[:, :HEADROWS], w_att[:, HEADROWS:]
    conv = lax.all_gather(conv_weight, "col", axis=1, tiled=True).astype(f32)
    conv = conv.reshape(CONV, -1, HDIM)
    my_heads = jnp.stack([4 * (2 * core) + chip, 4 * (2 * core + 1) + chip])
    kernel_conv = jnp.take(conv, my_heads, axis=1)
    first = core * half + chip * TILE

    def own(v):
        return lax.dynamic_slice_in_dim(v, first, TILE, 1)

    def dot(a, b, ca, cb):
        return lax.dot_general(a, b, (((ca,), (cb,)), ((), ())), preferred_element_type=f32)

    stream = xs.reshape(width, seq).astype(f32)
    inverse_one = lax.rsqrt(jnp.mean(stream * stream, 0) + EPSILON)
    low_one = (stream * inverse_one[None] * gain_one).astype(bf16)
    projected = dot(w_in.reshape(heads * HEADROWS, width), low_one, 1, 0)
    projected = projected.reshape(heads, HEADROWS, seq).transpose(2, 0, 1)
    query = projected[:, :, :FEAT].astype(bf16)
    keys = projected[:, :, FEAT : 2 * FEAT].astype(bf16)
    raw_values = projected[:, :, 2 * FEAT :]
    offsets = jnp.arange(seq, dtype=jnp.int32)
    values = convolve(raw_values, kernel_conv, offsets).astype(bf16)
    pieces = (query, keys, values, offsets)
    attended = attend_bin(pieces).reshape(seq, heads * HDIM).astype(bf16)
    part = dot(w_back.reshape(heads * HDIM, width), attended, 0, 1).astype(bf16)
    branch_mix = plane_sum(part.reshape(4, rows, seq), 3).reshape(width, TILE)
    stream_own = own(stream)
    middle = stream_own + branch_mix
    inverse_two = lax.rsqrt(jnp.mean(middle * middle, 0) + EPSILON)[None]
    low_two_own = (middle * inverse_two * gain_two).astype(bf16)
    low_two = plane_gather(low_two_own.reshape(4, rows, TILE), 4).reshape(width, seq)
    gate = dot(wg, low_two, 0, 0)
    up_proj = dot(wu, low_two, 0, 0)
    gate_sigmoid = jax.nn.sigmoid(gate)
    activated = gate * gate_sigmoid
    hidden = (activated * up_proj).astype(bf16)
    part = dot(wd, hidden, 1, 0).astype(bf16)
    branch_ffn = plane_sum(part.reshape(4, rows, seq), 5).reshape(width, TILE)
    result_full = middle + branch_ffn
    grad_result = gs.reshape(width, seq)
    grad_down = dot(grad_result, hidden, 1, 1).astype(bf16)
    grad_hidden = dot(wd, grad_result, 0, 0)
    grad_gate_part = (
        grad_hidden * up_proj * gate_sigmoid * (1.0 + gate * (1.0 - gate_sigmoid))
    ).astype(bf16)
    grad_up_part = (grad_hidden * activated).astype(bf16)
    grad_gate = dot(low_two, grad_gate_part, 1, 1).astype(bf16)
    grad_up = dot(low_two, grad_up_part, 1, 1).astype(bf16)
    part = (dot(wg, grad_gate_part, 1, 0) + dot(wu, grad_up_part, 1, 0)).astype(bf16)
    grad_normed_two = plane_sum(part.reshape(4, rows, seq), 6).reshape(width, TILE)
    dots_two = jnp.sum(grad_normed_two * gain_two * middle, 0)[None]
    grad_middle = own(grad_result).astype(f32) + (
        grad_normed_two * gain_two * inverse_two
        - middle * (inverse_two * inverse_two * inverse_two * dots_two / D)
    )
    gain_part_two = jnp.sum(grad_normed_two * middle * inverse_two, 1)
    g_mid = plane_gather(grad_middle.astype(bf16).reshape(4, rows, TILE), 7).reshape(width, seq)
    grad_out = dot(attended, g_mid, 0, 1).astype(bf16)
    grad_attended = dot(w_back.reshape(heads * HDIM, width), g_mid, 1, 0).astype(bf16)
    grad_attended = grad_attended.reshape(heads, HDIM, seq).transpose(2, 0, 1)
    grad_query, grad_keys, grad_values = attend_back(pieces + (grad_attended,))
    grad_raw, conv_part = convolve_back(grad_values, raw_values, kernel_conv, offsets)
    grad_projected = jnp.concatenate([grad_query, grad_keys, grad_raw], 2)
    grad_projected = grad_projected.reshape(seq, heads * HEADROWS).astype(bf16)
    grad_qkv = dot(grad_projected, low_one, 0, 1).astype(bf16)
    part = dot(w_in.reshape(heads * HEADROWS, width), grad_projected, 0, 1).astype(bf16)
    grad_normed_one = plane_sum(part.reshape(4, rows, seq), 8).reshape(width, TILE)
    inverse_own = lax.dynamic_slice_in_dim(inverse_one, first, TILE, 0)[None]
    dots_one = jnp.sum(grad_normed_one * gain_one * stream_own, 0)[None]
    grad_tokens = grad_middle + (
        grad_normed_one * gain_one * inverse_own
        - stream_own * (inverse_own * inverse_own * inverse_own * dots_one / D)
    )
    gain_part_one = jnp.sum(grad_normed_one * stream_own * inverse_own, 1)
    grad_ff = jnp.stack([grad_gate, grad_up, grad_down]).reshape(3, 4, rows, 5 * TILE)
    grad_at = jnp.concatenate(
        [grad_qkv.reshape(heads, HEADROWS, 4, rows), grad_out.reshape(heads, HDIM, 4, rows)], 1
    ).transpose(0, 2, 1, 3)
    out_ff, out_at, out_res, out_tok = scatter_out(
        grad_ff,
        grad_at,
        result_full.astype(bf16).reshape(4, rows, TILE),
        grad_tokens.astype(bf16).reshape(4, rows, TILE),
    )
    conv_all = jnp.zeros(conv.shape, f32).at[:, my_heads].set(conv_part)
    squares = jnp.stack(
        [
            jnp.sum(branch_mix * branch_mix),
            jnp.sum(branch_ffn * branch_ffn),
            jnp.sum(result_full * result_full),
        ]
    )
    conv_all, gain_one_all, gain_two_all, squares = lax.psum(
        (conv_all.reshape(CONV, -1), gain_part_one, gain_part_two, squares), ("row", "col")
    )
    conv_cols = conv_weight.shape[1]
    grad_conv = lax.dynamic_slice_in_dim(
        conv_all, lax.axis_index("col") * conv_cols, conv_cols, 1
    )
    pick = lambda v: lax.dynamic_slice_in_dim(v, chip * rows, rows, 0)
    out_at = out_at.astype(f32)
    return (
        out_res,
        out_tok.astype(f32),
        out_at[:, :HEADROWS].reshape(heads * HEADROWS, rows).T,
        grad_conv,
        out_at[:, HEADROWS:].reshape(heads * HDIM, rows),
        out_ff[0, :, :ffn_cols].astype(f32),
        out_ff[1, :, :ffn_cols].astype(f32),
        out_ff[2, :, :ffn_cols].astype(f32),
        pick(gain_one_all),
        pick(gain_two_all),
        jnp.sqrt(squares / (width * seq * 4)),
    )


def on_device(tokens, cotangent, lengths, deal_order, *weights):
    total_rows = tokens.shape[1] * lax.axis_size("col")
    planes = lax.axis_size("col") // 2
    if (
        lengths.shape[0] * LONGEST == total_rows
        and lax.axis_size("row") == 4
        and planes == 4
        and total_rows == planes * LONGEST
        and weights[0].shape[1] == 2 * (2 * FEAT + HDIM)
        and weights[3].shape[1] <= 5 * TILE
    ):
        return on_device_full(tokens, cotangent, *weights)
    return on_device_general(tokens, cotangent, lengths, deal_order, *weights)


def solution(mesh):
    in_specs = (
        P("row", "col"),
        P("row", "col"),
        P(),
        P(),
        P("row", "col"),
        P(None, "col"),
        P("col", "row"),
        P("row", "col"),
        P("row", "col"),
        P("row", "col"),
        P("row"),
        P("row"),
    )
    out_specs = (
        P("row", "col"),
        P("row", "col"),
        P("row", "col"),
        P(None, "col"),
        P("col", "row"),
        P("row", "col"),
        P("row", "col"),
        P("row", "col"),
        P("row"),
        P("row"),
        P(),
    )
    return jax.shard_map(
        on_device, mesh=mesh, in_specs=in_specs, out_specs=out_specs, check_vma=False
    )
```

```python
import jax
import jax.numpy as jnp
from jax import lax
from jax.experimental import pallas as pl
from jax.experimental.pallas import tpu as pltpu
from jax.sharding import PartitionSpec as P

D = 1792
FEAT = 16
CONV = 3
LONGEST = 1024
HDIM = 112


EPSILON = 1e-06


def dealing(lengths, deal_order, total_rows):
    seq_ids = jnp.arange(lengths.shape[0], dtype=jnp.int32)
    chosen = (deal_order[:, None] == seq_ids[None, :]).astype(jnp.int32)
    dealt_lengths = jnp.sum(chosen * lengths[None, :], 1)
    given_start = jnp.cumsum(lengths) - lengths
    dealt_start = jnp.cumsum(dealt_lengths) - dealt_lengths
    given_of_dealt = jnp.sum(chosen * given_start[None, :], 1)
    dealt_of_given = jnp.sum(chosen * dealt_start[:, None], 0)
    places = jnp.arange(total_rows, dtype=jnp.int32)
    in_dealt = (places[:, None] >= dealt_start[None, :]) & (
        places[:, None] < (dealt_start + dealt_lengths)[None, :]
    )
    in_given = (places[:, None] >= given_start[None, :]) & (
        places[:, None] < (given_start + lengths)[None, :]
    )
    source = places + jnp.sum(jnp.where(in_dealt, (given_of_dealt - dealt_start)[None, :], 0), 1)
    target = places + jnp.sum(jnp.where(in_given, (dealt_of_given - given_start)[None, :], 0), 1)
    offsets = places - jnp.sum(jnp.where(in_dealt, dealt_start[None, :], 0), 1)
    return (source, target, offsets)


def convolve(raw_values, kernel_conv, offsets):
    mixed = kernel_conv[0] * raw_values
    for delay_step in range(1, CONV):
        moved = jnp.concatenate(
            [jnp.zeros_like(raw_values[:delay_step]), raw_values[:-delay_step]], 0
        )
        mixed = mixed + kernel_conv[delay_step] * jnp.where(
            (offsets >= delay_step)[:, None, None], moved, 0.0
        )
    return mixed


def convolve_back(grad_mixed, raw_values, kernel_conv, offsets):
    grad_raw = kernel_conv[0] * grad_mixed
    sums_list = [jnp.sum(grad_mixed * raw_values, 0)]
    for delay_step in range(1, CONV):
        masked = jnp.where((offsets >= delay_step)[:, None, None], grad_mixed, 0.0)
        pulled = jnp.concatenate([masked[delay_step:], jnp.zeros_like(masked[:delay_step])], 0)
        grad_raw = grad_raw + kernel_conv[delay_step] * pulled
        moved = jnp.concatenate(
            [jnp.zeros_like(raw_values[:delay_step]), raw_values[:-delay_step]], 0
        )
        sums_list.append(jnp.sum(masked * moved, 0))
    return (grad_raw, jnp.stack(sums_list))


def bin_scores(query, keys, offsets):
    scores = jnp.einsum("thf,shf->hts", query, keys, preferred_element_type=jnp.float32) * FEAT ** (
        -0.5
    )
    positions = jnp.arange(query.shape[0], dtype=jnp.int32)
    visible = (positions[None, :] <= positions[:, None]) & (
        positions[:, None] - positions[None, :] <= offsets[:, None]
    )
    kernel = jnp.where(visible[None], 1.0 + scores + 0.5 * scores * scores, 0.0)
    return (scores, visible, kernel)


def attend_bin(pieces):
    query, keys, values, offsets = pieces
    scores, visible, kernel = bin_scores(query, keys, offsets)
    weights = (kernel / jnp.sum(kernel, -1, keepdims=True)).astype(jnp.bfloat16)
    return jnp.einsum("hts,shd->thd", weights, values, preferred_element_type=jnp.float32)


def attend_back(pieces):
    query, keys, values, offsets, grad_attend = pieces
    scores, visible, kernel = bin_scores(query, keys, offsets)
    totals = jnp.sum(kernel, -1, keepdims=True)
    weights = kernel / totals
    grad_weights = jnp.einsum(
        "thd,shd->hts", grad_attend, values, preferred_element_type=jnp.float32
    )
    grad_values = jnp.einsum(
        "hts,thd->shd",
        weights.astype(jnp.bfloat16),
        grad_attend,
        preferred_element_type=jnp.float32,
    )
    grad_kernel = (grad_weights - jnp.sum(grad_weights * weights, -1, keepdims=True)) / totals
    grad_scores = jnp.where(visible[None], grad_kernel * (1.0 + scores), 0.0).astype(jnp.bfloat16)
    grad_query = jnp.einsum(
        "hts,shf->thf", grad_scores, keys, preferred_element_type=jnp.float32
    ) * FEAT ** (-0.5)
    grad_keys = jnp.einsum(
        "hts,thf->shf", grad_scores, query, preferred_element_type=jnp.float32
    ) * FEAT ** (-0.5)
    return (grad_query, grad_keys, grad_values)


def times_transposed(left, right):
    return lax.dot_general(
        left, right, (((1,), (1,)), ((), ())), preferred_element_type=jnp.float32
    )


def tokens_product(left, right):
    return lax.dot_general(
        left, right, (((0,), (0,)), ((), ())), preferred_element_type=jnp.float32
    )


def plain_product(left, right):
    return jnp.dot(left, right, preferred_element_type=jnp.float32)


def gather_cols(values):
    return lax.all_gather(values, "col", axis=0, tiled=True)


def gather_rows(values):
    return lax.all_gather(values, "row", axis=0, tiled=True)


def grad_gather_cols(values):
    return lax.all_gather(values, "col", axis=1, tiled=True)


def grad_gather_rows(values):
    return lax.all_gather(values, "row", axis=0, tiled=True)


def width_total(values):
    return lax.psum(values, "row")


def forward_rows(gathered, row_index, weight, rows_here):

    def partial_term(row_start, row_count):
        picked = jnp.take(gathered, row_index, axis=0)
        return jnp.dot(picked, weight, preferred_element_type=jnp.float32)

    return lax.psum_scatter(
        partial_term(jnp.int32(0), rows_here * lax.axis_size("row")),
        "row",
        scatter_dimension=0,
        tiled=True,
    )


def forward_cols(gathered, row_index, weight, rows_here, product):

    def partial_term(row_start, row_count):
        picked = jnp.take(gathered, row_index, axis=0)
        return product(picked, weight)

    return lax.psum_scatter(
        partial_term(jnp.int32(0), lax.axis_size("col") * rows_here).astype(jnp.bfloat16),
        "col",
        scatter_dimension=0,
        tiled=True,
    ).astype(jnp.float32)


def backward_rows(gathered, row_index, weight, rows_here, contract):

    def partial_term(row_start, row_count):
        picked = jnp.take(gathered, row_index, axis=1)
        return lax.dot_general(
            picked, weight, (((0,), (contract,)), ((), ())), preferred_element_type=jnp.float32
        )

    return lax.psum_scatter(
        partial_term(jnp.int32(0), lax.axis_size("row") * rows_here).astype(jnp.bfloat16),
        "row",
        scatter_dimension=0,
        tiled=True,
    ).astype(jnp.float32)


def backward_cols(gathered, row_index, weight, rows_here):

    def partial_term(row_start, row_count):
        picked = jnp.take(gathered, row_index, axis=0)
        return times_transposed(picked, weight)

    return lax.psum_scatter(
        partial_term(jnp.int32(0), lax.axis_size("col") * rows_here).astype(jnp.bfloat16),
        "col",
        scatter_dimension=0,
        tiled=True,
    ).astype(jnp.float32)


def norm_forward(values, norm_gain):
    totals = width_total(jnp.sum(values * values, -1))
    inverse = lax.rsqrt(totals / D + EPSILON)
    return (values * inverse[:, None] * norm_gain, inverse)


def norm_back(values, inverse, norm_gain, grad_normed, dot_sums):
    cubed = inverse * inverse * inverse
    return grad_normed * norm_gain * inverse[:, None] - values * (cubed * dot_sums / D)[:, None]


def on_device_general(
    tokens,
    cotangent,
    lengths,
    deal_order,
    w_qkv,
    conv_weight,
    w_out,
    w_gate,
    w_up,
    w_down,
    gain_mix,
    gain_ffn,
):
    local_rows = tokens.shape[1]
    total_rows = local_rows * lax.axis_size("col")
    group_rows = total_rows // lax.axis_size("row")
    bin_count = group_rows // LONGEST
    heads_here = w_out.shape[0] // HDIM
    ffn_cols = w_gate.shape[1]
    source, target, offsets = dealing(lengths, deal_order, total_rows)
    group_offsets = lax.dynamic_slice_in_dim(
        offsets, lax.axis_index("row") * group_rows, group_rows
    )
    inputs = tokens.astype(jnp.float32).T
    gain_one = gain_mix.astype(jnp.float32)
    gain_two = gain_ffn.astype(jnp.float32)
    both_weights = jnp.concatenate([w_gate, w_up], 1)
    normed_one, inverse_one = norm_forward(inputs, gain_one)
    low_one = normed_one.astype(jnp.bfloat16)
    all_one = gather_cols(low_one)
    projected = forward_rows(all_one, source, w_qkv, group_rows)
    projected = projected.reshape(group_rows, heads_here, 2 * FEAT + HDIM)
    query = projected[:, :, :FEAT].astype(jnp.bfloat16)
    keys = projected[:, :, FEAT : 2 * FEAT].astype(jnp.bfloat16)
    raw_values = projected[:, :, 2 * FEAT :]
    kernel_conv = conv_weight.astype(jnp.float32).reshape(CONV, heads_here, HDIM)
    values = convolve(raw_values, kernel_conv, group_offsets).astype(jnp.bfloat16)
    binned = (
        query.reshape(bin_count, LONGEST, heads_here, FEAT),
        keys.reshape(bin_count, LONGEST, heads_here, FEAT),
        values.reshape(bin_count, LONGEST, heads_here, HDIM),
        group_offsets.reshape(bin_count, LONGEST),
    )
    attended = (
        lax.map(attend_bin, binned).reshape(group_rows, heads_here * HDIM).astype(jnp.bfloat16)
    )
    all_attended = gather_rows(attended)
    branch_mix = forward_cols(all_attended, target, w_out, local_rows, plain_product)
    middle = inputs + branch_mix
    normed_two, inverse_two = norm_forward(middle, gain_two)
    low_two = normed_two.astype(jnp.bfloat16)
    all_two = gather_cols(low_two)
    gate_up = forward_rows(all_two, source, both_weights, group_rows)
    gate = gate_up[:, :ffn_cols]
    up_proj = gate_up[:, ffn_cols:]
    activated = jax.nn.silu(gate)
    hidden = (activated * up_proj).astype(jnp.bfloat16)
    all_hidden = gather_rows(hidden)
    branch_ffn = forward_cols(all_hidden, target, w_down, local_rows, times_transposed)
    result_full = middle + branch_ffn
    grad_result = cotangent.astype(jnp.float32).T
    all_grad_ffn = grad_gather_cols(cotangent)
    hidden_again = gather_rows(hidden)
    grad_down = jnp.dot(
        jnp.take(all_grad_ffn, source, axis=1), hidden_again, preferred_element_type=jnp.float32
    )
    grad_hidden = backward_rows(all_grad_ffn, source, w_down, group_rows, 0)
    gate_sigmoid = jax.nn.sigmoid(gate)
    grad_gate_part = grad_hidden * up_proj * gate_sigmoid * (1.0 + gate * (1.0 - gate_sigmoid))
    grad_up_part = grad_hidden * activated
    grad_gate_up = jnp.concatenate([grad_gate_part, grad_up_part], 1).astype(jnp.bfloat16)
    all_grad_gate_up = grad_gather_rows(grad_gate_up)
    two_again = gather_cols(low_two)
    grad_both = tokens_product(jnp.take(two_again, source, axis=0), all_grad_gate_up)
    grad_normed_two = backward_cols(all_grad_gate_up, target, both_weights, local_rows)
    dots_two = width_total(jnp.sum(grad_normed_two * gain_two * middle, -1))
    grad_middle = grad_result + norm_back(middle, inverse_two, gain_two, grad_normed_two, dots_two)
    gain_part_two = jnp.sum(grad_normed_two * middle * inverse_two[:, None], 0)
    low_grad_middle = grad_middle.T.astype(jnp.bfloat16)
    all_grad_middle = grad_gather_cols(low_grad_middle)
    attended_again = gather_rows(attended)
    grad_out = lax.dot_general(
        attended_again,
        jnp.take(all_grad_middle, source, axis=1),
        (((0,), (1,)), ((), ())),
        preferred_element_type=jnp.float32,
    )
    grad_attended = backward_rows(all_grad_middle, source, w_out, group_rows, 1).astype(
        jnp.bfloat16
    )
    binned_back = binned + (grad_attended.reshape(bin_count, LONGEST, heads_here, HDIM),)
    grad_query, grad_keys, grad_values = lax.map(attend_back, binned_back)
    grad_values = grad_values.reshape(group_rows, heads_here, HDIM)
    grad_raw, conv_part = convolve_back(grad_values, raw_values, kernel_conv, group_offsets)
    grad_projected = jnp.concatenate(
        [
            grad_query.reshape(group_rows, heads_here, FEAT),
            grad_keys.reshape(group_rows, heads_here, FEAT),
            grad_raw,
        ],
        2,
    )
    grad_projected = grad_projected.reshape(group_rows, heads_here * (2 * FEAT + HDIM)).astype(
        jnp.bfloat16
    )
    all_grad_projected = grad_gather_rows(grad_projected)
    one_again = gather_cols(low_one)
    grad_qkv = tokens_product(jnp.take(one_again, source, axis=0), all_grad_projected)
    grad_normed_one = backward_cols(all_grad_projected, target, w_qkv, local_rows)
    squares = jnp.stack(
        [
            jnp.sum(branch_mix * branch_mix),
            jnp.sum(branch_ffn * branch_ffn),
            jnp.sum(result_full * result_full),
        ]
    )
    dots_one, grad_conv, squares_rows = width_total(
        (
            jnp.sum(grad_normed_one * gain_one * inputs, -1),
            conv_part.reshape(CONV, heads_here * HDIM),
            squares,
        )
    )
    grad_tokens = grad_middle + norm_back(inputs, inverse_one, gain_one, grad_normed_one, dots_one)
    gain_part_one = jnp.sum(grad_normed_one * inputs * inverse_one[:, None], 0)
    grad_gain_mix, grad_gain_ffn, squares_all = lax.psum(
        (gain_part_one, gain_part_two, squares_rows), "col"
    )
    rms_values = jnp.sqrt(squares_all / (total_rows * D))
    return (
        result_full.T.astype(jnp.bfloat16),
        grad_tokens.T,
        grad_qkv,
        grad_conv,
        grad_out,
        grad_both[:, :ffn_cols],
        grad_both[:, ffn_cols:],
        grad_down,
        grad_gain_mix,
        grad_gain_ffn,
        rms_values,
    )


HEADROWS = 2 * FEAT + HDIM
BLOCKROWS = HEADROWS + HDIM
TILE = 128
WIDE = 512
SPAN = 256
MARKS = 320
MESH = pl.DeviceIdType.MESH
ANY = pl.BlockSpec(memory_space=pl.ANY)
F32, BF16 = jnp.float32, jnp.bfloat16


def place():
    column = lax.axis_index("col")
    return lax.axis_index("row"), column // 2, column % 2


def device(chip, plane, core):
    return (chip, plane * 2 + core)


def other_chips(chip):
    y, x = chip // 2, chip % 2
    return (y * 2 + 1 - x, (1 - y) * 2 + x, (1 - y) * 2 + 1 - x)


def away(plane, step):
    if step == 1:
        return plane + 1 - 2 * (plane % 2)
    if step == 2:
        return (plane + 2) % 4
    return 3 - plane


def is_inner(plane):
    return ((plane + 1) // 2) % 2 == 1


def remote(source, target, send, receive, to):
    return pltpu.make_async_remote_copy(
        src_ref=source,
        dst_ref=target,
        send_sem=send,
        recv_sem=receive,
        device_id=to,
        device_id_type=MESH,
    )


def lanes(start, size=TILE):
    return pl.ds(pl.multiple_of(start, TILE), size)


def rows_at(start, size, step):
    return pl.ds(pl.multiple_of(start, step), size)


def no(flag):
    return jnp.logical_not(flag)


def dot(a, b, over_a, over_b):
    return lax.dot_general(
        a, b, (((over_a,), (over_b,)), ((), ())), preferred_element_type=F32
    )


class Marks:
    def __init__(self, ref):
        self.ref, self.used = ref, 0

    def one(self):
        self.used += 1
        return self.ref.at[self.used - 1]

    def many(self, count):
        base = self.used
        self.used += count
        return lambda i: self.ref.at[base + i]


class Spread:
    def __init__(self, ref, owner, chip, plane, core, marks):
        self.ref, self.owner, self.spot = ref, owner, (chip, plane, core)
        self.sends = marks.many(4)
        self.arrived = marks.one()
        self.mine = plane == owner
        self.relays = is_inner(plane) & (plane == away(owner, 2))

    def copy(self, step, send):
        chip, plane, core = self.spot
        return remote(
            self.ref, self.ref, self.sends(send), self.arrived,
            device(chip, away(plane, step), core),
        )

    def start(self, also=True):
        @pl.when(also & self.mine)
        def _():
            self.copy(1, 0).start()
            self.copy(2, 1).start()

        @pl.when(also & self.mine & is_inner(self.spot[1]))
        def _():
            self.copy(3, 2).start()

    def relay(self, also=True):
        @pl.when(also & self.relays)
        def _():
            self.copy(1, 3).wait_recv()
            self.copy(1, 3).start()

    def arrive(self, also=True):
        @pl.when(also & no(self.mine) & no(self.relays))
        def _():
            self.copy(1, 3).wait_recv()

    def finish(self, also=True):
        @pl.when(also & self.mine)
        def _():
            self.copy(1, 0).wait_send()
            self.copy(2, 1).wait_send()

        @pl.when(also & self.mine & is_inner(self.spot[1]))
        def _():
            self.copy(3, 2).wait_send()

        @pl.when(also & self.relays)
        def _():
            self.copy(1, 3).wait_send()


class Collect:
    def __init__(self, ref, slots, owner, chip, plane, core, marks):
        self.ref, self.slots, self.owner, self.spot = ref, slots, owner, (chip, plane, core)
        self.send = marks.one()
        self.arrived = marks.many(4)
        outer = no(is_inner(owner))
        self.mine = plane == owner
        self.first = plane == away(owner, 1)
        self.second = plane == away(owner, 2)
        self.third = plane == away(owner, 3)
        self.outer = outer

    def copy(self, step, slot):
        chip, plane, core = self.spot
        return remote(
            self.ref, self.slots.at[slot], self.send, self.arrived(slot),
            device(chip, away(plane, step), core),
        )

    def start(self, add):
        @pl.when(self.first)
        def _():
            self.copy(1, 0).start()

        @pl.when(self.third & self.outer)
        def _():
            self.copy(1, 3).start()

        @pl.when(self.third & no(self.outer))
        def _():
            self.copy(3, 2).start()

        @pl.when(self.second & no(self.outer))
        def _():
            self.copy(2, 1).start()

    def relay(self, add):
        @pl.when(self.second & self.outer)
        def _():
            self.copy(1, 3).wait_recv()
            add(self.slots.at[3])
            self.copy(2, 1).start()

    def total(self, add):
        @pl.when(self.mine)
        def _():
            self.copy(1, 0).wait_recv()
            add(self.slots.at[0])
            self.copy(1, 1).wait_recv()
            add(self.slots.at[1])

        @pl.when(self.mine & no(self.outer))
        def _():
            self.copy(1, 2).wait_recv()
            add(self.slots.at[2])

    def finish(self):
        @pl.when(no(self.mine))
        def _():
            self.copy(1, 0).wait_send()


def layer_kernel(
    wff, wat, tok, cot, gains,
    out_ff, out_at, out_res, out_tok, out_small, main_got, extra_got, att_got,
    ff, at, xs, gs, low2, part, acc3, gout, gat, from_mate, both, got, turned, hid, gg,
    gn, raw, qs, ks, vs, att, gatt, gproj, mid, gmid, normed, inv_all, inv_sum, small, small_a,
    small_b, sem, free_mate, free_chips,
):
    chip, plane, core = place()
    others = other_chips(chip)
    mate = device(chip, plane, 1 - core)
    marks = Marks(sem)
    rows = tok.shape[0]
    width = 4 * rows
    half = tok.shape[1]
    seq = 2 * half
    own_half = lanes(core * half, half)
    first = core * half + chip * TILE
    peers = [device(c, plane, core) for c in others]
    line = [device(chip, away(plane, step), core) for step in (1, 2, 3)]
    sides = [device(c, plane, 1 - core) for c in others]
    line_mates = [device(chip, away(plane, step), 1 - core) for step in (1, 2, 3)]

    barrier = pltpu.get_barrier_semaphore()
    partners = peers + [mate] + sides + line + line_mates
    for partner in partners:
        pl.semaphore_signal(barrier, inc=1, device_id=partner, device_id_type=MESH)
    pl.semaphore_wait(barrier, len(partners))

    def block_rows(c):
        return rows_at(c * rows, rows, rows)

    far_core = plane // 2
    holds_att = core == far_core
    holds_extra = holds_att & (chip // 2 == plane % 2)
    extra_plane = 2 * core + chip // 2
    extra_chip = (plane % 2) * 2 + core
    att_send, att_here = marks.many(2), marks.many(4)
    att_local = marks.one()

    def att_copy(h):
        return remote(
            wat.at[h], at.at[plane % 2, chip], att_send(h), att_here(chip),
            device(2 * core + h, plane, far_core),
        )

    def att_keep(h):
        return pltpu.make_async_copy(wat.at[h], at.at[plane % 2, chip], att_local)

    att_self = [(2 * core + h == chip) & holds_att for h in range(2)]
    for h in range(2):

        @pl.when(att_self[h])
        def _():
            att_keep(h).start()

        @pl.when(no(att_self[h]))
        def _():
            att_copy(h).start()

    def plane_spread(source, target_of, to_mate=True):
        send, receive = marks.many(3), marks.many(3)
        mate_send, mate_receive = marks.many(4), marks.many(4)
        keep = pltpu.make_async_copy(source, target_of(chip), marks.one())
        keep.start()
        copies = [
            remote(source, target_of(chip), send(p), receive(p), peers[p]) for p in range(3)
        ]
        for copy in copies:
            copy.start()
        crossing = []
        if to_mate:
            crossing.append(
                remote(source, target_of(chip), mate_send(3), mate_receive(3), mate)
            )
            crossing[0].start()

        def pass_on():
            for p in range(3):
                copies[p].wait_recv()
                if to_mate:
                    block = target_of(others[p])
                    crossing.append(remote(block, block, mate_send(p), mate_receive(p), mate))
                    crossing[-1].start()

        def finish():
            keep.wait()
            for copy in copies:
                copy.wait_send()
            for copy in crossing:
                copy.wait()

        return pass_on, finish

    tok_pass, tok_finish = plane_spread(tok, lambda c: xs.at[block_rows(c), own_half])
    gn_pass, gn_finish = plane_spread(gains, lambda c: gn.at[block_rows(c)], to_mate=False)

    main_send, main_here, main_local = marks.many(3), marks.many(3), marks.one()
    mains = []
    main_here_at = ff.at[:, block_rows(chip), lanes(plane * TILE)]
    for p in range(3):
        mains.append(
            remote(
                wff.at[:, :, lanes(others[p] * TILE)], main_here_at,
                main_send(p), main_here(p), peers[p],
            )
        )
        mains[-1].start()
    main_keep = pltpu.make_async_copy(wff.at[:, :, lanes(chip * TILE)], main_here_at, main_local)
    main_keep.start()

    extra_send, extra_here, extra_local = marks.one(), marks.many(4), marks.one()
    extra_self = (extra_chip == chip) & holds_att
    last = lanes(4 * TILE)

    def extra_copy():
        return remote(
            wff.at[:, :, last], ff.at[:, block_rows(chip), last], extra_send, extra_here(chip),
            device(extra_chip, plane, far_core),
        )

    def extra_keep():
        return pltpu.make_async_copy(
            wff.at[:, :, last], ff.at[:, block_rows(chip), last], extra_local
        )

    @pl.when(extra_self)
    def _():
        extra_keep().start()

    @pl.when(no(extra_self))
    def _():
        extra_copy().start()

    for h in range(2):

        @pl.when(att_self[h])
        def _():
            att_keep(h).wait()

        @pl.when(no(att_self[h]))
        def _():
            att_copy(h).wait_send()

    for c in range(4):

        @pl.when(holds_att & no((c == chip) & (core == chip // 2)))
        def _():
            remote(
                wat.at[0], at.at[plane % 2, c], att_send(0), att_here(c), mate
            ).wait_recv()

    att_line = [
        Spread(at.at[a], 2 * core + a, chip, plane, core, marks) for a in range(2)
    ]
    for item in att_line:
        item.start()

    tok_pass()
    gn_pass()
    gn_finish()
    tok_finish()
    cot_pass, cot_finish = plane_spread(cot, lambda c: gs.at[block_rows(c), own_half])

    main_keep.wait()
    for copy in mains:
        copy.wait()
    main_line = [
        Spread(ff.at[:, :, lanes(o * TILE)], o, chip, plane, core, marks) for o in range(4)
    ]
    for item in main_line:
        item.start()

    @pl.when(extra_self)
    def _():
        extra_keep().wait()

    @pl.when(no(extra_self))
    def _():
        extra_copy().wait_send()

    for c in range(4):

        @pl.when(holds_extra & no((c == chip) & (core == chip % 2)))
        def _():
            remote(
                wff.at[:, :, last], ff.at[:, block_rows(c), last], extra_send, extra_here(c), mate
            ).wait_recv()

    extra_line = Spread(ff.at[:, :, last], extra_plane, chip, plane, core, marks)
    extra_line.start()

    step_rows = 64

    def add_squares(i, total):
        x = xs[rows_at(i * step_rows, step_rows, step_rows)].astype(F32)
        return total + jnp.sum((x * x).reshape(step_rows // 8, 8, seq), 0)

    squares = lax.fori_loop(0, width // step_rows, add_squares, jnp.zeros((8, seq), F32))
    inv_all[...] = lax.rsqrt(jnp.sum(squares, 0, keepdims=True) / D + EPSILON)
    mid[...] = xs[:, lanes(first)].astype(F32)

    @pl.loop(0, width // step_rows)
    def _(i):
        at_rows = rows_at(i * step_rows, step_rows, step_rows)
        gain = gn[at_rows, 0:1].astype(F32)
        xs[at_rows] = (xs[at_rows].astype(F32) * inv_all[...] * gain).astype(BF16)

    for item in att_line:
        item.relay()
    for item in att_line:
        item.arrive()

    position = lax.broadcasted_iota(jnp.int32, (1, seq), 1)
    tail = lax.broadcasted_iota(jnp.int32, (HDIM, TILE), 1)

    def taps(h):
        columns = at[h, 0, HEADROWS:BLOCKROWS, WIDE - TILE : WIDE].astype(F32)
        return [columns[:, rows % TILE + j : rows % TILE + j + 1] for j in range(CONV)]

    @pl.loop(0, 2)
    def _(h):
        projected = dot(at[h, 0, :HEADROWS, :rows], xs[0:rows], 1, 0)
        for c in range(1, 4):
            projected += dot(at[h, c, :HEADROWS, :rows], xs[c * rows : (c + 1) * rows], 1, 0)
        qs[h] = (projected[:FEAT].astype(BF16).astype(F32) * FEAT**-0.5).astype(BF16)
        ks[h] = projected[FEAT : 2 * FEAT].astype(BF16)
        values = projected[2 * FEAT :]
        raw[h] = values
        tap = taps(h)
        mixed = tap[0] * values
        for j in range(1, CONV):
            moved = pltpu.roll(values, j, 1)
            mixed += tap[j] * jnp.where(position >= j, moved, 0.0)
        vs[h] = mixed.astype(BF16)

    def kernel_of(h, b):
        seen = (b + 1) * SPAN
        scores = dot(ks[h, :, :seen], qs[h, :, b * SPAN : seen], 0, 0)
        kernel = 1.0 + scores + 0.5 * scores * scores
        key_at = lax.broadcasted_iota(jnp.int32, (seen, SPAN), 0)
        query_at = lax.broadcasted_iota(jnp.int32, (seen, SPAN), 1) + b * SPAN
        visible = key_at <= query_at
        return scores, jnp.where(visible, kernel, 0.0), visible

    @pl.loop(0, 2)
    def _(h):
        for b in range(seq // SPAN):
            seen = (b + 1) * SPAN
            _, kernel, _ = kernel_of(h, b)
            inverse = 1.0 / jnp.sum(kernel, 0, keepdims=True)
            inv_sum[h, :, b * SPAN : seen] = inverse
            weights = (kernel * inverse).astype(BF16)
            att[h, :, b * SPAN : seen] = dot(vs[h, :, :seen], weights, 1, 0).astype(BF16)

    def plane_sum(fill, store, guard):
        fill((1 - core) * half)
        to_mate = remote(
            part.at[:, lanes((1 - core) * half, half)], from_mate,
            marks.one(), marks.one(), mate,
        )
        if guard:
            pl.semaphore_wait(free_mate, 1)
        to_mate.start()
        fill(core * half)
        to_mate.wait_recv()

        @pl.loop(0, 4)
        def _(c):
            both[block_rows(c)] = (
                part[block_rows(c), own_half].astype(F32) + from_mate[block_rows(c)].astype(F32)
            ).astype(BF16)

        pl.semaphore_signal(free_mate, inc=1, device_id=mate, device_id_type=MESH)
        if guard:
            pl.semaphore_wait(free_chips, 3)
        send, receive = marks.many(3), marks.many(3)
        copies = [
            remote(
                both.at[:, lanes(others[p] * TILE)], got.at[p], send(p), receive(p), peers[p]
            )
            for p in range(3)
        ]
        for copy in copies:
            copy.start()

        def finish():
            for copy in copies:
                copy.wait()

            @pl.loop(0, 4)
            def _(c):
                at_rows = block_rows(c)
                total = both[at_rows, lanes(chip * TILE)].astype(F32)
                for p in range(3):
                    total += got[p, at_rows].astype(F32)
                store(at_rows, total)

            for p in range(3):
                pl.semaphore_signal(free_chips, inc=1, device_id=peers[p], device_id_type=MESH)
            to_mate.wait_send()

        return finish

    def fill_branch(start):
        @pl.loop(0, 4)
        def _(c):
            where = lanes(start, half)
            total = dot(at[0, c, HEADROWS:, :rows], att[0, :, where], 0, 0)
            total += dot(at[1, c, HEADROWS:, :rows], att[1, :, where], 0, 0)
            part[block_rows(c), where] = total.astype(BF16)

    small[...] = jnp.zeros(small.shape, F32)
    square_at = lax.broadcasted_iota(jnp.int32, (1, WIDE), 1)

    def note_square(index, value):
        total = jnp.sum(value * value)
        small[0, 2:3, :] += jnp.where(square_at == index, total, 0.0)

    def store_branch(at_rows, total):
        note_square(0, total)
        gmid[at_rows] = total

    finish = plane_sum(fill_branch, store_branch, guard=False)
    cot_pass()
    finish()
    normed[...] = mid[...].astype(BF16)
    mid[...] += gmid[...]
    middle = mid[...]
    inverse_two = lax.rsqrt(jnp.sum(middle * middle, 0, keepdims=True) / D + EPSILON)
    gain_at = TILE // 2

    @pl.loop(0, 4)
    def _(c):
        at_rows = block_rows(c)
        gain = gn[at_rows, gain_at : gain_at + 1].astype(F32)
        both[at_rows, 0:TILE] = (mid[at_rows] * inverse_two * gain).astype(BF16)

    low_pass, low_finish = plane_spread(
        both.at[:, 0:TILE], lambda c: low2.at[:, lanes(core * half + c * TILE)]
    )
    cot_finish()
    low_pass()
    low_finish()

    @pl.loop(0, 4)
    def _(c):
        acc3[block_rows(c)] = jnp.zeros((rows, seq), F32)

    def feed(slot):
        where = lanes(slot * TILE)
        unit_rows = rows_at(slot * TILE, TILE, TILE)
        for m in range(3):
            turned[m * TILE : (m + 1) * TILE] = ff[m, :, where].T

        @pl.loop(0, seq // SPAN)
        def _(n):
            span = lanes(n * SPAN, SPAN)
            gate_up = dot(turned[: 2 * TILE], low2[:, span], 1, 0)
            grad_hidden = dot(turned[2 * TILE :], gs[:, span], 1, 0)
            gate, up = gate_up[:TILE], gate_up[TILE:]
            sigmoid = 1.0 / (1.0 + jnp.exp(-gate))
            activated = gate * sigmoid
            hid[unit_rows, span] = (activated * up).astype(BF16)
            gg[:TILE, span] = (
                grad_hidden * up * sigmoid * (1.0 + gate * (1.0 - sigmoid))
            ).astype(BF16)
            gg[TILE:, span] = (grad_hidden * activated).astype(BF16)

        @pl.loop(0, 4)
        def _(c):
            at_rows = block_rows(c)
            pair = jnp.concatenate([ff[0, at_rows, where], ff[1, at_rows, where]], 1)
            acc3[at_rows] += dot(pair, gg[...], 1, 0)
            grads = dot(low2[at_rows], gg[...], 1, 1).astype(BF16)
            gout[0, at_rows, where] = grads[:, :TILE]
            gout[1, at_rows, where] = grads[:, TILE:]
            gout[2, at_rows, where] = dot(gs[at_rows], hid[unit_rows], 1, 1).astype(BF16)

    main_back = [
        Collect(
            gout.at[:, :, lanes(o * TILE)], main_got, o, chip, plane, core, marks
        )
        for o in range(4)
    ]
    extra_back = Collect(gout.at[:, :, last], extra_got, extra_plane, chip, plane, core, marks)
    load_marks = marks.many(3)

    def add_tiles(slot):
        def add(source):
            loads = [
                pltpu.make_async_copy(source.at[m], part.at[:, lanes(m * TILE)], load_marks(m))
                for m in range(3)
            ]
            for load in loads:
                load.start()
            for load in loads:
                load.wait()
            where = lanes(slot * TILE)

            @pl.loop(0, 4)
            def _(c):
                at_rows = block_rows(c)
                for m in range(3):
                    gout[m, at_rows, where] = (
                        gout[m, at_rows, where].astype(F32)
                        + part[at_rows, m * TILE : (m + 1) * TILE].astype(F32)
                    ).astype(BF16)

        return add

    for item in main_line:
        item.relay()
    for item in main_line:
        item.arrive()
    extra_line.relay()
    extra_line.arrive()

    for step in (1, 0, 2, 3):
        slot = away(plane, step) if step else plane
        feed(slot)
    feed(4)
    for o in range(4):
        main_back[o].start(None)
    extra_back.start(None)
    for o in range(4):
        main_back[o].relay(add_tiles(o))
    extra_back.relay(add_tiles(4))

    def fill_grad_two(start):
        @pl.loop(0, 4)
        def _(c):
            where = lanes(start, half)
            part[block_rows(c), where] = acc3[block_rows(c), where].astype(BF16)

    def store_gmid(at_rows, total):
        gmid[at_rows] = total

    finish = plane_sum(fill_grad_two, store_gmid, guard=True)
    finish()

    def norm_back(source, inverse, gain_lane, small_row, base):
        def add_dots(c, total):
            at_rows = block_rows(c)
            gain = gn[at_rows, gain_lane : gain_lane + 1].astype(F32)
            return total + jnp.sum(gmid[at_rows] * gain * source(at_rows), 0, keepdims=True)

        dots = lax.fori_loop(0, 4, add_dots, jnp.zeros((1, TILE), F32))
        scaled = inverse * inverse * inverse * dots / D

        @pl.loop(0, 4)
        def _(c):
            at_rows = block_rows(c)
            gain = gn[at_rows, gain_lane : gain_lane + 1].astype(F32)
            grad, value = gmid[at_rows], source(at_rows)
            for_gain = jnp.sum((grad * value * inverse).T, 0, keepdims=True)
            small[c, small_row : small_row + 1, 0:rows] = for_gain
            gmid[at_rows] = base(at_rows) + (grad * gain * inverse - value * scaled)

    norm_back(
        lambda r: mid[r], inverse_two, gain_at, 1, lambda r: gs[r, lanes(first)].astype(F32)
    )
    both[:, 0:TILE] = gmid[...].astype(BF16)
    mid_pass, mid_finish = plane_spread(
        both.at[:, 0:TILE], lambda c: low2.at[:, lanes(core * half + c * TILE)]
    )

    def fill_ffn(start):
        @pl.loop(0, 4)
        def _(c):
            where = lanes(start, half)
            part[block_rows(c), where] = dot(
                ff[2, block_rows(c)], hid[:, where], 1, 0
            ).astype(BF16)

    mid_pass()
    mid_finish()

    def store_result(at_rows, total):
        note_square(1, total)
        total = mid[at_rows] + total
        note_square(2, total)
        normed_out = total.astype(BF16)
        both[at_rows, 0:TILE] = normed_out

    finish = plane_sum(fill_ffn, store_result, guard=True)

    @pl.loop(0, 2)
    def _(h):
        total = dot(at[h, 0, HEADROWS:, :rows], low2[0:rows], 1, 0)
        for c in range(1, 4):
            total += dot(at[h, c, HEADROWS:, :rows], low2[c * rows : (c + 1) * rows], 1, 0)
        gatt[h] = total.astype(BF16)

    @pl.loop(0, 2)
    def _(h):
        grad_keys = jnp.zeros((FEAT, seq), F32)
        grad_values = jnp.zeros((HDIM, seq), F32)

        def padded(value):
            short = seq - value.shape[1]
            if not short:
                return value
            return jnp.concatenate([value, jnp.zeros((value.shape[0], short), F32)], 1)

        for b in range(seq // SPAN):
            seen = (b + 1) * SPAN
            span = slice(b * SPAN, seen)
            scores, kernel, visible = kernel_of(h, b)
            inverse = inv_sum[h, :, span]
            weights = kernel * inverse
            grad_weights = dot(vs[h, :, :seen], gatt[h, :, span], 0, 0)
            grad_values += padded(dot(gatt[h, :, span], weights.astype(BF16), 1, 1))
            dots = jnp.sum(grad_weights * weights, 0, keepdims=True)
            grad_kernel = (grad_weights - dots) * inverse
            grad_scores = jnp.where(visible, grad_kernel * (1.0 + scores), 0.0).astype(BF16)
            gproj[h, :FEAT, span] = (
                dot(ks[h, :, :seen], grad_scores, 1, 0) * FEAT**-0.5
            ).astype(BF16)
            grad_keys += padded(dot(qs[h, :, span], grad_scores, 1, 1))
        gproj[h, FEAT : 2 * FEAT] = grad_keys.astype(BF16)
        tap = taps(h)
        grad_raw = tap[0] * grad_values
        sums = [jnp.sum(grad_values * raw[h], 1, keepdims=True)]
        for j in range(1, CONV):
            masked = jnp.where(position >= j, grad_values, 0.0)
            grad_raw += tap[j] * pltpu.roll(masked, seq - j, 1)
            sums.append(jnp.sum(masked * pltpu.roll(raw[h], j, 1), 1, keepdims=True))
        gproj[h, 2 * FEAT :] = grad_raw.astype(BF16)
        columns = jnp.zeros((HDIM, TILE), F32)
        for j in range(CONV):
            columns = jnp.where(tail == rows % TILE + j, sums[j], columns)
        for c in range(4):
            gat[h, c, HEADROWS:, WIDE - TILE :] = columns.astype(BF16)

    finish()
    res_send, res_here = marks.many(3), marks.many(3)
    tok_send, tok_here = marks.many(3), marks.many(3)
    kept = []

    def hand_out(source, target, send, receive):
        copies = [
            remote(
                source.at[block_rows(others[p])], target.at[:, lanes(chip * TILE)],
                send(p), receive(p), peers[p],
            )
            for p in range(3)
        ]
        for copy in copies:
            copy.start()
        kept.append(
            pltpu.make_async_copy(
                source.at[block_rows(chip)], target.at[:, lanes(chip * TILE)], marks.one()
            )
        )
        kept[-1].start()
        return copies

    turned_rows = both.at[:, 0:TILE]
    outs = hand_out(turned_rows, out_res, res_send, res_here)

    def fill_grad_one(start):
        @pl.loop(0, 4)
        def _(c):
            where = lanes(start, half)
            total = dot(at[0, c, :HEADROWS, :rows], gproj[0, :, where], 0, 0)
            total += dot(at[1, c, :HEADROWS, :rows], gproj[1, :, where], 0, 0)
            part[block_rows(c), where] = total.astype(BF16)

    acc3[:, 0:TILE] = gmid[...]
    for copy in outs:
        copy.wait()
    for copy in kept:
        copy.wait()
    finish = plane_sum(fill_grad_one, store_gmid, guard=True)

    @pl.loop(0, 2)
    def _(h):
        for c in range(4):
            block = slice(c * rows, (c + 1) * rows)
            gat[h, c, :HEADROWS, :rows] = dot(gproj[h], xs[block], 1, 1).astype(BF16)
            grad = dot(att[h], low2[block], 1, 1).astype(BF16)
            whole = rows // TILE * TILE
            gat[h, c, HEADROWS:, :whole] = grad[:, :whole]
            gat[h, c, HEADROWS:, whole:rows] = grad[:, whole:]

    att_back = [
        Collect(gat.at[a], att_got.at[a], 2 * core + a, chip, plane, core, marks)
        for a in range(2)
    ]
    for item in att_back:
        item.start(None)
    finish()

    inverse_own = inv_all[:, lanes(first)]
    norm_back(
        lambda r: normed[r].astype(F32), inverse_own, 0, 0, lambda r: acc3[r, 0:TILE]
    )
    both[:, TILE : 2 * TILE] = gmid[...].astype(BF16)
    outs = hand_out(both.at[:, TILE : 2 * TILE], out_tok, tok_send, tok_here)

    for c in range(1, 4):
        small[c, 2:3] = small[0, 2:3]
    a_send, a_here = marks.many(3), marks.many(3)
    trio = [
        remote(small.at[others[p]], small_a.at[p], a_send(p), a_here(p), peers[p])
        for p in range(3)
    ]
    for copy in trio:
        copy.start()
    for copy in trio:
        copy.wait()
    small_b[0] = small[chip] + small_a[0] + small_a[1] + small_a[2]
    b_send, b_here = marks.many(7), marks.many(7)
    seven = [
        remote(small_b.at[0], small_b.at[1 + i], b_send(i), b_here(i), to)
        for i, to in enumerate(line + [mate] + line_mates)
    ]
    for copy in seven:
        copy.start()

    add_own = add_tiles(plane)
    for o in range(4):
        main_back[o].total(add_own)
    back_send, back_here = marks.many(3), marks.many(3)
    mine = lanes(plane * TILE)
    backs = [
        remote(
            gout.at[:, block_rows(others[p]), mine], out_ff.at[:, :, lanes(chip * TILE)],
            back_send(p), back_here(p), peers[p],
        )
        for p in range(3)
    ]
    for copy in backs:
        copy.start()
    kept.append(
        pltpu.make_async_copy(
            gout.at[:, block_rows(chip), mine], out_ff.at[:, :, lanes(chip * TILE)], marks.one()
        )
    )
    kept[-1].start()

    extra_back.total(add_tiles(4))
    last_send, last_here, last_local = marks.many(4), marks.one(), marks.one()

    def last_copy(c):
        return remote(
            gout.at[:, block_rows(c), last], out_ff.at[:, :, last], last_send(c), last_here,
            device(c, plane, chip % 2),
        )

    def last_keep():
        return pltpu.make_async_copy(
            gout.at[:, block_rows(chip), last], out_ff.at[:, :, last], last_local
        )

    for c in range(4):
        same = (c == chip) & (core == chip % 2)

        @pl.when(holds_extra & same)
        def _():
            last_keep().start()

        @pl.when(holds_extra & no(same))
        def _():
            last_copy(c).start()

    def add_head(a):
        def add(source):
            loads = [
                pltpu.make_async_copy(
                    source.at[c], part.at[c * BLOCKROWS : (c + 1) * BLOCKROWS, 0:WIDE],
                    load_marks(0),
                )
                for c in range(4)
            ]
            for load in loads:
                load.start()
                load.wait()
            for c in range(4):
                gat[a, c] = (
                    gat[a, c].astype(F32)
                    + part[c * BLOCKROWS : (c + 1) * BLOCKROWS, 0:WIDE].astype(F32)
                ).astype(BF16)

        return add

    for a in range(2):
        att_back[a].relay(add_head(a))
    for a in range(2):
        att_back[a].total(add_head(a))
    head_send, head_here, head_local = marks.many(4), marks.many(2), marks.one()

    def head_copy(c):
        return remote(
            gat.at[plane % 2, c], out_at.at[chip % 2], head_send(c), head_here(chip % 2),
            device(c, plane, chip // 2),
        )

    def head_keep():
        return pltpu.make_async_copy(gat.at[plane % 2, chip], out_at.at[chip % 2], head_local)

    for c in range(4):
        same = (c == chip) & (core == chip // 2)

        @pl.when(holds_att & same)
        def _():
            head_keep().start()

        @pl.when(holds_att & no(same))
        def _():
            head_copy(c).start()

    for copy in seven:
        copy.wait()
    total = small_b[0]
    for i in range(7):
        total += small_b[1 + i]
    small_a[0] = total
    small_out = pltpu.make_async_copy(small_a.at[0], out_small, marks.one())
    small_out.start()
    kept.append(small_out)
    for item in att_line + main_line + [extra_line] + main_back + [extra_back] + att_back:
        item.finish()
    for copy in outs + backs:
        copy.wait()
    for copy in kept[1:]:
        copy.wait()
    for c in range(4):
        for holds, same, local, away_copy in (
            (holds_extra, (c == chip) & (core == chip % 2), last_keep, last_copy),
            (holds_att, (c == chip) & (core == chip // 2), head_keep, head_copy),
        ):

            @pl.when(holds & same)
            def _():
                local().wait()

            @pl.when(holds & no(same))
            def _():
                away_copy(c).wait_send()

    @pl.when(no(extra_self))
    def _():
        last_copy(0).wait_recv()

    for h in range(2):

        @pl.when(no(att_self[h]))
        def _():
            remote(
                gat.at[0, 0], out_at.at[h], head_send(0), head_here(h), mate
            ).wait_recv()

    pl.semaphore_wait(free_mate, 1)
    pl.semaphore_wait(free_chips, 3)
    assert marks.used <= MARKS, marks.used


def dma(*shape):
    return pltpu.SemaphoreType.DMA(shape)


def run_layer(wff, wat, tok, cot, gains):
    rows, half = tok.shape
    width, seq = 4 * rows, 2 * half
    shape = jax.ShapeDtypeStruct
    vmem = pltpu.VMEM
    tiles = (3, width, TILE)
    head = (4, BLOCKROWS, WIDE)
    return pl.pallas_call(
        layer_kernel,
        out_shape=[
            shape((3, rows, 5 * TILE), BF16),
            shape((2, BLOCKROWS, WIDE), BF16),
            shape((rows, half), BF16),
            shape((rows, half), BF16),
            shape((8, WIDE), F32),
            shape((4,) + tiles, BF16),
            shape((4,) + tiles, BF16),
            shape((2, 4) + head, BF16),
        ],
        in_specs=[ANY] * 5,
        out_specs=[ANY] * 8,
        scratch_shapes=[
            vmem((3, width, 5 * TILE), BF16),
            vmem((2,) + head, BF16),
            vmem((width, seq), BF16),
            vmem((width, seq), BF16),
            vmem((width, seq), BF16),
            vmem((width, seq), BF16),
            vmem((width, seq), F32),
            vmem((3, width, 5 * TILE), BF16),
            vmem((2,) + head, BF16),
            vmem((width, half), BF16),
            vmem((width, half), BF16),
            vmem((3, width, TILE), BF16),
            vmem((3 * TILE, width), BF16),
            vmem((5 * TILE, seq), BF16),
            vmem((2 * TILE, seq), BF16),
            vmem((width, TILE), BF16),
            vmem((2, HDIM, seq), F32),
            vmem((2, FEAT, seq), BF16),
            vmem((2, FEAT, seq), BF16),
            vmem((2, HDIM, seq), BF16),
            vmem((2, HDIM, seq), BF16),
            vmem((2, HDIM, seq), BF16),
            vmem((2, HEADROWS, seq), BF16),
            vmem((width, TILE), F32),
            vmem((width, TILE), F32),
            vmem((width, TILE), BF16),
            vmem((1, seq), F32),
            vmem((2, 1, seq), F32),
            vmem((4, 8, WIDE), F32),
            vmem((3, 8, WIDE), F32),
            vmem((8, 8, WIDE), F32),
            dma(MARKS),
            pltpu.SemaphoreType.REGULAR,
            pltpu.SemaphoreType.REGULAR,
        ],
        compiler_params=pltpu.CompilerParams(
            collective_id=0, has_side_effects=True, vmem_limit_bytes=63 * 2**20
        ),
        name="layer",
    )(wff, wat, tok, cot, gains)


def on_device_full(
    tokens, cotangent, w_qkv, conv_weight, w_out, w_gate, w_up, w_down, gain_mix, gain_ffn
):
    rows, half = tokens.shape
    ffn_cols = w_gate.shape[1]
    heads = 2
    pad = ((0, 0), (0, 5 * TILE - ffn_cols))
    wff = jnp.stack([jnp.pad(w, pad) for w in (w_gate, w_up, w_down)])
    upper = jnp.pad(
        w_qkv.T.reshape(heads, HEADROWS, rows), ((0, 0), (0, 0), (0, WIDE - rows))
    )
    lower = jnp.concatenate(
        [
            w_out.reshape(heads, HDIM, rows),
            conv_weight.T.reshape(heads, HDIM, CONV),
            jnp.zeros((heads, HDIM, WIDE - rows - CONV), BF16),
        ],
        2,
    )
    wat = jnp.concatenate([upper, lower], 1)
    gains = jnp.concatenate(
        [jnp.broadcast_to(g[:, None], (rows, TILE // 2)) for g in (gain_mix, gain_ffn)], 1
    )
    out_ff, out_at, out_res, out_tok, small = run_layer(wff, wat, tokens, cotangent, gains)[:5]
    out_at = out_at.astype(F32)
    return (
        out_res,
        out_tok.astype(F32),
        out_at[:, :HEADROWS, :rows].reshape(heads * HEADROWS, rows).T,
        out_at[:, HEADROWS:, rows : rows + CONV].reshape(heads * HDIM, CONV).T,
        out_at[:, HEADROWS:, :rows].reshape(heads * HDIM, rows),
        out_ff[0, :, :ffn_cols].astype(F32),
        out_ff[1, :, :ffn_cols].astype(F32),
        out_ff[2, :, :ffn_cols].astype(F32),
        small[0, :rows],
        small[1, :rows],
        jnp.sqrt(small[2, :3] / (8 * half * 4 * rows)),
    )


def on_device(tokens, cotangent, lengths, deal_order, *weights):
    total_rows = tokens.shape[1] * lax.axis_size("col")
    if (
        lengths.shape[0] * LONGEST == total_rows
        and lax.axis_size("row") == 4
        and lax.axis_size("col") == 8
        and total_rows == 4 * LONGEST
        and weights[0].shape[1] == 2 * HEADROWS
        and 4 * TILE < weights[3].shape[1] <= 5 * TILE
    ):
        return on_device_full(tokens, cotangent, *weights)
    return on_device_general(tokens, cotangent, lengths, deal_order, *weights)


def solution(mesh):
    in_specs = (
        P("row", "col"),
        P("row", "col"),
        P(),
        P(),
        P("row", "col"),
        P(None, "col"),
        P("col", "row"),
        P("row", "col"),
        P("row", "col"),
        P("row", "col"),
        P("row"),
        P("row"),
    )
    out_specs = (
        P("row", "col"),
        P("row", "col"),
        P("row", "col"),
        P(None, "col"),
        P("col", "row"),
        P("row", "col"),
        P("row", "col"),
        P("row", "col"),
        P("row"),
        P("row"),
        P(),
    )
    return jax.shard_map(
        on_device, mesh=mesh, in_specs=in_specs, out_specs=out_specs, check_vma=False
    )
```

```python
import jax
import jax.numpy as jnp
from jax import lax
from jax.experimental import pallas as pl
from jax.experimental.pallas import tpu as pltpu
from jax.sharding import PartitionSpec as P

D = 1792
FEAT = 16
CONV = 3
LONGEST = 1024
HDIM = 112


EPSILON = 1e-06


def dealing(lengths, deal_order, total_rows):
    seq_ids = jnp.arange(lengths.shape[0], dtype=jnp.int32)
    chosen = (deal_order[:, None] == seq_ids[None, :]).astype(jnp.int32)
    dealt_lengths = jnp.sum(chosen * lengths[None, :], 1)
    given_start = jnp.cumsum(lengths) - lengths
    dealt_start = jnp.cumsum(dealt_lengths) - dealt_lengths
    given_of_dealt = jnp.sum(chosen * given_start[None, :], 1)
    dealt_of_given = jnp.sum(chosen * dealt_start[:, None], 0)
    places = jnp.arange(total_rows, dtype=jnp.int32)
    in_dealt = (places[:, None] >= dealt_start[None, :]) & (
        places[:, None] < (dealt_start + dealt_lengths)[None, :]
    )
    in_given = (places[:, None] >= given_start[None, :]) & (
        places[:, None] < (given_start + lengths)[None, :]
    )
    source = places + jnp.sum(jnp.where(in_dealt, (given_of_dealt - dealt_start)[None, :], 0), 1)
    target = places + jnp.sum(jnp.where(in_given, (dealt_of_given - given_start)[None, :], 0), 1)
    offsets = places - jnp.sum(jnp.where(in_dealt, dealt_start[None, :], 0), 1)
    return (source, target, offsets)


def convolve(raw_values, kernel_conv, offsets):
    mixed = kernel_conv[0] * raw_values
    for delay_step in range(1, CONV):
        moved = jnp.concatenate(
            [jnp.zeros_like(raw_values[:delay_step]), raw_values[:-delay_step]], 0
        )
        mixed = mixed + kernel_conv[delay_step] * jnp.where(
            (offsets >= delay_step)[:, None, None], moved, 0.0
        )
    return mixed


def convolve_back(grad_mixed, raw_values, kernel_conv, offsets):
    grad_raw = kernel_conv[0] * grad_mixed
    sums_list = [jnp.sum(grad_mixed * raw_values, 0)]
    for delay_step in range(1, CONV):
        masked = jnp.where((offsets >= delay_step)[:, None, None], grad_mixed, 0.0)
        pulled = jnp.concatenate([masked[delay_step:], jnp.zeros_like(masked[:delay_step])], 0)
        grad_raw = grad_raw + kernel_conv[delay_step] * pulled
        moved = jnp.concatenate(
            [jnp.zeros_like(raw_values[:delay_step]), raw_values[:-delay_step]], 0
        )
        sums_list.append(jnp.sum(masked * moved, 0))
    return (grad_raw, jnp.stack(sums_list))


def bin_scores(query, keys, offsets):
    scores = jnp.einsum("thf,shf->hts", query, keys, preferred_element_type=jnp.float32) * FEAT ** (
        -0.5
    )
    positions = jnp.arange(query.shape[0], dtype=jnp.int32)
    visible = (positions[None, :] <= positions[:, None]) & (
        positions[:, None] - positions[None, :] <= offsets[:, None]
    )
    kernel = jnp.where(visible[None], 1.0 + scores + 0.5 * scores * scores, 0.0)
    return (scores, visible, kernel)


def attend_bin(pieces):
    query, keys, values, offsets = pieces
    scores, visible, kernel = bin_scores(query, keys, offsets)
    weights = (kernel / jnp.sum(kernel, -1, keepdims=True)).astype(jnp.bfloat16)
    return jnp.einsum("hts,shd->thd", weights, values, preferred_element_type=jnp.float32)


def attend_back(pieces):
    query, keys, values, offsets, grad_attend = pieces
    scores, visible, kernel = bin_scores(query, keys, offsets)
    totals = jnp.sum(kernel, -1, keepdims=True)
    weights = kernel / totals
    grad_weights = jnp.einsum(
        "thd,shd->hts", grad_attend, values, preferred_element_type=jnp.float32
    )
    grad_values = jnp.einsum(
        "hts,thd->shd",
        weights.astype(jnp.bfloat16),
        grad_attend,
        preferred_element_type=jnp.float32,
    )
    grad_kernel = (grad_weights - jnp.sum(grad_weights * weights, -1, keepdims=True)) / totals
    grad_scores = jnp.where(visible[None], grad_kernel * (1.0 + scores), 0.0).astype(jnp.bfloat16)
    grad_query = jnp.einsum(
        "hts,shf->thf", grad_scores, keys, preferred_element_type=jnp.float32
    ) * FEAT ** (-0.5)
    grad_keys = jnp.einsum(
        "hts,thf->shf", grad_scores, query, preferred_element_type=jnp.float32
    ) * FEAT ** (-0.5)
    return (grad_query, grad_keys, grad_values)


def times_transposed(left, right):
    return lax.dot_general(
        left, right, (((1,), (1,)), ((), ())), preferred_element_type=jnp.float32
    )


def tokens_product(left, right):
    return lax.dot_general(
        left, right, (((0,), (0,)), ((), ())), preferred_element_type=jnp.float32
    )


def plain_product(left, right):
    return jnp.dot(left, right, preferred_element_type=jnp.float32)


def gather_cols(values):
    return lax.all_gather(values, "col", axis=0, tiled=True)


def gather_rows(values):
    return lax.all_gather(values, "row", axis=0, tiled=True)


def grad_gather_cols(values):
    return lax.all_gather(values, "col", axis=1, tiled=True)


def grad_gather_rows(values):
    return lax.all_gather(values, "row", axis=0, tiled=True)


def width_total(values):
    return lax.psum(values, "row")


def forward_rows(gathered, row_index, weight, rows_here):

    def partial_term(row_start, row_count):
        picked = jnp.take(gathered, row_index, axis=0)
        return jnp.dot(picked, weight, preferred_element_type=jnp.float32)

    return lax.psum_scatter(
        partial_term(jnp.int32(0), rows_here * lax.axis_size("row")),
        "row",
        scatter_dimension=0,
        tiled=True,
    )


def forward_cols(gathered, row_index, weight, rows_here, product):

    def partial_term(row_start, row_count):
        picked = jnp.take(gathered, row_index, axis=0)
        return product(picked, weight)

    return lax.psum_scatter(
        partial_term(jnp.int32(0), lax.axis_size("col") * rows_here).astype(jnp.bfloat16),
        "col",
        scatter_dimension=0,
        tiled=True,
    ).astype(jnp.float32)


def backward_rows(gathered, row_index, weight, rows_here, contract):

    def partial_term(row_start, row_count):
        picked = jnp.take(gathered, row_index, axis=1)
        return lax.dot_general(
            picked, weight, (((0,), (contract,)), ((), ())), preferred_element_type=jnp.float32
        )

    return lax.psum_scatter(
        partial_term(jnp.int32(0), lax.axis_size("row") * rows_here).astype(jnp.bfloat16),
        "row",
        scatter_dimension=0,
        tiled=True,
    ).astype(jnp.float32)


def backward_cols(gathered, row_index, weight, rows_here):

    def partial_term(row_start, row_count):
        picked = jnp.take(gathered, row_index, axis=0)
        return times_transposed(picked, weight)

    return lax.psum_scatter(
        partial_term(jnp.int32(0), lax.axis_size("col") * rows_here).astype(jnp.bfloat16),
        "col",
        scatter_dimension=0,
        tiled=True,
    ).astype(jnp.float32)


def norm_forward(values, norm_gain):
    totals = width_total(jnp.sum(values * values, -1))
    inverse = lax.rsqrt(totals / D + EPSILON)
    return (values * inverse[:, None] * norm_gain, inverse)


def norm_back(values, inverse, norm_gain, grad_normed, dot_sums):
    cubed = inverse * inverse * inverse
    return grad_normed * norm_gain * inverse[:, None] - values * (cubed * dot_sums / D)[:, None]


def on_device_general(
    tokens,
    cotangent,
    lengths,
    deal_order,
    w_qkv,
    conv_weight,
    w_out,
    w_gate,
    w_up,
    w_down,
    gain_mix,
    gain_ffn,
):
    local_rows = tokens.shape[1]
    total_rows = local_rows * lax.axis_size("col")
    group_rows = total_rows // lax.axis_size("row")
    bin_count = group_rows // LONGEST
    heads_here = w_out.shape[0] // HDIM
    ffn_cols = w_gate.shape[1]
    source, target, offsets = dealing(lengths, deal_order, total_rows)
    group_offsets = lax.dynamic_slice_in_dim(
        offsets, lax.axis_index("row") * group_rows, group_rows
    )
    inputs = tokens.astype(jnp.float32).T
    gain_one = gain_mix.astype(jnp.float32)
    gain_two = gain_ffn.astype(jnp.float32)
    both_weights = jnp.concatenate([w_gate, w_up], 1)
    normed_one, inverse_one = norm_forward(inputs, gain_one)
    low_one = normed_one.astype(jnp.bfloat16)
    all_one = gather_cols(low_one)
    projected = forward_rows(all_one, source, w_qkv, group_rows)
    projected = projected.reshape(group_rows, heads_here, 2 * FEAT + HDIM)
    query = projected[:, :, :FEAT].astype(jnp.bfloat16)
    keys = projected[:, :, FEAT : 2 * FEAT].astype(jnp.bfloat16)
    raw_values = projected[:, :, 2 * FEAT :]
    kernel_conv = conv_weight.astype(jnp.float32).reshape(CONV, heads_here, HDIM)
    values = convolve(raw_values, kernel_conv, group_offsets).astype(jnp.bfloat16)
    binned = (
        query.reshape(bin_count, LONGEST, heads_here, FEAT),
        keys.reshape(bin_count, LONGEST, heads_here, FEAT),
        values.reshape(bin_count, LONGEST, heads_here, HDIM),
        group_offsets.reshape(bin_count, LONGEST),
    )
    attended = (
        lax.map(attend_bin, binned).reshape(group_rows, heads_here * HDIM).astype(jnp.bfloat16)
    )
    all_attended = gather_rows(attended)
    branch_mix = forward_cols(all_attended, target, w_out, local_rows, plain_product)
    middle = inputs + branch_mix
    normed_two, inverse_two = norm_forward(middle, gain_two)
    low_two = normed_two.astype(jnp.bfloat16)
    all_two = gather_cols(low_two)
    gate_up = forward_rows(all_two, source, both_weights, group_rows)
    gate = gate_up[:, :ffn_cols]
    up_proj = gate_up[:, ffn_cols:]
    activated = jax.nn.silu(gate)
    hidden = (activated * up_proj).astype(jnp.bfloat16)
    all_hidden = gather_rows(hidden)
    branch_ffn = forward_cols(all_hidden, target, w_down, local_rows, times_transposed)
    result_full = middle + branch_ffn
    grad_result = cotangent.astype(jnp.float32).T
    all_grad_ffn = grad_gather_cols(cotangent)
    hidden_again = gather_rows(hidden)
    grad_down = jnp.dot(
        jnp.take(all_grad_ffn, source, axis=1), hidden_again, preferred_element_type=jnp.float32
    )
    grad_hidden = backward_rows(all_grad_ffn, source, w_down, group_rows, 0)
    gate_sigmoid = jax.nn.sigmoid(gate)
    grad_gate_part = grad_hidden * up_proj * gate_sigmoid * (1.0 + gate * (1.0 - gate_sigmoid))
    grad_up_part = grad_hidden * activated
    grad_gate_up = jnp.concatenate([grad_gate_part, grad_up_part], 1).astype(jnp.bfloat16)
    all_grad_gate_up = grad_gather_rows(grad_gate_up)
    two_again = gather_cols(low_two)
    grad_both = tokens_product(jnp.take(two_again, source, axis=0), all_grad_gate_up)
    grad_normed_two = backward_cols(all_grad_gate_up, target, both_weights, local_rows)
    dots_two = width_total(jnp.sum(grad_normed_two * gain_two * middle, -1))
    grad_middle = grad_result + norm_back(middle, inverse_two, gain_two, grad_normed_two, dots_two)
    gain_part_two = jnp.sum(grad_normed_two * middle * inverse_two[:, None], 0)
    low_grad_middle = grad_middle.T.astype(jnp.bfloat16)
    all_grad_middle = grad_gather_cols(low_grad_middle)
    attended_again = gather_rows(attended)
    grad_out = lax.dot_general(
        attended_again,
        jnp.take(all_grad_middle, source, axis=1),
        (((0,), (1,)), ((), ())),
        preferred_element_type=jnp.float32,
    )
    grad_attended = backward_rows(all_grad_middle, source, w_out, group_rows, 1).astype(
        jnp.bfloat16
    )
    binned_back = binned + (grad_attended.reshape(bin_count, LONGEST, heads_here, HDIM),)
    grad_query, grad_keys, grad_values = lax.map(attend_back, binned_back)
    grad_values = grad_values.reshape(group_rows, heads_here, HDIM)
    grad_raw, conv_part = convolve_back(grad_values, raw_values, kernel_conv, group_offsets)
    grad_projected = jnp.concatenate(
        [
            grad_query.reshape(group_rows, heads_here, FEAT),
            grad_keys.reshape(group_rows, heads_here, FEAT),
            grad_raw,
        ],
        2,
    )
    grad_projected = grad_projected.reshape(group_rows, heads_here * (2 * FEAT + HDIM)).astype(
        jnp.bfloat16
    )
    all_grad_projected = grad_gather_rows(grad_projected)
    one_again = gather_cols(low_one)
    grad_qkv = tokens_product(jnp.take(one_again, source, axis=0), all_grad_projected)
    grad_normed_one = backward_cols(all_grad_projected, target, w_qkv, local_rows)
    squares = jnp.stack(
        [
            jnp.sum(branch_mix * branch_mix),
            jnp.sum(branch_ffn * branch_ffn),
            jnp.sum(result_full * result_full),
        ]
    )
    dots_one, grad_conv, squares_rows = width_total(
        (
            jnp.sum(grad_normed_one * gain_one * inputs, -1),
            conv_part.reshape(CONV, heads_here * HDIM),
            squares,
        )
    )
    grad_tokens = grad_middle + norm_back(inputs, inverse_one, gain_one, grad_normed_one, dots_one)
    gain_part_one = jnp.sum(grad_normed_one * inputs * inverse_one[:, None], 0)
    grad_gain_mix, grad_gain_ffn, squares_all = lax.psum(
        (gain_part_one, gain_part_two, squares_rows), "col"
    )
    rms_values = jnp.sqrt(squares_all / (total_rows * D))
    return (
        result_full.T.astype(jnp.bfloat16),
        grad_tokens.T,
        grad_qkv,
        grad_conv,
        grad_out,
        grad_both[:, :ffn_cols],
        grad_both[:, ffn_cols:],
        grad_down,
        grad_gain_mix,
        grad_gain_ffn,
        rms_values,
    )


HEADROWS = 2 * FEAT + HDIM
BLOCKROWS = HEADROWS + HDIM
TILE = 128
WIDE = 512
SPAN = 256
MARKS = 320
MESH = pl.DeviceIdType.MESH
ANY = pl.BlockSpec(memory_space=pl.ANY)
F32, BF16 = jnp.float32, jnp.bfloat16


def place():
    column = lax.axis_index("col")
    return lax.axis_index("row"), column // 2, column % 2


def device(chip, plane, core):
    return (chip, plane * 2 + core)


def other_chips(chip):
    y, x = chip // 2, chip % 2
    return (y * 2 + 1 - x, (1 - y) * 2 + x, (1 - y) * 2 + 1 - x)


def away(plane, step):
    if step == 1:
        return plane + 1 - 2 * (plane % 2)
    if step == 2:
        return (plane + 2) % 4
    return 3 - plane


def is_inner(plane):
    return ((plane + 1) // 2) % 2 == 1


def remote(source, target, send, receive, to):
    return pltpu.make_async_remote_copy(
        src_ref=source,
        dst_ref=target,
        send_sem=send,
        recv_sem=receive,
        device_id=to,
        device_id_type=MESH,
    )


def lanes(start, size=TILE):
    return pl.ds(pl.multiple_of(start, TILE), size)


def rows_at(start, size, step):
    return pl.ds(pl.multiple_of(start, step), size)


def no(flag):
    return jnp.logical_not(flag)


def dot(a, b, over_a, over_b):
    return lax.dot_general(
        a, b, (((over_a,), (over_b,)), ((), ())), preferred_element_type=F32
    )


class Marks:
    def __init__(self, ref):
        self.ref, self.used = ref, 0

    def one(self):
        self.used += 1
        return self.ref.at[self.used - 1]

    def many(self, count):
        base = self.used
        self.used += count
        return lambda i: self.ref.at[base + i]


class Spread:
    def __init__(self, ref, owner, chip, plane, core, marks, forward):
        self.ref, self.owner, self.spot = ref, owner, (chip, plane, core)
        self.sends = marks.many(4)
        self.arrived = marks.one()
        self.mine = plane == owner
        self.forward = forward
        self.relays = is_inner(plane) & (plane == away(owner, 2))

    def copy(self, step, send):
        chip, plane, core = self.spot
        return remote(
            self.ref, self.ref, self.sends(send), self.arrived,
            device(chip, away(plane, step), core),
        )

    def far(self):
        return self.mine & is_inner(self.spot[1]) if self.forward else self.mine

    def start(self):
        @pl.when(self.far())
        def _():
            self.copy(3, 2).start()

        @pl.when(self.mine)
        def _():
            self.copy(2, 1).start()
            self.copy(1, 0).start()

    def relay(self):
        @pl.when(self.relays)
        def _():
            self.copy(1, 3).wait_recv()
            self.copy(1, 3).start()

    def arrive(self):
        done = self.mine | self.relays if self.forward else self.mine

        @pl.when(no(done))
        def _():
            self.copy(1, 3).wait_recv()

    def finish(self):
        @pl.when(self.mine)
        def _():
            self.copy(1, 0).wait_send()
            self.copy(2, 1).wait_send()

        @pl.when(self.far())
        def _():
            self.copy(3, 2).wait_send()

        if self.forward:

            @pl.when(self.relays)
            def _():
                self.copy(1, 3).wait_send()


class MainTiles:
    def __init__(self, ff, chip, plane, core, marks):
        self.ff, self.spot = ff, (chip, plane, core)
        self.sends, self.here = marks.many(4), marks.many(3)
        self.inner = is_inner(plane)

    def copy(self, slot, to_step, send, receive):
        chip, plane, core = self.spot
        tiles = self.ff.at[:, :, lanes(slot * TILE)]
        return remote(
            tiles, tiles, self.sends(send), self.here(receive),
            device(chip, away(plane, to_step), core),
        )

    def start_all(self):
        near, next_on, far = [
            self.copy(self.spot[1], step, step - 1, step - 1) for step in (1, 2, 3)
        ]

        @pl.when(self.inner)
        def _():
            near.start()
            next_on.start()
            far.start()

        @pl.when(no(self.inner))
        def _():
            next_on.start()
            near.start()

    def relay(self):
        @pl.when(self.inner)
        def _():
            self.copy(self.spot[1], 1, 0, 1).wait_recv()
            self.copy(away(self.spot[1], 2), 1, 3, 2).start()

    def arrive(self, step):
        copy = self.copy(self.spot[1], 1, 0, step - 1)
        if step == 2:
            pl.when(no(self.inner))(copy.wait_recv)
        else:
            copy.wait_recv()

    def finish(self):
        for step in (1, 2):
            self.copy(self.spot[1], 1, step - 1, 0).wait_send()

        @pl.when(self.inner)
        def _():
            self.copy(self.spot[1], 1, 2, 0).wait_send()
            self.copy(self.spot[1], 1, 3, 0).wait_send()


class MainGrads:
    def __init__(self, gout, slots, chip, plane, core, marks):
        self.gout, self.slots, self.spot = gout, slots, (chip, plane, core)
        self.sends, self.here = marks.many(3), marks.many(4)
        self.inner = is_inner(plane)

    def copy(self, slot, to_step, send, receive):
        chip, plane, core = self.spot
        return remote(
            self.gout.at[:, :, lanes(slot * TILE)], self.slots.at[receive],
            self.sends(send), self.here(receive), device(chip, away(plane, to_step), core),
        )

    def start(self, step):
        plane = self.spot[1]
        if step == 1:
            self.copy(away(plane, 1), 1, 0, 0).start()
        if step == 2:
            pl.when(no(self.inner))(self.copy(away(plane, 2), 2, 1, 1).start)
        if step == 3:
            pl.when(self.inner)(self.copy(away(plane, 3), 3, 2, 2).start)
            pl.when(no(self.inner))(self.copy(away(plane, 3), 1, 2, 3).start)

    def relay(self, add):
        plane = self.spot[1]

        @pl.when(self.inner)
        def _():
            self.copy(plane, 1, 0, 3).wait_recv()
            add(self.slots.at[3])
            self.copy(away(plane, 2), 2, 1, 1).start()

    def total(self, add):
        plane = self.spot[1]
        for receive in range(2):
            self.copy(plane, 1, 0, receive).wait_recv()
            add(self.slots.at[receive])

        @pl.when(self.inner)
        def _():
            self.copy(plane, 1, 0, 2).wait_recv()
            add(self.slots.at[2])

    def finish(self):
        for send in range(3):
            self.copy(self.spot[1], 1, send, 0).wait_send()


class Collect:
    def __init__(self, ref, slots, owner, chip, plane, core, marks):
        self.ref, self.slots, self.owner, self.spot = ref, slots, owner, (chip, plane, core)
        self.send = marks.one()
        self.arrived = marks.many(4)
        outer = no(is_inner(owner))
        self.mine = plane == owner
        self.first = plane == away(owner, 1)
        self.second = plane == away(owner, 2)
        self.third = plane == away(owner, 3)
        self.outer = outer

    def copy(self, step, slot):
        chip, plane, core = self.spot
        return remote(
            self.ref, self.slots.at[slot], self.send, self.arrived(slot),
            device(chip, away(plane, step), core),
        )

    def start(self, add):
        @pl.when(self.first)
        def _():
            self.copy(1, 0).start()

        @pl.when(self.third & self.outer)
        def _():
            self.copy(1, 3).start()

        @pl.when(self.third & no(self.outer))
        def _():
            self.copy(3, 2).start()

        @pl.when(self.second & no(self.outer))
        def _():
            self.copy(2, 1).start()

    def relay(self, add):
        @pl.when(self.second & self.outer)
        def _():
            self.copy(1, 3).wait_recv()
            add(self.slots.at[3])
            self.copy(2, 1).start()

    def total(self, add):
        @pl.when(self.mine)
        def _():
            self.copy(1, 0).wait_recv()
            add(self.slots.at[0])
            self.copy(1, 1).wait_recv()
            add(self.slots.at[1])

        @pl.when(self.mine & no(self.outer))
        def _():
            self.copy(1, 2).wait_recv()
            add(self.slots.at[2])

    def finish(self):
        @pl.when(no(self.mine))
        def _():
            self.copy(1, 0).wait_send()


def layer_kernel(
    wff, wat, tok, cot, gains,
    out_ff, out_at, out_res, out_tok, out_small, main_got, extra_got, att_got,
    ff, at, xs, gs, low2, part, acc3, gout, gat, from_mate, both, got, turned, hid, gg,
    gn, gcol, raw, qs, ks, vs, att, gatt, gproj, mid, gmid, gsum, normed, sending, inv_all,
    inv_sum, small, small_a, small_b, sem, free_mate, free_chips,
):
    chip, plane, core = place()
    others = other_chips(chip)
    mate = device(chip, plane, 1 - core)
    marks = Marks(sem)
    rows = tok.shape[0]
    width = 4 * rows
    half = tok.shape[1]
    seq = 2 * half
    own_half = lanes(core * half, half)
    first = core * half + chip * TILE
    peers = [device(c, plane, core) for c in others]
    line = [device(chip, away(plane, step), core) for step in (1, 2, 3)]
    sides = [device(c, plane, 1 - core) for c in others]
    line_mates = [device(chip, away(plane, step), 1 - core) for step in (1, 2, 3)]

    barrier = pltpu.get_barrier_semaphore()
    partners = peers + [mate] + sides + line + line_mates
    for partner in partners:
        pl.semaphore_signal(barrier, inc=1, device_id=partner, device_id_type=MESH)
    pl.semaphore_wait(barrier, len(partners))

    def block_rows(c):
        return rows_at(c * rows, rows, rows)

    far_core = plane // 2
    holds_att = core == far_core
    holds_extra = holds_att & (chip // 2 == plane % 2)
    extra_plane = 2 * core + chip // 2
    extra_chip = (plane % 2) * 2 + core
    att_send, att_here = marks.many(2), marks.many(4)
    att_local = marks.one()

    def att_copy(h):
        return remote(
            wat.at[h], at.at[plane % 2, chip], att_send(h), att_here(chip),
            device(2 * core + h, plane, far_core),
        )

    def att_keep(h):
        return pltpu.make_async_copy(wat.at[h], at.at[plane % 2, chip], att_local)

    att_self = [(2 * core + h == chip) & holds_att for h in range(2)]
    for h in range(2):

        @pl.when(att_self[h])
        def _():
            att_keep(h).start()

        @pl.when(no(att_self[h]))
        def _():
            att_copy(h).start()

    class Gather:
        def __init__(self, source, target_of):
            self.source, self.target_of = source, target_of
            self.send, self.here = marks.many(4), marks.many(4)
            self.mate_send, self.mate_here = marks.many(4), marks.many(4)
            self.keep = pltpu.make_async_copy(source, target_of(chip), marks.one())
            self.copies = [
                remote(source, target_of(chip), self.send(p), self.here(p), peers[p])
                for p in range(2)
            ]
            for copy in self.copies:
                copy.start()
            self.keep.start()
            self.crossing = []
            self.cross(source, chip, 3)

        def cross(self, source, c, mark):
            copy = remote(
                source, self.target_of(c), self.mate_send(mark), self.mate_here(mark), mate
            )
            copy.start()
            self.crossing.append(copy)

        def halves(self, c):
            block = self.target_of(c)
            size = block.shape[0] // 2
            return block.at[0:size], block.at[size : 2 * size]

        def pass_on(self):
            self.copies[0].wait_recv()
            part_a = self.halves(others[0])[0]
            self.copies.append(remote(part_a, part_a, self.send(2), self.here(2), peers[1]))
            self.copies[2].start()
            self.cross(self.target_of(others[0]), others[0], 0)
            self.copies[1].wait_recv()
            part_b = self.halves(others[1])[1]
            self.copies.append(remote(part_b, part_b, self.send(3), self.here(3), peers[0]))
            self.copies[3].start()
            self.cross(self.target_of(others[1]), others[1], 1)

        def arrive(self):
            for copy in self.copies[2:]:
                copy.wait_recv()
            self.cross(self.target_of(others[2]), others[2], 2)
            for copy in self.crossing:
                copy.wait_recv()
            self.keep.wait()

        def finish(self):
            for copy in self.copies + self.crossing:
                copy.wait_send()

    tokens_in = Gather(tok, lambda c: xs.at[block_rows(c), own_half])
    gain_send, gain_here = marks.many(3), marks.many(3)
    gain_copies = [
        remote(gains, gn.at[chip], gain_send(p), gain_here(p), peers[p]) for p in range(3)
    ]
    gain_keep = pltpu.make_async_copy(gains, gn.at[chip], marks.one())
    for copy in gain_copies + [gain_keep]:
        copy.start()

    for h in range(2):

        @pl.when(att_self[h])
        def _():
            att_keep(h).wait()

        @pl.when(no(att_self[h]))
        def _():
            att_copy(h).wait_send()

    for c in range(4):

        @pl.when(holds_att & no((c == chip) & (core == chip // 2)))
        def _():
            remote(
                wat.at[0], at.at[plane % 2, c], att_send(0), att_here(c), mate
            ).wait_recv()

    out_rows, in_rows = pl.ds(HEADROWS, HDIM), pl.ds(0, HEADROWS)
    in_line, out_line = [
        [
            Spread(at.at[a, :, span], 2 * core + a, chip, plane, core, marks, forward=True)
            for a in range(2)
        ]
        for span in (in_rows, out_rows)
    ]
    for item in in_line + out_line:
        item.start()

    tokens_in.pass_on()
    main_send, main_here, main_local = marks.many(3), marks.many(3), marks.one()
    main_here_at = ff.at[:, block_rows(chip), lanes(plane * TILE)]
    mains = [
        remote(
            wff.at[:, :, lanes(others[p] * TILE)], main_here_at,
            main_send(p), main_here(p), peers[p],
        )
        for p in range(3)
    ]
    for copy in mains:
        copy.start()
    main_keep = pltpu.make_async_copy(wff.at[:, :, lanes(chip * TILE)], main_here_at, main_local)
    main_keep.start()

    extra_send, extra_here, extra_local = marks.one(), marks.many(4), marks.one()
    extra_self = (extra_chip == chip) & holds_att
    last = lanes(4 * TILE)

    def extra_copy():
        return remote(
            wff.at[:, :, last], ff.at[:, block_rows(chip), last], extra_send, extra_here(chip),
            device(extra_chip, plane, far_core),
        )

    def extra_keep():
        return pltpu.make_async_copy(
            wff.at[:, :, last], ff.at[:, block_rows(chip), last], extra_local
        )

    @pl.when(extra_self)
    def _():
        extra_keep().start()

    @pl.when(no(extra_self))
    def _():
        extra_copy().start()

    tokens_in.arrive()
    cot_in = Gather(cot, lambda c: gs.at[block_rows(c), own_half])
    for copy in gain_copies + [gain_keep]:
        copy.wait()

    for item in in_line:
        item.relay()
    @pl.loop(0, 4)
    def _(c):
        columns = gn[c].astype(F32).T
        gcol[block_rows(c), 0:16] = columns[:rows]

    step_rows = 64

    def add_squares(i, total):
        x = xs[rows_at(i * step_rows, step_rows, step_rows)].astype(F32)
        return total + jnp.sum((x * x).reshape(step_rows // 8, 8, seq), 0)

    squares = lax.fori_loop(0, width // step_rows, add_squares, jnp.zeros((8, seq), F32))
    inv_all[...] = lax.rsqrt(jnp.sum(squares, 0, keepdims=True) / D + EPSILON)
    tokens_in.finish()
    normed[...] = xs[:, lanes(first)]

    @pl.loop(0, width // step_rows)
    def _(i):
        at_rows = rows_at(i * step_rows, step_rows, step_rows)
        xs[at_rows] = (
            xs[at_rows].astype(F32) * inv_all[...] * gcol[at_rows, 0:1]
        ).astype(BF16)

    for item in out_line:
        item.relay()
    main_keep.wait()
    for copy in mains:
        copy.wait()
    main_line = MainTiles(ff, chip, plane, core, marks)
    main_line.start_all()

    @pl.when(extra_self)
    def _():
        extra_keep().wait()

    @pl.when(no(extra_self))
    def _():
        extra_copy().wait_send()

    for c in range(4):

        @pl.when(holds_extra & no((c == chip) & (core == chip % 2)))
        def _():
            remote(
                wff.at[:, :, last], ff.at[:, block_rows(c), last], extra_send, extra_here(c), mate
            ).wait_recv()

    extra_line = Spread(ff.at[:, :, last], extra_plane, chip, plane, core, marks, forward=True)
    extra_line.start()

    cot_in.pass_on()

    for item in in_line:
        item.arrive()

    position = lax.broadcasted_iota(jnp.int32, (1, seq), 1)
    tail = lax.broadcasted_iota(jnp.int32, (HDIM, TILE), 1)

    def taps(h):
        columns = at[h, 0, 2 * FEAT : HEADROWS, WIDE - TILE : WIDE].astype(F32)
        return [columns[:, rows % TILE + j : rows % TILE + j + 1] for j in range(CONV)]

    @pl.loop(0, 2)
    def _(h):
        projected = dot(at[h, 0, :HEADROWS, :rows], xs[0:rows], 1, 0)
        for c in range(1, 4):
            projected += dot(at[h, c, :HEADROWS, :rows], xs[c * rows : (c + 1) * rows], 1, 0)
        qs[h] = (projected[:FEAT].astype(BF16).astype(F32) * FEAT**-0.5).astype(BF16)
        ks[h] = projected[FEAT : 2 * FEAT].astype(BF16)
        values = projected[2 * FEAT :]
        raw[h] = values
        tap = taps(h)
        mixed = tap[0] * values
        for j in range(1, CONV):
            moved = pltpu.roll(values, j, 1)
            mixed += tap[j] * jnp.where(position >= j, moved, 0.0)
        vs[h] = mixed.astype(BF16)

    def kernel_of(h, b):
        seen = (b + 1) * SPAN
        scores = dot(ks[h, :, :seen], qs[h, :, b * SPAN : seen], 0, 0)
        kernel = 1.0 + scores + 0.5 * scores * scores
        key_at = lax.broadcasted_iota(jnp.int32, (seen, SPAN), 0)
        query_at = lax.broadcasted_iota(jnp.int32, (seen, SPAN), 1) + b * SPAN
        visible = key_at <= query_at
        return scores, jnp.where(visible, kernel, 0.0), visible

    @pl.loop(0, 2)
    def _(h):
        for b in range(seq // SPAN):
            seen = (b + 1) * SPAN
            _, kernel, _ = kernel_of(h, b)
            inverse = 1.0 / jnp.sum(kernel, 0, keepdims=True)
            inv_sum[h, :, b * SPAN : seen] = inverse
            weights = (kernel * inverse).astype(BF16)
            att[h, :, b * SPAN : seen] = dot(vs[h, :, :seen], weights, 1, 0).astype(BF16)

    for item in out_line:
        item.arrive()

    def default_got(i):
        return got.at[i]

    class Sum:
        def __init__(self, guard, both=both, got=None, share=True):
            self.guard, self.both, self.share = guard, both, share
            self.got = got or default_got

        def begin(self, fill):
            fill((1 - core) * half)
            self.to_mate = remote(
                part.at[:, lanes((1 - core) * half, half)], from_mate,
                marks.one(), marks.one(), mate,
            )
            if self.guard:
                pl.semaphore_wait(free_mate, 1)
            self.to_mate.start()
            fill(core * half)

        def combine(self):
            self.to_mate.wait_recv()

            @pl.loop(0, 4)
            def _(c):
                self.both[block_rows(c)] = (
                    part[block_rows(c), own_half].astype(F32)
                    + from_mate[block_rows(c)].astype(F32)
                ).astype(BF16)

            pl.semaphore_signal(free_mate, inc=1, device_id=mate, device_id_type=MESH)
            self.to_mate.wait_send()

        def piece(self, upper, c):
            size = width // 2
            return self.both.at[pl.ds(0 if upper else size, size), lanes(c * TILE)]

        def send(self):
            if self.guard and self.share:
                pl.semaphore_wait(free_chips, 2)
            size = width // 2
            top, bottom = pl.ds(0, size), pl.ds(size, size)
            send, here = marks.many(6), marks.many(6)
            self.across = [
                remote(self.piece(True, others[2]), self.got(2).at[top], send(0), here(0), peers[0]),
                remote(
                    self.piece(False, others[2]), self.got(2).at[bottom], send(1), here(1), peers[1]
                ),
            ]
            self.plain = [
                remote(self.piece(True, others[0]), self.got(0).at[top], send(2), here(2), peers[0]),
                remote(
                    self.piece(False, others[1]), self.got(1).at[bottom], send(3), here(3), peers[1]
                ),
            ]
            self.added = [
                remote(
                    self.piece(True, others[1]), self.got(1).at[top], send(4), here(4), peers[1]
                ),
                remote(
                    self.piece(False, others[0]), self.got(0).at[bottom], send(5), here(5), peers[0]
                ),
            ]
            for copy in self.across + self.plain:
                copy.start()

        def pass_on(self):
            size = width // 2
            quarter = size // 2
            for i, c in ((0, others[1]), (1, others[0])):
                self.across[i].wait_recv()
                for q in range(2):
                    at_rows = pl.ds(i * size + q * quarter, quarter)
                    self.both[at_rows, lanes(c * TILE)] = (
                        self.both[at_rows, lanes(c * TILE)].astype(F32) + self.got(2)[at_rows].astype(F32)
                    ).astype(BF16)
                self.added[i].start()

        def finish(self, store):
            for copy in self.plain + self.added:
                copy.wait()
            for copy in self.across:
                copy.wait_send()

            @pl.loop(0, 4)
            def _(c):
                at_rows = block_rows(c)
                total = self.both[at_rows, lanes(chip * TILE)].astype(F32)
                for p in range(2):
                    total += self.got(p)[at_rows].astype(F32)
                store(at_rows, total)

            for p in range(2 if self.share else 0):
                pl.semaphore_signal(free_chips, inc=1, device_id=peers[p], device_id_type=MESH)

    def fill_branch(start):
        @pl.loop(0, 4)
        def _(c):
            where = lanes(start, half)
            total = dot(at[0, c, HEADROWS:, :rows], att[0, :, where], 0, 0)
            total += dot(at[1, c, HEADROWS:, :rows], att[1, :, where], 0, 0)
            part[block_rows(c), where] = total.astype(BF16)

    small[...] = jnp.zeros(small.shape, F32)
    square_at = lax.broadcasted_iota(jnp.int32, (1, WIDE), 1)

    def note_square(index, value):
        total = jnp.sum(value * value)
        small[0, 2:3, :] += jnp.where(square_at == index, total, 0.0)

    def store_branch(at_rows, total):
        note_square(0, total)
        mid[at_rows] = normed[at_rows].astype(F32) + total

    branch_sum = Sum(guard=False)
    branch_sum.begin(fill_branch)
    cot_in.arrive()
    branch_sum.combine()
    branch_sum.send()
    branch_sum.pass_on()
    branch_sum.finish(store_branch)
    main_line.relay()
    middle = mid[...]
    inverse_two = lax.rsqrt(jnp.sum(middle * middle, 0, keepdims=True) / D + EPSILON)

    @pl.loop(0, 4)
    def _(c):
        at_rows = block_rows(c)
        sending[0, at_rows] = (mid[at_rows] * inverse_two * gcol[at_rows, 1:2]).astype(BF16)

    def token_block(c):
        return low2.at[:, lanes(core * half + c * TILE)]

    low_in = Gather(sending.at[0], token_block)
    cot_in.finish()

    @pl.loop(0, 4)
    def _(c):
        acc3[block_rows(c)] = jnp.zeros((rows, seq), F32)

    low_in.pass_on()
    low_in.arrive()
    low_in.finish()
    extra_line.relay()

    def feed(slot):
        where = lanes(slot * TILE)
        unit_rows = rows_at(slot * TILE, TILE, TILE)
        for m in range(3):
            turned[m * TILE : (m + 1) * TILE] = ff[m, :, where].T

        @pl.loop(0, seq // SPAN)
        def _(n):
            span = lanes(n * SPAN, SPAN)
            gate_up = dot(turned[: 2 * TILE], low2[:, span], 1, 0)
            grad_hidden = dot(turned[2 * TILE :], gs[:, span], 1, 0)
            gate, up = gate_up[:TILE], gate_up[TILE:]
            sigmoid = 1.0 / (1.0 + jnp.exp(-gate))
            activated = gate * sigmoid
            hid[unit_rows, span] = (activated * up).astype(BF16)
            gg[:TILE, span] = (
                grad_hidden * up * sigmoid * (1.0 + gate * (1.0 - sigmoid))
            ).astype(BF16)
            gg[TILE:, span] = (grad_hidden * activated).astype(BF16)

        @pl.loop(0, 4)
        def _(c):
            at_rows = block_rows(c)
            pair = jnp.concatenate([ff[0, at_rows, where], ff[1, at_rows, where]], 1)
            acc3[at_rows] += dot(pair, gg[...], 1, 0)
            grads = dot(low2[at_rows], gg[...], 1, 1).astype(BF16)
            gout[0, at_rows, where] = grads[:, :TILE]
            gout[1, at_rows, where] = grads[:, TILE:]
            gout[2, at_rows, where] = dot(gs[at_rows], hid[unit_rows], 1, 1).astype(BF16)

    main_back = MainGrads(gout, main_got, chip, plane, core, marks)
    extra_back = Collect(gout.at[:, :, last], extra_got, extra_plane, chip, plane, core, marks)
    load_marks = marks.many(3)

    def add_tiles(slot):
        def add(source):
            loads = [
                pltpu.make_async_copy(source.at[m], part.at[:, lanes(m * TILE)], load_marks(m))
                for m in range(3)
            ]
            for load in loads:
                load.start()
            for load in loads:
                load.wait()
            where = lanes(slot * TILE)

            @pl.loop(0, 4)
            def _(c):
                at_rows = block_rows(c)
                for m in range(3):
                    gout[m, at_rows, where] = (
                        gout[m, at_rows, where].astype(F32)
                        + part[at_rows, m * TILE : (m + 1) * TILE].astype(F32)
                    ).astype(BF16)

        return add

    slots = [away(plane, 1), plane, away(plane, 2), away(plane, 3), 4]
    inner = is_inner(plane)

    @pl.loop(0, 5)
    def _(turn):
        for i, step in ((0, 1), (2, 2), (3, 3)):

            @pl.when(turn == i)
            def _():
                main_line.arrive(step)

        @pl.when(turn == 4)
        def _():
            extra_line.arrive()

        slot = sum((turn == i).astype(jnp.int32) * slots[i] for i in range(5))
        feed(slot)

        @pl.when((turn == 0) & no(inner))
        def _():
            main_back.start(1)

        @pl.when((turn == 3) & no(inner))
        def _():
            main_back.start(3)
            main_back.start(2)

    @pl.when(inner)
    def _():
        main_back.start(1)
        main_back.start(3)

    extra_back.start(None)
    main_line.finish()

    def fill_grad_two(start):
        @pl.loop(0, 4)
        def _(c):
            where = lanes(start, half)
            part[block_rows(c), where] = acc3[block_rows(c), where].astype(BF16)

    def store_gsum(at_rows, total):
        gsum[at_rows] = total

    two_sum = Sum(guard=True)
    two_sum.begin(fill_grad_two)
    two_sum.combine()
    two_sum.send()
    two_sum.pass_on()

    def fill_ffn(start):
        @pl.loop(0, 4)
        def _(c):
            where = lanes(start, half)
            part[block_rows(c), where] = dot(
                ff[2, block_rows(c)], hid[:, where], 1, 0
            ).astype(BF16)

    ffn_sum = Sum(
        guard=True, both=ff.at[1, :, lanes(0, half)],
        got=lambda i: ff.at[0, :, lanes(i * TILE)], share=False,
    )
    ffn_sum.begin(fill_ffn)
    two_sum.finish(store_gsum)

    def norm_back(source, inverse, gain_lane, base, store):
        def add_dots(c, total):
            at_rows = block_rows(c)
            gain = gcol[at_rows, gain_lane : gain_lane + 1]
            return total + jnp.sum(gsum[at_rows] * gain * source(at_rows), 0, keepdims=True)

        dots = lax.fori_loop(0, 4, add_dots, jnp.zeros((1, TILE), F32))
        scaled = inverse * inverse * inverse * dots / D

        @pl.loop(0, 4)
        def _(c):
            at_rows = block_rows(c)
            gain = gcol[at_rows, gain_lane : gain_lane + 1]
            grad, value = gsum[at_rows], source(at_rows)
            store(at_rows, base(at_rows) + (grad * gain * inverse - value * scaled))

        def gain_back():
            @pl.loop(0, 4)
            def _(c):
                at_rows = block_rows(c)
                for_gain = jnp.sum((gsum[at_rows] * source(at_rows) * inverse).T, 0, keepdims=True)
                small[c, gain_lane : gain_lane + 1, 0:rows] = for_gain

        return gain_back

    def store_middle(at_rows, value):
        gmid[at_rows] = value
        sending[1, at_rows] = value.astype(BF16)

    gain_two_back = norm_back(
        lambda r: mid[r], inverse_two, 1, lambda r: gs[r, lanes(first)].astype(F32), store_middle
    )
    mid_in = Gather(sending.at[1], token_block)
    gain_two_back()
    ffn_sum.combine()
    mid_in.pass_on()
    ffn_sum.send()
    mid_in.arrive()

    @pl.loop(0, 2)
    def _(h):
        total = dot(at[h, 0, HEADROWS:, :rows], low2[0:rows], 1, 0)
        for c in range(1, 4):
            total += dot(at[h, c, HEADROWS:, :rows], low2[c * rows : (c + 1) * rows], 1, 0)
        gatt[h] = total.astype(BF16)

    main_back.relay(add_tiles(away(plane, 2)))

    @pl.loop(0, 2)
    def _(h):
        grad_keys = jnp.zeros((FEAT, seq), F32)
        grad_values = jnp.zeros((HDIM, seq), F32)

        def padded(value):
            short = seq - value.shape[1]
            if not short:
                return value
            return jnp.concatenate([value, jnp.zeros((value.shape[0], short), F32)], 1)

        for b in range(seq // SPAN):
            seen = (b + 1) * SPAN
            span = slice(b * SPAN, seen)
            scores, kernel, visible = kernel_of(h, b)
            inverse = inv_sum[h, :, span]
            weights = kernel * inverse
            grad_weights = dot(vs[h, :, :seen], gatt[h, :, span], 0, 0)
            grad_values += padded(dot(gatt[h, :, span], weights.astype(BF16), 1, 1))
            dots = jnp.sum(grad_weights * weights, 0, keepdims=True)
            grad_kernel = (grad_weights - dots) * inverse
            grad_scores = jnp.where(visible, grad_kernel * (1.0 + scores), 0.0).astype(BF16)
            gproj[h, :FEAT, span] = (
                dot(ks[h, :, :seen], grad_scores, 1, 0) * FEAT**-0.5
            ).astype(BF16)
            grad_keys += padded(dot(qs[h, :, span], grad_scores, 1, 1))
        gproj[h, FEAT : 2 * FEAT] = grad_keys.astype(BF16)
        tap = taps(h)
        grad_raw = tap[0] * grad_values
        sums = [jnp.sum(grad_values * raw[h], 1, keepdims=True)]
        for j in range(1, CONV):
            masked = jnp.where(position >= j, grad_values, 0.0)
            grad_raw += tap[j] * pltpu.roll(masked, seq - j, 1)
            sums.append(jnp.sum(masked * pltpu.roll(raw[h], j, 1), 1, keepdims=True))
        gproj[h, 2 * FEAT :] = grad_raw.astype(BF16)
        columns = jnp.zeros((HDIM, TILE), F32)
        for j in range(CONV):
            columns = jnp.where(tail == rows % TILE + j, sums[j], columns)
        for c in range(4):
            gat[h, c, 2 * FEAT : HEADROWS, WIDE - TILE :] = columns.astype(BF16)

    ffn_sum.pass_on()
    mid_in.finish()

    def fill_grad_one(start):
        @pl.loop(0, 4)
        def _(c):
            where = lanes(start, half)
            total = dot(at[0, c, :HEADROWS, :rows], gproj[0, :, where], 0, 0)
            total += dot(at[1, c, :HEADROWS, :rows], gproj[1, :, where], 0, 0)
            part[block_rows(c), where] = total.astype(BF16)

    one_sum = Sum(guard=True)
    one_sum.begin(fill_grad_one)
    one_sum.combine()
    one_sum.send()

    out_back, in_back = [
        [
            Collect(
                gat.at[a, :, span], att_got.at[a, :, :, span], 2 * core + a,
                chip, plane, core, marks,
            )
            for a in range(2)
        ]
        for span in (out_rows, in_rows)
    ]

    def head_grads(left, right, start, size):
        whole = rows // TILE * TILE

        @pl.loop(0, 2)
        def _(h):
            for c in range(4):
                grad = dot(left[h], right[c * rows : (c + 1) * rows], 1, 1).astype(BF16)
                gat[h, c, start : start + size, :whole] = grad[:, :whole]
                gat[h, c, start : start + size, whole:rows] = grad[:, whole:]

    head_grads(att, low2, HEADROWS, HDIM)
    for item in out_back:
        item.start(None)
    head_grads(gproj, xs, 0, HEADROWS)
    for item in in_back:
        item.start(None)

    def store_result(at_rows, total):
        note_square(1, total)
        total = mid[at_rows] + total
        note_square(2, total)
        sending[0, at_rows] = total.astype(BF16)

    one_sum.pass_on()

    def hand_out(source, target):
        send, here = marks.many(3), marks.many(3)
        copies = [
            remote(
                source.at[block_rows(others[p])], target.at[:, lanes(chip * TILE)],
                send(p), here(p), peers[p],
            )
            for p in range(3)
        ]
        copies.append(
            pltpu.make_async_copy(
                source.at[block_rows(chip)], target.at[:, lanes(chip * TILE)], marks.one()
            )
        )
        for copy in copies:
            copy.start()
        return copies

    ffn_sum.finish(store_result)
    pending = hand_out(sending.at[0], out_res)

    extra_back.relay(add_tiles(4))

    one_sum.finish(store_gsum)
    inverse_own = inv_all[:, lanes(first)]

    def store_tokens(at_rows, value):
        sending[1, at_rows] = value.astype(BF16)

    gain_one_back = norm_back(
        lambda r: normed[r].astype(F32), inverse_own, 0, lambda r: gmid[r], store_tokens
    )
    pending += hand_out(sending.at[1], out_tok)
    gain_one_back()

    for c in range(1, 4):
        small[c, 2:3] = small[0, 2:3]
    a_send, a_here = marks.many(3), marks.many(3)
    trio = [
        remote(small.at[others[p]], small_a.at[p], a_send(p), a_here(p), peers[p])
        for p in range(3)
    ]
    for copy in trio:
        copy.start()

    main_back.total(add_tiles(plane))
    back_send, back_here = marks.many(3), marks.many(3)
    mine = lanes(plane * TILE)
    back_to = out_ff.at[:, :, lanes(chip * TILE)]
    backs = [
        remote(
            gout.at[:, block_rows(others[p]), mine], back_to, back_send(p), back_here(p), peers[p]
        )
        for p in range(3)
    ]
    backs.append(
        pltpu.make_async_copy(gout.at[:, block_rows(chip), mine], back_to, marks.one())
    )
    for copy in backs:
        copy.start()
    pending += backs

    for copy in trio:
        copy.wait()
    small_b[0] = small[chip] + small_a[0] + small_a[1] + small_a[2]
    b_send, b_here = marks.many(7), marks.many(7)
    seven = [
        remote(small_b.at[0], small_b.at[1 + i], b_send(i), b_here(i), to)
        for i, to in enumerate(line + [mate] + line_mates)
    ]
    for copy in seven:
        copy.start()

    extra_back.total(add_tiles(4))
    last_send, last_here, last_local = marks.many(4), marks.one(), marks.one()

    def last_copy(c):
        return remote(
            gout.at[:, block_rows(c), last], out_ff.at[:, :, last], last_send(c), last_here,
            device(c, plane, chip % 2),
        )

    def last_keep():
        return pltpu.make_async_copy(
            gout.at[:, block_rows(chip), last], out_ff.at[:, :, last], last_local
        )

    for c in range(4):
        same = (c == chip) & (core == chip % 2)

        @pl.when(holds_extra & same)
        def _():
            last_keep().start()

        @pl.when(holds_extra & no(same))
        def _():
            last_copy(c).start()

    head_marks = marks.many(4)

    def add_head(a, start, size):
        def add(source):
            loads = [
                pltpu.make_async_copy(
                    source.at[c], part.at[c * BLOCKROWS : c * BLOCKROWS + size, 0:WIDE],
                    head_marks(c),
                )
                for c in range(4)
            ]
            for load in loads:
                load.start()
            for load in loads:
                load.wait()
            for c in range(4):
                gat[a, c, start : start + size] = (
                    gat[a, c, start : start + size].astype(F32)
                    + part[c * BLOCKROWS : c * BLOCKROWS + size, 0:WIDE].astype(F32)
                ).astype(BF16)

        return add

    for items, start, size in ((out_back, HEADROWS, HDIM), (in_back, 0, HEADROWS)):
        for a in range(2):
            items[a].relay(add_head(a, start, size))
    for items, start, size in ((out_back, HEADROWS, HDIM), (in_back, 0, HEADROWS)):
        for a in range(2):
            items[a].total(add_head(a, start, size))
    head_send, head_here, head_local = marks.many(4), marks.many(2), marks.one()

    def head_copy(c):
        return remote(
            gat.at[plane % 2, c], out_at.at[chip % 2], head_send(c), head_here(chip % 2),
            device(c, plane, chip // 2),
        )

    def head_keep():
        return pltpu.make_async_copy(gat.at[plane % 2, chip], out_at.at[chip % 2], head_local)

    for c in range(4):
        same = (c == chip) & (core == chip // 2)

        @pl.when(holds_att & same)
        def _():
            head_keep().start()

        @pl.when(holds_att & no(same))
        def _():
            head_copy(c).start()

    for copy in seven:
        copy.wait()
    total = small_b[0]
    for i in range(7):
        total += small_b[1 + i]
    small_a[0] = total
    small_out = pltpu.make_async_copy(small_a.at[0], out_small, marks.one())
    small_out.start()
    pending.append(small_out)
    for item in in_line + out_line + [extra_line, main_back, extra_back] + out_back + in_back:
        item.finish()
    for copy in pending:
        copy.wait()
    for c in range(4):
        for holds, same, local, away_copy in (
            (holds_extra, (c == chip) & (core == chip % 2), last_keep, last_copy),
            (holds_att, (c == chip) & (core == chip // 2), head_keep, head_copy),
        ):

            @pl.when(holds & same)
            def _():
                local().wait()

            @pl.when(holds & no(same))
            def _():
                away_copy(c).wait_send()

    @pl.when(no(extra_self))
    def _():
        last_copy(0).wait_recv()

    for h in range(2):

        @pl.when(no(att_self[h]))
        def _():
            remote(
                gat.at[0, 0], out_at.at[h], head_send(0), head_here(h), mate
            ).wait_recv()

    pl.semaphore_wait(free_mate, 1)
    pl.semaphore_wait(free_chips, 2)
    assert marks.used <= MARKS, marks.used


def dma(*shape):
    return pltpu.SemaphoreType.DMA(shape)


def run_layer(wff, wat, tok, cot, gains):
    rows, half = tok.shape
    width, seq = 4 * rows, 2 * half
    shape = jax.ShapeDtypeStruct
    vmem = pltpu.VMEM
    tiles = (3, width, TILE)
    head = (4, BLOCKROWS, WIDE)
    return pl.pallas_call(
        layer_kernel,
        out_shape=[
            shape((3, rows, 5 * TILE), BF16),
            shape((2, BLOCKROWS, WIDE), BF16),
            shape((rows, half), BF16),
            shape((rows, half), BF16),
            shape((8, WIDE), F32),
            shape((4,) + tiles, BF16),
            shape((4,) + tiles, BF16),
            shape((2, 4) + head, BF16),
        ],
        in_specs=[ANY] * 5,
        out_specs=[ANY] * 8,
        scratch_shapes=[
            vmem((3, width, 5 * TILE), BF16),
            vmem((2,) + head, BF16),
            vmem((width, seq), BF16),
            vmem((width, seq), BF16),
            vmem((width, seq), BF16),
            vmem((width, seq), BF16),
            vmem((width, seq), F32),
            vmem((3, width, 5 * TILE), BF16),
            vmem((2,) + head, BF16),
            vmem((width, half), BF16),
            vmem((width, half), BF16),
            vmem((3, width, TILE), BF16),
            vmem((3 * TILE, width), BF16),
            vmem((5 * TILE, seq), BF16),
            vmem((2 * TILE, seq), BF16),
            vmem((4, 16, WIDE), BF16),
            vmem((width, TILE), F32),
            vmem((2, HDIM, seq), F32),
            vmem((2, FEAT, seq), BF16),
            vmem((2, FEAT, seq), BF16),
            vmem((2, HDIM, seq), BF16),
            vmem((2, HDIM, seq), BF16),
            vmem((2, HDIM, seq), BF16),
            vmem((2, HEADROWS, seq), BF16),
            vmem((width, TILE), F32),
            vmem((width, TILE), F32),
            vmem((width, TILE), F32),
            vmem((width, TILE), BF16),
            vmem((2, width, TILE), BF16),
            vmem((1, seq), F32),
            vmem((2, 1, seq), F32),
            vmem((4, 8, WIDE), F32),
            vmem((3, 8, WIDE), F32),
            vmem((8, 8, WIDE), F32),
            dma(MARKS),
            pltpu.SemaphoreType.REGULAR,
            pltpu.SemaphoreType.REGULAR,
        ],
        compiler_params=pltpu.CompilerParams(
            collective_id=0, has_side_effects=True, vmem_limit_bytes=63 * 2**20
        ),
        name="layer",
    )(wff, wat, tok, cot, gains)


def on_device_full(
    tokens, cotangent, w_qkv, conv_weight, w_out, w_gate, w_up, w_down, gain_mix, gain_ffn
):
    rows, half = tokens.shape
    ffn_cols = w_gate.shape[1]
    heads = 2
    pad = ((0, 0), (0, 5 * TILE - ffn_cols))
    wff = jnp.stack([jnp.pad(w, pad) for w in (w_gate, w_up, w_down)])
    taps = jnp.pad(
        conv_weight.T.reshape(heads, HDIM, CONV),
        ((0, 0), (2 * FEAT, 0), (0, WIDE - rows - CONV)),
    )
    upper = jnp.concatenate([w_qkv.T.reshape(heads, HEADROWS, rows), taps], 2)
    lower = jnp.pad(w_out.reshape(heads, HDIM, rows), ((0, 0), (0, 0), (0, WIDE - rows)))
    wat = jnp.concatenate([upper, lower], 1)
    gains = jnp.pad(
        jnp.stack([gain_mix, gain_ffn]), ((0, 14), (0, WIDE - rows))
    )
    out_ff, out_at, out_res, out_tok, small = run_layer(wff, wat, tokens, cotangent, gains)[:5]
    out_at = out_at.astype(F32)
    return (
        out_res,
        out_tok.astype(F32),
        out_at[:, :HEADROWS, :rows].reshape(heads * HEADROWS, rows).T,
        out_at[:, 2 * FEAT : HEADROWS, rows : rows + CONV].reshape(heads * HDIM, CONV).T,
        out_at[:, HEADROWS:, :rows].reshape(heads * HDIM, rows),
        out_ff[0, :, :ffn_cols].astype(F32),
        out_ff[1, :, :ffn_cols].astype(F32),
        out_ff[2, :, :ffn_cols].astype(F32),
        small[0, :rows],
        small[1, :rows],
        jnp.sqrt(small[2, :3] / (8 * half * 4 * rows)),
    )


def on_device(tokens, cotangent, lengths, deal_order, *weights):
    total_rows = tokens.shape[1] * lax.axis_size("col")
    if (
        lengths.shape[0] * LONGEST == total_rows
        and lax.axis_size("row") == 4
        and lax.axis_size("col") == 8
        and total_rows == 4 * LONGEST
        and weights[0].shape[1] == 2 * HEADROWS
        and 4 * TILE < weights[3].shape[1] <= 5 * TILE
    ):
        return on_device_full(tokens, cotangent, *weights)
    return on_device_general(tokens, cotangent, lengths, deal_order, *weights)


def solution(mesh):
    in_specs = (
        P("row", "col"),
        P("row", "col"),
        P(),
        P(),
        P("row", "col"),
        P(None, "col"),
        P("col", "row"),
        P("row", "col"),
        P("row", "col"),
        P("row", "col"),
        P("row"),
        P("row"),
    )
    out_specs = (
        P("row", "col"),
        P("row", "col"),
        P("row", "col"),
        P(None, "col"),
        P("col", "row"),
        P("row", "col"),
        P("row", "col"),
        P("row", "col"),
        P("row"),
        P("row"),
        P(),
    )
    return jax.shard_map(
        on_device, mesh=mesh, in_specs=in_specs, out_specs=out_specs, check_vma=False
    )
```

```python
import jax
import jax.numpy as jnp
from jax import lax
from jax.experimental import pallas as pl
from jax.experimental.pallas import tpu as pltpu
from jax.sharding import PartitionSpec as P

D = 1792
FEAT = 16
CONV = 3
LONGEST = 1024
HDIM = 112


EPSILON = 1e-06


def dealing(lengths, deal_order, total_rows):
    seq_ids = jnp.arange(lengths.shape[0], dtype=jnp.int32)
    chosen = (deal_order[:, None] == seq_ids[None, :]).astype(jnp.int32)
    dealt_lengths = jnp.sum(chosen * lengths[None, :], 1)
    given_start = jnp.cumsum(lengths) - lengths
    dealt_start = jnp.cumsum(dealt_lengths) - dealt_lengths
    given_of_dealt = jnp.sum(chosen * given_start[None, :], 1)
    dealt_of_given = jnp.sum(chosen * dealt_start[:, None], 0)
    places = jnp.arange(total_rows, dtype=jnp.int32)
    in_dealt = (places[:, None] >= dealt_start[None, :]) & (
        places[:, None] < (dealt_start + dealt_lengths)[None, :]
    )
    in_given = (places[:, None] >= given_start[None, :]) & (
        places[:, None] < (given_start + lengths)[None, :]
    )
    source = places + jnp.sum(jnp.where(in_dealt, (given_of_dealt - dealt_start)[None, :], 0), 1)
    target = places + jnp.sum(jnp.where(in_given, (dealt_of_given - given_start)[None, :], 0), 1)
    offsets = places - jnp.sum(jnp.where(in_dealt, dealt_start[None, :], 0), 1)
    return (source, target, offsets)


def convolve(raw_values, kernel_conv, offsets):
    mixed = kernel_conv[0] * raw_values
    for delay_step in range(1, CONV):
        moved = jnp.concatenate(
            [jnp.zeros_like(raw_values[:delay_step]), raw_values[:-delay_step]], 0
        )
        mixed = mixed + kernel_conv[delay_step] * jnp.where(
            (offsets >= delay_step)[:, None, None], moved, 0.0
        )
    return mixed


def convolve_back(grad_mixed, raw_values, kernel_conv, offsets):
    grad_raw = kernel_conv[0] * grad_mixed
    sums_list = [jnp.sum(grad_mixed * raw_values, 0)]
    for delay_step in range(1, CONV):
        masked = jnp.where((offsets >= delay_step)[:, None, None], grad_mixed, 0.0)
        pulled = jnp.concatenate([masked[delay_step:], jnp.zeros_like(masked[:delay_step])], 0)
        grad_raw = grad_raw + kernel_conv[delay_step] * pulled
        moved = jnp.concatenate(
            [jnp.zeros_like(raw_values[:delay_step]), raw_values[:-delay_step]], 0
        )
        sums_list.append(jnp.sum(masked * moved, 0))
    return (grad_raw, jnp.stack(sums_list))


def bin_scores(query, keys, offsets):
    scores = jnp.einsum("thf,shf->hts", query, keys, preferred_element_type=jnp.float32) * FEAT ** (
        -0.5
    )
    positions = jnp.arange(query.shape[0], dtype=jnp.int32)
    visible = (positions[None, :] <= positions[:, None]) & (
        positions[:, None] - positions[None, :] <= offsets[:, None]
    )
    kernel = jnp.where(visible[None], 1.0 + scores + 0.5 * scores * scores, 0.0)
    return (scores, visible, kernel)


def attend_bin(pieces):
    query, keys, values, offsets = pieces
    scores, visible, kernel = bin_scores(query, keys, offsets)
    weights = (kernel / jnp.sum(kernel, -1, keepdims=True)).astype(jnp.bfloat16)
    return jnp.einsum("hts,shd->thd", weights, values, preferred_element_type=jnp.float32)


def attend_back(pieces):
    query, keys, values, offsets, grad_attend = pieces
    scores, visible, kernel = bin_scores(query, keys, offsets)
    totals = jnp.sum(kernel, -1, keepdims=True)
    weights = kernel / totals
    grad_weights = jnp.einsum(
        "thd,shd->hts", grad_attend, values, preferred_element_type=jnp.float32
    )
    grad_values = jnp.einsum(
        "hts,thd->shd",
        weights.astype(jnp.bfloat16),
        grad_attend,
        preferred_element_type=jnp.float32,
    )
    grad_kernel = (grad_weights - jnp.sum(grad_weights * weights, -1, keepdims=True)) / totals
    grad_scores = jnp.where(visible[None], grad_kernel * (1.0 + scores), 0.0).astype(jnp.bfloat16)
    grad_query = jnp.einsum(
        "hts,shf->thf", grad_scores, keys, preferred_element_type=jnp.float32
    ) * FEAT ** (-0.5)
    grad_keys = jnp.einsum(
        "hts,thf->shf", grad_scores, query, preferred_element_type=jnp.float32
    ) * FEAT ** (-0.5)
    return (grad_query, grad_keys, grad_values)


def times_transposed(left, right):
    return lax.dot_general(
        left, right, (((1,), (1,)), ((), ())), preferred_element_type=jnp.float32
    )


def tokens_product(left, right):
    return lax.dot_general(
        left, right, (((0,), (0,)), ((), ())), preferred_element_type=jnp.float32
    )


def plain_product(left, right):
    return jnp.dot(left, right, preferred_element_type=jnp.float32)


def gather_cols(values):
    return lax.all_gather(values, "col", axis=0, tiled=True)


def gather_rows(values):
    return lax.all_gather(values, "row", axis=0, tiled=True)


def grad_gather_cols(values):
    return lax.all_gather(values, "col", axis=1, tiled=True)


def grad_gather_rows(values):
    return lax.all_gather(values, "row", axis=0, tiled=True)


def width_total(values):
    return lax.psum(values, "row")


def forward_rows(gathered, row_index, weight, rows_here):

    def partial_term(row_start, row_count):
        picked = jnp.take(gathered, row_index, axis=0)
        return jnp.dot(picked, weight, preferred_element_type=jnp.float32)

    return lax.psum_scatter(
        partial_term(jnp.int32(0), rows_here * lax.axis_size("row")),
        "row",
        scatter_dimension=0,
        tiled=True,
    )


def forward_cols(gathered, row_index, weight, rows_here, product):

    def partial_term(row_start, row_count):
        picked = jnp.take(gathered, row_index, axis=0)
        return product(picked, weight)

    return lax.psum_scatter(
        partial_term(jnp.int32(0), lax.axis_size("col") * rows_here).astype(jnp.bfloat16),
        "col",
        scatter_dimension=0,
        tiled=True,
    ).astype(jnp.float32)


def backward_rows(gathered, row_index, weight, rows_here, contract):

    def partial_term(row_start, row_count):
        picked = jnp.take(gathered, row_index, axis=1)
        return lax.dot_general(
            picked, weight, (((0,), (contract,)), ((), ())), preferred_element_type=jnp.float32
        )

    return lax.psum_scatter(
        partial_term(jnp.int32(0), lax.axis_size("row") * rows_here).astype(jnp.bfloat16),
        "row",
        scatter_dimension=0,
        tiled=True,
    ).astype(jnp.float32)


def backward_cols(gathered, row_index, weight, rows_here):

    def partial_term(row_start, row_count):
        picked = jnp.take(gathered, row_index, axis=0)
        return times_transposed(picked, weight)

    return lax.psum_scatter(
        partial_term(jnp.int32(0), lax.axis_size("col") * rows_here).astype(jnp.bfloat16),
        "col",
        scatter_dimension=0,
        tiled=True,
    ).astype(jnp.float32)


def norm_forward(values, norm_gain):
    totals = width_total(jnp.sum(values * values, -1))
    inverse = lax.rsqrt(totals / D + EPSILON)
    return (values * inverse[:, None] * norm_gain, inverse)


def norm_back(values, inverse, norm_gain, grad_normed, dot_sums):
    cubed = inverse * inverse * inverse
    return grad_normed * norm_gain * inverse[:, None] - values * (cubed * dot_sums / D)[:, None]


def on_device_general(
    tokens,
    cotangent,
    lengths,
    deal_order,
    w_qkv,
    conv_weight,
    w_out,
    w_gate,
    w_up,
    w_down,
    gain_mix,
    gain_ffn,
):
    local_rows = tokens.shape[1]
    total_rows = local_rows * lax.axis_size("col")
    group_rows = total_rows // lax.axis_size("row")
    bin_count = group_rows // LONGEST
    heads_here = w_out.shape[0] // HDIM
    ffn_cols = w_gate.shape[1]
    source, target, offsets = dealing(lengths, deal_order, total_rows)
    group_offsets = lax.dynamic_slice_in_dim(
        offsets, lax.axis_index("row") * group_rows, group_rows
    )
    inputs = tokens.astype(jnp.float32).T
    gain_one = gain_mix.astype(jnp.float32)
    gain_two = gain_ffn.astype(jnp.float32)
    both_weights = jnp.concatenate([w_gate, w_up], 1)
    normed_one, inverse_one = norm_forward(inputs, gain_one)
    low_one = normed_one.astype(jnp.bfloat16)
    all_one = gather_cols(low_one)
    projected = forward_rows(all_one, source, w_qkv, group_rows)
    projected = projected.reshape(group_rows, heads_here, 2 * FEAT + HDIM)
    query = projected[:, :, :FEAT].astype(jnp.bfloat16)
    keys = projected[:, :, FEAT : 2 * FEAT].astype(jnp.bfloat16)
    raw_values = projected[:, :, 2 * FEAT :]
    kernel_conv = conv_weight.astype(jnp.float32).reshape(CONV, heads_here, HDIM)
    values = convolve(raw_values, kernel_conv, group_offsets).astype(jnp.bfloat16)
    binned = (
        query.reshape(bin_count, LONGEST, heads_here, FEAT),
        keys.reshape(bin_count, LONGEST, heads_here, FEAT),
        values.reshape(bin_count, LONGEST, heads_here, HDIM),
        group_offsets.reshape(bin_count, LONGEST),
    )
    attended = (
        lax.map(attend_bin, binned).reshape(group_rows, heads_here * HDIM).astype(jnp.bfloat16)
    )
    all_attended = gather_rows(attended)
    branch_mix = forward_cols(all_attended, target, w_out, local_rows, plain_product)
    middle = inputs + branch_mix
    normed_two, inverse_two = norm_forward(middle, gain_two)
    low_two = normed_two.astype(jnp.bfloat16)
    all_two = gather_cols(low_two)
    gate_up = forward_rows(all_two, source, both_weights, group_rows)
    gate = gate_up[:, :ffn_cols]
    up_proj = gate_up[:, ffn_cols:]
    activated = jax.nn.silu(gate)
    hidden = (activated * up_proj).astype(jnp.bfloat16)
    all_hidden = gather_rows(hidden)
    branch_ffn = forward_cols(all_hidden, target, w_down, local_rows, times_transposed)
    result_full = middle + branch_ffn
    grad_result = cotangent.astype(jnp.float32).T
    all_grad_ffn = grad_gather_cols(cotangent)
    hidden_again = gather_rows(hidden)
    grad_down = jnp.dot(
        jnp.take(all_grad_ffn, source, axis=1), hidden_again, preferred_element_type=jnp.float32
    )
    grad_hidden = backward_rows(all_grad_ffn, source, w_down, group_rows, 0)
    gate_sigmoid = jax.nn.sigmoid(gate)
    grad_gate_part = grad_hidden * up_proj * gate_sigmoid * (1.0 + gate * (1.0 - gate_sigmoid))
    grad_up_part = grad_hidden * activated
    grad_gate_up = jnp.concatenate([grad_gate_part, grad_up_part], 1).astype(jnp.bfloat16)
    all_grad_gate_up = grad_gather_rows(grad_gate_up)
    two_again = gather_cols(low_two)
    grad_both = tokens_product(jnp.take(two_again, source, axis=0), all_grad_gate_up)
    grad_normed_two = backward_cols(all_grad_gate_up, target, both_weights, local_rows)
    dots_two = width_total(jnp.sum(grad_normed_two * gain_two * middle, -1))
    grad_middle = grad_result + norm_back(middle, inverse_two, gain_two, grad_normed_two, dots_two)
    gain_part_two = jnp.sum(grad_normed_two * middle * inverse_two[:, None], 0)
    low_grad_middle = grad_middle.T.astype(jnp.bfloat16)
    all_grad_middle = grad_gather_cols(low_grad_middle)
    attended_again = gather_rows(attended)
    grad_out = lax.dot_general(
        attended_again,
        jnp.take(all_grad_middle, source, axis=1),
        (((0,), (1,)), ((), ())),
        preferred_element_type=jnp.float32,
    )
    grad_attended = backward_rows(all_grad_middle, source, w_out, group_rows, 1).astype(
        jnp.bfloat16
    )
    binned_back = binned + (grad_attended.reshape(bin_count, LONGEST, heads_here, HDIM),)
    grad_query, grad_keys, grad_values = lax.map(attend_back, binned_back)
    grad_values = grad_values.reshape(group_rows, heads_here, HDIM)
    grad_raw, conv_part = convolve_back(grad_values, raw_values, kernel_conv, group_offsets)
    grad_projected = jnp.concatenate(
        [
            grad_query.reshape(group_rows, heads_here, FEAT),
            grad_keys.reshape(group_rows, heads_here, FEAT),
            grad_raw,
        ],
        2,
    )
    grad_projected = grad_projected.reshape(group_rows, heads_here * (2 * FEAT + HDIM)).astype(
        jnp.bfloat16
    )
    all_grad_projected = grad_gather_rows(grad_projected)
    one_again = gather_cols(low_one)
    grad_qkv = tokens_product(jnp.take(one_again, source, axis=0), all_grad_projected)
    grad_normed_one = backward_cols(all_grad_projected, target, w_qkv, local_rows)
    squares = jnp.stack(
        [
            jnp.sum(branch_mix * branch_mix),
            jnp.sum(branch_ffn * branch_ffn),
            jnp.sum(result_full * result_full),
        ]
    )
    dots_one, grad_conv, squares_rows = width_total(
        (
            jnp.sum(grad_normed_one * gain_one * inputs, -1),
            conv_part.reshape(CONV, heads_here * HDIM),
            squares,
        )
    )
    grad_tokens = grad_middle + norm_back(inputs, inverse_one, gain_one, grad_normed_one, dots_one)
    gain_part_one = jnp.sum(grad_normed_one * inputs * inverse_one[:, None], 0)
    grad_gain_mix, grad_gain_ffn, squares_all = lax.psum(
        (gain_part_one, gain_part_two, squares_rows), "col"
    )
    rms_values = jnp.sqrt(squares_all / (total_rows * D))
    return (
        result_full.T.astype(jnp.bfloat16),
        grad_tokens.T,
        grad_qkv,
        grad_conv,
        grad_out,
        grad_both[:, :ffn_cols],
        grad_both[:, ffn_cols:],
        grad_down,
        grad_gain_mix,
        grad_gain_ffn,
        rms_values,
    )


HEADROWS = 2 * FEAT + HDIM
BLOCKROWS = HEADROWS + HDIM
TILE = 128
WIDE = 512
SPAN = 256
MARKS = 320
MESH = pl.DeviceIdType.MESH
ANY = pl.BlockSpec(memory_space=pl.ANY)
F32, BF16 = jnp.float32, jnp.bfloat16


def place():
    column = lax.axis_index("col")
    return lax.axis_index("row"), column // 2, column % 2


def device(chip, plane, core):
    return (chip, plane * 2 + core)


def other_chips(chip):
    y, x = chip // 2, chip % 2
    return (y * 2 + 1 - x, (1 - y) * 2 + x, (1 - y) * 2 + 1 - x)


def away(plane, step):
    if step == 1:
        return plane + 1 - 2 * (plane % 2)
    if step == 2:
        return (plane + 2) % 4
    return 3 - plane


def is_inner(plane):
    return ((plane + 1) // 2) % 2 == 1


def remote(source, target, send, receive, to):
    return pltpu.make_async_remote_copy(
        src_ref=source,
        dst_ref=target,
        send_sem=send,
        recv_sem=receive,
        device_id=to,
        device_id_type=MESH,
    )


def lanes(start, size=TILE):
    return pl.ds(pl.multiple_of(start, TILE), size)


def rows_at(start, size, step):
    return pl.ds(pl.multiple_of(start, step), size)


def no(flag):
    return jnp.logical_not(flag)


def dot(a, b, over_a, over_b):
    return lax.dot_general(
        a, b, (((over_a,), (over_b,)), ((), ())), preferred_element_type=F32
    )


class Marks:
    def __init__(self, ref):
        self.ref, self.used = ref, 0

    def one(self):
        self.used += 1
        return self.ref.at[self.used - 1]

    def many(self, count):
        base = self.used
        self.used += count
        return lambda i: self.ref.at[base + i]


class Spread:
    def __init__(self, ref, owner, chip, plane, core, marks):
        self.ref, self.spot = ref, (chip, plane, core)
        self.sends = marks.many(3)
        self.arrived = marks.one()
        inner = is_inner(plane)
        self.mine = plane == owner
        self.outer_owner = self.mine & no(inner)
        self.inner_owner = self.mine & inner
        far = (plane == away(owner, 2)) | ((plane == away(owner, 3)) & is_inner(owner))
        self.relays = inner & far

    def copy(self, step, send):
        chip, plane, core = self.spot
        return remote(
            self.ref, self.ref, self.sends(send), self.arrived,
            device(chip, away(plane, step), core),
        )

    def start(self):
        pl.when(self.outer_owner)(lambda: self.copy(2, 1).start())
        pl.when(self.inner_owner)(lambda: self.copy(3, 1).start())
        pl.when(self.mine)(lambda: self.copy(1, 0).start())

    def relay(self):
        @pl.when(self.relays)
        def _():
            self.copy(1, 2).wait_recv()
            self.copy(1, 2).start()

    def arrive(self):
        pl.when(no(self.mine | self.relays))(lambda: self.copy(1, 2).wait_recv())

    def finish(self):
        @pl.when(self.mine)
        def _():
            self.copy(1, 0).wait_send()
            self.copy(1, 1).wait_send()

        pl.when(self.relays)(lambda: self.copy(1, 2).wait_send())


class Chain:
    def __init__(self, ref, owner, chip, plane, core, marks):
        self.ref, self.spot = ref, (chip, plane, core)
        self.sends = marks.many(2)
        self.arrived = marks.one()
        inner = is_inner(plane)
        self.mine = plane == owner
        self.mine_inner = self.mine & inner
        self.from_end = inner & (plane == away(owner, 1))
        self.from_inner = inner & (plane == away(owner, 3))
        self.from_far = inner & (plane == away(owner, 2))
        self.waits = no(inner) & no(self.mine)

    def copy(self, step, send):
        chip, plane, core = self.spot
        return remote(
            self.ref, self.ref, self.sends(send), self.arrived,
            device(chip, away(plane, step), core),
        )

    def start(self):
        pl.when(self.mine)(lambda: self.copy(1, 0).start())
        pl.when(self.mine_inner)(lambda: self.copy(3, 1).start())

    def relay(self):
        pl.when(self.from_end | self.from_inner)(lambda: self.copy(1, 0).wait_recv())
        pl.when(self.from_end)(lambda: self.copy(3, 0).start())
        pl.when(self.from_inner)(lambda: self.copy(1, 0).start())

    def relay_far(self):
        @pl.when(self.from_far)
        def _():
            self.copy(1, 0).wait_recv()
            self.copy(1, 0).start()

    def arrive(self):
        pl.when(self.waits)(lambda: self.copy(1, 0).wait_recv())

    def finish(self):
        pl.when(no(self.waits))(lambda: self.copy(1, 0).wait_send())
        pl.when(self.mine_inner)(lambda: self.copy(3, 1).wait_send())


class MainTiles:
    def __init__(self, ff, chip, plane, core, marks):
        self.ff, self.spot = ff, (chip, plane, core)
        self.sends, self.here = marks.many(5), marks.many(3)
        self.inner = is_inner(plane)

    def copy(self, slot, to_step, send, receive):
        chip, plane, core = self.spot
        tiles = self.ff.at[:, :, lanes(slot * TILE)]
        return remote(
            tiles, tiles, self.sends(send), self.here(receive),
            device(chip, away(plane, to_step), core),
        )

    def got(self, step):
        self.copy(self.spot[1], 1, 0, step - 1).wait_recv()

    def start(self):
        plane = self.spot[1]
        self.copy(plane, 1, 0, 0).start()
        pl.when(self.inner)(lambda: self.copy(plane, 3, 2, 2).start())

    def relay(self):
        plane = self.spot[1]

        @pl.when(self.inner)
        def _():
            self.got(1)
            self.copy(away(plane, 1), 3, 1, 1).start()
            self.got(3)
            self.copy(away(plane, 3), 1, 3, 1).start()

    def relay_far(self):
        plane = self.spot[1]

        @pl.when(self.inner)
        def _():
            self.got(2)
            self.copy(away(plane, 2), 1, 4, 2).start()

    def arrive(self, step):
        pl.when(no(self.inner))(lambda: self.got(step))

    def finish(self):
        self.copy(self.spot[1], 1, 0, 0).wait_send()

        @pl.when(self.inner)
        def _():
            for send in range(1, 5):
                self.copy(self.spot[1], 1, send, 0).wait_send()


class MainGrads:
    def __init__(self, gout, slots, chip, plane, core, marks):
        self.gout, self.slots, self.spot = gout, slots, (chip, plane, core)
        self.sends, self.here = marks.many(3), marks.many(5)
        self.inner = is_inner(plane)

    def copy(self, slot, to_step, send, receive):
        chip, plane, core = self.spot
        return remote(
            self.gout.at[:, :, lanes(slot * TILE)], self.slots.at[receive],
            self.sends(send), self.here(receive), device(chip, away(plane, to_step), core),
        )

    def start(self, step):
        receive = {1: 0, 2: 4, 3: 3}[step]
        self.copy(away(self.spot[1], step), 1, step - 1, receive).start()

    def relay(self, step, add):
        @pl.when(self.inner)
        def _():
            receive = {2: 3, 3: 4}[step]
            self.copy(self.spot[1], 1, 0, receive).wait_recv()
            slot = away(self.spot[1], step)
            add(slot, self.slots.at[receive])
            self.copy(slot, step, step - 1, step - 1).start()

    def total(self, add):
        plane = self.spot[1]
        self.copy(plane, 1, 0, 0).wait_recv()
        add(plane, self.slots.at[0])

        @pl.when(no(self.inner))
        def _():
            self.copy(plane, 1, 0, 1).wait_recv()
            add(plane, self.slots.at[1])

        @pl.when(self.inner)
        def _():
            self.copy(plane, 1, 0, 2).wait_recv()
            add(plane, self.slots.at[2])

    def finish(self):
        for send in range(3):
            self.copy(self.spot[1], 1, send, 0).wait_send()


class Collect:
    def __init__(self, ref, slots, owner, chip, plane, core, marks):
        self.ref, self.slots, self.spot = ref, slots, (chip, plane, core)
        self.send = marks.one()
        self.arrived = marks.many(3)
        inner, inner_owner = is_inner(plane), is_inner(owner)
        self.mine = plane == owner
        self.mine_outer = self.mine & no(inner)
        self.mine_inner = self.mine & inner
        self.near = plane == away(owner, 1)
        second, third = plane == away(owner, 2), plane == away(owner, 3)
        self.hands = no(inner) & (second | third) & no(self.near)
        self.adds_second = inner & second & no(inner_owner)
        self.adds_third = inner & third & inner_owner

    def copy(self, step, slot):
        chip, plane, core = self.spot
        return remote(
            self.ref, self.slots.at[slot], self.send, self.arrived(slot),
            device(chip, away(plane, step), core),
        )

    def start(self):
        pl.when(self.near)(lambda: self.copy(1, 0).start())
        pl.when(self.hands)(lambda: self.copy(1, 2).start())

    def relay(self, add):
        @pl.when(self.adds_second | self.adds_third)
        def _():
            self.copy(1, 2).wait_recv()
            add(self.slots.at[2])

        pl.when(self.adds_second)(lambda: self.copy(2, 1).start())
        pl.when(self.adds_third)(lambda: self.copy(3, 1).start())

    def total(self, add):
        @pl.when(self.mine)
        def _():
            for slot in range(2):
                self.copy(1, slot).wait_recv()
                add(self.slots.at[slot])

    def finish(self):
        pl.when(no(self.mine))(lambda: self.copy(1, 0).wait_send())


def layer_kernel(
    wff, wat, tok, cot, gains,
    out_ff, out_at, out_res, out_tok, out_small, main_got, extra_got, att_got,
    ff, at, xs, gs, low2, part, acc3, gout, gat, from_mate, both, got, turned, hid, gg,
    gn, gcol, raw, qs, ks, vs, att, gatt, gproj, mid, gmid, gsum, normed, sending, inv_all,
    inv_sum, small, small_a, small_b, sem, free_mate, free_chips,
):
    chip, plane, core = place()
    others = other_chips(chip)
    mate = device(chip, plane, 1 - core)
    marks = Marks(sem)
    rows = tok.shape[0]
    width = 4 * rows
    half = tok.shape[1]
    seq = 2 * half
    own_half = lanes(core * half, half)
    first = core * half + chip * TILE
    peers = [device(c, plane, core) for c in others]
    line = [device(chip, away(plane, step), core) for step in (1, 2, 3)]
    sides = [device(c, plane, 1 - core) for c in others]
    line_mates = [device(chip, away(plane, step), 1 - core) for step in (1, 2, 3)]

    barrier = pltpu.get_barrier_semaphore()
    partners = peers + [mate] + sides + line + line_mates
    for partner in partners:
        pl.semaphore_signal(barrier, inc=1, device_id=partner, device_id_type=MESH)
    pl.semaphore_wait(barrier, len(partners))

    def block_rows(c):
        return rows_at(c * rows, rows, rows)

    far_core = plane // 2
    holds_att = core == far_core
    holds_extra = holds_att & (chip // 2 == plane % 2)
    extra_plane = 2 * core + chip // 2
    extra_chip = (plane % 2) * 2 + core
    att_send, att_here = marks.many(2), marks.many(4)
    att_local = marks.one()

    def att_copy(h):
        return remote(
            wat.at[h], at.at[plane % 2, chip], att_send(h), att_here(chip),
            device(2 * core + h, plane, far_core),
        )

    def att_keep(h):
        return pltpu.make_async_copy(wat.at[h], at.at[plane % 2, chip], att_local)

    att_self = [(2 * core + h == chip) & holds_att for h in range(2)]
    for h in range(2):

        @pl.when(att_self[h])
        def _():
            att_keep(h).start()

        @pl.when(no(att_self[h]))
        def _():
            att_copy(h).start()

    class Gather:
        def __init__(self, source, target_of):
            self.source, self.target_of = source, target_of
            self.send, self.here = marks.many(4), marks.many(4)
            self.mate_send, self.mate_here = marks.many(4), marks.many(4)
            self.keep = pltpu.make_async_copy(source, target_of(chip), marks.one())
            self.copies = [
                remote(source, target_of(chip), self.send(p), self.here(p), peers[p])
                for p in range(2)
            ]
            for copy in self.copies:
                copy.start()
            self.keep.start()
            self.crossing = []
            self.cross(source, chip, 3)

        def cross(self, source, c, mark):
            copy = remote(
                source, self.target_of(c), self.mate_send(mark), self.mate_here(mark), mate
            )
            copy.start()
            self.crossing.append(copy)

        def halves(self, c):
            block = self.target_of(c)
            size = block.shape[0] // 2
            return block.at[0:size], block.at[size : 2 * size]

        def pass_on(self):
            self.copies[0].wait_recv()
            part_a = self.halves(others[0])[0]
            self.copies.append(remote(part_a, part_a, self.send(2), self.here(2), peers[1]))
            self.copies[2].start()
            self.cross(self.target_of(others[0]), others[0], 0)
            self.copies[1].wait_recv()
            part_b = self.halves(others[1])[1]
            self.copies.append(remote(part_b, part_b, self.send(3), self.here(3), peers[0]))
            self.copies[3].start()
            self.cross(self.target_of(others[1]), others[1], 1)

        def arrive(self):
            for copy in self.copies[2:]:
                copy.wait_recv()
            self.cross(self.target_of(others[2]), others[2], 2)
            for copy in self.crossing:
                copy.wait_recv()
            self.keep.wait()

        def finish(self):
            for copy in self.copies + self.crossing:
                copy.wait_send()

    tokens_in = Gather(tok, lambda c: xs.at[block_rows(c), own_half])
    gain_send, gain_here = marks.many(3), marks.many(3)
    gain_copies = [
        remote(gains, gn.at[chip], gain_send(p), gain_here(p), peers[p]) for p in range(3)
    ]
    gain_keep = pltpu.make_async_copy(gains, gn.at[chip], marks.one())
    for copy in gain_copies + [gain_keep]:
        copy.start()

    for h in range(2):

        @pl.when(att_self[h])
        def _():
            att_keep(h).wait()

        @pl.when(no(att_self[h]))
        def _():
            att_copy(h).wait_send()

    for c in range(4):

        @pl.when(holds_att & no((c == chip) & (core == chip // 2)))
        def _():
            remote(
                wat.at[0], at.at[plane % 2, c], att_send(0), att_here(c), mate
            ).wait_recv()

    out_rows, in_rows = pl.ds(HEADROWS, HDIM), pl.ds(0, HEADROWS)
    in_line, out_line = [
        [
            Spread(at.at[a, :, span], 2 * core + a, chip, plane, core, marks)
            for a in range(2)
        ]
        for span in (in_rows, out_rows)
    ]
    for item in in_line + out_line:
        item.start()

    tokens_in.pass_on()
    main_send, main_here, main_local = marks.many(3), marks.many(3), marks.one()
    main_here_at = ff.at[:, block_rows(chip), lanes(plane * TILE)]
    mains = [
        remote(
            wff.at[:, :, lanes(others[p] * TILE)], main_here_at,
            main_send(p), main_here(p), peers[p],
        )
        for p in range(3)
    ]
    for copy in mains:
        copy.start()
    main_keep = pltpu.make_async_copy(wff.at[:, :, lanes(chip * TILE)], main_here_at, main_local)
    main_keep.start()

    extra_send, extra_here, extra_local = marks.one(), marks.many(4), marks.one()
    extra_self = (extra_chip == chip) & holds_att
    last = lanes(4 * TILE)

    def extra_copy():
        return remote(
            wff.at[:, :, last], ff.at[:, block_rows(chip), last], extra_send, extra_here(chip),
            device(extra_chip, plane, far_core),
        )

    def extra_keep():
        return pltpu.make_async_copy(
            wff.at[:, :, last], ff.at[:, block_rows(chip), last], extra_local
        )

    @pl.when(extra_self)
    def _():
        extra_keep().start()

    @pl.when(no(extra_self))
    def _():
        extra_copy().start()

    tokens_in.arrive()
    cot_in = Gather(cot, lambda c: gs.at[block_rows(c), own_half])
    for copy in gain_copies + [gain_keep]:
        copy.wait()

    for item in in_line:
        item.relay()
    @pl.loop(0, 4)
    def _(c):
        columns = gn[c].astype(F32).T
        gcol[block_rows(c), 0:16] = columns[:rows]

    step_rows = 64

    def add_squares(i, total):
        x = xs[rows_at(i * step_rows, step_rows, step_rows)].astype(F32)
        return total + jnp.sum((x * x).reshape(step_rows // 8, 8, seq), 0)

    squares = lax.fori_loop(0, width // step_rows, add_squares, jnp.zeros((8, seq), F32))
    inv_all[...] = lax.rsqrt(jnp.sum(squares, 0, keepdims=True) / D + EPSILON)
    tokens_in.finish()
    normed[...] = xs[:, lanes(first)]

    @pl.loop(0, width // step_rows)
    def _(i):
        at_rows = rows_at(i * step_rows, step_rows, step_rows)
        xs[at_rows] = (
            xs[at_rows].astype(F32) * inv_all[...] * gcol[at_rows, 0:1]
        ).astype(BF16)

    for item in out_line:
        item.relay()
    for item in in_line:
        item.arrive()

    position = lax.broadcasted_iota(jnp.int32, (1, seq), 1)
    tail = lax.broadcasted_iota(jnp.int32, (HDIM, TILE), 1)

    def taps(h):
        columns = at[h, 0, 2 * FEAT : HEADROWS, WIDE - TILE : WIDE].astype(F32)
        return [columns[:, rows % TILE + j : rows % TILE + j + 1] for j in range(CONV)]

    @pl.loop(0, 2)
    def _(h):
        projected = dot(at[h, 0, :HEADROWS, :rows], xs[0:rows], 1, 0)
        for c in range(1, 4):
            projected += dot(at[h, c, :HEADROWS, :rows], xs[c * rows : (c + 1) * rows], 1, 0)
        qs[h] = (projected[:FEAT].astype(BF16).astype(F32) * FEAT**-0.5).astype(BF16)
        ks[h] = projected[FEAT : 2 * FEAT].astype(BF16)
        values = projected[2 * FEAT :]
        raw[h] = values
        tap = taps(h)
        mixed = tap[0] * values
        for j in range(1, CONV):
            moved = pltpu.roll(values, j, 1)
            mixed += tap[j] * jnp.where(position >= j, moved, 0.0)
        vs[h] = mixed.astype(BF16)

    def kernel_of(h, b):
        seen = (b + 1) * SPAN
        scores = dot(ks[h, :, :seen], qs[h, :, b * SPAN : seen], 0, 0)
        kernel = 1.0 + scores + 0.5 * scores * scores
        key_at = lax.broadcasted_iota(jnp.int32, (seen, SPAN), 0)
        query_at = lax.broadcasted_iota(jnp.int32, (seen, SPAN), 1) + b * SPAN
        visible = key_at <= query_at
        return scores, jnp.where(visible, kernel, 0.0), visible

    @pl.loop(0, 2)
    def _(h):
        for b in range(seq // SPAN):
            seen = (b + 1) * SPAN
            _, kernel, _ = kernel_of(h, b)
            inverse = 1.0 / jnp.sum(kernel, 0, keepdims=True)
            inv_sum[h, :, b * SPAN : seen] = inverse
            weights = (kernel * inverse).astype(BF16)
            att[h, :, b * SPAN : seen] = dot(vs[h, :, :seen], weights, 1, 0).astype(BF16)

    main_keep.wait()
    for copy in mains:
        copy.wait()
    main_line = MainTiles(ff, chip, plane, core, marks)
    main_line.start()

    @pl.when(extra_self)
    def _():
        extra_keep().wait()

    @pl.when(no(extra_self))
    def _():
        extra_copy().wait_send()

    for c in range(4):

        @pl.when(holds_extra & no((c == chip) & (core == chip % 2)))
        def _():
            remote(
                wff.at[:, :, last], ff.at[:, block_rows(c), last], extra_send, extra_here(c), mate
            ).wait_recv()

    extra_line = Chain(ff.at[:, :, last], extra_plane, chip, plane, core, marks)
    extra_line.start()

    cot_in.pass_on()

    for item in out_line:
        item.arrive()

    def default_got(i):
        return got.at[i]

    class Sum:
        def __init__(self, guard, both=both, got=None, share=True):
            self.guard, self.both, self.share = guard, both, share
            self.got = got or default_got

        def begin(self, fill):
            fill((1 - core) * half)
            self.to_mate = remote(
                part.at[:, lanes((1 - core) * half, half)], from_mate,
                marks.one(), marks.one(), mate,
            )
            if self.guard:
                pl.semaphore_wait(free_mate, 1)
            self.to_mate.start()
            fill(core * half)

        def combine(self):
            self.to_mate.wait_recv()

            @pl.loop(0, 4)
            def _(c):
                self.both[block_rows(c)] = (
                    part[block_rows(c), own_half].astype(F32)
                    + from_mate[block_rows(c)].astype(F32)
                ).astype(BF16)

            pl.semaphore_signal(free_mate, inc=1, device_id=mate, device_id_type=MESH)
            self.to_mate.wait_send()

        def piece(self, upper, c):
            size = width // 2
            return self.both.at[pl.ds(0 if upper else size, size), lanes(c * TILE)]

        def send(self):
            if self.guard and self.share:
                pl.semaphore_wait(free_chips, 2)
            size = width // 2
            top, bottom = pl.ds(0, size), pl.ds(size, size)
            send, here = marks.many(6), marks.many(6)
            self.across = [
                remote(self.piece(True, others[2]), self.got(2).at[top], send(0), here(0), peers[0]),
                remote(
                    self.piece(False, others[2]), self.got(2).at[bottom], send(1), here(1), peers[1]
                ),
            ]
            self.plain = [
                remote(self.piece(True, others[0]), self.got(0).at[top], send(2), here(2), peers[0]),
                remote(
                    self.piece(False, others[1]), self.got(1).at[bottom], send(3), here(3), peers[1]
                ),
            ]
            self.added = [
                remote(
                    self.piece(True, others[1]), self.got(1).at[top], send(4), here(4), peers[1]
                ),
                remote(
                    self.piece(False, others[0]), self.got(0).at[bottom], send(5), here(5), peers[0]
                ),
            ]
            for copy in self.across + self.plain:
                copy.start()

        def pass_on(self):
            size = width // 2
            quarter = size // 2
            for i, c in ((0, others[1]), (1, others[0])):
                self.across[i].wait_recv()
                for q in range(2):
                    at_rows = pl.ds(i * size + q * quarter, quarter)
                    self.both[at_rows, lanes(c * TILE)] = (
                        self.both[at_rows, lanes(c * TILE)].astype(F32) + self.got(2)[at_rows].astype(F32)
                    ).astype(BF16)
                self.added[i].start()

        def finish(self, store):
            for copy in self.plain + self.added:
                copy.wait()
            for copy in self.across:
                copy.wait_send()

            @pl.loop(0, 4)
            def _(c):
                at_rows = block_rows(c)
                total = self.both[at_rows, lanes(chip * TILE)].astype(F32)
                for p in range(2):
                    total += self.got(p)[at_rows].astype(F32)
                store(at_rows, total)

            for p in range(2 if self.share else 0):
                pl.semaphore_signal(free_chips, inc=1, device_id=peers[p], device_id_type=MESH)

    def fill_branch(start):
        @pl.loop(0, 4)
        def _(c):
            where = lanes(start, half)
            total = dot(at[0, c, HEADROWS:, :rows], att[0, :, where], 0, 0)
            total += dot(at[1, c, HEADROWS:, :rows], att[1, :, where], 0, 0)
            part[block_rows(c), where] = total.astype(BF16)

    small[...] = jnp.zeros(small.shape, F32)
    square_at = lax.broadcasted_iota(jnp.int32, (1, WIDE), 1)

    def note_square(index, value):
        total = jnp.sum(value * value)
        small[0, 2:3, :] += jnp.where(square_at == index, total, 0.0)

    def store_branch(at_rows, total):
        note_square(0, total)
        mid[at_rows] = normed[at_rows].astype(F32) + total

    branch_sum = Sum(guard=False)
    branch_sum.begin(fill_branch)
    cot_in.arrive()
    branch_sum.combine()
    branch_sum.send()
    branch_sum.pass_on()
    branch_sum.finish(store_branch)
    main_line.relay()
    middle = mid[...]
    inverse_two = lax.rsqrt(jnp.sum(middle * middle, 0, keepdims=True) / D + EPSILON)

    @pl.loop(0, 4)
    def _(c):
        at_rows = block_rows(c)
        sending[0, at_rows] = (mid[at_rows] * inverse_two * gcol[at_rows, 1:2]).astype(BF16)

    def token_block(c):
        return low2.at[:, lanes(core * half + c * TILE)]

    low_in = Gather(sending.at[0], token_block)
    cot_in.finish()

    @pl.loop(0, 4)
    def _(c):
        acc3[block_rows(c)] = jnp.zeros((rows, seq), F32)

    low_in.pass_on()
    low_in.arrive()
    low_in.finish()

    extra_line.relay()
    main_line.relay_far()
    def feed(slot):
        where = lanes(slot * TILE)
        unit_rows = rows_at(slot * TILE, TILE, TILE)
        for m in range(3):
            turned[m * TILE : (m + 1) * TILE] = ff[m, :, where].T

        @pl.loop(0, seq // SPAN)
        def _(n):
            span = lanes(n * SPAN, SPAN)
            gate_up = dot(turned[: 2 * TILE], low2[:, span], 1, 0)
            grad_hidden = dot(turned[2 * TILE :], gs[:, span], 1, 0)
            gate, up = gate_up[:TILE], gate_up[TILE:]
            sigmoid = 1.0 / (1.0 + jnp.exp(-gate))
            activated = gate * sigmoid
            hid[unit_rows, span] = (activated * up).astype(BF16)
            gg[:TILE, span] = (
                grad_hidden * up * sigmoid * (1.0 + gate * (1.0 - sigmoid))
            ).astype(BF16)
            gg[TILE:, span] = (grad_hidden * activated).astype(BF16)

        @pl.loop(0, 4)
        def _(c):
            at_rows = block_rows(c)
            pair = jnp.concatenate([ff[0, at_rows, where], ff[1, at_rows, where]], 1)
            acc3[at_rows] += dot(pair, gg[...], 1, 0)
            grads = dot(low2[at_rows], gg[...], 1, 1).astype(BF16)
            gout[0, at_rows, where] = grads[:, :TILE]
            gout[1, at_rows, where] = grads[:, TILE:]
            gout[2, at_rows, where] = dot(gs[at_rows], hid[unit_rows], 1, 1).astype(BF16)

    main_back = MainGrads(gout, main_got, chip, plane, core, marks)
    extra_back = Collect(gout.at[:, :, last], extra_got, extra_plane, chip, plane, core, marks)
    load_marks = marks.many(3)

    def add_tiles(slot, source):
        loads = [
            pltpu.make_async_copy(source.at[m], ff.at[2, :, lanes(m * TILE)], load_marks(m))
            for m in range(3)
        ]
        for load in loads:
            load.start()
        for load in loads:
            load.wait()
        where = lanes(slot * TILE)

        @pl.loop(0, 4)
        def _(c):
            at_rows = block_rows(c)
            for m in range(3):
                gout[m, at_rows, where] = (
                    gout[m, at_rows, where].astype(F32)
                    + ff[2, at_rows, m * TILE : (m + 1) * TILE].astype(F32)
                ).astype(BF16)

    def add_extra(source):
        add_tiles(4, source)

    slots = [away(plane, 1), plane, away(plane, 2), away(plane, 3), 4]
    inner = is_inner(plane)

    @pl.loop(0, 5)
    def _(turn):
        pl.when(turn == 2)(lambda: extra_line.relay_far())

        for i, step in ((0, 1), (2, 2), (3, 3)):

            @pl.when(turn == i)
            def _():
                main_line.arrive(step)

        @pl.when(turn == 4)
        def _():
            extra_line.arrive()

        slot = sum((turn == i).astype(jnp.int32) * slots[i] for i in range(5))
        feed(slot)

        for i, step in ((0, 1), (2, 2), (3, 3)):

            @pl.when((turn == i) & no(inner))
            def _():
                main_back.start(step)

    pl.when(inner)(lambda: main_back.start(1))

    extra_back.start()
    main_line.finish()

    def fill_grad_two(start):
        @pl.loop(0, 4)
        def _(c):
            where = lanes(start, half)
            part[block_rows(c), where] = acc3[block_rows(c), where].astype(BF16)

    def store_gsum(at_rows, total):
        gsum[at_rows] = total

    two_sum = Sum(guard=True)
    two_sum.begin(fill_grad_two)
    two_sum.combine()
    two_sum.send()
    two_sum.pass_on()

    def fill_ffn(start):
        @pl.loop(0, 4)
        def _(c):
            where = lanes(start, half)
            part[block_rows(c), where] = dot(
                ff[2, block_rows(c)], hid[:, where], 1, 0
            ).astype(BF16)

    ffn_sum = Sum(
        guard=True, both=ff.at[1, :, lanes(0, half)],
        got=lambda i: ff.at[0, :, lanes(i * TILE)], share=False,
    )
    ffn_sum.begin(fill_ffn)
    two_sum.finish(store_gsum)

    main_back.relay(3, add_tiles)
    def norm_back(source, inverse, gain_lane, base, store):
        def add_dots(c, total):
            at_rows = block_rows(c)
            gain = gcol[at_rows, gain_lane : gain_lane + 1]
            return total + jnp.sum(gsum[at_rows] * gain * source(at_rows), 0, keepdims=True)

        dots = lax.fori_loop(0, 4, add_dots, jnp.zeros((1, TILE), F32))
        scaled = inverse * inverse * inverse * dots / D

        @pl.loop(0, 4)
        def _(c):
            at_rows = block_rows(c)
            gain = gcol[at_rows, gain_lane : gain_lane + 1]
            grad, value = gsum[at_rows], source(at_rows)
            store(at_rows, base(at_rows) + (grad * gain * inverse - value * scaled))

        def gain_back():
            @pl.loop(0, 4)
            def _(c):
                at_rows = block_rows(c)
                for_gain = jnp.sum((gsum[at_rows] * source(at_rows) * inverse).T, 0, keepdims=True)
                small[c, gain_lane : gain_lane + 1, 0:rows] = for_gain

        return gain_back

    def store_middle(at_rows, value):
        gmid[at_rows] = value
        sending[1, at_rows] = value.astype(BF16)

    gain_two_back = norm_back(
        lambda r: mid[r], inverse_two, 1, lambda r: gs[r, lanes(first)].astype(F32), store_middle
    )
    mid_in = Gather(sending.at[1], token_block)
    gain_two_back()
    ffn_sum.combine()
    mid_in.pass_on()
    ffn_sum.send()
    mid_in.arrive()

    @pl.loop(0, 2)
    def _(h):
        total = dot(at[h, 0, HEADROWS:, :rows], low2[0:rows], 1, 0)
        for c in range(1, 4):
            total += dot(at[h, c, HEADROWS:, :rows], low2[c * rows : (c + 1) * rows], 1, 0)
        gatt[h] = total.astype(BF16)

    main_back.relay(2, add_tiles)

    out_back, in_back = [
        [
            Collect(
                gat.at[a, :, span], att_got.at[a, :, :, span], 2 * core + a,
                chip, plane, core, marks,
            )
            for a in range(2)
        ]
        for span in (out_rows, in_rows)
    ]

    def head_grads(left, right, start, size):
        whole = rows // TILE * TILE

        @pl.loop(0, 2)
        def _(h):
            for c in range(4):
                grad = dot(left[h], right[c * rows : (c + 1) * rows], 1, 1).astype(BF16)
                gat[h, c, start : start + size, :whole] = grad[:, :whole]
                gat[h, c, start : start + size, whole:rows] = grad[:, whole:]

    head_grads(att, low2, HEADROWS, HDIM)
    for item in out_back:
        item.start()


    @pl.loop(0, 2)
    def _(h):
        grad_keys = jnp.zeros((FEAT, seq), F32)
        grad_values = jnp.zeros((HDIM, seq), F32)

        def padded(value):
            short = seq - value.shape[1]
            if not short:
                return value
            return jnp.concatenate([value, jnp.zeros((value.shape[0], short), F32)], 1)

        for b in range(seq // SPAN):
            seen = (b + 1) * SPAN
            span = slice(b * SPAN, seen)
            scores, kernel, visible = kernel_of(h, b)
            inverse = inv_sum[h, :, span]
            weights = kernel * inverse
            grad_weights = dot(vs[h, :, :seen], gatt[h, :, span], 0, 0)
            grad_values += padded(dot(gatt[h, :, span], weights.astype(BF16), 1, 1))
            dots = jnp.sum(grad_weights * weights, 0, keepdims=True)
            grad_kernel = (grad_weights - dots) * inverse
            grad_scores = jnp.where(visible, grad_kernel * (1.0 + scores), 0.0).astype(BF16)
            gproj[h, :FEAT, span] = (
                dot(ks[h, :, :seen], grad_scores, 1, 0) * FEAT**-0.5
            ).astype(BF16)
            grad_keys += padded(dot(qs[h, :, span], grad_scores, 1, 1))
        gproj[h, FEAT : 2 * FEAT] = grad_keys.astype(BF16)
        tap = taps(h)
        grad_raw = tap[0] * grad_values
        sums = [jnp.sum(grad_values * raw[h], 1, keepdims=True)]
        for j in range(1, CONV):
            masked = jnp.where(position >= j, grad_values, 0.0)
            grad_raw += tap[j] * pltpu.roll(masked, seq - j, 1)
            sums.append(jnp.sum(masked * pltpu.roll(raw[h], j, 1), 1, keepdims=True))
        gproj[h, 2 * FEAT :] = grad_raw.astype(BF16)
        columns = jnp.zeros((HDIM, TILE), F32)
        for j in range(CONV):
            columns = jnp.where(tail == rows % TILE + j, sums[j], columns)
        for c in range(4):
            gat[h, c, 2 * FEAT : HEADROWS, WIDE - TILE :] = columns.astype(BF16)

    head_grads(gproj, xs, 0, HEADROWS)
    for item in in_back:
        item.start()

    ffn_sum.pass_on()
    mid_in.finish()

    def fill_grad_one(start):
        @pl.loop(0, 4)
        def _(c):
            where = lanes(start, half)
            total = dot(at[0, c, :HEADROWS, :rows], gproj[0, :, where], 0, 0)
            total += dot(at[1, c, :HEADROWS, :rows], gproj[1, :, where], 0, 0)
            part[block_rows(c), where] = total.astype(BF16)

    one_sum = Sum(guard=True)
    one_sum.begin(fill_grad_one)
    one_sum.combine()
    one_sum.send()
    extra_back.relay(add_extra)

    def store_result(at_rows, total):
        note_square(1, total)
        total = mid[at_rows] + total
        note_square(2, total)
        sending[0, at_rows] = total.astype(BF16)

    one_sum.pass_on()

    def hand_out(source, target):
        send, here = marks.many(3), marks.many(3)
        copies = [
            remote(
                source.at[block_rows(others[p])], target.at[:, lanes(chip * TILE)],
                send(p), here(p), peers[p],
            )
            for p in range(3)
        ]
        copies.append(
            pltpu.make_async_copy(
                source.at[block_rows(chip)], target.at[:, lanes(chip * TILE)], marks.one()
            )
        )
        for copy in copies:
            copy.start()
        return copies

    ffn_sum.finish(store_result)
    pending = hand_out(sending.at[0], out_res)


    one_sum.finish(store_gsum)
    inverse_own = inv_all[:, lanes(first)]

    def store_tokens(at_rows, value):
        sending[1, at_rows] = value.astype(BF16)

    gain_one_back = norm_back(
        lambda r: normed[r].astype(F32), inverse_own, 0, lambda r: gmid[r], store_tokens
    )
    pending += hand_out(sending.at[1], out_tok)
    gain_one_back()

    for c in range(1, 4):
        small[c, 2:3] = small[0, 2:3]
    a_send, a_here = marks.many(3), marks.many(3)
    trio = [
        remote(small.at[others[p]], small_a.at[p], a_send(p), a_here(p), peers[p])
        for p in range(3)
    ]
    for copy in trio:
        copy.start()

    main_back.total(add_tiles)
    back_send, back_here = marks.many(3), marks.many(3)
    mine = lanes(plane * TILE)
    back_to = out_ff.at[:, :, lanes(chip * TILE)]
    backs = [
        remote(
            gout.at[:, block_rows(others[p]), mine], back_to, back_send(p), back_here(p), peers[p]
        )
        for p in range(3)
    ]
    backs.append(
        pltpu.make_async_copy(gout.at[:, block_rows(chip), mine], back_to, marks.one())
    )
    for copy in backs:
        copy.start()
    pending += backs

    for copy in trio:
        copy.wait()
    small_b[0] = small[chip] + small_a[0] + small_a[1] + small_a[2]
    b_send, b_here = marks.many(7), marks.many(7)
    seven = [
        remote(small_b.at[0], small_b.at[1 + i], b_send(i), b_here(i), to)
        for i, to in enumerate(line + [mate] + line_mates)
    ]
    for copy in seven:
        copy.start()

    extra_back.total(add_extra)
    last_send, last_here, last_local = marks.many(4), marks.one(), marks.one()

    def last_copy(c):
        return remote(
            gout.at[:, block_rows(c), last], out_ff.at[:, :, last], last_send(c), last_here,
            device(c, plane, chip % 2),
        )

    def last_keep():
        return pltpu.make_async_copy(
            gout.at[:, block_rows(chip), last], out_ff.at[:, :, last], last_local
        )

    for c in range(4):
        same = (c == chip) & (core == chip % 2)

        @pl.when(holds_extra & same)
        def _():
            last_keep().start()

        @pl.when(holds_extra & no(same))
        def _():
            last_copy(c).start()

    head_marks = marks.many(4)

    def add_head(a, start, size):
        def add(source):
            loads = [
                pltpu.make_async_copy(
                    source.at[c], part.at[c * BLOCKROWS : c * BLOCKROWS + size, 0:WIDE],
                    head_marks(c),
                )
                for c in range(4)
            ]
            for load in loads:
                load.start()
            for load in loads:
                load.wait()
            for c in range(4):
                gat[a, c, start : start + size] = (
                    gat[a, c, start : start + size].astype(F32)
                    + part[c * BLOCKROWS : c * BLOCKROWS + size, 0:WIDE].astype(F32)
                ).astype(BF16)

        return add

    for items, start, size in ((out_back, HEADROWS, HDIM), (in_back, 0, HEADROWS)):
        for a in range(2):
            items[a].relay(add_head(a, start, size))
    for items, start, size in ((out_back, HEADROWS, HDIM), (in_back, 0, HEADROWS)):
        for a in range(2):
            items[a].total(add_head(a, start, size))
    head_send, head_here, head_local = marks.many(4), marks.many(2), marks.one()

    def head_copy(c):
        return remote(
            gat.at[plane % 2, c], out_at.at[chip % 2], head_send(c), head_here(chip % 2),
            device(c, plane, chip // 2),
        )

    def head_keep():
        return pltpu.make_async_copy(gat.at[plane % 2, chip], out_at.at[chip % 2], head_local)

    for c in range(4):
        same = (c == chip) & (core == chip // 2)

        @pl.when(holds_att & same)
        def _():
            head_keep().start()

        @pl.when(holds_att & no(same))
        def _():
            head_copy(c).start()

    for copy in seven:
        copy.wait()
    total = small_b[0]
    for i in range(7):
        total += small_b[1 + i]
    small_a[0] = total
    small_out = pltpu.make_async_copy(small_a.at[0], out_small, marks.one())
    small_out.start()
    pending.append(small_out)
    for item in in_line + out_line + [extra_line, main_back, extra_back] + out_back + in_back:
        item.finish()
    for copy in pending:
        copy.wait()
    for c in range(4):
        for holds, same, local, away_copy in (
            (holds_extra, (c == chip) & (core == chip % 2), last_keep, last_copy),
            (holds_att, (c == chip) & (core == chip // 2), head_keep, head_copy),
        ):

            @pl.when(holds & same)
            def _():
                local().wait()

            @pl.when(holds & no(same))
            def _():
                away_copy(c).wait_send()

    @pl.when(no(extra_self))
    def _():
        last_copy(0).wait_recv()

    for h in range(2):

        @pl.when(no(att_self[h]))
        def _():
            remote(
                gat.at[0, 0], out_at.at[h], head_send(0), head_here(h), mate
            ).wait_recv()

    pl.semaphore_wait(free_mate, 1)
    pl.semaphore_wait(free_chips, 2)
    assert marks.used <= MARKS, marks.used


def dma(*shape):
    return pltpu.SemaphoreType.DMA(shape)


def run_layer(wff, wat, tok, cot, gains):
    rows, half = tok.shape
    width, seq = 4 * rows, 2 * half
    shape = jax.ShapeDtypeStruct
    vmem = pltpu.VMEM
    tiles = (3, width, TILE)
    head = (4, BLOCKROWS, WIDE)
    return pl.pallas_call(
        layer_kernel,
        out_shape=[
            shape((3, rows, 5 * TILE), BF16),
            shape((2, BLOCKROWS, WIDE), BF16),
            shape((rows, half), BF16),
            shape((rows, half), BF16),
            shape((8, WIDE), F32),
            shape((5,) + tiles, BF16),
            shape((4,) + tiles, BF16),
            shape((2, 4) + head, BF16),
        ],
        in_specs=[ANY] * 5,
        out_specs=[ANY] * 8,
        scratch_shapes=[
            vmem((3, width, 5 * TILE), BF16),
            vmem((2,) + head, BF16),
            vmem((width, seq), BF16),
            vmem((width, seq), BF16),
            vmem((width, seq), BF16),
            vmem((width, seq), BF16),
            vmem((width, seq), F32),
            vmem((3, width, 5 * TILE), BF16),
            vmem((2,) + head, BF16),
            vmem((width, half), BF16),
            vmem((width, half), BF16),
            vmem((3, width, TILE), BF16),
            vmem((3 * TILE, width), BF16),
            vmem((5 * TILE, seq), BF16),
            vmem((2 * TILE, seq), BF16),
            vmem((4, 16, WIDE), BF16),
            vmem((width, TILE), F32),
            vmem((2, HDIM, seq), F32),
            vmem((2, FEAT, seq), BF16),
            vmem((2, FEAT, seq), BF16),
            vmem((2, HDIM, seq), BF16),
            vmem((2, HDIM, seq), BF16),
            vmem((2, HDIM, seq), BF16),
            vmem((2, HEADROWS, seq), BF16),
            vmem((width, TILE), F32),
            vmem((width, TILE), F32),
            vmem((width, TILE), F32),
            vmem((width, TILE), BF16),
            vmem((2, width, TILE), BF16),
            vmem((1, seq), F32),
            vmem((2, 1, seq), F32),
            vmem((4, 8, WIDE), F32),
            vmem((3, 8, WIDE), F32),
            vmem((8, 8, WIDE), F32),
            dma(MARKS),
            pltpu.SemaphoreType.REGULAR,
            pltpu.SemaphoreType.REGULAR,
        ],
        compiler_params=pltpu.CompilerParams(
            collective_id=0, has_side_effects=True, vmem_limit_bytes=63 * 2**20
        ),
        name="layer",
    )(wff, wat, tok, cot, gains)


def on_device_full(
    tokens, cotangent, w_qkv, conv_weight, w_out, w_gate, w_up, w_down, gain_mix, gain_ffn
):
    rows, half = tokens.shape
    ffn_cols = w_gate.shape[1]
    heads = 2
    pad = ((0, 0), (0, 5 * TILE - ffn_cols))
    wff = jnp.stack([jnp.pad(w, pad) for w in (w_gate, w_up, w_down)])
    taps = jnp.pad(
        conv_weight.T.reshape(heads, HDIM, CONV),
        ((0, 0), (2 * FEAT, 0), (0, WIDE - rows - CONV)),
    )
    upper = jnp.concatenate([w_qkv.T.reshape(heads, HEADROWS, rows), taps], 2)
    lower = jnp.pad(w_out.reshape(heads, HDIM, rows), ((0, 0), (0, 0), (0, WIDE - rows)))
    wat = jnp.concatenate([upper, lower], 1)
    gains = jnp.pad(
        jnp.stack([gain_mix, gain_ffn]), ((0, 14), (0, WIDE - rows))
    )
    out_ff, out_at, out_res, out_tok, small = run_layer(wff, wat, tokens, cotangent, gains)[:5]
    out_at = out_at.astype(F32)
    return (
        out_res,
        out_tok.astype(F32),
        out_at[:, :HEADROWS, :rows].reshape(heads * HEADROWS, rows).T,
        out_at[:, 2 * FEAT : HEADROWS, rows : rows + CONV].reshape(heads * HDIM, CONV).T,
        out_at[:, HEADROWS:, :rows].reshape(heads * HDIM, rows),
        out_ff[0, :, :ffn_cols].astype(F32),
        out_ff[1, :, :ffn_cols].astype(F32),
        out_ff[2, :, :ffn_cols].astype(F32),
        small[0, :rows],
        small[1, :rows],
        jnp.sqrt(small[2, :3] / (8 * half * 4 * rows)),
    )


def on_device(tokens, cotangent, lengths, deal_order, *weights):
    total_rows = tokens.shape[1] * lax.axis_size("col")
    if (
        lengths.shape[0] * LONGEST == total_rows
        and lax.axis_size("row") == 4
        and lax.axis_size("col") == 8
        and total_rows == 4 * LONGEST
        and weights[0].shape[1] == 2 * HEADROWS
        and 4 * TILE < weights[3].shape[1] <= 5 * TILE
    ):
        return on_device_full(tokens, cotangent, *weights)
    return on_device_general(tokens, cotangent, lengths, deal_order, *weights)


def solution(mesh):
    in_specs = (
        P("row", "col"),
        P("row", "col"),
        P(),
        P(),
        P("row", "col"),
        P(None, "col"),
        P("col", "row"),
        P("row", "col"),
        P("row", "col"),
        P("row", "col"),
        P("row"),
        P("row"),
    )
    out_specs = (
        P("row", "col"),
        P("row", "col"),
        P("row", "col"),
        P(None, "col"),
        P("col", "row"),
        P("row", "col"),
        P("row", "col"),
        P("row", "col"),
        P("row"),
        P("row"),
        P(),
    )
    return jax.shard_map(
        on_device, mesh=mesh, in_specs=in_specs, out_specs=out_specs, check_vma=False
    )
```

```python
import functools

import jax
import jax.numpy as jnp
from jax import lax
from jax.experimental import pallas as pl
from jax.experimental.pallas import tpu as pltpu
from jax.sharding import PartitionSpec as P

D = 1792
FEAT = 16
CONV = 3
LONGEST = 1024
HDIM = 112


EPSILON = 1e-06


def dealing(lengths, deal_order, total_rows):
    seq_ids = jnp.arange(lengths.shape[0], dtype=jnp.int32)
    chosen = (deal_order[:, None] == seq_ids[None, :]).astype(jnp.int32)
    dealt_lengths = jnp.sum(chosen * lengths[None, :], 1)
    given_start = jnp.cumsum(lengths) - lengths
    dealt_start = jnp.cumsum(dealt_lengths) - dealt_lengths
    given_of_dealt = jnp.sum(chosen * given_start[None, :], 1)
    dealt_of_given = jnp.sum(chosen * dealt_start[:, None], 0)
    places = jnp.arange(total_rows, dtype=jnp.int32)
    in_dealt = (places[:, None] >= dealt_start[None, :]) & (
        places[:, None] < (dealt_start + dealt_lengths)[None, :]
    )
    in_given = (places[:, None] >= given_start[None, :]) & (
        places[:, None] < (given_start + lengths)[None, :]
    )
    source = places + jnp.sum(jnp.where(in_dealt, (given_of_dealt - dealt_start)[None, :], 0), 1)
    target = places + jnp.sum(jnp.where(in_given, (dealt_of_given - given_start)[None, :], 0), 1)
    offsets = places - jnp.sum(jnp.where(in_dealt, dealt_start[None, :], 0), 1)
    return (source, target, offsets)


def convolve(raw_values, kernel_conv, offsets):
    mixed = kernel_conv[0] * raw_values
    for delay_step in range(1, CONV):
        moved = jnp.concatenate(
            [jnp.zeros_like(raw_values[:delay_step]), raw_values[:-delay_step]], 0
        )
        mixed = mixed + kernel_conv[delay_step] * jnp.where(
            (offsets >= delay_step)[:, None, None], moved, 0.0
        )
    return mixed


def convolve_back(grad_mixed, raw_values, kernel_conv, offsets):
    grad_raw = kernel_conv[0] * grad_mixed
    sums_list = [jnp.sum(grad_mixed * raw_values, 0)]
    for delay_step in range(1, CONV):
        masked = jnp.where((offsets >= delay_step)[:, None, None], grad_mixed, 0.0)
        pulled = jnp.concatenate([masked[delay_step:], jnp.zeros_like(masked[:delay_step])], 0)
        grad_raw = grad_raw + kernel_conv[delay_step] * pulled
        moved = jnp.concatenate(
            [jnp.zeros_like(raw_values[:delay_step]), raw_values[:-delay_step]], 0
        )
        sums_list.append(jnp.sum(masked * moved, 0))
    return (grad_raw, jnp.stack(sums_list))


def bin_scores(query, keys, offsets):
    scores = jnp.einsum("thf,shf->hts", query, keys, preferred_element_type=jnp.float32) * FEAT ** (
        -0.5
    )
    positions = jnp.arange(query.shape[0], dtype=jnp.int32)
    visible = (positions[None, :] <= positions[:, None]) & (
        positions[:, None] - positions[None, :] <= offsets[:, None]
    )
    kernel = jnp.where(visible[None], 1.0 + scores + 0.5 * scores * scores, 0.0)
    return (scores, visible, kernel)


def attend_bin(pieces):
    query, keys, values, offsets = pieces
    scores, visible, kernel = bin_scores(query, keys, offsets)
    weights = (kernel / jnp.sum(kernel, -1, keepdims=True)).astype(jnp.bfloat16)
    return jnp.einsum("hts,shd->thd", weights, values, preferred_element_type=jnp.float32)


def attend_back(pieces):
    query, keys, values, offsets, grad_attend = pieces
    scores, visible, kernel = bin_scores(query, keys, offsets)
    totals = jnp.sum(kernel, -1, keepdims=True)
    weights = kernel / totals
    grad_weights = jnp.einsum(
        "thd,shd->hts", grad_attend, values, preferred_element_type=jnp.float32
    )
    grad_values = jnp.einsum(
        "hts,thd->shd",
        weights.astype(jnp.bfloat16),
        grad_attend,
        preferred_element_type=jnp.float32,
    )
    grad_kernel = (grad_weights - jnp.sum(grad_weights * weights, -1, keepdims=True)) / totals
    grad_scores = jnp.where(visible[None], grad_kernel * (1.0 + scores), 0.0).astype(jnp.bfloat16)
    grad_query = jnp.einsum(
        "hts,shf->thf", grad_scores, keys, preferred_element_type=jnp.float32
    ) * FEAT ** (-0.5)
    grad_keys = jnp.einsum(
        "hts,thf->shf", grad_scores, query, preferred_element_type=jnp.float32
    ) * FEAT ** (-0.5)
    return (grad_query, grad_keys, grad_values)


def times_transposed(left, right):
    return lax.dot_general(
        left, right, (((1,), (1,)), ((), ())), preferred_element_type=jnp.float32
    )


def tokens_product(left, right):
    return lax.dot_general(
        left, right, (((0,), (0,)), ((), ())), preferred_element_type=jnp.float32
    )


def plain_product(left, right):
    return jnp.dot(left, right, preferred_element_type=jnp.float32)


def gather_cols(values):
    return lax.all_gather(values, "col", axis=0, tiled=True)


def gather_rows(values):
    return lax.all_gather(values, "row", axis=0, tiled=True)


def grad_gather_cols(values):
    return lax.all_gather(values, "col", axis=1, tiled=True)


def grad_gather_rows(values):
    return lax.all_gather(values, "row", axis=0, tiled=True)


def width_total(values):
    return lax.psum(values, "row")


def forward_rows(gathered, row_index, weight, rows_here):

    def partial_term(row_start, row_count):
        picked = jnp.take(gathered, row_index, axis=0)
        return jnp.dot(picked, weight, preferred_element_type=jnp.float32)

    return lax.psum_scatter(
        partial_term(jnp.int32(0), rows_here * lax.axis_size("row")),
        "row",
        scatter_dimension=0,
        tiled=True,
    )


def forward_cols(gathered, row_index, weight, rows_here, product):

    def partial_term(row_start, row_count):
        picked = jnp.take(gathered, row_index, axis=0)
        return product(picked, weight)

    return lax.psum_scatter(
        partial_term(jnp.int32(0), lax.axis_size("col") * rows_here).astype(jnp.bfloat16),
        "col",
        scatter_dimension=0,
        tiled=True,
    ).astype(jnp.float32)


def backward_rows(gathered, row_index, weight, rows_here, contract):

    def partial_term(row_start, row_count):
        picked = jnp.take(gathered, row_index, axis=1)
        return lax.dot_general(
            picked, weight, (((0,), (contract,)), ((), ())), preferred_element_type=jnp.float32
        )

    return lax.psum_scatter(
        partial_term(jnp.int32(0), lax.axis_size("row") * rows_here).astype(jnp.bfloat16),
        "row",
        scatter_dimension=0,
        tiled=True,
    ).astype(jnp.float32)


def backward_cols(gathered, row_index, weight, rows_here):

    def partial_term(row_start, row_count):
        picked = jnp.take(gathered, row_index, axis=0)
        return times_transposed(picked, weight)

    return lax.psum_scatter(
        partial_term(jnp.int32(0), lax.axis_size("col") * rows_here).astype(jnp.bfloat16),
        "col",
        scatter_dimension=0,
        tiled=True,
    ).astype(jnp.float32)


def norm_forward(values, norm_gain):
    totals = width_total(jnp.sum(values * values, -1))
    inverse = lax.rsqrt(totals / D + EPSILON)
    return (values * inverse[:, None] * norm_gain, inverse)


def norm_back(values, inverse, norm_gain, grad_normed, dot_sums):
    cubed = inverse * inverse * inverse
    return grad_normed * norm_gain * inverse[:, None] - values * (cubed * dot_sums / D)[:, None]


def on_device_general(
    tokens,
    cotangent,
    lengths,
    deal_order,
    w_qkv,
    conv_weight,
    w_out,
    w_gate,
    w_up,
    w_down,
    gain_mix,
    gain_ffn,
):
    local_rows = tokens.shape[1]
    total_rows = local_rows * lax.axis_size("col")
    group_rows = total_rows // lax.axis_size("row")
    bin_count = group_rows // LONGEST
    heads_here = w_out.shape[0] // HDIM
    ffn_cols = w_gate.shape[1]
    source, target, offsets = dealing(lengths, deal_order, total_rows)
    group_offsets = lax.dynamic_slice_in_dim(
        offsets, lax.axis_index("row") * group_rows, group_rows
    )
    inputs = tokens.astype(jnp.float32).T
    gain_one = gain_mix.astype(jnp.float32)
    gain_two = gain_ffn.astype(jnp.float32)
    both_weights = jnp.concatenate([w_gate, w_up], 1)
    normed_one, inverse_one = norm_forward(inputs, gain_one)
    low_one = normed_one.astype(jnp.bfloat16)
    all_one = gather_cols(low_one)
    projected = forward_rows(all_one, source, w_qkv, group_rows)
    projected = projected.reshape(group_rows, heads_here, 2 * FEAT + HDIM)
    query = projected[:, :, :FEAT].astype(jnp.bfloat16)
    keys = projected[:, :, FEAT : 2 * FEAT].astype(jnp.bfloat16)
    raw_values = projected[:, :, 2 * FEAT :]
    kernel_conv = conv_weight.astype(jnp.float32).reshape(CONV, heads_here, HDIM)
    values = convolve(raw_values, kernel_conv, group_offsets).astype(jnp.bfloat16)
    binned = (
        query.reshape(bin_count, LONGEST, heads_here, FEAT),
        keys.reshape(bin_count, LONGEST, heads_here, FEAT),
        values.reshape(bin_count, LONGEST, heads_here, HDIM),
        group_offsets.reshape(bin_count, LONGEST),
    )
    attended = (
        lax.map(attend_bin, binned).reshape(group_rows, heads_here * HDIM).astype(jnp.bfloat16)
    )
    all_attended = gather_rows(attended)
    branch_mix = forward_cols(all_attended, target, w_out, local_rows, plain_product)
    middle = inputs + branch_mix
    normed_two, inverse_two = norm_forward(middle, gain_two)
    low_two = normed_two.astype(jnp.bfloat16)
    all_two = gather_cols(low_two)
    gate_up = forward_rows(all_two, source, both_weights, group_rows)
    gate = gate_up[:, :ffn_cols]
    up_proj = gate_up[:, ffn_cols:]
    activated = jax.nn.silu(gate)
    hidden = (activated * up_proj).astype(jnp.bfloat16)
    all_hidden = gather_rows(hidden)
    branch_ffn = forward_cols(all_hidden, target, w_down, local_rows, times_transposed)
    result_full = middle + branch_ffn
    grad_result = cotangent.astype(jnp.float32).T
    all_grad_ffn = grad_gather_cols(cotangent)
    hidden_again = gather_rows(hidden)
    grad_down = jnp.dot(
        jnp.take(all_grad_ffn, source, axis=1), hidden_again, preferred_element_type=jnp.float32
    )
    grad_hidden = backward_rows(all_grad_ffn, source, w_down, group_rows, 0)
    gate_sigmoid = jax.nn.sigmoid(gate)
    grad_gate_part = grad_hidden * up_proj * gate_sigmoid * (1.0 + gate * (1.0 - gate_sigmoid))
    grad_up_part = grad_hidden * activated
    grad_gate_up = jnp.concatenate([grad_gate_part, grad_up_part], 1).astype(jnp.bfloat16)
    all_grad_gate_up = grad_gather_rows(grad_gate_up)
    two_again = gather_cols(low_two)
    grad_both = tokens_product(jnp.take(two_again, source, axis=0), all_grad_gate_up)
    grad_normed_two = backward_cols(all_grad_gate_up, target, both_weights, local_rows)
    dots_two = width_total(jnp.sum(grad_normed_two * gain_two * middle, -1))
    grad_middle = grad_result + norm_back(middle, inverse_two, gain_two, grad_normed_two, dots_two)
    gain_part_two = jnp.sum(grad_normed_two * middle * inverse_two[:, None], 0)
    low_grad_middle = grad_middle.T.astype(jnp.bfloat16)
    all_grad_middle = grad_gather_cols(low_grad_middle)
    attended_again = gather_rows(attended)
    grad_out = lax.dot_general(
        attended_again,
        jnp.take(all_grad_middle, source, axis=1),
        (((0,), (1,)), ((), ())),
        preferred_element_type=jnp.float32,
    )
    grad_attended = backward_rows(all_grad_middle, source, w_out, group_rows, 1).astype(
        jnp.bfloat16
    )
    binned_back = binned + (grad_attended.reshape(bin_count, LONGEST, heads_here, HDIM),)
    grad_query, grad_keys, grad_values = lax.map(attend_back, binned_back)
    grad_values = grad_values.reshape(group_rows, heads_here, HDIM)
    grad_raw, conv_part = convolve_back(grad_values, raw_values, kernel_conv, group_offsets)
    grad_projected = jnp.concatenate(
        [
            grad_query.reshape(group_rows, heads_here, FEAT),
            grad_keys.reshape(group_rows, heads_here, FEAT),
            grad_raw,
        ],
        2,
    )
    grad_projected = grad_projected.reshape(group_rows, heads_here * (2 * FEAT + HDIM)).astype(
        jnp.bfloat16
    )
    all_grad_projected = grad_gather_rows(grad_projected)
    one_again = gather_cols(low_one)
    grad_qkv = tokens_product(jnp.take(one_again, source, axis=0), all_grad_projected)
    grad_normed_one = backward_cols(all_grad_projected, target, w_qkv, local_rows)
    squares = jnp.stack(
        [
            jnp.sum(branch_mix * branch_mix),
            jnp.sum(branch_ffn * branch_ffn),
            jnp.sum(result_full * result_full),
        ]
    )
    dots_one, grad_conv, squares_rows = width_total(
        (
            jnp.sum(grad_normed_one * gain_one * inputs, -1),
            conv_part.reshape(CONV, heads_here * HDIM),
            squares,
        )
    )
    grad_tokens = grad_middle + norm_back(inputs, inverse_one, gain_one, grad_normed_one, dots_one)
    gain_part_one = jnp.sum(grad_normed_one * inputs * inverse_one[:, None], 0)
    grad_gain_mix, grad_gain_ffn, squares_all = lax.psum(
        (gain_part_one, gain_part_two, squares_rows), "col"
    )
    rms_values = jnp.sqrt(squares_all / (total_rows * D))
    return (
        result_full.T.astype(jnp.bfloat16),
        grad_tokens.T,
        grad_qkv,
        grad_conv,
        grad_out,
        grad_both[:, :ffn_cols],
        grad_both[:, ffn_cols:],
        grad_down,
        grad_gain_mix,
        grad_gain_ffn,
        rms_values,
    )


HEADROWS = 2 * FEAT + HDIM
BLOCKROWS = HEADROWS + HDIM
TILE = 128
WIDE = 512
SPAN = 256
MARKS = 420
MESH = pl.DeviceIdType.MESH
ANY = pl.BlockSpec(memory_space=pl.ANY)
F32, BF16 = jnp.float32, jnp.bfloat16


def place():
    column = lax.axis_index("col")
    return lax.axis_index("row"), column // 2, column % 2


def device(chip, plane, core):
    return (chip, plane * 2 + core)


def other_chips(chip):
    y, x = chip // 2, chip % 2
    return (y * 2 + 1 - x, (1 - y) * 2 + x, (1 - y) * 2 + 1 - x)


def away(plane, step):
    if step == 1:
        return plane + 1 - 2 * (plane % 2)
    if step == 2:
        return (plane + 2) % 4
    return 3 - plane


def is_inner(plane):
    return ((plane + 1) // 2) % 2 == 1


def remote(source, target, send, receive, to):
    return pltpu.make_async_remote_copy(
        src_ref=source,
        dst_ref=target,
        send_sem=send,
        recv_sem=receive,
        device_id=to,
        device_id_type=MESH,
    )


def lanes(start, size=TILE):
    return pl.ds(pl.multiple_of(start, TILE), size)


def rows_at(start, size, step):
    return pl.ds(pl.multiple_of(start, step), size)


def no(flag):
    return jnp.logical_not(flag)


def dot(a, b, over_a, over_b):
    return lax.dot_general(
        a, b, (((over_a,), (over_b,)), ((), ())), preferred_element_type=F32
    )


class Marks:
    def __init__(self, ref):
        self.ref, self.used = ref, 0

    def one(self):
        self.used += 1
        return self.ref.at[self.used - 1]

    def many(self, count):
        base = self.used
        self.used += count
        return lambda i: self.ref.at[base + i]


class Spread:
    def __init__(self, ref, owner, chip, plane, core, marks):
        self.ref, self.spot = ref, (chip, plane, core)
        self.sends = marks.many(3)
        self.arrived = marks.one()
        inner = is_inner(plane)
        self.mine = plane == owner
        self.outer_owner = self.mine & no(inner)
        self.inner_owner = self.mine & inner
        far = (plane == away(owner, 2)) | ((plane == away(owner, 3)) & is_inner(owner))
        self.relays = inner & far

    def copy(self, step, send):
        chip, plane, core = self.spot
        return remote(
            self.ref, self.ref, self.sends(send), self.arrived,
            device(chip, away(plane, step), core),
        )

    def start(self):
        pl.when(self.outer_owner)(lambda: self.copy(2, 1).start())
        pl.when(self.inner_owner)(lambda: self.copy(3, 1).start())
        pl.when(self.mine)(lambda: self.copy(1, 0).start())

    def relay(self):
        @pl.when(self.relays)
        def _():
            self.copy(1, 2).wait_recv()
            self.copy(1, 2).start()

    def arrive(self):
        pl.when(no(self.mine | self.relays))(lambda: self.copy(1, 2).wait_recv())

    def finish(self):
        @pl.when(self.mine)
        def _():
            self.copy(1, 0).wait_send()
            self.copy(1, 1).wait_send()

        pl.when(self.relays)(lambda: self.copy(1, 2).wait_send())


class Chain:
    def __init__(self, ref, owner, chip, plane, core, marks):
        self.ref, self.spot = ref, (chip, plane, core)
        self.sends = marks.many(2)
        self.arrived = marks.one()
        inner = is_inner(plane)
        self.mine = plane == owner
        self.mine_inner, self.mine_outer = self.mine & inner, self.mine & no(inner)
        self.from_end = inner & (plane == away(owner, 1))
        self.from_inner = inner & (plane == away(owner, 3))
        self.from_far = inner & (plane == away(owner, 2))
        self.waits = no(inner) & no(self.mine)

    def copy(self, step, send):
        chip, plane, core = self.spot
        return remote(
            self.ref, self.ref, self.sends(send), self.arrived,
            device(chip, away(plane, step), core),
        )

    def start(self):
        pl.when(self.mine_outer)(lambda: self.copy(1, 0).start())

    def start_inner(self):
        @pl.when(self.mine_inner)
        def _():
            self.copy(3, 1).start()
            self.copy(1, 0).start()

    def relay(self):
        pl.when(self.from_end | self.from_inner)(lambda: self.copy(1, 0).wait_recv())
        pl.when(self.from_end)(lambda: self.copy(3, 0).start())
        pl.when(self.from_inner)(lambda: self.copy(1, 0).start())

    def relay_far(self):
        @pl.when(self.from_far)
        def _():
            self.copy(1, 0).wait_recv()
            self.copy(1, 0).start()

    def arrive(self):
        pl.when(self.waits)(lambda: self.copy(1, 0).wait_recv())

    def finish(self):
        pl.when(no(self.waits))(lambda: self.copy(1, 0).wait_send())
        pl.when(self.mine_inner)(lambda: self.copy(3, 1).wait_send())


class MainTiles:
    def __init__(self, ff, chip, plane, core, marks):
        self.ff, self.spot = ff, (chip, plane, core)
        self.sends, self.here = marks.many(5), marks.many(3)
        self.inner = is_inner(plane)

    def copy(self, slot, to_step, send, receive):
        chip, plane, core = self.spot
        tiles = self.ff.at[:, :, lanes(slot * TILE)]
        return remote(
            tiles, tiles, self.sends(send), self.here(receive),
            device(chip, away(plane, to_step), core),
        )

    def got(self, step):
        self.copy(self.spot[1], 1, 0, step - 1).wait_recv()

    def start(self):
        plane = self.spot[1]
        self.copy(plane, 1, 0, 0).start()
        pl.when(self.inner)(lambda: self.copy(plane, 3, 2, 2).start())

    def relay(self):
        plane = self.spot[1]

        @pl.when(self.inner)
        def _():
            self.got(1)
            self.copy(away(plane, 1), 3, 1, 1).start()
            self.got(3)
            self.copy(away(plane, 3), 1, 3, 1).start()

    def relay_far(self):
        plane = self.spot[1]

        @pl.when(self.inner)
        def _():
            self.got(2)
            self.copy(away(plane, 2), 1, 4, 2).start()

    def arrive(self, step):
        pl.when(no(self.inner))(lambda: self.got(step))

    def finish(self):
        self.copy(self.spot[1], 1, 0, 0).wait_send()

        @pl.when(self.inner)
        def _():
            for send in range(1, 5):
                self.copy(self.spot[1], 1, send, 0).wait_send()


class MainGrads:
    def __init__(self, gout, slots, chip, plane, core, marks):
        self.gout, self.slots, self.spot = gout, slots, (chip, plane, core)
        self.sends, self.here = marks.many(3), marks.many(5)
        self.inner = is_inner(plane)

    def copy(self, slot, to_step, send, receive):
        chip, plane, core = self.spot
        return remote(
            self.gout.at[:, :, lanes(slot * TILE)], self.slots.at[receive],
            self.sends(send), self.here(receive), device(chip, away(plane, to_step), core),
        )

    def start(self, step):
        receive = {1: 0, 2: 4, 3: 3}[step]
        self.copy(away(self.spot[1], step), 1, step - 1, receive).start()

    def relay(self, step, add):
        @pl.when(self.inner)
        def _():
            receive = {2: 3, 3: 4}[step]
            self.copy(self.spot[1], 1, 0, receive).wait_recv()
            slot = away(self.spot[1], step)
            add(slot, self.slots.at[receive])
            self.copy(slot, step, step - 1, step - 1).start()

    def total(self, add):
        plane = self.spot[1]
        self.copy(plane, 1, 0, 0).wait_recv()
        add(plane, self.slots.at[0])

        @pl.when(no(self.inner))
        def _():
            self.copy(plane, 1, 0, 1).wait_recv()
            add(plane, self.slots.at[1])

        @pl.when(self.inner)
        def _():
            self.copy(plane, 1, 0, 2).wait_recv()
            add(plane, self.slots.at[2])

    def finish(self):
        for send in range(3):
            self.copy(self.spot[1], 1, send, 0).wait_send()


class Collect:
    def __init__(self, ref, slots, owner, chip, plane, core, marks):
        self.ref, self.slots, self.spot = ref, slots, (chip, plane, core)
        self.send = marks.one()
        self.arrived = marks.many(3)
        inner, inner_owner = is_inner(plane), is_inner(owner)
        self.mine = plane == owner
        self.mine_outer = self.mine & no(inner)
        self.mine_inner = self.mine & inner
        self.near = plane == away(owner, 1)
        second, third = plane == away(owner, 2), plane == away(owner, 3)
        self.hands = no(inner) & (second | third) & no(self.near)
        self.adds_second = inner & second & no(inner_owner)
        self.adds_third = inner & third & inner_owner

    def copy(self, step, slot):
        chip, plane, core = self.spot
        return remote(
            self.ref, self.slots.at[slot], self.send, self.arrived(slot),
            device(chip, away(plane, step), core),
        )

    def start(self):
        pl.when(self.near)(lambda: self.copy(1, 0).start())
        pl.when(self.hands)(lambda: self.copy(1, 2).start())

    def relay(self, add):
        @pl.when(self.adds_second | self.adds_third)
        def _():
            self.copy(1, 2).wait_recv()
            add(self.slots.at[2])

        pl.when(self.adds_second)(lambda: self.copy(2, 1).start())
        pl.when(self.adds_third)(lambda: self.copy(3, 1).start())

    def total(self, add):
        @pl.when(self.mine)
        def _():
            for slot in range(2):
                self.copy(1, slot).wait_recv()
                add(self.slots.at[slot])

    def finish(self):
        pl.when(no(self.mine))(lambda: self.copy(1, 0).wait_send())


def layer_kernel(
    w_gate, w_up, w_down, w_qkv, w_out, conv, gain_mix, gain_ffn, tok, cot,
    out_ff, out_at, out_res, out_tok, out_small, main_got, extra_got, att_got,
    ff, at, xs, gs, low2, part, acc3, gout, gat, from_mate, both, got, turned, hid, gg,
    gn, gcol, raw, qs, ks, vs, att, gatt, gproj, mid, gmid, gsum, normed, sending, inv_all,
    inv_sum, small, small_a, small_b, raw_ff, raw_qkv, raw_out, raw_conv, tapped, last_tile, wat,
    gains, gain_rows, sem, free_mate, free_chips,
):
    chip, plane, core = place()
    others = other_chips(chip)
    mate = device(chip, plane, 1 - core)
    marks = Marks(sem)
    rows = tok.shape[0]
    width = 4 * rows
    half = tok.shape[1]
    seq = 2 * half
    own_half = lanes(core * half, half)
    first = core * half + chip * TILE
    peers = [device(c, plane, core) for c in others]
    line = [device(chip, away(plane, step), core) for step in (1, 2, 3)]
    sides = [device(c, plane, 1 - core) for c in others]
    line_mates = [device(chip, away(plane, step), 1 - core) for step in (1, 2, 3)]

    barrier = pltpu.get_barrier_semaphore()
    partners = peers + [mate] + sides + line + line_mates
    for partner in partners:
        pl.semaphore_signal(barrier, inc=1, device_id=partner, device_id_type=MESH)

    def block_rows(c):
        return rows_at(c * rows, rows, rows)

    ffn_weights = (w_gate, w_up, w_down)
    ffn_cols = w_gate.shape[1]
    early = marks.many(8)
    loads = [
        pltpu.make_async_copy(source, target, early(i))
        for i, (source, target) in enumerate(
            (
                (w_qkv, raw_qkv), (w_out, raw_out), (conv, raw_conv),
                (gain_mix, gain_rows[0]), (gain_ffn, gain_rows[1]),
            )
        )
    ]
    ffn_loads = [
        pltpu.make_async_copy(ffn_weights[m], raw_ff.at[m], early(5 + m)) for m in range(3)
    ]
    for load in loads + ffn_loads:
        load.start()
    for load in loads:
        load.wait()
    for i in range(2):
        gains[i] = gain_rows[i][...].reshape(1, rows)
    tapped[...] = jnp.zeros(tapped.shape, F32)
    tapped[0:CONV, 0 : 2 * HDIM] = raw_conv[...].astype(F32)
    tap_rows = tapped[...].T
    tail = lax.broadcasted_iota(jnp.int32, (HDIM, TILE), 1)
    spare = rows % TILE
    for h in range(2):
        wat[h, :HEADROWS, :rows] = raw_qkv[h * HEADROWS : (h + 1) * HEADROWS]
        wat[h, HEADROWS:, :rows] = raw_out[h * HDIM : (h + 1) * HDIM]
        columns = wat[h, 2 * FEAT : HEADROWS, WIDE - TILE :].astype(F32)
        for j in range(CONV):
            column = tap_rows[h * HDIM : (h + 1) * HDIM, j : j + 1]
            columns = jnp.where(tail == spare + j, column, columns)
        wat[h, 2 * FEAT : HEADROWS, WIDE - TILE :] = columns.astype(BF16)
    for load in ffn_loads:
        load.wait()
    short = ffn_cols - 4 * TILE
    for m in range(3):
        last_tile[m, :, 0:short] = raw_ff[m, :, 4 * TILE :]
        last_tile[m, :, short:] = jnp.zeros((rows, TILE - short), BF16)

    pl.semaphore_wait(barrier, len(partners))

    far_core = plane // 2
    holds_att = core == far_core
    holds_extra = holds_att & (chip // 2 == plane % 2)
    extra_plane = 2 * core + chip // 2
    extra_chip = (plane % 2) * 2 + core
    out_rows, in_rows = pl.ds(HEADROWS, HDIM), pl.ds(0, HEADROWS)
    att_self = [(2 * core + h == chip) & holds_att for h in range(2)]

    class Heads:
        def __init__(self, span):
            self.span, self.local = span, marks.one()
            self.send, self.here = marks.many(2), marks.many(4)

        def copy(self, h):
            return remote(
                wat.at[h, self.span], at.at[plane % 2, chip, self.span], self.send(h),
                self.here(chip), device(2 * core + h, plane, far_core),
            )

        def keep(self, h):
            return pltpu.make_async_copy(
                wat.at[h, self.span], at.at[plane % 2, chip, self.span], self.local
            )

        def start(self):
            for h in range(2):
                pl.when(att_self[h])(lambda: self.keep(h).start())
                pl.when(no(att_self[h]))(lambda: self.copy(h).start())

        def arrive(self):
            for h in range(2):
                pl.when(att_self[h])(lambda: self.keep(h).wait())

            for c in range(4):

                @pl.when(holds_att & no((c == chip) & (core == chip // 2)))
                def _():
                    remote(
                        wat.at[0, self.span], at.at[plane % 2, c, self.span], self.send(0),
                        self.here(c), mate,
                    ).wait_recv()

        def finish(self):
            for h in range(2):
                pl.when(no(att_self[h]))(lambda: self.copy(h).wait_send())

    heads_in, heads_out = Heads(in_rows), Heads(out_rows)
    heads_in.start()
    heads_out.start()

    class Gather:
        def __init__(self, source, target_of):
            self.source, self.target_of = source, target_of
            self.send, self.here = marks.many(6), marks.many(6)
            self.mate_send, self.mate_here = marks.many(4), marks.many(4)
            self.keep = pltpu.make_async_copy(source, target_of(chip), marks.one())
            mine = self.halves(source)
            there = self.halves(target_of(chip))
            self.copies = {
                mark: remote(
                    mine[half], there[half], self.send(mark), self.here(mark), peers[p]
                )
                for mark, half, p in ((0, 0, 0), (3, 1, 1), (1, 1, 0), (2, 0, 1))
            }
            for copy in self.copies.values():
                copy.start()
            self.keep.start()
            self.crossing = []
            self.cross(source, chip, 3)

        def cross(self, source, c, mark):
            copy = remote(
                source, self.target_of(c), self.mate_send(mark), self.mate_here(mark), mate
            )
            copy.start()
            self.crossing.append(copy)

        def halves(self, block):
            size = block.shape[0] // 2
            return block.at[0:size], block.at[size : 2 * size]

        def pass_on(self):
            for mark, half, p, onward in ((0, 0, 0, 4), (3, 1, 1, 5)):
                self.copies[mark].wait_recv()
                block = self.halves(self.target_of(others[p]))[half]
                self.copies[onward] = remote(
                    block, block, self.send(onward), self.here(onward), peers[1 - p]
                )
                self.copies[onward].start()
            for mark, p in ((1, 0), (2, 1)):
                self.copies[mark].wait_recv()
                self.cross(self.target_of(others[p]), others[p], p)

        def arrive(self):
            for mark in (4, 5):
                self.copies[mark].wait_recv()
            self.cross(self.target_of(others[2]), others[2], 2)
            for copy in self.crossing:
                copy.wait_recv()
            self.keep.wait()

        def finish(self):
            for copy in list(self.copies.values()) + self.crossing:
                copy.wait_send()

    tokens_in = Gather(tok, lambda c: xs.at[block_rows(c), own_half])
    gain_send, gain_here = marks.many(3), marks.many(3)
    gain_copies = [
        remote(gains, gn.at[chip], gain_send(p), gain_here(p), peers[p]) for p in range(3)
    ]
    gain_keep = pltpu.make_async_copy(gains, gn.at[chip], marks.one())
    for copy in gain_copies + [gain_keep]:
        copy.start()

    in_line, out_line = [
        [
            Spread(at.at[a, :, span], 2 * core + a, chip, plane, core, marks)
            for a in range(2)
        ]
        for span in (in_rows, out_rows)
    ]
    heads_in.arrive()
    for item in in_line:
        item.start()
    heads_out.arrive()
    for item in out_line:
        item.start()
    heads_in.finish()
    heads_out.finish()

    tokens_in.pass_on()
    main_send, main_here, main_local = marks.many(9), marks.many(9), marks.many(3)
    main_here_at = [ff.at[m, block_rows(chip), lanes(plane * TILE)] for m in range(3)]
    mains = [
        remote(
            ffn_weights[m].at[:, lanes(others[p] * TILE)], main_here_at[m],
            main_send(3 * p + m), main_here(3 * p + m), peers[p],
        )
        for p in range(3)
        for m in range(3)
    ]
    mains += [
        pltpu.make_async_copy(
            ffn_weights[m].at[:, lanes(chip * TILE)], main_here_at[m], main_local(m)
        )
        for m in range(3)
    ]
    for copy in mains:
        copy.start()

    extra_send, extra_here, extra_local = marks.one(), marks.many(4), marks.one()
    extra_self = (extra_chip == chip) & holds_att
    last = lanes(4 * TILE)

    def extra_copy():
        return remote(
            last_tile, ff.at[:, block_rows(chip), last], extra_send, extra_here(chip),
            device(extra_chip, plane, far_core),
        )

    def extra_keep():
        return pltpu.make_async_copy(
            last_tile, ff.at[:, block_rows(chip), last], extra_local
        )

    @pl.when(extra_self)
    def _():
        extra_keep().start()

    @pl.when(no(extra_self))
    def _():
        extra_copy().start()

    for item in in_line:
        item.relay()
    tokens_in.arrive()
    cot_in = Gather(cot, lambda c: gs.at[block_rows(c), own_half])
    for copy in gain_copies + [gain_keep]:
        copy.wait()

    for item in out_line:
        item.relay()
    @pl.loop(0, 4)
    def _(c):
        pair = jnp.concatenate(
            [gn[c, 0].astype(F32), gn[c, 1].astype(F32), jnp.zeros((6, rows), F32)], 0
        )
        gcol[block_rows(c), 0:8] = pair.T

    step_rows = 64

    def add_squares(i, total):
        x = xs[rows_at(i * step_rows, step_rows, step_rows)].astype(F32)
        return total + jnp.sum((x * x).reshape(step_rows // 8, 8, seq), 0)

    squares = lax.fori_loop(0, width // step_rows, add_squares, jnp.zeros((8, seq), F32))
    inv_all[...] = lax.rsqrt(jnp.sum(squares, 0, keepdims=True) / D + EPSILON)
    tokens_in.finish()
    normed[...] = xs[:, lanes(first)]

    @pl.loop(0, width // step_rows)
    def _(i):
        at_rows = rows_at(i * step_rows, step_rows, step_rows)
        xs[at_rows] = (
            xs[at_rows].astype(F32) * inv_all[...] * gcol[at_rows, 0:1]
        ).astype(BF16)

    for item in in_line:
        item.arrive()

    position = lax.broadcasted_iota(jnp.int32, (1, seq), 1)

    def taps(h):
        columns = at[h, 0, 2 * FEAT : HEADROWS, WIDE - TILE : WIDE].astype(F32)
        return [columns[:, rows % TILE + j : rows % TILE + j + 1] for j in range(CONV)]

    @pl.loop(0, 2)
    def _(h):
        projected = dot(at[h, 0, :HEADROWS, :rows], xs[0:rows], 1, 0)
        for c in range(1, 4):
            projected += dot(at[h, c, :HEADROWS, :rows], xs[c * rows : (c + 1) * rows], 1, 0)
        qs[h] = (projected[:FEAT].astype(BF16).astype(F32) * FEAT**-0.5).astype(BF16)
        ks[h] = projected[FEAT : 2 * FEAT].astype(BF16)
        values = projected[2 * FEAT :]
        raw[h] = values
        tap = taps(h)
        mixed = tap[0] * values
        for j in range(1, CONV):
            moved = pltpu.roll(values, j, 1)
            mixed += tap[j] * jnp.where(position >= j, moved, 0.0)
        vs[h] = mixed.astype(BF16)

    def kernel_of(h, b):
        seen = (b + 1) * SPAN
        scores = dot(ks[h, :, :seen], qs[h, :, b * SPAN : seen], 0, 0)
        kernel = 1.0 + scores + 0.5 * scores * scores
        key_at = lax.broadcasted_iota(jnp.int32, (seen, SPAN), 0)
        query_at = lax.broadcasted_iota(jnp.int32, (seen, SPAN), 1) + b * SPAN
        visible = key_at <= query_at
        return scores, jnp.where(visible, kernel, 0.0), visible

    @pl.loop(0, 2)
    def _(h):
        for b in range(seq // SPAN):
            seen = (b + 1) * SPAN
            _, kernel, _ = kernel_of(h, b)
            inverse = 1.0 / jnp.sum(kernel, 0, keepdims=True)
            inv_sum[h, :, b * SPAN : seen] = inverse
            weights = (kernel * inverse).astype(BF16)
            att[h, :, b * SPAN : seen] = dot(vs[h, :, :seen], weights, 1, 0).astype(BF16)

    for copy in mains:
        copy.wait()
    main_line = MainTiles(ff, chip, plane, core, marks)
    main_line.start()

    @pl.when(extra_self)
    def _():
        extra_keep().wait()

    @pl.when(no(extra_self))
    def _():
        extra_copy().wait_send()

    for c in range(4):

        @pl.when(holds_extra & no((c == chip) & (core == chip % 2)))
        def _():
            remote(
                last_tile, ff.at[:, block_rows(c), last], extra_send, extra_here(c), mate
            ).wait_recv()

    extra_line = Chain(ff.at[:, :, last], extra_plane, chip, plane, core, marks)
    extra_line.start()

    for item in out_line:
        item.arrive()

    def default_got(i):
        return got.at[i]

    class Sum:
        def __init__(self, guard, both=both, got=None, share=True, at_once=True):
            self.guard, self.both, self.share, self.at_once = guard, both, share, at_once
            self.got = got or default_got

        def begin(self, fill):
            fill((1 - core) * half)
            send, here = marks.many(4), marks.many(4)
            self.order = (others[2], others[0], others[1], chip)
            self.to_mate = [
                remote(
                    part.at[:, lanes((1 - core) * half + c * TILE)],
                    from_mate.at[:, lanes(c * TILE)], send(i), here(i), mate,
                )
                for i, c in enumerate(self.order)
            ]
            if self.guard:
                pl.semaphore_wait(free_mate, 1)
            for copy in self.to_mate:
                copy.start()
            fill(core * half)

        def combine(self):
            self.prepare()
            for i, c in enumerate(self.order):
                self.to_mate[i].wait_recv()
                where, own = lanes(c * TILE), lanes(core * half + c * TILE)

                @pl.loop(0, 4)
                def _(b):
                    at_rows = block_rows(b)
                    self.both[at_rows, where] = (
                        part[at_rows, own].astype(F32) + from_mate[at_rows, where].astype(F32)
                    ).astype(BF16)

                if self.at_once:
                    self.send(i)
            pl.semaphore_signal(free_mate, inc=1, device_id=mate, device_id_type=MESH)
            for copy in self.to_mate:
                copy.wait_send()

        def piece(self, upper, c):
            size = width // 2
            return self.both.at[pl.ds(0 if upper else size, size), lanes(c * TILE)]

        def prepare(self):
            size = width // 2
            top, bottom = pl.ds(0, size), pl.ds(size, size)
            send, here = marks.many(6), marks.many(6)
            x, y, across = others
            self.across = [
                remote(self.piece(True, across), self.got(2).at[top], send(0), here(0), peers[0]),
                remote(
                    self.piece(False, across), self.got(2).at[bottom], send(1), here(1), peers[1]
                ),
            ]
            self.plain = [
                remote(self.piece(True, x), self.got(0).at[top], send(2), here(2), peers[0]),
                remote(self.piece(False, y), self.got(1).at[bottom], send(3), here(3), peers[1]),
            ]
            self.added = [
                remote(self.piece(True, y), self.got(1).at[top], send(4), here(4), peers[1]),
                remote(self.piece(False, x), self.got(0).at[bottom], send(5), here(5), peers[0]),
            ]

        def send(self, i):
            if i == 0:
                if self.guard and self.share:
                    pl.semaphore_wait(free_chips, 2)
                for copy in self.across:
                    copy.start()
            elif i < 3:
                self.plain[i - 1].start()

        def send_all(self):
            for i in range(3):
                self.send(i)

        def pass_on(self):
            size = width // 2
            quarter = size // 2
            for i, c in ((0, others[1]), (1, others[0])):
                self.across[i].wait_recv()
                for q in range(2):
                    at_rows = pl.ds(i * size + q * quarter, quarter)
                    self.both[at_rows, lanes(c * TILE)] = (
                        self.both[at_rows, lanes(c * TILE)].astype(F32) + self.got(2)[at_rows].astype(F32)
                    ).astype(BF16)
                self.added[i].start()

        def finish(self, store):
            for copy in self.plain + self.added:
                copy.wait()
            for copy in self.across:
                copy.wait_send()

            @pl.loop(0, 4)
            def _(c):
                at_rows = block_rows(c)
                total = self.both[at_rows, lanes(chip * TILE)].astype(F32)
                for p in range(2):
                    total += self.got(p)[at_rows].astype(F32)
                store(at_rows, total)

            for p in range(2 if self.share else 0):
                pl.semaphore_signal(free_chips, inc=1, device_id=peers[p], device_id_type=MESH)

    def fill_branch(start):
        @pl.loop(0, 4)
        def _(c):
            where = lanes(start, half)
            total = dot(at[0, c, HEADROWS:, :rows], att[0, :, where], 0, 0)
            total += dot(at[1, c, HEADROWS:, :rows], att[1, :, where], 0, 0)
            part[block_rows(c), where] = total.astype(BF16)

    small[...] = jnp.zeros(small.shape, F32)
    square_at = lax.broadcasted_iota(jnp.int32, (1, WIDE), 1)

    def note_square(index, value):
        total = jnp.sum(value * value)
        small[0, 2:3, :] += jnp.where(square_at == index, total, 0.0)

    def store_branch(at_rows, total):
        note_square(0, total)
        mid[at_rows] = normed[at_rows].astype(F32) + total

    branch_sum = Sum(guard=False)
    branch_sum.begin(fill_branch)
    cot_in.pass_on()
    cot_in.arrive()
    branch_sum.combine()
    branch_sum.pass_on()
    main_line.relay()
    extra_line.start_inner()
    branch_sum.finish(store_branch)
    middle = mid[...]
    inverse_two = lax.rsqrt(jnp.sum(middle * middle, 0, keepdims=True) / D + EPSILON)

    @pl.loop(0, 4)
    def _(c):
        at_rows = block_rows(c)
        sending[0, at_rows] = (mid[at_rows] * inverse_two * gcol[at_rows, 1:2]).astype(BF16)

    def token_block(c):
        return low2.at[:, lanes(core * half + c * TILE)]

    low_in = Gather(sending.at[0], token_block)
    cot_in.finish()

    @pl.loop(0, 4)
    def _(c):
        acc3[block_rows(c)] = jnp.zeros((rows, seq), F32)

    low_in.pass_on()
    low_in.arrive()
    low_in.finish()

    main_line.relay_far()
    extra_line.relay()
    def feed(slot):
        where = lanes(slot * TILE)
        unit_rows = rows_at(slot * TILE, TILE, TILE)
        for m in range(3):
            turned[m * TILE : (m + 1) * TILE] = ff[m, :, where].T

        @pl.loop(0, seq // SPAN)
        def _(n):
            span = lanes(n * SPAN, SPAN)
            gate_up = dot(turned[: 2 * TILE], low2[:, span], 1, 0)
            grad_hidden = dot(turned[2 * TILE :], gs[:, span], 1, 0)
            gate, up = gate_up[:TILE], gate_up[TILE:]
            sigmoid = 1.0 / (1.0 + jnp.exp(-gate))
            activated = gate * sigmoid
            hid[unit_rows, span] = (activated * up).astype(BF16)
            gg[:TILE, span] = (
                grad_hidden * up * sigmoid * (1.0 + gate * (1.0 - sigmoid))
            ).astype(BF16)
            gg[TILE:, span] = (grad_hidden * activated).astype(BF16)

        @pl.loop(0, 4)
        def _(c):
            at_rows = block_rows(c)
            pair = jnp.concatenate([ff[0, at_rows, where], ff[1, at_rows, where]], 1)
            acc3[at_rows] += dot(pair, gg[...], 1, 0)
            grads = dot(low2[at_rows], gg[...], 1, 1).astype(BF16)
            gout[0, at_rows, where] = grads[:, :TILE]
            gout[1, at_rows, where] = grads[:, TILE:]
            gout[2, at_rows, where] = dot(gs[at_rows], hid[unit_rows], 1, 1).astype(BF16)

    main_back = MainGrads(gout, main_got, chip, plane, core, marks)
    extra_back = Collect(gout.at[:, :, last], extra_got, extra_plane, chip, plane, core, marks)
    load_marks = marks.many(3)

    def add_tiles(slot, source):
        loads = [
            pltpu.make_async_copy(source.at[m], ff.at[2, :, lanes(m * TILE)], load_marks(m))
            for m in range(3)
        ]
        for load in loads:
            load.start()
        for load in loads:
            load.wait()
        where = lanes(slot * TILE)

        @pl.loop(0, 4)
        def _(c):
            at_rows = block_rows(c)
            for m in range(3):
                gout[m, at_rows, where] = (
                    gout[m, at_rows, where].astype(F32)
                    + ff[2, at_rows, m * TILE : (m + 1) * TILE].astype(F32)
                ).astype(BF16)

    def add_extra(source):
        add_tiles(4, source)

    slots = [away(plane, 1), plane, away(plane, 2), away(plane, 3), 4]
    inner = is_inner(plane)

    @pl.loop(0, 5)
    def _(turn):
        pl.when(turn == 2)(lambda: extra_line.relay_far())

        for i, step in ((0, 1), (2, 2), (3, 3)):

            @pl.when(turn == i)
            def _():
                main_line.arrive(step)

        @pl.when(turn == 4)
        def _():
            extra_line.arrive()

        slot = sum((turn == i).astype(jnp.int32) * slots[i] for i in range(5))
        feed(slot)

        for i, step in ((0, 1), (2, 2), (3, 3)):

            @pl.when((turn == i) & no(inner))
            def _():
                main_back.start(step)

    pl.when(inner)(lambda: main_back.start(1))

    extra_back.start()
    main_line.finish()

    def fill_grad_two(start):
        @pl.loop(0, 4)
        def _(c):
            where = lanes(start, half)
            part[block_rows(c), where] = acc3[block_rows(c), where].astype(BF16)

    def store_gsum(at_rows, total):
        gsum[at_rows] = total

    two_sum = Sum(guard=True)
    two_sum.begin(fill_grad_two)
    two_sum.combine()
    two_sum.pass_on()

    def fill_ffn(start):
        @pl.loop(0, 4)
        def _(c):
            where = lanes(start, half)
            part[block_rows(c), where] = dot(
                ff[2, block_rows(c)], hid[:, where], 1, 0
            ).astype(BF16)

    ffn_sum = Sum(
        guard=True, both=ff.at[1, :, lanes(0, half)],
        got=lambda i: ff.at[0, :, lanes(i * TILE)], share=False,
        at_once=False,
    )
    ffn_sum.begin(fill_ffn)
    two_sum.finish(store_gsum)

    main_back.relay(3, add_tiles)
    def norm_back(source, inverse, gain_lane, base, store):
        def add_dots(c, total):
            at_rows = block_rows(c)
            gain = gcol[at_rows, gain_lane : gain_lane + 1]
            return total + jnp.sum(gsum[at_rows] * gain * source(at_rows), 0, keepdims=True)

        dots = lax.fori_loop(0, 4, add_dots, jnp.zeros((1, TILE), F32))
        scaled = inverse * inverse * inverse * dots / D

        @pl.loop(0, 4)
        def _(c):
            at_rows = block_rows(c)
            gain = gcol[at_rows, gain_lane : gain_lane + 1]
            grad, value = gsum[at_rows], source(at_rows)
            store(at_rows, base(at_rows) + (grad * gain * inverse - value * scaled))

        def gain_back():
            @pl.loop(0, 4)
            def _(c):
                at_rows = block_rows(c)
                for_gain = jnp.sum((gsum[at_rows] * source(at_rows) * inverse).T, 0, keepdims=True)
                small[c, gain_lane : gain_lane + 1, 0:rows] = for_gain

        return gain_back

    def store_middle(at_rows, value):
        gmid[at_rows] = value
        sending[1, at_rows] = value.astype(BF16)

    gain_two_back = norm_back(
        lambda r: mid[r], inverse_two, 1, lambda r: gs[r, lanes(first)].astype(F32), store_middle
    )
    mid_in = Gather(sending.at[1], token_block)
    gain_two_back()
    ffn_sum.combine()
    mid_in.pass_on()
    ffn_sum.send_all()
    mid_in.arrive()

    @pl.loop(0, 2)
    def _(h):
        total = dot(at[h, 0, HEADROWS:, :rows], low2[0:rows], 1, 0)
        for c in range(1, 4):
            total += dot(at[h, c, HEADROWS:, :rows], low2[c * rows : (c + 1) * rows], 1, 0)
        gatt[h] = total.astype(BF16)

    main_back.relay(2, add_tiles)

    out_back, in_back = [
        [
            Collect(
                gat.at[a, :, span], att_got.at[a, :, :, span], 2 * core + a,
                chip, plane, core, marks,
            )
            for a in range(2)
        ]
        for span in (out_rows, in_rows)
    ]

    def head_grads(left, right, start, size):
        whole = rows // TILE * TILE

        @pl.loop(0, 2)
        def _(h):
            for c in range(4):
                grad = dot(left[h], right[c * rows : (c + 1) * rows], 1, 1).astype(BF16)
                gat[h, c, start : start + size, :whole] = grad[:, :whole]
                gat[h, c, start : start + size, whole:rows] = grad[:, whole:]

    head_grads(att, low2, HEADROWS, HDIM)
    for item in out_back:
        item.start()


    @pl.loop(0, 2)
    def _(h):
        grad_keys = jnp.zeros((FEAT, seq), F32)
        grad_values = jnp.zeros((HDIM, seq), F32)

        def padded(value):
            short = seq - value.shape[1]
            if not short:
                return value
            return jnp.concatenate([value, jnp.zeros((value.shape[0], short), F32)], 1)

        for b in range(seq // SPAN):
            seen = (b + 1) * SPAN
            span = slice(b * SPAN, seen)
            scores, kernel, visible = kernel_of(h, b)
            inverse = inv_sum[h, :, span]
            weights = kernel * inverse
            grad_weights = dot(vs[h, :, :seen], gatt[h, :, span], 0, 0)
            grad_values += padded(dot(gatt[h, :, span], weights.astype(BF16), 1, 1))
            dots = jnp.sum(grad_weights * weights, 0, keepdims=True)
            grad_kernel = (grad_weights - dots) * inverse
            grad_scores = jnp.where(visible, grad_kernel * (1.0 + scores), 0.0).astype(BF16)
            gproj[h, :FEAT, span] = (
                dot(ks[h, :, :seen], grad_scores, 1, 0) * FEAT**-0.5
            ).astype(BF16)
            grad_keys += padded(dot(qs[h, :, span], grad_scores, 1, 1))
        gproj[h, FEAT : 2 * FEAT] = grad_keys.astype(BF16)
        tap = taps(h)
        grad_raw = tap[0] * grad_values
        sums = [jnp.sum(grad_values * raw[h], 1, keepdims=True)]
        for j in range(1, CONV):
            masked = jnp.where(position >= j, grad_values, 0.0)
            grad_raw += tap[j] * pltpu.roll(masked, seq - j, 1)
            sums.append(jnp.sum(masked * pltpu.roll(raw[h], j, 1), 1, keepdims=True))
        gproj[h, 2 * FEAT :] = grad_raw.astype(BF16)
        columns = jnp.zeros((HDIM, TILE), F32)
        for j in range(CONV):
            columns = jnp.where(tail == rows % TILE + j, sums[j], columns)
        for c in range(4):
            gat[h, c, 2 * FEAT : HEADROWS, WIDE - TILE :] = columns.astype(BF16)

    head_grads(gproj, xs, 0, HEADROWS)
    for item in in_back:
        item.start()

    ffn_sum.pass_on()
    mid_in.finish()

    def fill_grad_one(start):
        @pl.loop(0, 4)
        def _(c):
            where = lanes(start, half)
            total = dot(at[0, c, :HEADROWS, :rows], gproj[0, :, where], 0, 0)
            total += dot(at[1, c, :HEADROWS, :rows], gproj[1, :, where], 0, 0)
            part[block_rows(c), where] = total.astype(BF16)

    one_sum = Sum(guard=True)
    one_sum.begin(fill_grad_one)
    one_sum.combine()
    extra_back.relay(add_extra)

    def store_result(at_rows, total):
        note_square(1, total)
        total = mid[at_rows] + total
        note_square(2, total)
        sending[0, at_rows] = total.astype(BF16)

    one_sum.pass_on()

    def hand_out(source, target):
        send, here = marks.many(3), marks.many(3)
        copies = [
            remote(
                source.at[block_rows(others[p])], target.at[:, lanes(chip * TILE)],
                send(p), here(p), peers[p],
            )
            for p in range(3)
        ]
        copies.append(
            pltpu.make_async_copy(
                source.at[block_rows(chip)], target.at[:, lanes(chip * TILE)], marks.one()
            )
        )
        for copy in copies:
            copy.start()
        return copies

    ffn_sum.finish(store_result)
    pending = hand_out(sending.at[0], out_res)


    one_sum.finish(store_gsum)
    inverse_own = inv_all[:, lanes(first)]

    def store_tokens(at_rows, value):
        sending[1, at_rows] = value.astype(BF16)

    gain_one_back = norm_back(
        lambda r: normed[r].astype(F32), inverse_own, 0, lambda r: gmid[r], store_tokens
    )
    pending += hand_out(sending.at[1], out_tok)
    gain_one_back()

    for c in range(1, 4):
        small[c, 2:3] = small[0, 2:3]
    a_send, a_here = marks.many(3), marks.many(3)
    trio = [
        remote(small.at[others[p]], small_a.at[p], a_send(p), a_here(p), peers[p])
        for p in range(3)
    ]
    for copy in trio:
        copy.start()

    main_back.total(add_tiles)
    back_send, back_here = marks.many(3), marks.many(3)
    mine = lanes(plane * TILE)
    back_to = out_ff.at[:, :, lanes(chip * TILE)]
    backs = [
        remote(
            gout.at[:, block_rows(others[p]), mine], back_to, back_send(p), back_here(p), peers[p]
        )
        for p in range(3)
    ]
    backs.append(
        pltpu.make_async_copy(gout.at[:, block_rows(chip), mine], back_to, marks.one())
    )
    for copy in backs:
        copy.start()
    pending += backs

    for copy in trio:
        copy.wait()
    small_b[0] = small[chip] + small_a[0] + small_a[1] + small_a[2]
    b_send, b_here = marks.many(7), marks.many(7)
    seven = [
        remote(small_b.at[0], small_b.at[1 + i], b_send(i), b_here(i), to)
        for i, to in enumerate(line + [mate] + line_mates)
    ]
    for copy in seven:
        copy.start()

    extra_back.total(add_extra)
    last_send, last_here, last_local = marks.many(4), marks.one(), marks.one()

    def last_copy(c):
        return remote(
            gout.at[:, block_rows(c), last], out_ff.at[:, :, last], last_send(c), last_here,
            device(c, plane, chip % 2),
        )

    def last_keep():
        return pltpu.make_async_copy(
            gout.at[:, block_rows(chip), last], out_ff.at[:, :, last], last_local
        )

    for c in range(4):
        same = (c == chip) & (core == chip % 2)

        @pl.when(holds_extra & same)
        def _():
            last_keep().start()

        @pl.when(holds_extra & no(same))
        def _():
            last_copy(c).start()

    head_marks = marks.many(4)

    def add_head(a, start, size):
        def add(source):
            loads = [
                pltpu.make_async_copy(
                    source.at[c], part.at[c * BLOCKROWS : c * BLOCKROWS + size, 0:WIDE],
                    head_marks(c),
                )
                for c in range(4)
            ]
            for load in loads:
                load.start()
            for load in loads:
                load.wait()
            for c in range(4):
                gat[a, c, start : start + size] = (
                    gat[a, c, start : start + size].astype(F32)
                    + part[c * BLOCKROWS : c * BLOCKROWS + size, 0:WIDE].astype(F32)
                ).astype(BF16)

        return add

    for items, start, size in ((out_back, HEADROWS, HDIM), (in_back, 0, HEADROWS)):
        for a in range(2):
            items[a].relay(add_head(a, start, size))
    class HeadsBack:
        def __init__(self, span):
            self.span, self.local = span, marks.one()
            self.send, self.here = marks.many(4), marks.many(2)

        def same(self, c):
            return (c == chip) & (core == chip // 2)

        def copy(self, c):
            return remote(
                gat.at[plane % 2, c, self.span], out_at.at[chip % 2, self.span], self.send(c),
                self.here(chip % 2), device(c, plane, chip // 2),
            )

        def keep(self):
            return pltpu.make_async_copy(
                gat.at[plane % 2, chip, self.span], out_at.at[chip % 2, self.span], self.local
            )

        def start(self):
            for c in range(4):
                pl.when(holds_att & self.same(c))(lambda: self.keep().start())
                pl.when(holds_att & no(self.same(c)))(lambda: self.copy(c).start())

        def finish(self):
            for c in range(4):
                pl.when(holds_att & self.same(c))(lambda: self.keep().wait())
                pl.when(holds_att & no(self.same(c)))(lambda: self.copy(c).wait_send())

            for h in range(2):

                @pl.when(no(att_self[h]))
                def _():
                    remote(
                        gat.at[0, 0, self.span], out_at.at[h, self.span], self.send(0),
                        self.here(h), mate,
                    ).wait_recv()

    heads_back = []
    for items, start, size in ((out_back, HEADROWS, HDIM), (in_back, 0, HEADROWS)):
        for a in range(2):
            items[a].total(add_head(a, start, size))
        heads_back.append(HeadsBack(pl.ds(start, size)))
        heads_back[-1].start()

    for copy in seven:
        copy.wait()
    total = small_b[0]
    for i in range(7):
        total += small_b[1 + i]
    small_a[0] = total
    small_out = pltpu.make_async_copy(small_a.at[0], out_small, marks.one())
    small_out.start()
    pending.append(small_out)
    for item in in_line + out_line + [extra_line, main_back, extra_back] + out_back + in_back:
        item.finish()
    for copy in pending:
        copy.wait()
    for c in range(4):
        same = (c == chip) & (core == chip % 2)
        pl.when(holds_extra & same)(lambda: last_keep().wait())
        pl.when(holds_extra & no(same))(lambda: last_copy(c).wait_send())

    @pl.when(no(extra_self))
    def _():
        last_copy(0).wait_recv()

    for item in heads_back:
        item.finish()

    pl.semaphore_wait(free_mate, 1)
    pl.semaphore_wait(free_chips, 2)
    assert marks.used <= MARKS, marks.used


def dma(*shape):
    return pltpu.SemaphoreType.DMA(shape)


def run_layer(w_gate, w_up, w_down, w_qkv, w_out, conv, gain_mix, gain_ffn, tok, cot):
    rows, half = tok.shape
    width, seq = 4 * rows, 2 * half
    shape = jax.ShapeDtypeStruct
    vmem = pltpu.VMEM
    tiles = (3, width, TILE)
    head = (4, BLOCKROWS, WIDE)
    return pl.pallas_call(
        layer_kernel,
        out_shape=[
            shape((3, rows, 5 * TILE), BF16),
            shape((2, BLOCKROWS, WIDE), BF16),
            shape((rows, half), BF16),
            shape((rows, half), BF16),
            shape((8, WIDE), F32),
            shape((5,) + tiles, BF16),
            shape((4,) + tiles, BF16),
            shape((2, 4) + head, BF16),
        ],
        in_specs=[ANY] * 10,
        out_specs=[ANY] * 8,
        scratch_shapes=[
            vmem((3, width, 5 * TILE), BF16),
            vmem((2,) + head, BF16),
            vmem((width, seq), BF16),
            vmem((width, seq), BF16),
            vmem((width, seq), BF16),
            vmem((width, seq), BF16),
            vmem((width, seq), F32),
            vmem((3, width, 5 * TILE), BF16),
            vmem((2,) + head, BF16),
            vmem((width, half), BF16),
            vmem((width, half), BF16),
            vmem((3, width, TILE), BF16),
            vmem((3 * TILE, width), BF16),
            vmem((5 * TILE, seq), BF16),
            vmem((2 * TILE, seq), BF16),
            vmem((4, 2, 1, rows), BF16),
            vmem((width, TILE), F32),
            vmem((2, HDIM, seq), F32),
            vmem((2, FEAT, seq), BF16),
            vmem((2, FEAT, seq), BF16),
            vmem((2, HDIM, seq), BF16),
            vmem((2, HDIM, seq), BF16),
            vmem((2, HDIM, seq), BF16),
            vmem((2, HEADROWS, seq), BF16),
            vmem((width, TILE), F32),
            vmem((width, TILE), F32),
            vmem((width, TILE), F32),
            vmem((width, TILE), BF16),
            vmem((2, width, TILE), BF16),
            vmem((1, seq), F32),
            vmem((2, 1, seq), F32),
            vmem((4, 8, WIDE), F32),
            vmem((3, 8, WIDE), F32),
            vmem((8, 8, WIDE), F32),
            vmem((3,) + w_gate.shape, BF16),
            vmem(w_qkv.shape, BF16),
            vmem(w_out.shape, BF16),
            vmem(conv.shape, BF16),
            vmem((8, 2 * TILE), F32),
            vmem((3, rows, TILE), BF16),
            vmem((2, BLOCKROWS, WIDE), BF16),
            vmem((2, 1, rows), BF16),
            [vmem((rows,), BF16)] * 2,
            dma(MARKS),
            pltpu.SemaphoreType.REGULAR,
            pltpu.SemaphoreType.REGULAR,
        ],
        compiler_params=pltpu.CompilerParams(
            collective_id=0, has_side_effects=True, vmem_limit_bytes=63 * 2**20
        ),
        name="layer",
    )(w_gate, w_up, w_down, w_qkv, w_out, conv, gain_mix, gain_ffn, tok, cot)


def outputs_kernel(
    count, ff, at, tok, small, to_tok, to_qkv, to_conv, to_out, to_gate, to_up, to_down,
    to_mix, to_ffn, to_rms, ff_in, at_in, tok_in, small_in, tok_out, qkv_out, conv_out, out_out,
    ff_out, rms_out, sem,
):
    rows, cols = to_gate.shape
    marks = Marks(sem)
    loads = [
        pltpu.make_async_copy(source, target, marks.one())
        for source, target in (
            [(tok, tok_in), (at, at_in)] + [(ff.at[m], ff_in.at[m]) for m in range(3)]
            + [(small, small_in)]
        )
    ]
    for load in loads:
        load.start()
    stores = []

    def store(source, target):
        stores.append(pltpu.make_async_copy(source, target, marks.one()))
        stores[-1].start()

    loads[0].wait()
    tok_out[...] = tok_in[...].astype(F32)
    store(tok_out, to_tok)
    loads[1].wait()
    for h in range(2):
        qkv_out[h * HEADROWS : (h + 1) * HEADROWS] = at_in[h, :HEADROWS, :rows].astype(F32)
        out_out[h * HDIM : (h + 1) * HDIM] = at_in[h, HEADROWS:, :rows].astype(F32)
    store(qkv_out, to_qkv)
    store(out_out, to_out)
    taps = jnp.concatenate(
        [at_in[h, 2 * FEAT : HEADROWS, WIDE - TILE :].astype(F32) for h in range(2)], 0
    )
    conv_out[...] = taps.T[rows % TILE : rows % TILE + CONV]
    store(conv_out, to_conv)
    for m, target in enumerate((to_gate, to_up, to_down)):
        loads[2 + m].wait()
        ff_out[m] = ff_in[m, :, :cols].astype(F32)
        store(ff_out.at[m], target)
    loads[5].wait()
    rms_out[0] = small_in[0:1, :rows]
    rms_out[1] = small_in[1:2, :rows]
    rms_out[2] = jnp.sqrt(small_in[2:3, :rows] / count)
    for i, target in enumerate((to_mix, to_ffn, to_rms)):
        store(rms_out.at[i], target)
    for copy in stores:
        copy.wait()


def outputs(ff, at, tok, small, ffn_cols, count):
    rows, half = tok.shape
    shape = jax.ShapeDtypeStruct
    shapes = [
        (rows, half), (2 * HEADROWS, rows), (CONV, 2 * HDIM), (2 * HDIM, rows),
        (rows, ffn_cols), (rows, ffn_cols), (rows, ffn_cols), (1, rows), (1, rows), (1, rows),
    ]
    vmem = pltpu.VMEM
    return pl.pallas_call(
        functools.partial(outputs_kernel, count),
        out_shape=[shape(s, F32) for s in shapes],
        in_specs=[ANY] * 4,
        out_specs=[ANY] * 10,
        scratch_shapes=[
            vmem(ff.shape, BF16), vmem(at.shape, BF16), vmem(tok.shape, BF16),
            vmem(small.shape, F32), vmem(shapes[0], F32), vmem(shapes[1], F32),
            vmem(shapes[2], F32), vmem(shapes[3], F32), vmem((3,) + shapes[4], F32),
            vmem((3,) + shapes[7], F32), dma(24),
        ],
        compiler_params=pltpu.CompilerParams(vmem_limit_bytes=60 * 2**20),
        name="outputs",
    )(ff, at, tok, small)


def on_device_full(
    tokens, cotangent, w_qkv, conv_weight, w_out, w_gate, w_up, w_down, gain_mix, gain_ffn
):
    rows, half = tokens.shape
    ffn_cols = w_gate.shape[1]
    out_ff, out_at, out_res, out_tok, small = run_layer(
        w_gate, w_up, w_down, w_qkv.T, w_out, conv_weight, gain_mix, gain_ffn,
        tokens, cotangent,
    )[:5]
    grads = outputs(out_ff, out_at, out_tok, small, ffn_cols, 8 * half * 4 * rows)
    to_tok, to_qkv, to_conv, to_out, to_gate, to_up, to_down, to_mix, to_ffn, to_rms = grads
    return (
        out_res, to_tok, to_qkv.T, to_conv, to_out, to_gate, to_up, to_down,
        to_mix[0], to_ffn[0], to_rms[0, :3],
    )


def on_device(tokens, cotangent, lengths, deal_order, *weights):
    total_rows = tokens.shape[1] * lax.axis_size("col")
    if (
        lengths.shape[0] * LONGEST == total_rows
        and lax.axis_size("row") == 4
        and lax.axis_size("col") == 8
        and total_rows == 4 * LONGEST
        and weights[0].shape[1] == 2 * HEADROWS
        and 4 * TILE < weights[3].shape[1] <= 5 * TILE
    ):
        return on_device_full(tokens, cotangent, *weights)
    return on_device_general(tokens, cotangent, lengths, deal_order, *weights)


def solution(mesh):
    in_specs = (
        P("row", "col"),
        P("row", "col"),
        P(),
        P(),
        P("row", "col"),
        P(None, "col"),
        P("col", "row"),
        P("row", "col"),
        P("row", "col"),
        P("row", "col"),
        P("row"),
        P("row"),
    )
    out_specs = (
        P("row", "col"),
        P("row", "col"),
        P("row", "col"),
        P(None, "col"),
        P("col", "row"),
        P("row", "col"),
        P("row", "col"),
        P("row", "col"),
        P("row"),
        P("row"),
        P(),
    )
    return jax.shard_map(
        on_device, mesh=mesh, in_specs=in_specs, out_specs=out_specs, check_vma=False
    )
```

```python
import functools

import jax
import jax.numpy as jnp
from jax import lax
from jax.experimental import pallas as pl
from jax.experimental.pallas import tpu as pltpu
from jax.sharding import PartitionSpec as P

D = 1792
FEAT = 16
CONV = 3
LONGEST = 1024
HDIM = 112


EPSILON = 1e-06


def dealing(lengths, deal_order, total_rows):
    seq_ids = jnp.arange(lengths.shape[0], dtype=jnp.int32)
    chosen = (deal_order[:, None] == seq_ids[None, :]).astype(jnp.int32)
    dealt_lengths = jnp.sum(chosen * lengths[None, :], 1)
    given_start = jnp.cumsum(lengths) - lengths
    dealt_start = jnp.cumsum(dealt_lengths) - dealt_lengths
    given_of_dealt = jnp.sum(chosen * given_start[None, :], 1)
    dealt_of_given = jnp.sum(chosen * dealt_start[:, None], 0)
    places = jnp.arange(total_rows, dtype=jnp.int32)
    in_dealt = (places[:, None] >= dealt_start[None, :]) & (
        places[:, None] < (dealt_start + dealt_lengths)[None, :]
    )
    in_given = (places[:, None] >= given_start[None, :]) & (
        places[:, None] < (given_start + lengths)[None, :]
    )
    source = places + jnp.sum(jnp.where(in_dealt, (given_of_dealt - dealt_start)[None, :], 0), 1)
    target = places + jnp.sum(jnp.where(in_given, (dealt_of_given - given_start)[None, :], 0), 1)
    offsets = places - jnp.sum(jnp.where(in_dealt, dealt_start[None, :], 0), 1)
    return (source, target, offsets)


def convolve(raw_values, kernel_conv, offsets):
    mixed = kernel_conv[0] * raw_values
    for delay_step in range(1, CONV):
        moved = jnp.concatenate(
            [jnp.zeros_like(raw_values[:delay_step]), raw_values[:-delay_step]], 0
        )
        mixed = mixed + kernel_conv[delay_step] * jnp.where(
            (offsets >= delay_step)[:, None, None], moved, 0.0
        )
    return mixed


def convolve_back(grad_mixed, raw_values, kernel_conv, offsets):
    grad_raw = kernel_conv[0] * grad_mixed
    sums_list = [jnp.sum(grad_mixed * raw_values, 0)]
    for delay_step in range(1, CONV):
        masked = jnp.where((offsets >= delay_step)[:, None, None], grad_mixed, 0.0)
        pulled = jnp.concatenate([masked[delay_step:], jnp.zeros_like(masked[:delay_step])], 0)
        grad_raw = grad_raw + kernel_conv[delay_step] * pulled
        moved = jnp.concatenate(
            [jnp.zeros_like(raw_values[:delay_step]), raw_values[:-delay_step]], 0
        )
        sums_list.append(jnp.sum(masked * moved, 0))
    return (grad_raw, jnp.stack(sums_list))


def bin_scores(query, keys, offsets):
    scores = jnp.einsum("thf,shf->hts", query, keys, preferred_element_type=jnp.float32) * FEAT ** (
        -0.5
    )
    positions = jnp.arange(query.shape[0], dtype=jnp.int32)
    visible = (positions[None, :] <= positions[:, None]) & (
        positions[:, None] - positions[None, :] <= offsets[:, None]
    )
    kernel = jnp.where(visible[None], 1.0 + scores + 0.5 * scores * scores, 0.0)
    return (scores, visible, kernel)


def attend_bin(pieces):
    query, keys, values, offsets = pieces
    scores, visible, kernel = bin_scores(query, keys, offsets)
    weights = (kernel / jnp.sum(kernel, -1, keepdims=True)).astype(jnp.bfloat16)
    return jnp.einsum("hts,shd->thd", weights, values, preferred_element_type=jnp.float32)


def attend_back(pieces):
    query, keys, values, offsets, grad_attend = pieces
    scores, visible, kernel = bin_scores(query, keys, offsets)
    totals = jnp.sum(kernel, -1, keepdims=True)
    weights = kernel / totals
    grad_weights = jnp.einsum(
        "thd,shd->hts", grad_attend, values, preferred_element_type=jnp.float32
    )
    grad_values = jnp.einsum(
        "hts,thd->shd",
        weights.astype(jnp.bfloat16),
        grad_attend,
        preferred_element_type=jnp.float32,
    )
    grad_kernel = (grad_weights - jnp.sum(grad_weights * weights, -1, keepdims=True)) / totals
    grad_scores = jnp.where(visible[None], grad_kernel * (1.0 + scores), 0.0).astype(jnp.bfloat16)
    grad_query = jnp.einsum(
        "hts,shf->thf", grad_scores, keys, preferred_element_type=jnp.float32
    ) * FEAT ** (-0.5)
    grad_keys = jnp.einsum(
        "hts,thf->shf", grad_scores, query, preferred_element_type=jnp.float32
    ) * FEAT ** (-0.5)
    return (grad_query, grad_keys, grad_values)


def times_transposed(left, right):
    return lax.dot_general(
        left, right, (((1,), (1,)), ((), ())), preferred_element_type=jnp.float32
    )


def tokens_product(left, right):
    return lax.dot_general(
        left, right, (((0,), (0,)), ((), ())), preferred_element_type=jnp.float32
    )


def plain_product(left, right):
    return jnp.dot(left, right, preferred_element_type=jnp.float32)


def gather_cols(values):
    return lax.all_gather(values, "col", axis=0, tiled=True)


def gather_rows(values):
    return lax.all_gather(values, "row", axis=0, tiled=True)


def grad_gather_cols(values):
    return lax.all_gather(values, "col", axis=1, tiled=True)


def grad_gather_rows(values):
    return lax.all_gather(values, "row", axis=0, tiled=True)


def width_total(values):
    return lax.psum(values, "row")


def forward_rows(gathered, row_index, weight, rows_here):

    def partial_term(row_start, row_count):
        picked = jnp.take(gathered, row_index, axis=0)
        return jnp.dot(picked, weight, preferred_element_type=jnp.float32)

    return lax.psum_scatter(
        partial_term(jnp.int32(0), rows_here * lax.axis_size("row")),
        "row",
        scatter_dimension=0,
        tiled=True,
    )


def forward_cols(gathered, row_index, weight, rows_here, product):

    def partial_term(row_start, row_count):
        picked = jnp.take(gathered, row_index, axis=0)
        return product(picked, weight)

    return lax.psum_scatter(
        partial_term(jnp.int32(0), lax.axis_size("col") * rows_here).astype(jnp.bfloat16),
        "col",
        scatter_dimension=0,
        tiled=True,
    ).astype(jnp.float32)


def backward_rows(gathered, row_index, weight, rows_here, contract):

    def partial_term(row_start, row_count):
        picked = jnp.take(gathered, row_index, axis=1)
        return lax.dot_general(
            picked, weight, (((0,), (contract,)), ((), ())), preferred_element_type=jnp.float32
        )

    return lax.psum_scatter(
        partial_term(jnp.int32(0), lax.axis_size("row") * rows_here).astype(jnp.bfloat16),
        "row",
        scatter_dimension=0,
        tiled=True,
    ).astype(jnp.float32)


def backward_cols(gathered, row_index, weight, rows_here):

    def partial_term(row_start, row_count):
        picked = jnp.take(gathered, row_index, axis=0)
        return times_transposed(picked, weight)

    return lax.psum_scatter(
        partial_term(jnp.int32(0), lax.axis_size("col") * rows_here).astype(jnp.bfloat16),
        "col",
        scatter_dimension=0,
        tiled=True,
    ).astype(jnp.float32)


def norm_forward(values, norm_gain):
    totals = width_total(jnp.sum(values * values, -1))
    inverse = lax.rsqrt(totals / D + EPSILON)
    return (values * inverse[:, None] * norm_gain, inverse)


def norm_back(values, inverse, norm_gain, grad_normed, dot_sums):
    cubed = inverse * inverse * inverse
    return grad_normed * norm_gain * inverse[:, None] - values * (cubed * dot_sums / D)[:, None]


def on_device_general(
    tokens,
    cotangent,
    lengths,
    deal_order,
    w_qkv,
    conv_weight,
    w_out,
    w_gate,
    w_up,
    w_down,
    gain_mix,
    gain_ffn,
):
    local_rows = tokens.shape[1]
    total_rows = local_rows * lax.axis_size("col")
    group_rows = total_rows // lax.axis_size("row")
    bin_count = group_rows // LONGEST
    heads_here = w_out.shape[0] // HDIM
    ffn_cols = w_gate.shape[1]
    source, target, offsets = dealing(lengths, deal_order, total_rows)
    group_offsets = lax.dynamic_slice_in_dim(
        offsets, lax.axis_index("row") * group_rows, group_rows
    )
    inputs = tokens.astype(jnp.float32).T
    gain_one = gain_mix.astype(jnp.float32)
    gain_two = gain_ffn.astype(jnp.float32)
    both_weights = jnp.concatenate([w_gate, w_up], 1)
    normed_one, inverse_one = norm_forward(inputs, gain_one)
    low_one = normed_one.astype(jnp.bfloat16)
    all_one = gather_cols(low_one)
    projected = forward_rows(all_one, source, w_qkv, group_rows)
    projected = projected.reshape(group_rows, heads_here, 2 * FEAT + HDIM)
    query = projected[:, :, :FEAT].astype(jnp.bfloat16)
    keys = projected[:, :, FEAT : 2 * FEAT].astype(jnp.bfloat16)
    raw_values = projected[:, :, 2 * FEAT :]
    kernel_conv = conv_weight.astype(jnp.float32).reshape(CONV, heads_here, HDIM)
    values = convolve(raw_values, kernel_conv, group_offsets).astype(jnp.bfloat16)
    binned = (
        query.reshape(bin_count, LONGEST, heads_here, FEAT),
        keys.reshape(bin_count, LONGEST, heads_here, FEAT),
        values.reshape(bin_count, LONGEST, heads_here, HDIM),
        group_offsets.reshape(bin_count, LONGEST),
    )
    attended = (
        lax.map(attend_bin, binned).reshape(group_rows, heads_here * HDIM).astype(jnp.bfloat16)
    )
    all_attended = gather_rows(attended)
    branch_mix = forward_cols(all_attended, target, w_out, local_rows, plain_product)
    middle = inputs + branch_mix
    normed_two, inverse_two = norm_forward(middle, gain_two)
    low_two = normed_two.astype(jnp.bfloat16)
    all_two = gather_cols(low_two)
    gate_up = forward_rows(all_two, source, both_weights, group_rows)
    gate = gate_up[:, :ffn_cols]
    up_proj = gate_up[:, ffn_cols:]
    activated = jax.nn.silu(gate)
    hidden = (activated * up_proj).astype(jnp.bfloat16)
    all_hidden = gather_rows(hidden)
    branch_ffn = forward_cols(all_hidden, target, w_down, local_rows, times_transposed)
    result_full = middle + branch_ffn
    grad_result = cotangent.astype(jnp.float32).T
    all_grad_ffn = grad_gather_cols(cotangent)
    hidden_again = gather_rows(hidden)
    grad_down = jnp.dot(
        jnp.take(all_grad_ffn, source, axis=1), hidden_again, preferred_element_type=jnp.float32
    )
    grad_hidden = backward_rows(all_grad_ffn, source, w_down, group_rows, 0)
    gate_sigmoid = jax.nn.sigmoid(gate)
    grad_gate_part = grad_hidden * up_proj * gate_sigmoid * (1.0 + gate * (1.0 - gate_sigmoid))
    grad_up_part = grad_hidden * activated
    grad_gate_up = jnp.concatenate([grad_gate_part, grad_up_part], 1).astype(jnp.bfloat16)
    all_grad_gate_up = grad_gather_rows(grad_gate_up)
    two_again = gather_cols(low_two)
    grad_both = tokens_product(jnp.take(two_again, source, axis=0), all_grad_gate_up)
    grad_normed_two = backward_cols(all_grad_gate_up, target, both_weights, local_rows)
    dots_two = width_total(jnp.sum(grad_normed_two * gain_two * middle, -1))
    grad_middle = grad_result + norm_back(middle, inverse_two, gain_two, grad_normed_two, dots_two)
    gain_part_two = jnp.sum(grad_normed_two * middle * inverse_two[:, None], 0)
    low_grad_middle = grad_middle.T.astype(jnp.bfloat16)
    all_grad_middle = grad_gather_cols(low_grad_middle)
    attended_again = gather_rows(attended)
    grad_out = lax.dot_general(
        attended_again,
        jnp.take(all_grad_middle, source, axis=1),
        (((0,), (1,)), ((), ())),
        preferred_element_type=jnp.float32,
    )
    grad_attended = backward_rows(all_grad_middle, source, w_out, group_rows, 1).astype(
        jnp.bfloat16
    )
    binned_back = binned + (grad_attended.reshape(bin_count, LONGEST, heads_here, HDIM),)
    grad_query, grad_keys, grad_values = lax.map(attend_back, binned_back)
    grad_values = grad_values.reshape(group_rows, heads_here, HDIM)
    grad_raw, conv_part = convolve_back(grad_values, raw_values, kernel_conv, group_offsets)
    grad_projected = jnp.concatenate(
        [
            grad_query.reshape(group_rows, heads_here, FEAT),
            grad_keys.reshape(group_rows, heads_here, FEAT),
            grad_raw,
        ],
        2,
    )
    grad_projected = grad_projected.reshape(group_rows, heads_here * (2 * FEAT + HDIM)).astype(
        jnp.bfloat16
    )
    all_grad_projected = grad_gather_rows(grad_projected)
    one_again = gather_cols(low_one)
    grad_qkv = tokens_product(jnp.take(one_again, source, axis=0), all_grad_projected)
    grad_normed_one = backward_cols(all_grad_projected, target, w_qkv, local_rows)
    squares = jnp.stack(
        [
            jnp.sum(branch_mix * branch_mix),
            jnp.sum(branch_ffn * branch_ffn),
            jnp.sum(result_full * result_full),
        ]
    )
    dots_one, grad_conv, squares_rows = width_total(
        (
            jnp.sum(grad_normed_one * gain_one * inputs, -1),
            conv_part.reshape(CONV, heads_here * HDIM),
            squares,
        )
    )
    grad_tokens = grad_middle + norm_back(inputs, inverse_one, gain_one, grad_normed_one, dots_one)
    gain_part_one = jnp.sum(grad_normed_one * inputs * inverse_one[:, None], 0)
    grad_gain_mix, grad_gain_ffn, squares_all = lax.psum(
        (gain_part_one, gain_part_two, squares_rows), "col"
    )
    rms_values = jnp.sqrt(squares_all / (total_rows * D))
    return (
        result_full.T.astype(jnp.bfloat16),
        grad_tokens.T,
        grad_qkv,
        grad_conv,
        grad_out,
        grad_both[:, :ffn_cols],
        grad_both[:, ffn_cols:],
        grad_down,
        grad_gain_mix,
        grad_gain_ffn,
        rms_values,
    )


HEADROWS = 2 * FEAT + HDIM
BLOCKROWS = HEADROWS + HDIM
TILE = 128
WIDE = 512
SPAN = 256
MARKS = 292
MESH = pl.DeviceIdType.MESH
ANY = pl.BlockSpec(memory_space=pl.ANY)
F32, BF16 = jnp.float32, jnp.bfloat16


def place():
    column = lax.axis_index("col")
    return lax.axis_index("row"), column // 2, column % 2


def device(chip, plane, core):
    return (chip, plane * 2 + core)


def other_chips(chip):
    y, x = chip // 2, chip % 2
    return (y * 2 + 1 - x, (1 - y) * 2 + x, (1 - y) * 2 + 1 - x)


def away(plane, step):
    if step == 1:
        return plane + 1 - 2 * (plane % 2)
    if step == 2:
        return (plane + 2) % 4
    return 3 - plane


def is_inner(plane):
    return ((plane + 1) // 2) % 2 == 1


def remote(source, target, send, receive, to):
    return pltpu.make_async_remote_copy(
        src_ref=source,
        dst_ref=target,
        send_sem=send,
        recv_sem=receive,
        device_id=to,
        device_id_type=MESH,
    )


def lanes(start, size=TILE):
    return pl.ds(pl.multiple_of(start, TILE), size)


def rows_at(start, size, step):
    return pl.ds(pl.multiple_of(start, step), size)


def no(flag):
    return jnp.logical_not(flag)


def dot(a, b, over_a, over_b):
    return lax.dot_general(
        a, b, (((over_a,), (over_b,)), ((), ())), preferred_element_type=F32
    )


class Marks:
    def __init__(self, ref):
        self.ref, self.used = ref, 0

    def one(self):
        self.used += 1
        return self.ref.at[self.used - 1]

    def many(self, count):
        base = self.used
        self.used += count
        return lambda i: self.ref.at[base + i]


class Spread:
    def __init__(self, ref, owner, chip, plane, core, marks):
        self.ref, self.spot = ref, (chip, plane, core)
        self.sends = marks.many(3)
        self.arrived = marks.one()
        inner = is_inner(plane)
        self.mine = plane == owner
        self.outer_owner = self.mine & no(inner)
        self.inner_owner = self.mine & inner
        far = (plane == away(owner, 2)) | ((plane == away(owner, 3)) & is_inner(owner))
        self.relays = inner & far

    def copy(self, step, send):
        chip, plane, core = self.spot
        return remote(
            self.ref, self.ref, self.sends(send), self.arrived,
            device(chip, away(plane, step), core),
        )

    def start(self):
        pl.when(self.outer_owner)(lambda: self.copy(2, 1).start())
        pl.when(self.inner_owner)(lambda: self.copy(3, 1).start())
        pl.when(self.mine)(lambda: self.copy(1, 0).start())

    def relay(self):
        @pl.when(self.relays)
        def _():
            self.copy(1, 2).wait_recv()
            self.copy(1, 2).start()

    def arrive(self):
        pl.when(no(self.mine | self.relays))(lambda: self.copy(1, 2).wait_recv())

    def finish(self):
        @pl.when(self.mine)
        def _():
            self.copy(1, 0).wait_send()
            self.copy(1, 1).wait_send()

        pl.when(self.relays)(lambda: self.copy(1, 2).wait_send())


class Chain:
    def __init__(self, ref, owner, chip, plane, core, marks):
        self.ref, self.spot = ref, (chip, plane, core)
        self.sends = marks.many(2)
        self.arrived = marks.one()
        inner = is_inner(plane)
        self.mine = plane == owner
        self.mine_inner, self.mine_outer = self.mine & inner, self.mine & no(inner)
        self.from_end = inner & (plane == away(owner, 1))
        self.from_inner = inner & (plane == away(owner, 3))
        self.from_far = inner & (plane == away(owner, 2))
        self.waits = no(inner) & no(self.mine)

    def copy(self, step, send):
        chip, plane, core = self.spot
        return remote(
            self.ref, self.ref, self.sends(send), self.arrived,
            device(chip, away(plane, step), core),
        )

    def start(self):
        pl.when(self.mine_outer)(lambda: self.copy(1, 0).start())

    def start_inner(self):
        @pl.when(self.mine_inner)
        def _():
            self.copy(3, 1).start()
            self.copy(1, 0).start()

    def relay(self):
        pl.when(self.from_end | self.from_inner)(lambda: self.copy(1, 0).wait_recv())
        pl.when(self.from_end)(lambda: self.copy(3, 0).start())
        pl.when(self.from_inner)(lambda: self.copy(1, 0).start())

    def relay_far(self):
        @pl.when(self.from_far)
        def _():
            self.copy(1, 0).wait_recv()
            self.copy(1, 0).start()

    def arrive(self):
        pl.when(self.waits)(lambda: self.copy(1, 0).wait_recv())

    def finish(self):
        pl.when(no(self.waits))(lambda: self.copy(1, 0).wait_send())
        pl.when(self.mine_inner)(lambda: self.copy(3, 1).wait_send())


class MainTiles:
    def __init__(self, ff, chip, plane, core, marks):
        self.ff, self.spot = ff, (chip, plane, core)
        self.sends, self.here = marks.many(5), marks.many(3)
        self.inner = is_inner(plane)

    def copy(self, slot, to_step, send, receive):
        chip, plane, core = self.spot
        tiles = self.ff.at[:, :, lanes(slot * TILE)]
        return remote(
            tiles, tiles, self.sends(send), self.here(receive),
            device(chip, away(plane, to_step), core),
        )

    def got(self, step):
        self.copy(self.spot[1], 1, 0, step - 1).wait_recv()

    def start(self):
        plane = self.spot[1]
        self.copy(plane, 1, 0, 0).start()
        pl.when(self.inner)(lambda: self.copy(plane, 3, 2, 2).start())

    def relay(self):
        plane = self.spot[1]

        @pl.when(self.inner)
        def _():
            self.got(1)
            self.copy(away(plane, 1), 3, 1, 1).start()
            self.got(3)
            self.copy(away(plane, 3), 1, 3, 1).start()

    def relay_far(self):
        plane = self.spot[1]

        @pl.when(self.inner)
        def _():
            self.got(2)
            self.copy(away(plane, 2), 1, 4, 2).start()

    def arrive(self, step):
        pl.when(no(self.inner))(lambda: self.got(step))

    def finish(self):
        self.copy(self.spot[1], 1, 0, 0).wait_send()

        @pl.when(self.inner)
        def _():
            for send in range(1, 5):
                self.copy(self.spot[1], 1, send, 0).wait_send()


class MainGrads:
    def __init__(self, gout, slots, chip, plane, core, marks):
        self.gout, self.slots, self.spot = gout, slots, (chip, plane, core)
        self.sends, self.here = marks.many(3), marks.many(5)
        self.inner = is_inner(plane)

    def copy(self, slot, to_step, send, receive):
        chip, plane, core = self.spot
        return remote(
            self.gout.at[:, :, lanes(slot * TILE)], self.slots.at[receive],
            self.sends(send), self.here(receive), device(chip, away(plane, to_step), core),
        )

    def start(self, step):
        receive = {1: 0, 2: 4, 3: 3}[step]
        self.copy(away(self.spot[1], step), 1, step - 1, receive).start()

    def relay(self, step, add):
        @pl.when(self.inner)
        def _():
            receive = {2: 3, 3: 4}[step]
            self.copy(self.spot[1], 1, 0, receive).wait_recv()
            slot = away(self.spot[1], step)
            add(slot, self.slots.at[receive])
            self.copy(slot, step, step - 1, step - 1).start()

    def total(self, add):
        plane = self.spot[1]
        self.copy(plane, 1, 0, 0).wait_recv()
        add(plane, self.slots.at[0])

        @pl.when(no(self.inner))
        def _():
            self.copy(plane, 1, 0, 1).wait_recv()
            add(plane, self.slots.at[1])

        @pl.when(self.inner)
        def _():
            self.copy(plane, 1, 0, 2).wait_recv()
            add(plane, self.slots.at[2])

    def finish(self):
        for send in range(3):
            self.copy(self.spot[1], 1, send, 0).wait_send()


class Collect:
    def __init__(self, ref, slots, owner, chip, plane, core, marks):
        self.ref, self.slots, self.spot = ref, slots, (chip, plane, core)
        self.send = marks.one()
        self.arrived = marks.many(3)
        inner, inner_owner = is_inner(plane), is_inner(owner)
        self.mine = plane == owner
        self.mine_outer = self.mine & no(inner)
        self.mine_inner = self.mine & inner
        self.near = plane == away(owner, 1)
        second, third = plane == away(owner, 2), plane == away(owner, 3)
        self.hands = no(inner) & (second | third) & no(self.near)
        self.adds_second = inner & second & no(inner_owner)
        self.adds_third = inner & third & inner_owner

    def copy(self, step, slot):
        chip, plane, core = self.spot
        return remote(
            self.ref, self.slots.at[slot], self.send, self.arrived(slot),
            device(chip, away(plane, step), core),
        )

    def start(self):
        pl.when(self.near)(lambda: self.copy(1, 0).start())
        pl.when(self.hands)(lambda: self.copy(1, 2).start())

    def relay(self, add):
        @pl.when(self.adds_second | self.adds_third)
        def _():
            self.copy(1, 2).wait_recv()
            add(self.slots.at[2])

        pl.when(self.adds_second)(lambda: self.copy(2, 1).start())
        pl.when(self.adds_third)(lambda: self.copy(3, 1).start())

    def total(self, add):
        @pl.when(self.mine)
        def _():
            for slot in range(2):
                self.copy(1, slot).wait_recv()
                add(self.slots.at[slot])

    def finish(self):
        pl.when(no(self.mine))(lambda: self.copy(1, 0).wait_send())


def layer_kernel(
    w_gate, w_up, w_down, w_qkv, w_out, conv, gain_mix, gain_ffn, tok, cot,
    out_ff, out_at, out_res, out_tok, out_small, main_got, extra_got, att_got, tail_got,
    ff, at, xs, gs, low2, part, acc3, gout, gat, from_mate, both, got, turned, hid, gg,
    gn, gcol, raw, qs, ks, vs, att, gatt, gproj, mid, gmid, gsum, normed, sending, inv_all,
    inv_sum, small, small_a, small_b, raw_ff, raw_qkv, raw_out, raw_conv, tapped,
    gains, gain_rows, packed, packed_back, at_tail, gat_tail, sem, free_mate, free_chips,
):
    chip, plane, core = place()
    others = other_chips(chip)
    mate = device(chip, plane, 1 - core)
    marks = Marks(sem)
    rows = tok.shape[0]
    width = 4 * rows
    half = tok.shape[1]
    seq = 2 * half
    own_half = lanes(core * half, half)
    first = core * half + chip * TILE
    peers = [device(c, plane, core) for c in others]
    line = [device(chip, away(plane, step), core) for step in (1, 2, 3)]
    sides = [device(c, plane, 1 - core) for c in others]
    line_mates = [device(chip, away(plane, step), 1 - core) for step in (1, 2, 3)]

    barrier = pltpu.get_barrier_semaphore()
    partners = peers + [mate] + sides + line + line_mates
    for partner in partners:
        pl.semaphore_signal(barrier, inc=1, device_id=partner, device_id_type=MESH)

    def block_rows(c):
        return rows_at(c * rows, rows, rows)

    ffn_weights = (w_gate, w_up, w_down)
    ffn_cols = w_gate.shape[1]
    wat, last_tile = gat.at[:, 0], packed_back.at[:, 0:rows]
    early = marks.many(6)
    loads = [
        pltpu.make_async_copy(source, target, early(i))
        for i, (source, target) in enumerate(
            (
                (w_qkv, raw_qkv), (w_out, raw_out), (conv, raw_conv),
                (gain_mix, gain_rows[0]), (gain_ffn, gain_rows[1]),
            )
        )
    ]
    for load in loads:
        load.start()
    for load in loads:
        load.wait()
    for i in range(2):
        gains[i] = gain_rows[i][...].reshape(1, rows)
    tapped[...] = jnp.zeros(tapped.shape, F32)
    tapped[0:CONV, 0 : 2 * HDIM] = raw_conv[...].astype(F32)
    tap_rows = tapped[...].T
    tail = lax.broadcasted_iota(jnp.int32, (HDIM, TILE), 1)
    spare = rows % TILE
    for h in range(2):
        wat[h, :HEADROWS, :rows] = raw_qkv[h * HEADROWS : (h + 1) * HEADROWS]
        wat[h, HEADROWS:, :rows] = raw_out[h * HDIM : (h + 1) * HDIM]
        columns = wat[h, 2 * FEAT : HEADROWS, WIDE - TILE :].astype(F32)
        for j in range(CONV):
            column = tap_rows[h * HDIM : (h + 1) * HDIM, j : j + 1]
            columns = jnp.where(tail == spare + j, column, columns)
        wat[h, 2 * FEAT : HEADROWS, WIDE - TILE :] = columns.astype(BF16)
    pl.semaphore_wait(barrier, len(partners))

    far_core = plane // 2
    holds_att = core == far_core
    holds_extra = holds_att & (chip // 2 == plane % 2)
    extra_plane = 2 * core + chip // 2
    extra_chip = (plane % 2) * 2 + core
    out_rows, in_rows = pl.ds(HEADROWS, HDIM), pl.ds(0, HEADROWS)
    whole = rows // TILE * TILE
    lead = 16
    tail_in, tail_out = pl.ds(0, lead + HEADROWS), pl.ds(lead + HEADROWS, HDIM)

    def leftover(ref, p):
        pair = [ref[c * rows + whole : (c + 1) * rows] for c in (2 * p, 2 * p + 1)]
        return jnp.concatenate(pair, 0)

    def heads_times(h, start, size, right):
        tails = slice(lead + start, lead + start + size)
        total = dot(at_tail[h, 0, tails], leftover(right, 0), 1, 0)
        total += dot(at_tail[h, 1, tails], leftover(right, 1), 1, 0)
        for c in range(4):
            total += dot(
                at[h, c, start : start + size, :whole], right[c * rows : c * rows + whole], 1, 0
            )
        return total

    def heads_spread(start, size, left, where, target):
        tails = slice(lead + start, lead + start + size)

        @pl.loop(0, 4)
        def _(c):
            total = dot(at[0, c, start : start + size, :whole], left[0, :, where], 0, 0)
            total += dot(at[1, c, start : start + size, :whole], left[1, :, where], 0, 0)
            target[rows_at(c * rows, whole, 16), where] = total.astype(BF16)

        for p in range(2):
            total = dot(at_tail[0, p, tails], left[0, :, where], 0, 0)
            total += dot(at_tail[1, p, tails], left[1, :, where], 0, 0)
            for i, c in enumerate((2 * p, 2 * p + 1)):
                size_left = rows - whole
                target[c * rows + whole : (c + 1) * rows, where] = total[
                    i * size_left : (i + 1) * size_left
                ].astype(BF16)

    lane_at = lax.broadcasted_iota(jnp.int32, (1, TILE), 1)

    def pack_heads(start, size):
        a = plane % 2
        for p in range(2):
            even, odd = [
                at[a, 2 * p + i, start : start + size, whole:].astype(F32) for i in range(2)
            ]
            tile = jnp.where(lane_at < spare, even, pltpu.roll(odd, spare, 1))
            at_tail[a, p, lead + start : lead + start + size] = tile.astype(BF16)

    def pack_taps():
        a = plane % 2
        columns = at[a, 0, 2 * FEAT : HEADROWS, whole:].astype(F32).T
        at_tail[a, 0, 0:lead, 0:HDIM] = columns[spare : spare + lead].astype(BF16)

    def unpack_heads(start, size):
        a = plane % 2
        for p in range(2):
            tile = gat_tail[a, p, lead + start : lead + start + size].astype(F32)
            for i, half_tile in enumerate((tile, pltpu.roll(tile, spare, 1))):
                gat[a, 2 * p + i, start : start + size, whole:] = half_tile.astype(BF16)

    def unpack_taps():
        a = plane % 2
        columns = gat_tail[a, 0, 0:lead, 0:HDIM].astype(F32).T
        for c in range(4):
            tile = gat[a, c, 2 * FEAT : HEADROWS, whole:].astype(F32)
            for j in range(CONV):
                tile = jnp.where(tail == spare + j, columns[:, j : j + 1], tile)
            gat[a, c, 2 * FEAT : HEADROWS, whole:] = tile.astype(BF16)

    att_self = [(2 * core + h == chip) & holds_att for h in range(2)]

    class Heads:
        def __init__(self, span):
            self.span, self.local = span, marks.one()
            self.send, self.here = marks.many(2), marks.many(4)

        def copy(self, h):
            return remote(
                wat.at[h, self.span], at.at[plane % 2, chip, self.span], self.send(h),
                self.here(chip), device(2 * core + h, plane, far_core),
            )

        def keep(self, h):
            return pltpu.make_async_copy(
                wat.at[h, self.span], at.at[plane % 2, chip, self.span], self.local
            )

        def start(self):
            for h in range(2):
                pl.when(att_self[h])(lambda: self.keep(h).start())
                pl.when(no(att_self[h]))(lambda: self.copy(h).start())

        def arrive(self):
            for h in range(2):
                pl.when(att_self[h])(lambda: self.keep(h).wait())

            for c in range(4):

                @pl.when(holds_att & no((c == chip) & (core == chip // 2)))
                def _():
                    remote(
                        wat.at[0, self.span], at.at[plane % 2, c, self.span], self.send(0),
                        self.here(c), mate,
                    ).wait_recv()

        def finish(self):
            for h in range(2):
                pl.when(no(att_self[h]))(lambda: self.copy(h).wait_send())

    heads_in, heads_out = Heads(in_rows), Heads(out_rows)
    heads_in.start()
    heads_out.start()

    class Gather:
        def __init__(self, source, target_of, earlier=None):
            self.source, self.target_of = source, target_of
            self.marks = earlier.marks if earlier else [marks.many(6), marks.many(6)] + [
                marks.many(4), marks.many(4), marks.one()
            ]
            self.send, self.here, self.mate_send, self.mate_here, kept = self.marks
            self.keep = pltpu.make_async_copy(source, target_of(chip), kept)
            mine = self.halves(source)
            there = self.halves(target_of(chip))
            self.copies = {
                mark: remote(
                    mine[half], there[half], self.send(mark), self.here(mark), peers[p]
                )
                for mark, half, p in ((0, 0, 0), (3, 1, 1), (1, 1, 0), (2, 0, 1))
            }
            for copy in self.copies.values():
                copy.start()
            self.keep.start()
            self.crossing = []
            self.cross(source, chip, 3)

        def cross(self, source, c, mark):
            copy = remote(
                source, self.target_of(c), self.mate_send(mark), self.mate_here(mark), mate
            )
            copy.start()
            self.crossing.append(copy)

        def halves(self, block):
            size = block.shape[0] // 2
            return block.at[0:size], block.at[size : 2 * size]

        def pass_on(self):
            for mark, half, p, onward in ((0, 0, 0, 4), (3, 1, 1, 5)):
                self.copies[mark].wait_recv()
                block = self.halves(self.target_of(others[p]))[half]
                self.copies[onward] = remote(
                    block, block, self.send(onward), self.here(onward), peers[1 - p]
                )
                self.copies[onward].start()
            for mark, p in ((1, 0), (2, 1)):
                self.copies[mark].wait_recv()
                self.cross(self.target_of(others[p]), others[p], p)

        def arrive(self):
            for mark in (4, 5):
                self.copies[mark].wait_recv()
            self.cross(self.target_of(others[2]), others[2], 2)
            for copy in self.crossing:
                copy.wait_recv()
            self.keep.wait()

        def finish(self):
            for copy in list(self.copies.values()) + self.crossing:
                copy.wait_send()

    tokens_in = Gather(tok, lambda c: xs.at[block_rows(c), own_half])
    gain_send, gain_here = marks.many(3), marks.many(3)
    gain_copies = [
        remote(gains, gn.at[chip], gain_send(p), gain_here(p), peers[p]) for p in range(3)
    ]
    gain_keep = pltpu.make_async_copy(gains, gn.at[chip], marks.one())
    for copy in gain_copies + [gain_keep]:
        copy.start()

    in_line, out_line = [
        [
            Spread(ref, 2 * core + a, chip, plane, core, marks)
            for a in range(2)
            for ref in (at.at[a, :, span, 0:whole], at_tail.at[a, :, tail_span])
        ]
        for span, tail_span in ((in_rows, tail_in), (out_rows, tail_out))
    ]
    heads_in.arrive()

    @pl.when(holds_att)
    def _():
        pack_heads(0, HEADROWS)
        pack_taps()

    for item in in_line:
        item.start()
    heads_out.arrive()
    pl.when(holds_att)(lambda: pack_heads(HEADROWS, HDIM))
    for item in out_line:
        item.start()
    heads_in.finish()
    heads_out.finish()

    tokens_in.pass_on()
    main_send, main_here, main_local = marks.many(9), marks.many(9), marks.many(3)
    main_here_at = [ff.at[m, block_rows(chip), lanes(plane * TILE)] for m in range(3)]
    mains = [
        remote(
            ffn_weights[m].at[:, lanes(others[p] * TILE)], main_here_at[m],
            main_send(3 * p + m), main_here(3 * p + m), peers[p],
        )
        for p in range(3)
        for m in range(3)
    ]
    mains += [
        pltpu.make_async_copy(
            ffn_weights[m].at[:, lanes(chip * TILE)], main_here_at[m], main_local(m)
        )
        for m in range(3)
    ]
    for copy in mains:
        copy.start()

    short = ffn_cols - 4 * TILE
    for m in range(3):
        load = pltpu.make_async_copy(ffn_weights[m], raw_ff, early(5))
        load.start()
        load.wait()
        last_tile[m, :, 0:short] = raw_ff[:, 4 * TILE :]
        last_tile[m, :, short:] = jnp.zeros((rows, TILE - short), BF16)

    extra_send, extra_here, extra_local = marks.one(), marks.many(4), marks.one()
    extra_self = (extra_chip == chip) & holds_att
    last = lanes(4 * TILE)

    def extra_copy():
        return remote(
            last_tile, ff.at[:, block_rows(chip), last], extra_send, extra_here(chip),
            device(extra_chip, plane, far_core),
        )

    def extra_keep():
        return pltpu.make_async_copy(
            last_tile, ff.at[:, block_rows(chip), last], extra_local
        )

    @pl.when(extra_self)
    def _():
        extra_keep().start()

    @pl.when(no(extra_self))
    def _():
        extra_copy().start()

    for item in in_line:
        item.relay()
    tokens_in.arrive()
    cot_in = Gather(cot, lambda c: gs.at[block_rows(c), own_half])
    for copy in gain_copies + [gain_keep]:
        copy.wait()

    for item in out_line:
        item.relay()
    @pl.loop(0, 4)
    def _(c):
        pair = jnp.concatenate(
            [gn[c, 0].astype(F32), gn[c, 1].astype(F32), jnp.zeros((6, rows), F32)], 0
        )
        gcol[block_rows(c), 0:8] = pair.T.astype(BF16)

    step_rows = 64

    def add_squares(i, total):
        x = xs[rows_at(i * step_rows, step_rows, step_rows)].astype(F32)
        return total + jnp.sum((x * x).reshape(step_rows // 8, 8, seq), 0)

    squares = lax.fori_loop(0, width // step_rows, add_squares, jnp.zeros((8, seq), F32))
    inv_all[...] = lax.rsqrt(jnp.sum(squares, 0, keepdims=True) / D + EPSILON)
    tokens_in.finish()
    normed[...] = xs[:, lanes(first)]

    @pl.loop(0, width // step_rows)
    def _(i):
        at_rows = rows_at(i * step_rows, step_rows, step_rows)
        xs[at_rows] = (
            xs[at_rows].astype(F32) * inv_all[...] * gcol[at_rows, 0:1].astype(F32)
        ).astype(BF16)

    for item in in_line:
        item.arrive()

    position = lax.broadcasted_iota(jnp.int32, (1, seq), 1)

    def taps(h):
        columns = at_tail[h, 0, 0:lead, 0:HDIM].astype(F32).T
        return [columns[:, j : j + 1] for j in range(CONV)]

    @pl.loop(0, 2)
    def _(h):
        projected = heads_times(h, 0, HEADROWS, xs)
        qs[h] = (projected[:FEAT].astype(BF16).astype(F32) * FEAT**-0.5).astype(BF16)
        ks[h] = projected[FEAT : 2 * FEAT].astype(BF16)
        values = projected[2 * FEAT :]
        raw[h] = values
        tap = taps(h)
        mixed = tap[0] * values
        for j in range(1, CONV):
            moved = pltpu.roll(values, j, 1)
            mixed += tap[j] * jnp.where(position >= j, moved, 0.0)
        vs[h] = mixed.astype(BF16)

    def kernel_of(h, b):
        seen = (b + 1) * SPAN
        scores = dot(ks[h, :, :seen], qs[h, :, b * SPAN : seen], 0, 0)
        kernel = 1.0 + scores + 0.5 * scores * scores
        key_at = lax.broadcasted_iota(jnp.int32, (seen, SPAN), 0)
        query_at = lax.broadcasted_iota(jnp.int32, (seen, SPAN), 1) + b * SPAN
        visible = key_at <= query_at
        return scores, jnp.where(visible, kernel, 0.0), visible

    @pl.loop(0, 2)
    def _(h):
        for b in range(seq // SPAN):
            seen = (b + 1) * SPAN
            _, kernel, _ = kernel_of(h, b)
            inverse = 1.0 / jnp.sum(kernel, 0, keepdims=True)
            inv_sum[h, :, b * SPAN : seen] = inverse
            weights = (kernel * inverse).astype(BF16)
            att[h, :, b * SPAN : seen] = dot(vs[h, :, :seen], weights, 1, 0).astype(BF16)

    for copy in mains:
        copy.wait()
    main_line = MainTiles(ff, chip, plane, core, marks)
    main_line.start()

    @pl.when(extra_self)
    def _():
        extra_keep().wait()

    @pl.when(no(extra_self))
    def _():
        extra_copy().wait_send()

    for c in range(4):

        @pl.when(holds_extra & no((c == chip) & (core == chip % 2)))
        def _():
            remote(
                last_tile, ff.at[:, block_rows(c), last], extra_send, extra_here(c), mate
            ).wait_recv()

    third = short // 3
    unit_at = lax.broadcasted_iota(jnp.int32, (rows, TILE), 1)

    def pack(source, target):
        @pl.loop(0, 3)
        def _(m):
            fourth = source[m, 3 * rows :, last].astype(F32)
            for b in range(3):
                own = source[m, b * rows : (b + 1) * rows, last].astype(F32)
                moved = pltpu.roll(fourth, (short - b * third) % TILE, 1)
                target[m, b * rows : (b + 1) * rows] = jnp.where(
                    unit_at < short, own, moved
                ).astype(BF16)

    def unpack(source, target):
        @pl.loop(0, 3)
        def _(m):
            fourth = jnp.zeros((rows, TILE), F32)
            for b in range(3):
                block = source[m, b * rows : (b + 1) * rows].astype(F32)
                target[m, b * rows : (b + 1) * rows, last] = jnp.where(
                    unit_at < short, block, 0.0
                ).astype(BF16)
                moved = pltpu.roll(block, (b * third - short) % TILE, 1)
                here = (unit_at >= b * third) & (unit_at < (b + 1) * third)
                fourth = jnp.where(here, moved, fourth)
            target[m, 3 * rows :, last] = fourth.astype(BF16)

    pl.when(holds_extra)(lambda: pack(ff, packed))
    extra_line = Chain(packed, extra_plane, chip, plane, core, marks)
    extra_line.start()

    for item in out_line:
        item.arrive()

    def default_got(i):
        return got.at[i]

    class Sum:
        def __init__(
            self, guard, earlier=None, both=both, got=None, share=True, at_once=True
        ):
            self.marks = earlier.marks if earlier else [marks.many(4), marks.many(4)] + [
                marks.many(6), marks.many(6)
            ]
            self.guard, self.both, self.share, self.at_once = guard, both, share, at_once
            self.got = got or default_got

        def begin(self, fill):
            fill((1 - core) * half)
            send, here = self.marks[:2]
            self.order = (others[2], others[0], others[1], chip)
            self.to_mate = [
                remote(
                    part.at[:, lanes((1 - core) * half + c * TILE)],
                    from_mate.at[:, lanes(c * TILE)], send(i), here(i), mate,
                )
                for i, c in enumerate(self.order)
            ]
            if self.guard:
                pl.semaphore_wait(free_mate, 1)
            for copy in self.to_mate:
                copy.start()
            fill(core * half)

        def combine(self):
            self.prepare()
            for i, c in enumerate(self.order):
                self.to_mate[i].wait_recv()
                where, own = lanes(c * TILE), lanes(core * half + c * TILE)

                @pl.loop(0, 4)
                def _(b):
                    at_rows = block_rows(b)
                    self.both[at_rows, where] = (
                        part[at_rows, own].astype(F32) + from_mate[at_rows, where].astype(F32)
                    ).astype(BF16)

                if self.at_once:
                    self.send(i)
            pl.semaphore_signal(free_mate, inc=1, device_id=mate, device_id_type=MESH)
            for copy in self.to_mate:
                copy.wait_send()

        def piece(self, upper, c):
            size = width // 2
            return self.both.at[pl.ds(0 if upper else size, size), lanes(c * TILE)]

        def prepare(self):
            size = width // 2
            top, bottom = pl.ds(0, size), pl.ds(size, size)
            send, here = self.marks[2:]
            x, y, across = others
            self.across = [
                remote(self.piece(True, across), self.got(2).at[top], send(0), here(0), peers[0]),
                remote(
                    self.piece(False, across), self.got(2).at[bottom], send(1), here(1), peers[1]
                ),
            ]
            self.plain = [
                remote(self.piece(True, x), self.got(0).at[top], send(2), here(2), peers[0]),
                remote(self.piece(False, y), self.got(1).at[bottom], send(3), here(3), peers[1]),
            ]
            self.added = [
                remote(self.piece(True, y), self.got(1).at[top], send(4), here(4), peers[1]),
                remote(self.piece(False, x), self.got(0).at[bottom], send(5), here(5), peers[0]),
            ]

        def send(self, i):
            if i == 0:
                if self.guard and self.share:
                    pl.semaphore_wait(free_chips, 2)
                for copy in self.across:
                    copy.start()
            elif i < 3:
                self.plain[i - 1].start()

        def send_all(self):
            for i in range(3):
                self.send(i)

        def pass_on(self):
            size = width // 2
            quarter = size // 2
            for i, c in ((0, others[1]), (1, others[0])):
                self.across[i].wait_recv()
                for q in range(2):
                    at_rows = pl.ds(i * size + q * quarter, quarter)
                    self.both[at_rows, lanes(c * TILE)] = (
                        self.both[at_rows, lanes(c * TILE)].astype(F32) + self.got(2)[at_rows].astype(F32)
                    ).astype(BF16)
                self.added[i].start()

        def finish(self, store):
            for copy in self.plain + self.added:
                copy.wait()
            for copy in self.across:
                copy.wait_send()

            @pl.loop(0, 4)
            def _(c):
                at_rows = block_rows(c)
                total = self.both[at_rows, lanes(chip * TILE)].astype(F32)
                for p in range(2):
                    total += self.got(p)[at_rows].astype(F32)
                store(at_rows, total)

            for p in range(2 if self.share else 0):
                pl.semaphore_signal(free_chips, inc=1, device_id=peers[p], device_id_type=MESH)

    def fill_branch(start):
        heads_spread(HEADROWS, HDIM, att, lanes(start, half), part)

    small[...] = jnp.zeros(small.shape, F32)
    square_at = lax.broadcasted_iota(jnp.int32, (1, WIDE), 1)

    def note_square(index, value):
        total = jnp.sum(value * value)
        small[0, 2:3, :] += jnp.where(square_at == index, total, 0.0)

    def store_branch(at_rows, total):
        note_square(0, total)
        mid[at_rows] = normed[at_rows].astype(F32) + total

    branch_sum = Sum(guard=False)
    branch_sum.begin(fill_branch)
    cot_in.pass_on()
    cot_in.arrive()
    branch_sum.combine()
    branch_sum.pass_on()
    main_line.relay()
    extra_line.start_inner()
    branch_sum.finish(store_branch)
    middle = mid[...]
    inverse_two = lax.rsqrt(jnp.sum(middle * middle, 0, keepdims=True) / D + EPSILON)

    @pl.loop(0, 4)
    def _(c):
        at_rows = block_rows(c)
        sending[0, at_rows] = (mid[at_rows] * inverse_two * gcol[at_rows, 1:2].astype(F32)).astype(BF16)

    def token_block(c):
        return low2.at[:, lanes(core * half + c * TILE)]

    low_in = Gather(sending.at[0], token_block, tokens_in)
    cot_in.finish()

    @pl.loop(0, 4)
    def _(c):
        acc3[block_rows(c)] = jnp.zeros((rows, seq), F32)

    low_in.pass_on()
    low_in.arrive()
    low_in.finish()

    main_line.relay_far()
    extra_line.relay()
    def feed(slot):
        where = lanes(slot * TILE)
        unit_rows = rows_at(slot * TILE, TILE, TILE)
        for m in range(3):
            turned[m * TILE : (m + 1) * TILE] = ff[m, :, where].T

        @pl.loop(0, seq // SPAN)
        def _(n):
            span = lanes(n * SPAN, SPAN)
            gate_up = dot(turned[: 2 * TILE], low2[:, span], 1, 0)
            grad_hidden = dot(turned[2 * TILE :], gs[:, span], 1, 0)
            gate, up = gate_up[:TILE], gate_up[TILE:]
            sigmoid = 1.0 / (1.0 + jnp.exp(-gate))
            activated = gate * sigmoid
            hid[unit_rows, span] = (activated * up).astype(BF16)
            gg[:TILE, span] = (
                grad_hidden * up * sigmoid * (1.0 + gate * (1.0 - sigmoid))
            ).astype(BF16)
            gg[TILE:, span] = (grad_hidden * activated).astype(BF16)

        @pl.loop(0, 4)
        def _(c):
            at_rows = block_rows(c)
            pair = jnp.concatenate([ff[0, at_rows, where], ff[1, at_rows, where]], 1)
            acc3[at_rows] += dot(pair, gg[...], 1, 0)
            grads = dot(low2[at_rows], gg[...], 1, 1).astype(BF16)
            gout[0, at_rows, where] = grads[:, :TILE]
            gout[1, at_rows, where] = grads[:, TILE:]
            gout[2, at_rows, where] = dot(gs[at_rows], hid[unit_rows], 1, 1).astype(BF16)

    main_back = MainGrads(gout, main_got, chip, plane, core, marks)
    extra_back = Collect(packed_back, extra_got, extra_plane, chip, plane, core, marks)
    load_marks = marks.many(3)

    spare_lanes = [lanes((1 - core) * half + m * TILE) for m in range(3)]

    def add_tiles(slot, source):
        loads = [
            pltpu.make_async_copy(source.at[m], gs.at[:, spare_lanes[m]], load_marks(m))
            for m in range(3)
        ]
        for load in loads:
            load.start()
        for load in loads:
            load.wait()
        where = lanes(slot * TILE)

        @pl.loop(0, 4)
        def _(c):
            at_rows = block_rows(c)
            for m in range(3):
                gout[m, at_rows, where] = (
                    gout[m, at_rows, where].astype(F32)
                    + gs[at_rows, spare_lanes[m]].astype(F32)
                ).astype(BF16)

    def add_extra(source):
        packed_rows = slice(0, 3 * rows)
        loads = [
            pltpu.make_async_copy(source.at[m], gs.at[packed_rows, spare_lanes[m]], load_marks(m))
            for m in range(3)
        ]
        for load in loads:
            load.start()
        for load in loads:
            load.wait()

        @pl.loop(0, 3)
        def _(b):
            at_rows = block_rows(b)
            for m in range(3):
                packed_back[m, at_rows] = (
                    packed_back[m, at_rows].astype(F32)
                    + gs[at_rows, spare_lanes[m]].astype(F32)
                ).astype(BF16)

    slots = [away(plane, 1), plane, away(plane, 2), away(plane, 3), 4]
    inner = is_inner(plane)

    @pl.loop(0, 5)
    def _(turn):
        pl.when(turn == 2)(lambda: extra_line.relay_far())

        for i, step in ((0, 1), (2, 2), (3, 3)):

            @pl.when(turn == i)
            def _():
                main_line.arrive(step)

        @pl.when(turn == 4)
        def _():
            extra_line.arrive()
            unpack(packed, ff)

        slot = sum((turn == i).astype(jnp.int32) * slots[i] for i in range(5))
        feed(slot)

        for i, step in ((0, 1), (2, 2), (3, 3)):

            @pl.when((turn == i) & no(inner))
            def _():
                main_back.start(step)

    pl.when(inner)(lambda: main_back.start(1))

    pack(gout, packed_back)
    extra_back.start()
    main_line.finish()

    def fill_grad_two(start):
        @pl.loop(0, 4)
        def _(c):
            where = lanes(start, half)
            part[block_rows(c), where] = acc3[block_rows(c), where].astype(BF16)

    def store_gsum(at_rows, total):
        gsum[at_rows] = total

    two_sum = Sum(True, branch_sum)
    two_sum.begin(fill_grad_two)
    two_sum.combine()
    main_back.relay(3, add_tiles)
    two_sum.pass_on()

    def fill_ffn(start):
        @pl.loop(0, 4)
        def _(c):
            where = lanes(start, half)
            part[block_rows(c), where] = dot(
                ff[2, block_rows(c)], hid[:, where], 1, 0
            ).astype(BF16)

    ffn_sum = Sum(
        guard=True, both=ff.at[1, :, lanes(0, half)],
        got=lambda i: ff.at[0, :, lanes(i * TILE)], share=False,
        at_once=False,
    )
    ffn_sum.begin(fill_ffn)
    two_sum.finish(store_gsum)

    def norm_back(source, inverse, gain_lane, base, store):
        def add_dots(c, total):
            at_rows = block_rows(c)
            gain = gcol[at_rows, gain_lane : gain_lane + 1].astype(F32)
            return total + jnp.sum(gsum[at_rows] * gain * source(at_rows), 0, keepdims=True)

        dots = lax.fori_loop(0, 4, add_dots, jnp.zeros((1, TILE), F32))
        scaled = inverse * inverse * inverse * dots / D

        @pl.loop(0, 4)
        def _(c):
            at_rows = block_rows(c)
            gain = gcol[at_rows, gain_lane : gain_lane + 1].astype(F32)
            grad, value = gsum[at_rows], source(at_rows)
            store(at_rows, base(at_rows) + (grad * gain * inverse - value * scaled))

        def gain_back():
            @pl.loop(0, 4)
            def _(c):
                at_rows = block_rows(c)
                for_gain = jnp.sum((gsum[at_rows] * source(at_rows) * inverse).T, 0, keepdims=True)
                small[c, gain_lane : gain_lane + 1, 0:rows] = for_gain

        return gain_back

    def store_middle(at_rows, value):
        gmid[at_rows] = value
        sending[1, at_rows] = value.astype(BF16)

    gain_two_back = norm_back(
        lambda r: mid[r], inverse_two, 1, lambda r: gs[r, lanes(first)].astype(F32), store_middle
    )
    mid_in = Gather(sending.at[1], token_block, tokens_in)
    gain_two_back()
    ffn_sum.combine()
    mid_in.pass_on()
    ffn_sum.send_all()
    mid_in.arrive()

    @pl.loop(0, 2)
    def _(h):
        total = heads_times(h, HEADROWS, HDIM, low2)
        gatt[h] = total.astype(BF16)

    main_back.relay(2, add_tiles)

    out_back, in_back = [
        [
            Collect(ref, slots_, 2 * core + a, chip, plane, core, marks)
            for a in range(2)
            for ref, slots_ in (
                (gat.at[a, :, span, 0:whole], att_got.at[a, :, :, span]),
                (gat_tail.at[a, :, tail_span], tail_got.at[a, :, :, tail_span]),
            )
        ]
        for span, tail_span in ((out_rows, tail_out), (in_rows, tail_in))
    ]

    def head_grads(left, right, start, size):
        @pl.loop(0, 2)
        def _(h):
            for c in range(4):
                gat[h, c, start : start + size, :whole] = dot(
                    left[h], right[c * rows : c * rows + whole], 1, 1
                ).astype(BF16)
            for p in range(2):
                gat_tail[h, p, lead + start : lead + start + size] = dot(
                    left[h], leftover(right, p), 1, 1
                ).astype(BF16)

    head_grads(att, low2, HEADROWS, HDIM)
    for item in out_back:
        item.start()


    @pl.loop(0, 2)
    def _(h):
        grad_keys = jnp.zeros((FEAT, seq), F32)
        grad_values = jnp.zeros((HDIM, seq), F32)

        def padded(value):
            short = seq - value.shape[1]
            if not short:
                return value
            return jnp.concatenate([value, jnp.zeros((value.shape[0], short), F32)], 1)

        for b in range(seq // SPAN):
            seen = (b + 1) * SPAN
            span = slice(b * SPAN, seen)
            scores, kernel, visible = kernel_of(h, b)
            inverse = inv_sum[h, :, span]
            weights = kernel * inverse
            grad_weights = dot(vs[h, :, :seen], gatt[h, :, span], 0, 0)
            grad_values += padded(dot(gatt[h, :, span], weights.astype(BF16), 1, 1))
            dots = jnp.sum(grad_weights * weights, 0, keepdims=True)
            grad_kernel = (grad_weights - dots) * inverse
            grad_scores = jnp.where(visible, grad_kernel * (1.0 + scores), 0.0).astype(BF16)
            gproj[h, :FEAT, span] = (
                dot(ks[h, :, :seen], grad_scores, 1, 0) * FEAT**-0.5
            ).astype(BF16)
            grad_keys += padded(dot(qs[h, :, span], grad_scores, 1, 1))
        gproj[h, FEAT : 2 * FEAT] = grad_keys.astype(BF16)
        tap = taps(h)
        grad_raw = tap[0] * grad_values
        sums = [jnp.sum(grad_values * raw[h], 1, keepdims=True)]
        for j in range(1, CONV):
            masked = jnp.where(position >= j, grad_values, 0.0)
            grad_raw += tap[j] * pltpu.roll(masked, seq - j, 1)
            sums.append(jnp.sum(masked * pltpu.roll(raw[h], j, 1), 1, keepdims=True))
        gproj[h, 2 * FEAT :] = grad_raw.astype(BF16)
        columns = jnp.zeros((HDIM, TILE), F32)
        for j in range(CONV):
            columns = jnp.where(tail == j, sums[j], columns)
        gat_tail[h, 0, 0:lead, 0:HDIM] = columns.T[0:lead].astype(BF16)

    head_grads(gproj, xs, 0, HEADROWS)
    for item in in_back:
        item.start()

    ffn_sum.pass_on()
    mid_in.finish()

    def fill_grad_one(start):
        heads_spread(0, HEADROWS, gproj, lanes(start, half), part)

    one_sum = Sum(True, branch_sum)
    one_sum.begin(fill_grad_one)
    one_sum.combine()
    extra_back.relay(add_extra)

    def store_result(at_rows, total):
        note_square(1, total)
        total = mid[at_rows] + total
        note_square(2, total)
        sending[0, at_rows] = total.astype(BF16)

    one_sum.pass_on()

    def hand_out(source, target):
        send, here = marks.many(3), marks.many(3)
        copies = [
            remote(
                source.at[block_rows(others[p])], target.at[:, lanes(chip * TILE)],
                send(p), here(p), peers[p],
            )
            for p in range(3)
        ]
        copies.append(
            pltpu.make_async_copy(
                source.at[block_rows(chip)], target.at[:, lanes(chip * TILE)], marks.one()
            )
        )
        for copy in copies:
            copy.start()
        return copies

    ffn_sum.finish(store_result)
    pending = hand_out(sending.at[0], out_res)


    one_sum.finish(store_gsum)
    head_marks = marks.many(4)

    def add_head(i, start, size, tail_start, tail_size):
        a, is_tail = i // 2, i % 2
        target, count = (gat_tail, 2) if is_tail else (gat, 4)
        begin, extent = (tail_start, tail_size) if is_tail else (start, size)
        wide = TILE if is_tail else whole

        def add(source):
            loads = [
                pltpu.make_async_copy(
                    source.at[c], part.at[c * BLOCKROWS : c * BLOCKROWS + extent, 0:wide],
                    head_marks(c),
                )
                for c in range(count)
            ]
            for load in loads:
                load.start()
            for load in loads:
                load.wait()
            for c in range(count):
                target[a, c, begin : begin + extent, 0:wide] = (
                    target[a, c, begin : begin + extent, 0:wide].astype(F32)
                    + part[c * BLOCKROWS : c * BLOCKROWS + extent, 0:wide].astype(F32)
                ).astype(BF16)

        return add

    def add_out(i):
        return add_head(i, HEADROWS, HDIM, lead + HEADROWS, HDIM)

    def add_in(i):
        return add_head(i, 0, HEADROWS, 0, lead + HEADROWS)

    for i in range(4):
        out_back[i].relay(add_out(i))

    inverse_own = inv_all[:, lanes(first)]

    def store_tokens(at_rows, value):
        sending[1, at_rows] = value.astype(BF16)

    gain_one_back = norm_back(
        lambda r: normed[r].astype(F32), inverse_own, 0, lambda r: gmid[r], store_tokens
    )
    pending += hand_out(sending.at[1], out_tok)
    gain_one_back()

    for c in range(1, 4):
        small[c, 2:3] = small[0, 2:3]
    a_send, a_here = marks.many(3), marks.many(3)
    trio = [
        remote(small.at[others[p]], small_a.at[p], a_send(p), a_here(p), peers[p])
        for p in range(3)
    ]
    for copy in trio:
        copy.start()

    main_back.total(add_tiles)
    back_send, back_here = marks.many(3), marks.many(3)
    mine = lanes(plane * TILE)
    back_to = out_ff.at[:, :, lanes(chip * TILE)]
    backs = [
        remote(
            gout.at[:, block_rows(others[p]), mine], back_to, back_send(p), back_here(p), peers[p]
        )
        for p in range(3)
    ]
    backs.append(
        pltpu.make_async_copy(gout.at[:, block_rows(chip), mine], back_to, marks.one())
    )
    for copy in backs:
        copy.start()
    pending += backs

    extra_back.total(add_extra)
    pl.when(holds_extra)(lambda: unpack(packed_back, gout))
    last_send, last_here, last_local = marks.many(4), marks.one(), marks.one()

    def last_copy(c):
        return remote(
            gout.at[:, block_rows(c), last], out_ff.at[:, :, last], last_send(c), last_here,
            device(c, plane, chip % 2),
        )

    def last_keep():
        return pltpu.make_async_copy(
            gout.at[:, block_rows(chip), last], out_ff.at[:, :, last], last_local
        )

    for c in range(4):
        same = (c == chip) & (core == chip % 2)

        @pl.when(holds_extra & same)
        def _():
            last_keep().start()

        @pl.when(holds_extra & no(same))
        def _():
            last_copy(c).start()

    for i in range(4):
        in_back[i].relay(add_in(i))
    for copy in trio:
        copy.wait()
    small_b[0] = small[chip] + small_a[0] + small_a[1] + small_a[2]
    b_send, b_here = marks.many(7), marks.many(7)
    seven = [
        remote(small_b.at[0], small_b.at[1 + i], b_send(i), b_here(i), to)
        for i, to in enumerate(line + [mate] + line_mates)
    ]
    for copy in seven:
        copy.start()

    class HeadsBack:
        def __init__(self, span):
            self.span, self.local = span, marks.one()
            self.send, self.here = marks.many(4), marks.many(2)

        def same(self, c):
            return (c == chip) & (core == chip // 2)

        def copy(self, c):
            return remote(
                gat.at[plane % 2, c, self.span], out_at.at[chip % 2, self.span], self.send(c),
                self.here(chip % 2), device(c, plane, chip // 2),
            )

        def keep(self):
            return pltpu.make_async_copy(
                gat.at[plane % 2, chip, self.span], out_at.at[chip % 2, self.span], self.local
            )

        def start(self):
            for c in range(4):
                pl.when(holds_att & self.same(c))(lambda: self.keep().start())
                pl.when(holds_att & no(self.same(c)))(lambda: self.copy(c).start())

        def finish(self):
            for c in range(4):
                pl.when(holds_att & self.same(c))(lambda: self.keep().wait())
                pl.when(holds_att & no(self.same(c)))(lambda: self.copy(c).wait_send())

            for h in range(2):

                @pl.when(no(att_self[h]))
                def _():
                    remote(
                        gat.at[0, 0, self.span], out_at.at[h, self.span], self.send(0),
                        self.here(h), mate,
                    ).wait_recv()

    heads_back = [HeadsBack(out_rows), HeadsBack(in_rows)]
    for i in range(4):
        out_back[i].total(add_out(i))
    pl.when(holds_att)(lambda: unpack_heads(HEADROWS, HDIM))
    heads_back[0].start()
    for i in range(4):
        in_back[i].total(add_in(i))

    @pl.when(holds_att)
    def _():
        unpack_heads(0, HEADROWS)
        unpack_taps()

    heads_back[1].start()

    for copy in seven:
        copy.wait()
    total = small_b[0]
    for i in range(7):
        total += small_b[1 + i]
    small_a[0] = total
    small_out = pltpu.make_async_copy(small_a.at[0], out_small, marks.one())
    small_out.start()
    pending.append(small_out)
    for item in in_line + out_line + [extra_line, main_back, extra_back] + out_back + in_back:
        item.finish()
    for copy in pending:
        copy.wait()
    for c in range(4):
        same = (c == chip) & (core == chip % 2)
        pl.when(holds_extra & same)(lambda: last_keep().wait())
        pl.when(holds_extra & no(same))(lambda: last_copy(c).wait_send())

    @pl.when(no(extra_self))
    def _():
        last_copy(0).wait_recv()

    for item in heads_back:
        item.finish()

    pl.semaphore_wait(free_mate, 1)
    pl.semaphore_wait(free_chips, 2)
    assert marks.used <= MARKS, marks.used


def dma(*shape):
    return pltpu.SemaphoreType.DMA(shape)


def run_layer(w_gate, w_up, w_down, w_qkv, w_out, conv, gain_mix, gain_ffn, tok, cot):
    rows, half = tok.shape
    width, seq = 4 * rows, 2 * half
    shape = jax.ShapeDtypeStruct
    vmem = pltpu.VMEM
    tiles = (3, width, TILE)
    head = (4, BLOCKROWS, WIDE)
    return pl.pallas_call(
        layer_kernel,
        out_shape=[
            shape((3, rows, 5 * TILE), BF16),
            shape((2, BLOCKROWS, WIDE), BF16),
            shape((rows, half), BF16),
            shape((rows, half), BF16),
            shape((8, WIDE), F32),
            shape((5,) + tiles, BF16),
            shape((3, 3, 3 * rows, TILE), BF16),
            shape((2, 3, 4, BLOCKROWS, rows // TILE * TILE), BF16),
            shape((2, 3, 2, 16 + BLOCKROWS, TILE), BF16),
        ],
        in_specs=[ANY] * 10,
        out_specs=[ANY] * 9,
        scratch_shapes=[
            vmem((3, width, 5 * TILE), BF16),
            vmem((2,) + head, BF16),
            vmem((width, seq), BF16),
            vmem((width, seq), BF16),
            vmem((width, seq), BF16),
            vmem((width, seq), BF16),
            vmem((width, seq), F32),
            vmem((3, width, 5 * TILE), BF16),
            vmem((2,) + head, BF16),
            vmem((width, half), BF16),
            vmem((width, half), BF16),
            vmem((3, width, TILE), BF16),
            vmem((3 * TILE, width), BF16),
            vmem((5 * TILE, seq), BF16),
            vmem((2 * TILE, seq), BF16),
            vmem((4, 2, 1, rows), BF16),
            vmem((width, TILE), BF16),
            vmem((2, HDIM, seq), F32),
            vmem((2, FEAT, seq), BF16),
            vmem((2, FEAT, seq), BF16),
            vmem((2, HDIM, seq), BF16),
            vmem((2, HDIM, seq), BF16),
            vmem((2, HDIM, seq), BF16),
            vmem((2, HEADROWS, seq), BF16),
            vmem((width, TILE), F32),
            vmem((width, TILE), F32),
            vmem((width, TILE), F32),
            vmem((width, TILE), BF16),
            vmem((2, width, TILE), BF16),
            vmem((1, seq), F32),
            vmem((2, 1, seq), F32),
            vmem((4, 8, WIDE), F32),
            vmem((3, 8, WIDE), F32),
            vmem((8, 8, WIDE), F32),
            vmem(w_gate.shape, BF16),
            vmem(w_qkv.shape, BF16),
            vmem(w_out.shape, BF16),
            vmem(conv.shape, BF16),
            vmem((8, 2 * TILE), F32),
            vmem((2, 1, rows), BF16),
            [vmem((rows,), BF16)] * 2,
            vmem((3, 3 * rows, TILE), BF16),
            vmem((3, 3 * rows, TILE), BF16),
            vmem((2, 2, 16 + BLOCKROWS, TILE), BF16),
            vmem((2, 2, 16 + BLOCKROWS, TILE), BF16),
            dma(MARKS),
            pltpu.SemaphoreType.REGULAR,
            pltpu.SemaphoreType.REGULAR,
        ],
        compiler_params=pltpu.CompilerParams(
            collective_id=0, has_side_effects=True, vmem_limit_bytes=63 * 2**20
        ),
        name="layer",
    )(w_gate, w_up, w_down, w_qkv, w_out, conv, gain_mix, gain_ffn, tok, cot)


def outputs_kernel(
    count, ff, at, tok, small, to_tok, to_qkv, to_conv, to_out, to_gate, to_up, to_down,
    to_mix, to_ffn, to_rms, ff_in, at_in, tok_in, small_in, tok_out, qkv_out, conv_out, out_out,
    ff_out, rms_out, sem,
):
    rows, cols = to_gate.shape
    marks = Marks(sem)
    loads = [
        pltpu.make_async_copy(source, target, marks.one())
        for source, target in (
            [(tok, tok_in), (at, at_in)] + [(ff.at[m], ff_in.at[m]) for m in range(3)]
            + [(small, small_in)]
        )
    ]
    for load in loads:
        load.start()
    stores = []

    def store(source, target):
        stores.append(pltpu.make_async_copy(source, target, marks.one()))
        stores[-1].start()

    loads[0].wait()
    tok_out[...] = tok_in[...].astype(F32)
    store(tok_out, to_tok)
    loads[1].wait()
    for h in range(2):
        qkv_out[h * HEADROWS : (h + 1) * HEADROWS] = at_in[h, :HEADROWS, :rows].astype(F32)
        out_out[h * HDIM : (h + 1) * HDIM] = at_in[h, HEADROWS:, :rows].astype(F32)
    store(qkv_out, to_qkv)
    store(out_out, to_out)
    taps = jnp.concatenate(
        [at_in[h, 2 * FEAT : HEADROWS, WIDE - TILE :].astype(F32) for h in range(2)], 0
    )
    conv_out[...] = taps.T[rows % TILE : rows % TILE + CONV]
    store(conv_out, to_conv)
    for m, target in enumerate((to_gate, to_up, to_down)):
        loads[2 + m].wait()
        ff_out[m] = ff_in[m, :, :cols].astype(F32)
        store(ff_out.at[m], target)
    loads[5].wait()
    for i, target in enumerate((to_mix, to_ffn, to_rms)):
        row = small_in[i : i + 1, :rows].reshape(rows)
        rms_out[i][...] = jnp.sqrt(row / count) if i == 2 else row
        store(rms_out[i], target)
    for copy in stores:
        copy.wait()


def outputs(ff, at, tok, small, ffn_cols, count):
    rows, half = tok.shape
    shape = jax.ShapeDtypeStruct
    shapes = [
        (rows, half), (2 * HEADROWS, rows), (CONV, 2 * HDIM), (2 * HDIM, rows),
        (rows, ffn_cols), (rows, ffn_cols), (rows, ffn_cols), (rows,), (rows,), (rows,),
    ]
    vmem = pltpu.VMEM
    return pl.pallas_call(
        functools.partial(outputs_kernel, count),
        out_shape=[shape(s, F32) for s in shapes],
        in_specs=[ANY] * 4,
        out_specs=[ANY] * 10,
        scratch_shapes=[
            vmem(ff.shape, BF16), vmem(at.shape, BF16), vmem(tok.shape, BF16),
            vmem(small.shape, F32), vmem(shapes[0], F32), vmem(shapes[1], F32),
            vmem(shapes[2], F32), vmem(shapes[3], F32), vmem((3,) + shapes[4], F32),
            [vmem(shapes[7], F32)] * 3, dma(24),
        ],
        compiler_params=pltpu.CompilerParams(vmem_limit_bytes=60 * 2**20),
        name="outputs",
    )(ff, at, tok, small)


def on_device_full(
    tokens, cotangent, w_qkv, conv_weight, w_out, w_gate, w_up, w_down, gain_mix, gain_ffn
):
    rows, half = tokens.shape
    ffn_cols = w_gate.shape[1]
    out_ff, out_at, out_res, out_tok, small = run_layer(
        w_gate, w_up, w_down, w_qkv.T, w_out, conv_weight, gain_mix, gain_ffn,
        tokens, cotangent,
    )[:5]
    grads = outputs(out_ff, out_at, out_tok, small, ffn_cols, 8 * half * 4 * rows)
    to_tok, to_qkv, to_conv, to_out, to_gate, to_up, to_down, to_mix, to_ffn, to_rms = grads
    return (
        out_res, to_tok, to_qkv.T, to_conv, to_out, to_gate, to_up, to_down,
        to_mix, to_ffn, to_rms[:3],
    )


def on_device(tokens, cotangent, lengths, deal_order, *weights):
    total_rows = tokens.shape[1] * lax.axis_size("col")
    if (
        lengths.shape[0] * LONGEST == total_rows
        and lax.axis_size("row") == 4
        and lax.axis_size("col") == 8
        and total_rows == 4 * LONGEST
        and weights[0].shape[1] == 2 * HEADROWS
        and weights[3].shape[1] == 4 * TILE + 96
    ):
        return on_device_full(tokens, cotangent, *weights)
    return on_device_general(tokens, cotangent, lengths, deal_order, *weights)


def solution(mesh):
    in_specs = (
        P("row", "col"),
        P("row", "col"),
        P(),
        P(),
        P("row", "col"),
        P(None, "col"),
        P("col", "row"),
        P("row", "col"),
        P("row", "col"),
        P("row", "col"),
        P("row"),
        P("row"),
    )
    out_specs = (
        P("row", "col"),
        P("row", "col"),
        P("row", "col"),
        P(None, "col"),
        P("col", "row"),
        P("row", "col"),
        P("row", "col"),
        P("row", "col"),
        P("row"),
        P("row"),
        P(),
    )
    return jax.shard_map(
        on_device, mesh=mesh, in_specs=in_specs, out_specs=out_specs, check_vma=False
    )
```

```python
import functools

import jax
import jax.numpy as jnp
from jax import lax
from jax.experimental import pallas as pl
from jax.experimental.pallas import tpu as pltpu
from jax.sharding import PartitionSpec as P

D = 1792
FEAT = 16
CONV = 3
LONGEST = 1024
HDIM = 112


EPSILON = 1e-06


def dealing(lengths, deal_order, total_rows):
    seq_ids = jnp.arange(lengths.shape[0], dtype=jnp.int32)
    chosen = (deal_order[:, None] == seq_ids[None, :]).astype(jnp.int32)
    dealt_lengths = jnp.sum(chosen * lengths[None, :], 1)
    given_start = jnp.cumsum(lengths) - lengths
    dealt_start = jnp.cumsum(dealt_lengths) - dealt_lengths
    given_of_dealt = jnp.sum(chosen * given_start[None, :], 1)
    dealt_of_given = jnp.sum(chosen * dealt_start[:, None], 0)
    places = jnp.arange(total_rows, dtype=jnp.int32)
    in_dealt = (places[:, None] >= dealt_start[None, :]) & (
        places[:, None] < (dealt_start + dealt_lengths)[None, :]
    )
    in_given = (places[:, None] >= given_start[None, :]) & (
        places[:, None] < (given_start + lengths)[None, :]
    )
    source = places + jnp.sum(jnp.where(in_dealt, (given_of_dealt - dealt_start)[None, :], 0), 1)
    target = places + jnp.sum(jnp.where(in_given, (dealt_of_given - given_start)[None, :], 0), 1)
    offsets = places - jnp.sum(jnp.where(in_dealt, dealt_start[None, :], 0), 1)
    return (source, target, offsets)


def convolve(raw_values, kernel_conv, offsets):
    mixed = kernel_conv[0] * raw_values
    for delay_step in range(1, CONV):
        moved = jnp.concatenate(
            [jnp.zeros_like(raw_values[:delay_step]), raw_values[:-delay_step]], 0
        )
        mixed = mixed + kernel_conv[delay_step] * jnp.where(
            (offsets >= delay_step)[:, None, None], moved, 0.0
        )
    return mixed


def convolve_back(grad_mixed, raw_values, kernel_conv, offsets):
    grad_raw = kernel_conv[0] * grad_mixed
    sums_list = [jnp.sum(grad_mixed * raw_values, 0)]
    for delay_step in range(1, CONV):
        masked = jnp.where((offsets >= delay_step)[:, None, None], grad_mixed, 0.0)
        pulled = jnp.concatenate([masked[delay_step:], jnp.zeros_like(masked[:delay_step])], 0)
        grad_raw = grad_raw + kernel_conv[delay_step] * pulled
        moved = jnp.concatenate(
            [jnp.zeros_like(raw_values[:delay_step]), raw_values[:-delay_step]], 0
        )
        sums_list.append(jnp.sum(masked * moved, 0))
    return (grad_raw, jnp.stack(sums_list))


def bin_scores(query, keys, offsets):
    scores = jnp.einsum("thf,shf->hts", query, keys, preferred_element_type=jnp.float32) * FEAT ** (
        -0.5
    )
    positions = jnp.arange(query.shape[0], dtype=jnp.int32)
    visible = (positions[None, :] <= positions[:, None]) & (
        positions[:, None] - positions[None, :] <= offsets[:, None]
    )
    kernel = jnp.where(visible[None], 1.0 + scores + 0.5 * scores * scores, 0.0)
    return (scores, visible, kernel)


def attend_bin(pieces):
    query, keys, values, offsets = pieces
    scores, visible, kernel = bin_scores(query, keys, offsets)
    weights = (kernel / jnp.sum(kernel, -1, keepdims=True)).astype(jnp.bfloat16)
    return jnp.einsum("hts,shd->thd", weights, values, preferred_element_type=jnp.float32)


def attend_back(pieces):
    query, keys, values, offsets, grad_attend = pieces
    scores, visible, kernel = bin_scores(query, keys, offsets)
    totals = jnp.sum(kernel, -1, keepdims=True)
    weights = kernel / totals
    grad_weights = jnp.einsum(
        "thd,shd->hts", grad_attend, values, preferred_element_type=jnp.float32
    )
    grad_values = jnp.einsum(
        "hts,thd->shd",
        weights.astype(jnp.bfloat16),
        grad_attend,
        preferred_element_type=jnp.float32,
    )
    grad_kernel = (grad_weights - jnp.sum(grad_weights * weights, -1, keepdims=True)) / totals
    grad_scores = jnp.where(visible[None], grad_kernel * (1.0 + scores), 0.0).astype(jnp.bfloat16)
    grad_query = jnp.einsum(
        "hts,shf->thf", grad_scores, keys, preferred_element_type=jnp.float32
    ) * FEAT ** (-0.5)
    grad_keys = jnp.einsum(
        "hts,thf->shf", grad_scores, query, preferred_element_type=jnp.float32
    ) * FEAT ** (-0.5)
    return (grad_query, grad_keys, grad_values)


def times_transposed(left, right):
    return lax.dot_general(
        left, right, (((1,), (1,)), ((), ())), preferred_element_type=jnp.float32
    )


def tokens_product(left, right):
    return lax.dot_general(
        left, right, (((0,), (0,)), ((), ())), preferred_element_type=jnp.float32
    )


def plain_product(left, right):
    return jnp.dot(left, right, preferred_element_type=jnp.float32)


def gather_cols(values):
    return lax.all_gather(values, "col", axis=0, tiled=True)


def gather_rows(values):
    return lax.all_gather(values, "row", axis=0, tiled=True)


def grad_gather_cols(values):
    return lax.all_gather(values, "col", axis=1, tiled=True)


def grad_gather_rows(values):
    return lax.all_gather(values, "row", axis=0, tiled=True)


def width_total(values):
    return lax.psum(values, "row")


def forward_rows(gathered, row_index, weight, rows_here):

    def partial_term(row_start, row_count):
        picked = jnp.take(gathered, row_index, axis=0)
        return jnp.dot(picked, weight, preferred_element_type=jnp.float32)

    return lax.psum_scatter(
        partial_term(jnp.int32(0), rows_here * lax.axis_size("row")),
        "row",
        scatter_dimension=0,
        tiled=True,
    )


def forward_cols(gathered, row_index, weight, rows_here, product):

    def partial_term(row_start, row_count):
        picked = jnp.take(gathered, row_index, axis=0)
        return product(picked, weight)

    return lax.psum_scatter(
        partial_term(jnp.int32(0), lax.axis_size("col") * rows_here).astype(jnp.bfloat16),
        "col",
        scatter_dimension=0,
        tiled=True,
    ).astype(jnp.float32)


def backward_rows(gathered, row_index, weight, rows_here, contract):

    def partial_term(row_start, row_count):
        picked = jnp.take(gathered, row_index, axis=1)
        return lax.dot_general(
            picked, weight, (((0,), (contract,)), ((), ())), preferred_element_type=jnp.float32
        )

    return lax.psum_scatter(
        partial_term(jnp.int32(0), lax.axis_size("row") * rows_here).astype(jnp.bfloat16),
        "row",
        scatter_dimension=0,
        tiled=True,
    ).astype(jnp.float32)


def backward_cols(gathered, row_index, weight, rows_here):

    def partial_term(row_start, row_count):
        picked = jnp.take(gathered, row_index, axis=0)
        return times_transposed(picked, weight)

    return lax.psum_scatter(
        partial_term(jnp.int32(0), lax.axis_size("col") * rows_here).astype(jnp.bfloat16),
        "col",
        scatter_dimension=0,
        tiled=True,
    ).astype(jnp.float32)


def norm_forward(values, norm_gain):
    totals = width_total(jnp.sum(values * values, -1))
    inverse = lax.rsqrt(totals / D + EPSILON)
    return (values * inverse[:, None] * norm_gain, inverse)


def norm_back(values, inverse, norm_gain, grad_normed, dot_sums):
    cubed = inverse * inverse * inverse
    return grad_normed * norm_gain * inverse[:, None] - values * (cubed * dot_sums / D)[:, None]


def on_device_general(
    tokens,
    cotangent,
    lengths,
    deal_order,
    w_qkv,
    conv_weight,
    w_out,
    w_gate,
    w_up,
    w_down,
    gain_mix,
    gain_ffn,
):
    local_rows = tokens.shape[1]
    total_rows = local_rows * lax.axis_size("col")
    group_rows = total_rows // lax.axis_size("row")
    bin_count = group_rows // LONGEST
    heads_here = w_out.shape[0] // HDIM
    ffn_cols = w_gate.shape[1]
    source, target, offsets = dealing(lengths, deal_order, total_rows)
    group_offsets = lax.dynamic_slice_in_dim(
        offsets, lax.axis_index("row") * group_rows, group_rows
    )
    inputs = tokens.astype(jnp.float32).T
    gain_one = gain_mix.astype(jnp.float32)
    gain_two = gain_ffn.astype(jnp.float32)
    both_weights = jnp.concatenate([w_gate, w_up], 1)
    normed_one, inverse_one = norm_forward(inputs, gain_one)
    low_one = normed_one.astype(jnp.bfloat16)
    all_one = gather_cols(low_one)
    projected = forward_rows(all_one, source, w_qkv, group_rows)
    projected = projected.reshape(group_rows, heads_here, 2 * FEAT + HDIM)
    query = projected[:, :, :FEAT].astype(jnp.bfloat16)
    keys = projected[:, :, FEAT : 2 * FEAT].astype(jnp.bfloat16)
    raw_values = projected[:, :, 2 * FEAT :]
    kernel_conv = conv_weight.astype(jnp.float32).reshape(CONV, heads_here, HDIM)
    values = convolve(raw_values, kernel_conv, group_offsets).astype(jnp.bfloat16)
    binned = (
        query.reshape(bin_count, LONGEST, heads_here, FEAT),
        keys.reshape(bin_count, LONGEST, heads_here, FEAT),
        values.reshape(bin_count, LONGEST, heads_here, HDIM),
        group_offsets.reshape(bin_count, LONGEST),
    )
    attended = (
        lax.map(attend_bin, binned).reshape(group_rows, heads_here * HDIM).astype(jnp.bfloat16)
    )
    all_attended = gather_rows(attended)
    branch_mix = forward_cols(all_attended, target, w_out, local_rows, plain_product)
    middle = inputs + branch_mix
    normed_two, inverse_two = norm_forward(middle, gain_two)
    low_two = normed_two.astype(jnp.bfloat16)
    all_two = gather_cols(low_two)
    gate_up = forward_rows(all_two, source, both_weights, group_rows)
    gate = gate_up[:, :ffn_cols]
    up_proj = gate_up[:, ffn_cols:]
    activated = jax.nn.silu(gate)
    hidden = (activated * up_proj).astype(jnp.bfloat16)
    all_hidden = gather_rows(hidden)
    branch_ffn = forward_cols(all_hidden, target, w_down, local_rows, times_transposed)
    result_full = middle + branch_ffn
    grad_result = cotangent.astype(jnp.float32).T
    all_grad_ffn = grad_gather_cols(cotangent)
    hidden_again = gather_rows(hidden)
    grad_down = jnp.dot(
        jnp.take(all_grad_ffn, source, axis=1), hidden_again, preferred_element_type=jnp.float32
    )
    grad_hidden = backward_rows(all_grad_ffn, source, w_down, group_rows, 0)
    gate_sigmoid = jax.nn.sigmoid(gate)
    grad_gate_part = grad_hidden * up_proj * gate_sigmoid * (1.0 + gate * (1.0 - gate_sigmoid))
    grad_up_part = grad_hidden * activated
    grad_gate_up = jnp.concatenate([grad_gate_part, grad_up_part], 1).astype(jnp.bfloat16)
    all_grad_gate_up = grad_gather_rows(grad_gate_up)
    two_again = gather_cols(low_two)
    grad_both = tokens_product(jnp.take(two_again, source, axis=0), all_grad_gate_up)
    grad_normed_two = backward_cols(all_grad_gate_up, target, both_weights, local_rows)
    dots_two = width_total(jnp.sum(grad_normed_two * gain_two * middle, -1))
    grad_middle = grad_result + norm_back(middle, inverse_two, gain_two, grad_normed_two, dots_two)
    gain_part_two = jnp.sum(grad_normed_two * middle * inverse_two[:, None], 0)
    low_grad_middle = grad_middle.T.astype(jnp.bfloat16)
    all_grad_middle = grad_gather_cols(low_grad_middle)
    attended_again = gather_rows(attended)
    grad_out = lax.dot_general(
        attended_again,
        jnp.take(all_grad_middle, source, axis=1),
        (((0,), (1,)), ((), ())),
        preferred_element_type=jnp.float32,
    )
    grad_attended = backward_rows(all_grad_middle, source, w_out, group_rows, 1).astype(
        jnp.bfloat16
    )
    binned_back = binned + (grad_attended.reshape(bin_count, LONGEST, heads_here, HDIM),)
    grad_query, grad_keys, grad_values = lax.map(attend_back, binned_back)
    grad_values = grad_values.reshape(group_rows, heads_here, HDIM)
    grad_raw, conv_part = convolve_back(grad_values, raw_values, kernel_conv, group_offsets)
    grad_projected = jnp.concatenate(
        [
            grad_query.reshape(group_rows, heads_here, FEAT),
            grad_keys.reshape(group_rows, heads_here, FEAT),
            grad_raw,
        ],
        2,
    )
    grad_projected = grad_projected.reshape(group_rows, heads_here * (2 * FEAT + HDIM)).astype(
        jnp.bfloat16
    )
    all_grad_projected = grad_gather_rows(grad_projected)
    one_again = gather_cols(low_one)
    grad_qkv = tokens_product(jnp.take(one_again, source, axis=0), all_grad_projected)
    grad_normed_one = backward_cols(all_grad_projected, target, w_qkv, local_rows)
    squares = jnp.stack(
        [
            jnp.sum(branch_mix * branch_mix),
            jnp.sum(branch_ffn * branch_ffn),
            jnp.sum(result_full * result_full),
        ]
    )
    dots_one, grad_conv, squares_rows = width_total(
        (
            jnp.sum(grad_normed_one * gain_one * inputs, -1),
            conv_part.reshape(CONV, heads_here * HDIM),
            squares,
        )
    )
    grad_tokens = grad_middle + norm_back(inputs, inverse_one, gain_one, grad_normed_one, dots_one)
    gain_part_one = jnp.sum(grad_normed_one * inputs * inverse_one[:, None], 0)
    grad_gain_mix, grad_gain_ffn, squares_all = lax.psum(
        (gain_part_one, gain_part_two, squares_rows), "col"
    )
    rms_values = jnp.sqrt(squares_all / (total_rows * D))
    return (
        result_full.T.astype(jnp.bfloat16),
        grad_tokens.T,
        grad_qkv,
        grad_conv,
        grad_out,
        grad_both[:, :ffn_cols],
        grad_both[:, ffn_cols:],
        grad_down,
        grad_gain_mix,
        grad_gain_ffn,
        rms_values,
    )


HEADROWS = 2 * FEAT + HDIM
BLOCKROWS = HEADROWS + HDIM
TILE = 128
WIDE = 512
SPAN = 256
MARKS = 292
MESH = pl.DeviceIdType.MESH
ANY = pl.BlockSpec(memory_space=pl.ANY)
F32, BF16 = jnp.float32, jnp.bfloat16


def place():
    column = lax.axis_index("col")
    return lax.axis_index("row"), column // 2, column % 2


def device(chip, plane, core):
    return (chip, plane * 2 + core)


def other_chips(chip):
    y, x = chip // 2, chip % 2
    return (y * 2 + 1 - x, (1 - y) * 2 + x, (1 - y) * 2 + 1 - x)


def away(plane, step):
    if step == 1:
        return plane + 1 - 2 * (plane % 2)
    if step == 2:
        return (plane + 2) % 4
    return 3 - plane


def is_inner(plane):
    return ((plane + 1) // 2) % 2 == 1


def remote(source, target, send, receive, to):
    return pltpu.make_async_remote_copy(
        src_ref=source,
        dst_ref=target,
        send_sem=send,
        recv_sem=receive,
        device_id=to,
        device_id_type=MESH,
    )


def lanes(start, size=TILE):
    return pl.ds(pl.multiple_of(start, TILE), size)


def rows_at(start, size, step):
    return pl.ds(pl.multiple_of(start, step), size)


def no(flag):
    return jnp.logical_not(flag)


def dot(a, b, over_a, over_b):
    return lax.dot_general(
        a, b, (((over_a,), (over_b,)), ((), ())), preferred_element_type=F32
    )


class Marks:
    def __init__(self, ref):
        self.ref, self.used = ref, 0

    def one(self):
        self.used += 1
        return self.ref.at[self.used - 1]

    def many(self, count):
        base = self.used
        self.used += count
        return lambda i: self.ref.at[base + i]


class Spread:
    def __init__(self, ref, owner, chip, plane, core, marks):
        self.ref, self.spot = ref, (chip, plane, core)
        self.sends = marks.many(3)
        self.arrived = marks.one()
        inner = is_inner(plane)
        self.mine = plane == owner
        self.outer_owner = self.mine & no(inner)
        self.inner_owner = self.mine & inner
        far = (plane == away(owner, 2)) | ((plane == away(owner, 3)) & is_inner(owner))
        self.relays = inner & far

    def copy(self, step, send):
        chip, plane, core = self.spot
        return remote(
            self.ref, self.ref, self.sends(send), self.arrived,
            device(chip, away(plane, step), core),
        )

    def start(self):
        pl.when(self.outer_owner)(lambda: self.copy(2, 1).start())
        pl.when(self.inner_owner)(lambda: self.copy(3, 1).start())
        pl.when(self.mine)(lambda: self.copy(1, 0).start())

    def relay(self):
        @pl.when(self.relays)
        def _():
            self.copy(1, 2).wait_recv()
            self.copy(1, 2).start()

    def arrive(self):
        pl.when(no(self.mine | self.relays))(lambda: self.copy(1, 2).wait_recv())

    def finish(self):
        @pl.when(self.mine)
        def _():
            self.copy(1, 0).wait_send()
            self.copy(1, 1).wait_send()

        pl.when(self.relays)(lambda: self.copy(1, 2).wait_send())


class Chain:
    def __init__(self, ref, owner, chip, plane, core, marks):
        self.ref, self.spot = ref, (chip, plane, core)
        self.sends = marks.many(2)
        self.arrived = marks.one()
        inner = is_inner(plane)
        self.mine = plane == owner
        self.mine_inner, self.mine_outer = self.mine & inner, self.mine & no(inner)
        self.from_end = inner & (plane == away(owner, 1))
        self.from_inner = inner & (plane == away(owner, 3))
        self.from_far = inner & (plane == away(owner, 2))
        self.waits = no(inner) & no(self.mine)

    def copy(self, step, send):
        chip, plane, core = self.spot
        return remote(
            self.ref, self.ref, self.sends(send), self.arrived,
            device(chip, away(plane, step), core),
        )

    def start(self):
        pl.when(self.mine_outer)(lambda: self.copy(1, 0).start())

    def start_inner(self):
        @pl.when(self.mine_inner)
        def _():
            self.copy(3, 1).start()
            self.copy(1, 0).start()

    def relay(self):
        pl.when(self.from_end | self.from_inner)(lambda: self.copy(1, 0).wait_recv())
        pl.when(self.from_end)(lambda: self.copy(3, 0).start())
        pl.when(self.from_inner)(lambda: self.copy(1, 0).start())

    def relay_far(self):
        @pl.when(self.from_far)
        def _():
            self.copy(1, 0).wait_recv()
            self.copy(1, 0).start()

    def arrive(self):
        pl.when(self.waits)(lambda: self.copy(1, 0).wait_recv())

    def finish(self):
        pl.when(no(self.waits))(lambda: self.copy(1, 0).wait_send())
        pl.when(self.mine_inner)(lambda: self.copy(3, 1).wait_send())


class MainTiles:
    def __init__(self, ff, chip, plane, core, marks):
        self.ff, self.spot = ff, (chip, plane, core)
        self.sends, self.here = marks.many(5), marks.many(3)
        self.inner = is_inner(plane)

    def copy(self, slot, to_step, send, receive):
        chip, plane, core = self.spot
        tiles = self.ff.at[:, :, lanes(slot * TILE)]
        return remote(
            tiles, tiles, self.sends(send), self.here(receive),
            device(chip, away(plane, to_step), core),
        )

    def got(self, step):
        self.copy(self.spot[1], 1, 0, step - 1).wait_recv()

    def start(self):
        plane = self.spot[1]
        self.copy(plane, 1, 0, 0).start()
        pl.when(self.inner)(lambda: self.copy(plane, 3, 2, 2).start())

    def relay(self):
        plane = self.spot[1]

        @pl.when(self.inner)
        def _():
            self.got(1)
            self.copy(away(plane, 1), 3, 1, 1).start()
            self.got(3)
            self.copy(away(plane, 3), 1, 3, 1).start()

    def relay_far(self):
        plane = self.spot[1]

        @pl.when(self.inner)
        def _():
            self.got(2)
            self.copy(away(plane, 2), 1, 4, 2).start()

    def arrive(self, step):
        pl.when(no(self.inner))(lambda: self.got(step))

    def finish(self):
        self.copy(self.spot[1], 1, 0, 0).wait_send()

        @pl.when(self.inner)
        def _():
            for send in range(1, 5):
                self.copy(self.spot[1], 1, send, 0).wait_send()


class MainGrads:
    def __init__(self, gout, slots, chip, plane, core, marks):
        self.gout, self.slots, self.spot = gout, slots, (chip, plane, core)
        self.sends, self.here = marks.many(3), marks.many(5)
        self.inner = is_inner(plane)

    def copy(self, slot, to_step, send, receive):
        chip, plane, core = self.spot
        return remote(
            self.gout.at[:, :, lanes(slot * TILE)], self.slots.at[receive],
            self.sends(send), self.here(receive), device(chip, away(plane, to_step), core),
        )

    def start_rows(self, at_rows):
        chip, plane, core = self.spot
        slot = away(plane, 1)
        remote(
            self.gout.at[:, at_rows, lanes(slot * TILE)], self.slots.at[0, :, at_rows],
            self.sends(0), self.here(0), device(chip, slot, core),
        ).start()

    def start(self, step):
        receive = {1: 0, 2: 4, 3: 3}[step]
        self.copy(away(self.spot[1], step), 1, step - 1, receive).start()

    def relay(self, step, add):
        @pl.when(self.inner)
        def _():
            receive = {2: 3, 3: 4}[step]
            self.copy(self.spot[1], 1, 0, receive).wait_recv()
            slot = away(self.spot[1], step)
            add(slot, self.slots.at[receive])
            self.copy(slot, step, step - 1, step - 1).start()

    def total(self, add):
        plane = self.spot[1]
        self.copy(plane, 1, 0, 0).wait_recv()
        add(plane, self.slots.at[0])

        @pl.when(no(self.inner))
        def _():
            self.copy(plane, 1, 0, 1).wait_recv()
            add(plane, self.slots.at[1])

        @pl.when(self.inner)
        def _():
            self.copy(plane, 1, 0, 2).wait_recv()
            add(plane, self.slots.at[2])

    def finish(self):
        for send in range(3):
            self.copy(self.spot[1], 1, send, 0).wait_send()


class Collect:
    def __init__(self, ref, slots, owner, chip, plane, core, marks):
        self.ref, self.slots, self.spot = ref, slots, (chip, plane, core)
        self.send = marks.one()
        self.arrived = marks.many(3)
        inner, inner_owner = is_inner(plane), is_inner(owner)
        self.mine = plane == owner
        self.mine_outer = self.mine & no(inner)
        self.mine_inner = self.mine & inner
        self.near = plane == away(owner, 1)
        second, third = plane == away(owner, 2), plane == away(owner, 3)
        self.hands = no(inner) & (second | third) & no(self.near)
        self.adds_second = inner & second & no(inner_owner)
        self.adds_third = inner & third & inner_owner

    def copy(self, step, slot):
        chip, plane, core = self.spot
        return remote(
            self.ref, self.slots.at[slot], self.send, self.arrived(slot),
            device(chip, away(plane, step), core),
        )

    def start(self):
        pl.when(self.near)(lambda: self.copy(1, 0).start())
        pl.when(self.hands)(lambda: self.copy(1, 2).start())

    def relay(self, add):
        @pl.when(self.adds_second | self.adds_third)
        def _():
            self.copy(1, 2).wait_recv()
            add(self.slots.at[2])

        pl.when(self.adds_second)(lambda: self.copy(2, 1).start())
        pl.when(self.adds_third)(lambda: self.copy(3, 1).start())

    def total(self, add):
        @pl.when(self.mine)
        def _():
            for slot in range(2):
                self.copy(1, slot).wait_recv()
                add(self.slots.at[slot])

    def finish(self):
        pl.when(no(self.mine))(lambda: self.copy(1, 0).wait_send())


def layer_kernel(
    w_gate, w_up, w_down, w_qkv, w_out, conv, gain_mix, gain_ffn, tok, cot,
    out_ff, out_at, out_res, out_tok, out_small, main_got, extra_got, att_got, tail_got,
    ff, at, xs, gs, low2, part, acc3, gout, gat, from_mate, both, got, turned, hid, gg,
    gn, gcol, raw, qs, ks, vs, att, gatt, gproj, mid, gmid, gsum, normed, sending, inv_all,
    inv_sum, small, small_a, small_b, raw_ff, raw_qkv, raw_out, raw_conv, tapped,
    gains, gain_rows, packed, packed_back, at_tail, gat_tail, sem, free_mate, free_chips,
):
    chip, plane, core = place()
    others = other_chips(chip)
    mate = device(chip, plane, 1 - core)
    marks = Marks(sem)
    rows = tok.shape[0]
    width = 4 * rows
    half = tok.shape[1]
    seq = 2 * half
    own_half = lanes(core * half, half)
    first = core * half + chip * TILE
    peers = [device(c, plane, core) for c in others]
    line = [device(chip, away(plane, step), core) for step in (1, 2, 3)]
    sides = [device(c, plane, 1 - core) for c in others]
    line_mates = [device(chip, away(plane, step), 1 - core) for step in (1, 2, 3)]

    barrier = pltpu.get_barrier_semaphore()
    partners = peers + [mate] + sides + line + line_mates
    for partner in partners:
        pl.semaphore_signal(barrier, inc=1, device_id=partner, device_id_type=MESH)

    def block_rows(c):
        return rows_at(c * rows, rows, rows)

    ffn_weights = (w_gate, w_up, w_down)
    ffn_cols = w_gate.shape[1]
    wat, last_tile = gat.at[:, 0], packed_back.at[:, 0:rows]
    early = marks.many(6)
    loads = [
        pltpu.make_async_copy(source, target, early(i))
        for i, (source, target) in enumerate(
            (
                (w_qkv, raw_qkv), (w_out, raw_out), (conv, raw_conv),
                (gain_mix, gain_rows[0]), (gain_ffn, gain_rows[1]),
            )
        )
    ]
    for load in loads:
        load.start()
    for load in loads:
        load.wait()
    for i in range(2):
        gains[i] = gain_rows[i][...].reshape(1, rows)
    tapped[...] = jnp.zeros(tapped.shape, F32)
    tapped[0:CONV, 0 : 2 * HDIM] = raw_conv[...].astype(F32)
    tap_rows = tapped[...].T
    tail = lax.broadcasted_iota(jnp.int32, (HDIM, TILE), 1)
    spare = rows % TILE
    for h in range(2):
        wat[h, :HEADROWS, :rows] = raw_qkv[h * HEADROWS : (h + 1) * HEADROWS]
        wat[h, HEADROWS:, :rows] = raw_out[h * HDIM : (h + 1) * HDIM]
        columns = wat[h, 2 * FEAT : HEADROWS, WIDE - TILE :].astype(F32)
        for j in range(CONV):
            column = tap_rows[h * HDIM : (h + 1) * HDIM, j : j + 1]
            columns = jnp.where(tail == spare + j, column, columns)
        wat[h, 2 * FEAT : HEADROWS, WIDE - TILE :] = columns.astype(BF16)
    pl.semaphore_wait(barrier, len(partners))

    far_core = plane // 2
    holds_att = core == far_core
    holds_extra = holds_att & (chip // 2 == plane % 2)
    extra_plane = 2 * core + chip // 2
    extra_chip = (plane % 2) * 2 + core
    out_rows, in_rows = pl.ds(HEADROWS, HDIM), pl.ds(0, HEADROWS)
    whole = rows // TILE * TILE
    lead = 16
    tail_in, tail_out = pl.ds(0, lead + HEADROWS), pl.ds(lead + HEADROWS, HDIM)

    def leftover(ref, p):
        pair = [ref[c * rows + whole : (c + 1) * rows] for c in (2 * p, 2 * p + 1)]
        return jnp.concatenate(pair, 0)

    def heads_times(h, start, size, right):
        tails = slice(lead + start, lead + start + size)
        total = dot(at_tail[h, 0, tails], leftover(right, 0), 1, 0)
        total += dot(at_tail[h, 1, tails], leftover(right, 1), 1, 0)
        for c in range(4):
            total += dot(
                at[h, c, start : start + size, :whole], right[c * rows : c * rows + whole], 1, 0
            )
        return total

    def heads_spread(start, size, left, where, target):
        tails = slice(lead + start, lead + start + size)

        @pl.loop(0, 4)
        def _(c):
            total = dot(at[0, c, start : start + size, :whole], left[0, :, where], 0, 0)
            total += dot(at[1, c, start : start + size, :whole], left[1, :, where], 0, 0)
            target[rows_at(c * rows, whole, 16), where] = total.astype(BF16)

        for p in range(2):
            total = dot(at_tail[0, p, tails], left[0, :, where], 0, 0)
            total += dot(at_tail[1, p, tails], left[1, :, where], 0, 0)
            for i, c in enumerate((2 * p, 2 * p + 1)):
                size_left = rows - whole
                target[c * rows + whole : (c + 1) * rows, where] = total[
                    i * size_left : (i + 1) * size_left
                ].astype(BF16)

    lane_at = lax.broadcasted_iota(jnp.int32, (1, TILE), 1)

    def pack_heads(start, size):
        a = plane % 2
        for p in range(2):
            even, odd = [
                at[a, 2 * p + i, start : start + size, whole:].astype(F32) for i in range(2)
            ]
            tile = jnp.where(lane_at < spare, even, pltpu.roll(odd, spare, 1))
            at_tail[a, p, lead + start : lead + start + size] = tile.astype(BF16)

    def pack_taps():
        a = plane % 2
        columns = at[a, 0, 2 * FEAT : HEADROWS, whole:].astype(F32).T
        at_tail[a, 0, 0:lead, 0:HDIM] = columns[spare : spare + lead].astype(BF16)

    def unpack_heads(start, size):
        a = plane % 2
        for p in range(2):
            tile = gat_tail[a, p, lead + start : lead + start + size].astype(F32)
            for i, half_tile in enumerate((tile, pltpu.roll(tile, spare, 1))):
                gat[a, 2 * p + i, start : start + size, whole:] = half_tile.astype(BF16)

    def unpack_taps():
        a = plane % 2
        columns = gat_tail[a, 0, 0:lead, 0:HDIM].astype(F32).T
        for c in range(4):
            tile = gat[a, c, 2 * FEAT : HEADROWS, whole:].astype(F32)
            for j in range(CONV):
                tile = jnp.where(tail == spare + j, columns[:, j : j + 1], tile)
            gat[a, c, 2 * FEAT : HEADROWS, whole:] = tile.astype(BF16)

    att_self = [(2 * core + h == chip) & holds_att for h in range(2)]

    class Heads:
        def __init__(self, span):
            self.span, self.local = span, marks.one()
            self.send, self.here = marks.many(2), marks.many(4)

        def copy(self, h):
            return remote(
                wat.at[h, self.span], at.at[plane % 2, chip, self.span], self.send(h),
                self.here(chip), device(2 * core + h, plane, far_core),
            )

        def keep(self, h):
            return pltpu.make_async_copy(
                wat.at[h, self.span], at.at[plane % 2, chip, self.span], self.local
            )

        def start(self):
            for h in range(2):
                pl.when(att_self[h])(lambda: self.keep(h).start())
                pl.when(no(att_self[h]))(lambda: self.copy(h).start())

        def arrive(self):
            for h in range(2):
                pl.when(att_self[h])(lambda: self.keep(h).wait())

            for c in range(4):

                @pl.when(holds_att & no((c == chip) & (core == chip // 2)))
                def _():
                    remote(
                        wat.at[0, self.span], at.at[plane % 2, c, self.span], self.send(0),
                        self.here(c), mate,
                    ).wait_recv()

        def finish(self):
            for h in range(2):
                pl.when(no(att_self[h]))(lambda: self.copy(h).wait_send())

    heads_in, heads_out = Heads(in_rows), Heads(out_rows)
    heads_in.start()
    heads_out.start()

    class Gather:
        def __init__(self, source, target_of, earlier=None):
            self.source, self.target_of = source, target_of
            self.marks = earlier.marks if earlier else [marks.many(6), marks.many(6)] + [
                marks.many(4), marks.many(4), marks.one()
            ]
            self.send, self.here, self.mate_send, self.mate_here, kept = self.marks
            self.keep = pltpu.make_async_copy(source, target_of(chip), kept)
            mine = self.halves(source)
            there = self.halves(target_of(chip))
            self.copies = {
                mark: remote(
                    mine[half], there[half], self.send(mark), self.here(mark), peers[p]
                )
                for mark, half, p in ((0, 0, 0), (3, 1, 1), (1, 1, 0), (2, 0, 1))
            }
            for copy in self.copies.values():
                copy.start()
            self.keep.start()
            self.crossing = []
            self.cross(source, chip, 3)

        def cross(self, source, c, mark):
            copy = remote(
                source, self.target_of(c), self.mate_send(mark), self.mate_here(mark), mate
            )
            copy.start()
            self.crossing.append(copy)

        def halves(self, block):
            size = block.shape[0] // 2
            return block.at[0:size], block.at[size : 2 * size]

        def pass_on(self):
            for mark, half, p, onward in ((0, 0, 0, 4), (3, 1, 1, 5)):
                self.copies[mark].wait_recv()
                block = self.halves(self.target_of(others[p]))[half]
                self.copies[onward] = remote(
                    block, block, self.send(onward), self.here(onward), peers[1 - p]
                )
                self.copies[onward].start()
            for mark, p in ((1, 0), (2, 1)):
                self.copies[mark].wait_recv()
                self.cross(self.target_of(others[p]), others[p], p)

        def arrive(self):
            for mark in (4, 5):
                self.copies[mark].wait_recv()
            self.cross(self.target_of(others[2]), others[2], 2)
            for copy in self.crossing:
                copy.wait_recv()
            self.keep.wait()

        def finish(self):
            for copy in list(self.copies.values()) + self.crossing:
                copy.wait_send()

    tokens_in = Gather(tok, lambda c: xs.at[block_rows(c), own_half])
    gain_send, gain_here = marks.many(3), marks.many(3)
    gain_copies = [
        remote(gains, gn.at[chip], gain_send(p), gain_here(p), peers[p]) for p in range(3)
    ]
    gain_keep = pltpu.make_async_copy(gains, gn.at[chip], marks.one())
    for copy in gain_copies + [gain_keep]:
        copy.start()

    in_line, out_line = [
        [
            Spread(ref, 2 * core + a, chip, plane, core, marks)
            for a in range(2)
            for ref in (at.at[a, :, span, 0:whole], at_tail.at[a, :, tail_span])
        ]
        for span, tail_span in ((in_rows, tail_in), (out_rows, tail_out))
    ]
    heads_in.arrive()

    @pl.when(holds_att)
    def _():
        pack_heads(0, HEADROWS)
        pack_taps()

    for item in in_line:
        item.start()
    heads_out.arrive()
    pl.when(holds_att)(lambda: pack_heads(HEADROWS, HDIM))
    for item in out_line:
        item.start()
    heads_in.finish()
    heads_out.finish()

    short = ffn_cols - 4 * TILE
    for m in range(3):
        load = pltpu.make_async_copy(ffn_weights[m], raw_ff, early(5))
        load.start()
        load.wait()
        last_tile[m, :, 0:short] = raw_ff[:, 4 * TILE :]
        last_tile[m, :, short:] = jnp.zeros((rows, TILE - short), BF16)

    tokens_in.pass_on()
    main_send, main_here, main_local = marks.many(9), marks.many(9), marks.many(3)
    main_here_at = [ff.at[m, block_rows(chip), lanes(plane * TILE)] for m in range(3)]
    mains = [
        remote(
            ffn_weights[m].at[:, lanes(others[p] * TILE)], main_here_at[m],
            main_send(3 * p + m), main_here(3 * p + m), peers[p],
        )
        for p in range(3)
        for m in range(3)
    ]
    mains += [
        pltpu.make_async_copy(
            ffn_weights[m].at[:, lanes(chip * TILE)], main_here_at[m], main_local(m)
        )
        for m in range(3)
    ]
    for copy in mains:
        copy.start()

    extra_send, extra_here, extra_local = marks.one(), marks.many(4), marks.one()
    extra_self = (extra_chip == chip) & holds_att
    last = lanes(4 * TILE)

    def extra_copy():
        return remote(
            last_tile, ff.at[:, block_rows(chip), last], extra_send, extra_here(chip),
            device(extra_chip, plane, far_core),
        )

    def extra_keep():
        return pltpu.make_async_copy(
            last_tile, ff.at[:, block_rows(chip), last], extra_local
        )

    @pl.when(extra_self)
    def _():
        extra_keep().start()

    @pl.when(no(extra_self))
    def _():
        extra_copy().start()

    for item in in_line:
        item.relay()
    tokens_in.arrive()
    cot_in = Gather(cot, lambda c: gs.at[block_rows(c), own_half])
    for copy in gain_copies + [gain_keep]:
        copy.wait()

    for item in out_line:
        item.relay()
    @pl.loop(0, 4)
    def _(c):
        pair = jnp.concatenate(
            [gn[c, 0].astype(F32), gn[c, 1].astype(F32), jnp.zeros((6, rows), F32)], 0
        )
        gcol[block_rows(c), 0:8] = pair.T.astype(BF16)

    step_rows = 64

    def add_squares(i, total):
        x = xs[rows_at(i * step_rows, step_rows, step_rows)].astype(F32)
        return total + jnp.sum((x * x).reshape(step_rows // 8, 8, seq), 0)

    squares = lax.fori_loop(0, width // step_rows, add_squares, jnp.zeros((8, seq), F32))
    inv_all[...] = lax.rsqrt(jnp.sum(squares, 0, keepdims=True) / D + EPSILON)
    tokens_in.finish()
    normed[...] = xs[:, lanes(first)]

    @pl.loop(0, width // step_rows)
    def _(i):
        at_rows = rows_at(i * step_rows, step_rows, step_rows)
        xs[at_rows] = (
            xs[at_rows].astype(F32) * inv_all[...] * gcol[at_rows, 0:1].astype(F32)
        ).astype(BF16)

    for item in in_line:
        item.arrive()

    position = lax.broadcasted_iota(jnp.int32, (1, seq), 1)

    def taps(h):
        columns = at_tail[h, 0, 0:lead, 0:HDIM].astype(F32).T
        return [columns[:, j : j + 1] for j in range(CONV)]

    @pl.loop(0, 2)
    def _(h):
        projected = heads_times(h, 0, HEADROWS, xs)
        qs[h] = (projected[:FEAT].astype(BF16).astype(F32) * FEAT**-0.5).astype(BF16)
        ks[h] = projected[FEAT : 2 * FEAT].astype(BF16)
        values = projected[2 * FEAT :]
        raw[h] = values
        tap = taps(h)
        mixed = tap[0] * values
        for j in range(1, CONV):
            moved = pltpu.roll(values, j, 1)
            mixed += tap[j] * jnp.where(position >= j, moved, 0.0)
        vs[h] = mixed.astype(BF16)

    def kernel_of(h, b):
        seen = (b + 1) * SPAN
        scores = dot(ks[h, :, :seen], qs[h, :, b * SPAN : seen], 0, 0)
        kernel = 1.0 + scores + 0.5 * scores * scores
        key_at = lax.broadcasted_iota(jnp.int32, (seen, SPAN), 0)
        query_at = lax.broadcasted_iota(jnp.int32, (seen, SPAN), 1) + b * SPAN
        visible = key_at <= query_at
        return scores, jnp.where(visible, kernel, 0.0), visible

    @pl.loop(0, 2)
    def _(h):
        for b in range(seq // SPAN):
            seen = (b + 1) * SPAN
            _, kernel, _ = kernel_of(h, b)
            inverse = 1.0 / jnp.sum(kernel, 0, keepdims=True)
            inv_sum[h, :, b * SPAN : seen] = inverse
            weights = (kernel * inverse).astype(BF16)
            att[h, :, b * SPAN : seen] = dot(vs[h, :, :seen], weights, 1, 0).astype(BF16)

    for copy in mains:
        copy.wait()
    main_line = MainTiles(ff, chip, plane, core, marks)
    main_line.start()

    @pl.when(extra_self)
    def _():
        extra_keep().wait()

    @pl.when(no(extra_self))
    def _():
        extra_copy().wait_send()

    for c in range(4):

        @pl.when(holds_extra & no((c == chip) & (core == chip % 2)))
        def _():
            remote(
                last_tile, ff.at[:, block_rows(c), last], extra_send, extra_here(c), mate
            ).wait_recv()

    third = short // 3
    unit_at = lax.broadcasted_iota(jnp.int32, (rows, TILE), 1)

    def pack(source, target):
        @pl.loop(0, 3)
        def _(m):
            fourth = source[m, 3 * rows :, last].astype(F32)
            for b in range(3):
                own = source[m, b * rows : (b + 1) * rows, last].astype(F32)
                moved = pltpu.roll(fourth, (short - b * third) % TILE, 1)
                target[m, b * rows : (b + 1) * rows] = jnp.where(
                    unit_at < short, own, moved
                ).astype(BF16)

    def unpack(source, target):
        @pl.loop(0, 3)
        def _(m):
            fourth = jnp.zeros((rows, TILE), F32)
            for b in range(3):
                block = source[m, b * rows : (b + 1) * rows].astype(F32)
                target[m, b * rows : (b + 1) * rows, last] = jnp.where(
                    unit_at < short, block, 0.0
                ).astype(BF16)
                moved = pltpu.roll(block, (b * third - short) % TILE, 1)
                here = (unit_at >= b * third) & (unit_at < (b + 1) * third)
                fourth = jnp.where(here, moved, fourth)
            target[m, 3 * rows :, last] = fourth.astype(BF16)

    pl.when(holds_extra)(lambda: pack(ff, packed))
    extra_line = Chain(packed, extra_plane, chip, plane, core, marks)
    extra_line.start()

    for item in out_line:
        item.arrive()

    def default_got(i):
        return got.at[i]

    class Sum:
        def __init__(
            self, guard, earlier=None, both=both, got=None, share=True, at_once=True
        ):
            self.marks = earlier.marks if earlier else [marks.many(4), marks.many(4)] + [
                marks.many(6), marks.many(6)
            ]
            self.guard, self.both, self.share, self.at_once = guard, both, share, at_once
            self.got = got or default_got

        def begin(self, fill):
            fill((1 - core) * half)
            send, here = self.marks[:2]
            self.order = (others[2], others[0], others[1], chip)
            self.to_mate = [
                remote(
                    part.at[:, lanes((1 - core) * half + c * TILE)],
                    from_mate.at[:, lanes(c * TILE)], send(i), here(i), mate,
                )
                for i, c in enumerate(self.order)
            ]
            if self.guard:
                pl.semaphore_wait(free_mate, 1)
            for copy in self.to_mate:
                copy.start()
            fill(core * half)

        def release(self):
            pl.semaphore_signal(free_mate, inc=1, device_id=mate, device_id_type=MESH)

        def combine(self):
            self.prepare()
            for i, c in enumerate(self.order):
                self.to_mate[i].wait_recv()
                where, own = lanes(c * TILE), lanes(core * half + c * TILE)

                @pl.loop(0, 4)
                def _(b):
                    at_rows = block_rows(b)
                    self.both[at_rows, where] = (
                        part[at_rows, own].astype(F32) + from_mate[at_rows, where].astype(F32)
                    ).astype(BF16)

                if self.at_once:
                    self.send(i)
            for copy in self.to_mate:
                copy.wait_send()

        def piece(self, upper, c):
            size = width // 2
            return self.both.at[pl.ds(0 if upper else size, size), lanes(c * TILE)]

        def prepare(self):
            size = width // 2
            top, bottom = pl.ds(0, size), pl.ds(size, size)
            send, here = self.marks[2:]
            x, y, across = others
            self.across = [
                remote(self.piece(True, across), self.got(2).at[top], send(0), here(0), peers[0]),
                remote(
                    self.piece(False, across), self.got(2).at[bottom], send(1), here(1), peers[1]
                ),
            ]
            self.plain = [
                remote(self.piece(True, x), self.got(0).at[top], send(2), here(2), peers[0]),
                remote(self.piece(False, y), self.got(1).at[bottom], send(3), here(3), peers[1]),
            ]
            self.added = [
                remote(self.piece(True, y), self.got(1).at[top], send(4), here(4), peers[1]),
                remote(self.piece(False, x), self.got(0).at[bottom], send(5), here(5), peers[0]),
            ]

        def send(self, i):
            if i == 0:
                if self.guard and self.share:
                    pl.semaphore_wait(free_chips, 2)
                for copy in self.across:
                    copy.start()
            elif i < 3:
                self.plain[i - 1].start()

        def send_all(self):
            for i in range(3):
                self.send(i)

        def pass_on(self):
            size = width // 2
            quarter = size // 2
            for i, c in ((0, others[1]), (1, others[0])):
                self.across[i].wait_recv()
                for q in range(2):
                    at_rows = pl.ds(i * size + q * quarter, quarter)
                    self.both[at_rows, lanes(c * TILE)] = (
                        self.both[at_rows, lanes(c * TILE)].astype(F32) + self.got(2)[at_rows].astype(F32)
                    ).astype(BF16)
                self.added[i].start()

        def finish(self, store):
            for copy in self.plain + self.added:
                copy.wait()
            for copy in self.across:
                copy.wait_send()

            @pl.loop(0, 4)
            def _(c):
                at_rows = block_rows(c)
                total = self.both[at_rows, lanes(chip * TILE)].astype(F32)
                for p in range(2):
                    total += self.got(p)[at_rows].astype(F32)
                store(at_rows, total)

            for p in range(2 if self.share else 0):
                pl.semaphore_signal(free_chips, inc=1, device_id=peers[p], device_id_type=MESH)

    def fill_branch(start):
        heads_spread(HEADROWS, HDIM, att, lanes(start, half), part)

    small[...] = jnp.zeros(small.shape, F32)
    square_at = lax.broadcasted_iota(jnp.int32, (1, WIDE), 1)

    def note_square(index, value):
        total = jnp.sum(value * value)
        small[0, 2:3, :] += jnp.where(square_at == index, total, 0.0)

    def store_branch(at_rows, total):
        note_square(0, total)
        mid[at_rows] = normed[at_rows].astype(F32) + total

    branch_sum = Sum(guard=False)
    branch_sum.begin(fill_branch)
    cot_in.pass_on()
    branch_sum.combine()
    branch_sum.release()
    branch_sum.pass_on()
    main_line.relay()
    extra_line.start_inner()
    branch_sum.finish(store_branch)
    middle = mid[...]
    inverse_two = lax.rsqrt(jnp.sum(middle * middle, 0, keepdims=True) / D + EPSILON)

    @pl.loop(0, 4)
    def _(c):
        at_rows = block_rows(c)
        sending[0, at_rows] = (mid[at_rows] * inverse_two * gcol[at_rows, 1:2].astype(F32)).astype(BF16)

    def token_block(c):
        return low2.at[:, lanes(core * half + c * TILE)]

    low_in = Gather(sending.at[0], token_block, tokens_in)
    cot_in.arrive()
    cot_in.finish()

    @pl.loop(0, 4)
    def _(c):
        acc3[block_rows(c)] = jnp.zeros((rows, seq), F32)

    low_in.pass_on()
    low_in.arrive()
    low_in.finish()

    main_line.relay_far()
    extra_line.relay()
    def feed_units(slot):
        where = lanes(slot * TILE)
        unit_rows = rows_at(slot * TILE, TILE, TILE)
        for m in range(3):
            turned[m * TILE : (m + 1) * TILE] = ff[m, :, where].T

        @pl.loop(0, seq // SPAN)
        def _(n):
            span = lanes(n * SPAN, SPAN)
            gate_up = dot(turned[: 2 * TILE], low2[:, span], 1, 0)
            grad_hidden = dot(turned[2 * TILE :], gs[:, span], 1, 0)
            gate, up = gate_up[:TILE], gate_up[TILE:]
            sigmoid = 1.0 / (1.0 + jnp.exp(-gate))
            activated = gate * sigmoid
            hid[unit_rows, span] = (activated * up).astype(BF16)
            gg[:TILE, span] = (
                grad_hidden * up * sigmoid * (1.0 + gate * (1.0 - sigmoid))
            ).astype(BF16)
            gg[TILE:, span] = (grad_hidden * activated).astype(BF16)

    def feed_input(slot, at_rows):
        where = lanes(slot * TILE)
        pair = jnp.concatenate([ff[0, at_rows, where], ff[1, at_rows, where]], 1)
        acc3[at_rows] += dot(pair, gg[...], 1, 0)

    def feed_weights(slot, at_rows):
        where = lanes(slot * TILE)
        unit_rows = rows_at(slot * TILE, TILE, TILE)
        grads = dot(low2[at_rows], gg[...], 1, 1).astype(BF16)
        gout[0, at_rows, where] = grads[:, :TILE]
        gout[1, at_rows, where] = grads[:, TILE:]
        gout[2, at_rows, where] = dot(gs[at_rows], hid[unit_rows], 1, 1).astype(BF16)

    main_back = MainGrads(gout, main_got, chip, plane, core, marks)
    extra_back = Collect(packed_back, extra_got, extra_plane, chip, plane, core, marks)
    load_marks = marks.many(3)

    spare_lanes = [lanes((1 - core) * half + m * TILE) for m in range(3)]

    def add_tiles(slot, source):
        loads = [
            pltpu.make_async_copy(source.at[m], gs.at[:, spare_lanes[m]], load_marks(m))
            for m in range(3)
        ]
        for load in loads:
            load.start()
        for load in loads:
            load.wait()
        where = lanes(slot * TILE)

        @pl.loop(0, 4)
        def _(c):
            at_rows = block_rows(c)
            for m in range(3):
                gout[m, at_rows, where] = (
                    gout[m, at_rows, where].astype(F32)
                    + gs[at_rows, spare_lanes[m]].astype(F32)
                ).astype(BF16)

    def add_extra(source):
        packed_rows = slice(0, 3 * rows)
        loads = [
            pltpu.make_async_copy(source.at[m], gs.at[packed_rows, spare_lanes[m]], load_marks(m))
            for m in range(3)
        ]
        for load in loads:
            load.start()
        for load in loads:
            load.wait()

        @pl.loop(0, 3)
        def _(b):
            at_rows = block_rows(b)
            for m in range(3):
                packed_back[m, at_rows] = (
                    packed_back[m, at_rows].astype(F32)
                    + gs[at_rows, spare_lanes[m]].astype(F32)
                ).astype(BF16)

    slots = [away(plane, 1), plane, away(plane, 2), away(plane, 3)]
    inner = is_inner(plane)

    @pl.loop(0, 4)
    def _(turn):
        pl.when(turn == 2)(lambda: extra_line.relay_far())

        for i, step in ((0, 1), (2, 2), (3, 3)):

            @pl.when(turn == i)
            def _():
                main_line.arrive(step)

        slot = sum((turn == i).astype(jnp.int32) * slots[i] for i in range(4))
        feed_units(slot)

        @pl.loop(0, 4)
        def _(c):
            feed_input(slot, block_rows(c))
            feed_weights(slot, block_rows(c))
            pl.when((turn == 0) & no(inner))(lambda: main_back.start_rows(block_rows(c)))

        for i, step in ((2, 2), (3, 3)):

            @pl.when((turn == i) & no(inner))
            def _():
                main_back.start(step)

    extra_line.arrive()
    unpack(packed, ff)
    feed_units(4)

    @pl.loop(0, 4)
    def _(c):
        feed_input(4, block_rows(c))

    main_line.finish()

    def fill_grad_two(start):
        @pl.loop(0, 4)
        def _(c):
            where = lanes(start, half)
            part[block_rows(c), where] = acc3[block_rows(c), where].astype(BF16)

    def store_gsum(at_rows, total):
        gsum[at_rows] = total

    two_sum = Sum(True, branch_sum)
    two_sum.begin(fill_grad_two)
    two_sum.combine()
    @pl.loop(0, 4)
    def _(c):
        feed_weights(4, block_rows(c))

    two_sum.release()
    pl.when(inner)(lambda: main_back.start(1))
    pack(gout, packed_back)
    extra_back.start()
    main_back.relay(3, add_tiles)
    two_sum.pass_on()

    def fill_ffn(start):
        @pl.loop(0, 4)
        def _(c):
            where = lanes(start, half)
            part[block_rows(c), where] = dot(
                ff[2, block_rows(c)], hid[:, where], 1, 0
            ).astype(BF16)

    ffn_sum = Sum(
        guard=True, both=ff.at[1, :, lanes(0, half)],
        got=lambda i: ff.at[0, :, lanes(i * TILE)], share=False,
        at_once=False,
    )
    ffn_sum.begin(fill_ffn)
    two_sum.finish(store_gsum)

    def norm_back(source, inverse, gain_lane, base, store):
        def add_dots(c, total):
            at_rows = block_rows(c)
            gain = gcol[at_rows, gain_lane : gain_lane + 1].astype(F32)
            return total + jnp.sum(gsum[at_rows] * gain * source(at_rows), 0, keepdims=True)

        dots = lax.fori_loop(0, 4, add_dots, jnp.zeros((1, TILE), F32))
        scaled = inverse * inverse * inverse * dots / D

        @pl.loop(0, 4)
        def _(c):
            at_rows = block_rows(c)
            gain = gcol[at_rows, gain_lane : gain_lane + 1].astype(F32)
            grad, value = gsum[at_rows], source(at_rows)
            store(at_rows, base(at_rows) + (grad * gain * inverse - value * scaled))

        def gain_back():
            @pl.loop(0, 4)
            def _(c):
                at_rows = block_rows(c)
                for_gain = jnp.sum((gsum[at_rows] * source(at_rows) * inverse).T, 0, keepdims=True)
                small[c, gain_lane : gain_lane + 1, 0:rows] = for_gain

        return gain_back

    def store_middle(at_rows, value):
        gmid[at_rows] = value
        sending[1, at_rows] = value.astype(BF16)

    gain_two_back = norm_back(
        lambda r: mid[r], inverse_two, 1, lambda r: gs[r, lanes(first)].astype(F32), store_middle
    )
    mid_in = Gather(sending.at[1], token_block, tokens_in)
    gain_two_back()
    ffn_sum.combine()
    ffn_sum.release()
    mid_in.pass_on()
    ffn_sum.send_all()
    mid_in.arrive()

    @pl.loop(0, 2)
    def _(h):
        total = heads_times(h, HEADROWS, HDIM, low2)
        gatt[h] = total.astype(BF16)

    main_back.relay(2, add_tiles)

    out_back, in_back = [
        [
            Collect(ref, slots_, 2 * core + a, chip, plane, core, marks)
            for a in range(2)
            for ref, slots_ in (
                (gat.at[a, :, span, 0:whole], att_got.at[a, :, :, span]),
                (gat_tail.at[a, :, tail_span], tail_got.at[a, :, :, tail_span]),
            )
        ]
        for span, tail_span in ((out_rows, tail_out), (in_rows, tail_in))
    ]

    def head_grads(left, right, start, size):
        @pl.loop(0, 2)
        def _(h):
            for c in range(4):
                gat[h, c, start : start + size, :whole] = dot(
                    left[h], right[c * rows : c * rows + whole], 1, 1
                ).astype(BF16)
            for p in range(2):
                gat_tail[h, p, lead + start : lead + start + size] = dot(
                    left[h], leftover(right, p), 1, 1
                ).astype(BF16)

    head_grads(att, low2, HEADROWS, HDIM)
    for item in out_back:
        item.start()


    @pl.loop(0, 2)
    def _(h):
        grad_keys = jnp.zeros((FEAT, seq), F32)
        grad_values = jnp.zeros((HDIM, seq), F32)

        def padded(value):
            short = seq - value.shape[1]
            if not short:
                return value
            return jnp.concatenate([value, jnp.zeros((value.shape[0], short), F32)], 1)

        for b in range(seq // SPAN):
            seen = (b + 1) * SPAN
            span = slice(b * SPAN, seen)
            scores, kernel, visible = kernel_of(h, b)
            inverse = inv_sum[h, :, span]
            weights = kernel * inverse
            grad_weights = dot(vs[h, :, :seen], gatt[h, :, span], 0, 0)
            grad_values += padded(dot(gatt[h, :, span], weights.astype(BF16), 1, 1))
            dots = jnp.sum(grad_weights * weights, 0, keepdims=True)
            grad_kernel = (grad_weights - dots) * inverse
            grad_scores = jnp.where(visible, grad_kernel * (1.0 + scores), 0.0).astype(BF16)
            gproj[h, :FEAT, span] = (
                dot(ks[h, :, :seen], grad_scores, 1, 0) * FEAT**-0.5
            ).astype(BF16)
            grad_keys += padded(dot(qs[h, :, span], grad_scores, 1, 1))
        gproj[h, FEAT : 2 * FEAT] = grad_keys.astype(BF16)
        tap = taps(h)
        grad_raw = tap[0] * grad_values
        sums = [jnp.sum(grad_values * raw[h], 1, keepdims=True)]
        for j in range(1, CONV):
            masked = jnp.where(position >= j, grad_values, 0.0)
            grad_raw += tap[j] * pltpu.roll(masked, seq - j, 1)
            sums.append(jnp.sum(masked * pltpu.roll(raw[h], j, 1), 1, keepdims=True))
        gproj[h, 2 * FEAT :] = grad_raw.astype(BF16)
        columns = jnp.zeros((HDIM, TILE), F32)
        for j in range(CONV):
            columns = jnp.where(tail == j, sums[j], columns)
        gat_tail[h, 0, 0:lead, 0:HDIM] = columns.T[0:lead].astype(BF16)

    head_grads(gproj, xs, 0, HEADROWS)
    for item in in_back:
        item.start()

    ffn_sum.pass_on()
    mid_in.finish()

    def fill_grad_one(start):
        heads_spread(0, HEADROWS, gproj, lanes(start, half), part)

    one_sum = Sum(True, branch_sum)
    one_sum.begin(fill_grad_one)
    one_sum.combine()
    one_sum.release()
    extra_back.relay(add_extra)

    def store_result(at_rows, total):
        note_square(1, total)
        total = mid[at_rows] + total
        note_square(2, total)
        sending[0, at_rows] = total.astype(BF16)

    one_sum.pass_on()

    def hand_out(source, target):
        send, here = marks.many(3), marks.many(3)
        copies = [
            remote(
                source.at[block_rows(others[p])], target.at[:, lanes(chip * TILE)],
                send(p), here(p), peers[p],
            )
            for p in range(3)
        ]
        copies.append(
            pltpu.make_async_copy(
                source.at[block_rows(chip)], target.at[:, lanes(chip * TILE)], marks.one()
            )
        )
        for copy in copies:
            copy.start()
        return copies

    ffn_sum.finish(store_result)
    pending = hand_out(sending.at[0], out_res)


    one_sum.finish(store_gsum)
    head_marks = marks.many(4)

    def add_head(i, start, size, tail_start, tail_size):
        a, is_tail = i // 2, i % 2
        target, count = (gat_tail, 2) if is_tail else (gat, 4)
        begin, extent = (tail_start, tail_size) if is_tail else (start, size)
        wide = TILE if is_tail else whole

        def add(source):
            loads = [
                pltpu.make_async_copy(
                    source.at[c], part.at[c * BLOCKROWS : c * BLOCKROWS + extent, 0:wide],
                    head_marks(c),
                )
                for c in range(count)
            ]
            for load in loads:
                load.start()
            for load in loads:
                load.wait()
            for c in range(count):
                target[a, c, begin : begin + extent, 0:wide] = (
                    target[a, c, begin : begin + extent, 0:wide].astype(F32)
                    + part[c * BLOCKROWS : c * BLOCKROWS + extent, 0:wide].astype(F32)
                ).astype(BF16)

        return add

    def add_out(i):
        return add_head(i, HEADROWS, HDIM, lead + HEADROWS, HDIM)

    def add_in(i):
        return add_head(i, 0, HEADROWS, 0, lead + HEADROWS)

    for i in range(4):
        out_back[i].relay(add_out(i))

    inverse_own = inv_all[:, lanes(first)]

    def store_tokens(at_rows, value):
        sending[1, at_rows] = value.astype(BF16)

    gain_one_back = norm_back(
        lambda r: normed[r].astype(F32), inverse_own, 0, lambda r: gmid[r], store_tokens
    )
    pending += hand_out(sending.at[1], out_tok)
    gain_one_back()

    for c in range(1, 4):
        small[c, 2:3] = small[0, 2:3]
    a_send, a_here = marks.many(3), marks.many(3)
    trio = [
        remote(small.at[others[p]], small_a.at[p], a_send(p), a_here(p), peers[p])
        for p in range(3)
    ]
    for copy in trio:
        copy.start()

    main_back.total(add_tiles)
    back_send, back_here = marks.many(3), marks.many(3)
    mine = lanes(plane * TILE)
    back_to = out_ff.at[:, :, lanes(chip * TILE)]
    backs = [
        remote(
            gout.at[:, block_rows(others[p]), mine], back_to, back_send(p), back_here(p), peers[p]
        )
        for p in range(3)
    ]
    backs.append(
        pltpu.make_async_copy(gout.at[:, block_rows(chip), mine], back_to, marks.one())
    )
    for copy in backs:
        copy.start()
    pending += backs

    extra_back.total(add_extra)
    pl.when(holds_extra)(lambda: unpack(packed_back, gout))
    last_send, last_here, last_local = marks.many(4), marks.one(), marks.one()

    def last_copy(c):
        return remote(
            gout.at[:, block_rows(c), last], out_ff.at[:, :, last], last_send(c), last_here,
            device(c, plane, chip % 2),
        )

    def last_keep():
        return pltpu.make_async_copy(
            gout.at[:, block_rows(chip), last], out_ff.at[:, :, last], last_local
        )

    for c in range(4):
        same = (c == chip) & (core == chip % 2)

        @pl.when(holds_extra & same)
        def _():
            last_keep().start()

        @pl.when(holds_extra & no(same))
        def _():
            last_copy(c).start()

    for i in range(4):
        in_back[i].relay(add_in(i))
    for copy in trio:
        copy.wait()
    small_b[0] = small[chip] + small_a[0] + small_a[1] + small_a[2]
    b_send, b_here = marks.many(7), marks.many(7)
    seven = [
        remote(small_b.at[0], small_b.at[1 + i], b_send(i), b_here(i), to)
        for i, to in enumerate(line + [mate] + line_mates)
    ]
    for copy in seven:
        copy.start()

    class HeadsBack:
        def __init__(self, span):
            self.span, self.local = span, marks.one()
            self.send, self.here = marks.many(4), marks.many(2)

        def same(self, c):
            return (c == chip) & (core == chip // 2)

        def copy(self, c):
            return remote(
                gat.at[plane % 2, c, self.span], out_at.at[chip % 2, self.span], self.send(c),
                self.here(chip % 2), device(c, plane, chip // 2),
            )

        def keep(self):
            return pltpu.make_async_copy(
                gat.at[plane % 2, chip, self.span], out_at.at[chip % 2, self.span], self.local
            )

        def start(self):
            for c in range(4):
                pl.when(holds_att & self.same(c))(lambda: self.keep().start())
                pl.when(holds_att & no(self.same(c)))(lambda: self.copy(c).start())

        def finish(self):
            for c in range(4):
                pl.when(holds_att & self.same(c))(lambda: self.keep().wait())
                pl.when(holds_att & no(self.same(c)))(lambda: self.copy(c).wait_send())

            for h in range(2):

                @pl.when(no(att_self[h]))
                def _():
                    remote(
                        gat.at[0, 0, self.span], out_at.at[h, self.span], self.send(0),
                        self.here(h), mate,
                    ).wait_recv()

    heads_back = [HeadsBack(out_rows), HeadsBack(in_rows)]
    for i in range(4):
        out_back[i].total(add_out(i))
    pl.when(holds_att)(lambda: unpack_heads(HEADROWS, HDIM))
    heads_back[0].start()
    for i in range(4):
        in_back[i].total(add_in(i))

    @pl.when(holds_att)
    def _():
        unpack_heads(0, HEADROWS)
        unpack_taps()

    heads_back[1].start()

    for copy in seven:
        copy.wait()
    total = small_b[0]
    for i in range(7):
        total += small_b[1 + i]
    small_a[0] = total
    small_out = pltpu.make_async_copy(small_a.at[0], out_small, marks.one())
    small_out.start()
    pending.append(small_out)
    for item in in_line + out_line + [extra_line, main_back, extra_back] + out_back + in_back:
        item.finish()
    for copy in pending:
        copy.wait()
    for c in range(4):
        same = (c == chip) & (core == chip % 2)
        pl.when(holds_extra & same)(lambda: last_keep().wait())
        pl.when(holds_extra & no(same))(lambda: last_copy(c).wait_send())

    @pl.when(no(extra_self))
    def _():
        last_copy(0).wait_recv()

    for item in heads_back:
        item.finish()

    pl.semaphore_wait(free_mate, 1)
    pl.semaphore_wait(free_chips, 2)
    assert marks.used <= MARKS, marks.used


def dma(*shape):
    return pltpu.SemaphoreType.DMA(shape)


def run_layer(w_gate, w_up, w_down, w_qkv, w_out, conv, gain_mix, gain_ffn, tok, cot):
    rows, half = tok.shape
    width, seq = 4 * rows, 2 * half
    shape = jax.ShapeDtypeStruct
    vmem = pltpu.VMEM
    tiles = (3, width, TILE)
    head = (4, BLOCKROWS, WIDE)
    return pl.pallas_call(
        layer_kernel,
        out_shape=[
            shape((3, rows, 5 * TILE), BF16),
            shape((2, BLOCKROWS, WIDE), BF16),
            shape((rows, half), BF16),
            shape((rows, half), BF16),
            shape((8, WIDE), F32),
            shape((5,) + tiles, BF16),
            shape((3, 3, 3 * rows, TILE), BF16),
            shape((2, 3, 4, BLOCKROWS, rows // TILE * TILE), BF16),
            shape((2, 3, 2, 16 + BLOCKROWS, TILE), BF16),
        ],
        in_specs=[ANY] * 10,
        out_specs=[ANY] * 9,
        scratch_shapes=[
            vmem((3, width, 5 * TILE), BF16),
            vmem((2,) + head, BF16),
            vmem((width, seq), BF16),
            vmem((width, seq), BF16),
            vmem((width, seq), BF16),
            vmem((width, seq), BF16),
            vmem((width, seq), F32),
            vmem((3, width, 5 * TILE), BF16),
            vmem((2,) + head, BF16),
            vmem((width, half), BF16),
            vmem((width, half), BF16),
            vmem((3, width, TILE), BF16),
            vmem((3 * TILE, width), BF16),
            vmem((5 * TILE, seq), BF16),
            vmem((2 * TILE, seq), BF16),
            vmem((4, 2, 1, rows), BF16),
            vmem((width, TILE), BF16),
            vmem((2, HDIM, seq), F32),
            vmem((2, FEAT, seq), BF16),
            vmem((2, FEAT, seq), BF16),
            vmem((2, HDIM, seq), BF16),
            vmem((2, HDIM, seq), BF16),
            vmem((2, HDIM, seq), BF16),
            vmem((2, HEADROWS, seq), BF16),
            vmem((width, TILE), F32),
            vmem((width, TILE), F32),
            vmem((width, TILE), F32),
            vmem((width, TILE), BF16),
            vmem((2, width, TILE), BF16),
            vmem((1, seq), F32),
            vmem((2, 1, seq), F32),
            vmem((4, 8, WIDE), F32),
            vmem((3, 8, WIDE), F32),
            vmem((8, 8, WIDE), F32),
            vmem(w_gate.shape, BF16),
            vmem(w_qkv.shape, BF16),
            vmem(w_out.shape, BF16),
            vmem(conv.shape, BF16),
            vmem((8, 2 * TILE), F32),
            vmem((2, 1, rows), BF16),
            [vmem((rows,), BF16)] * 2,
            vmem((3, 3 * rows, TILE), BF16),
            vmem((3, 3 * rows, TILE), BF16),
            vmem((2, 2, 16 + BLOCKROWS, TILE), BF16),
            vmem((2, 2, 16 + BLOCKROWS, TILE), BF16),
            dma(MARKS),
            pltpu.SemaphoreType.REGULAR,
            pltpu.SemaphoreType.REGULAR,
        ],
        compiler_params=pltpu.CompilerParams(
            collective_id=0, has_side_effects=True, vmem_limit_bytes=63 * 2**20
        ),
        name="layer",
    )(w_gate, w_up, w_down, w_qkv, w_out, conv, gain_mix, gain_ffn, tok, cot)


def outputs_kernel(
    count, ff, at, tok, small, to_tok, to_qkv, to_conv, to_out, to_gate, to_up, to_down,
    to_mix, to_ffn, to_rms, ff_in, at_in, tok_in, small_in, tok_out, qkv_out, conv_out, out_out,
    ff_out, rms_out, sem,
):
    rows, cols = to_gate.shape
    marks = Marks(sem)
    loads = [
        pltpu.make_async_copy(source, target, marks.one())
        for source, target in (
            [(tok, tok_in), (at, at_in)] + [(ff.at[m], ff_in.at[m]) for m in range(3)]
            + [(small, small_in)]
        )
    ]
    for load in loads:
        load.start()
    stores = []

    def store(source, target):
        stores.append(pltpu.make_async_copy(source, target, marks.one()))
        stores[-1].start()

    loads[0].wait()
    tok_out[...] = tok_in[...].astype(F32)
    store(tok_out, to_tok)
    loads[1].wait()
    for h in range(2):
        qkv_out[h * HEADROWS : (h + 1) * HEADROWS] = at_in[h, :HEADROWS, :rows].astype(F32)
        out_out[h * HDIM : (h + 1) * HDIM] = at_in[h, HEADROWS:, :rows].astype(F32)
    store(qkv_out, to_qkv)
    store(out_out, to_out)
    taps = jnp.concatenate(
        [at_in[h, 2 * FEAT : HEADROWS, WIDE - TILE :].astype(F32) for h in range(2)], 0
    )
    conv_out[...] = taps.T[rows % TILE : rows % TILE + CONV]
    store(conv_out, to_conv)
    for m, target in enumerate((to_gate, to_up, to_down)):
        loads[2 + m].wait()
        ff_out[m] = ff_in[m, :, :cols].astype(F32)
        store(ff_out.at[m], target)
    loads[5].wait()
    for i, target in enumerate((to_mix, to_ffn, to_rms)):
        row = small_in[i : i + 1, :rows].reshape(rows)
        rms_out[i][...] = jnp.sqrt(row / count) if i == 2 else row
        store(rms_out[i], target)
    for copy in stores:
        copy.wait()


def outputs(ff, at, tok, small, ffn_cols, count):
    rows, half = tok.shape
    shape = jax.ShapeDtypeStruct
    shapes = [
        (rows, half), (2 * HEADROWS, rows), (CONV, 2 * HDIM), (2 * HDIM, rows),
        (rows, ffn_cols), (rows, ffn_cols), (rows, ffn_cols), (rows,), (rows,), (rows,),
    ]
    vmem = pltpu.VMEM
    return pl.pallas_call(
        functools.partial(outputs_kernel, count),
        out_shape=[shape(s, F32) for s in shapes],
        in_specs=[ANY] * 4,
        out_specs=[ANY] * 10,
        scratch_shapes=[
            vmem(ff.shape, BF16), vmem(at.shape, BF16), vmem(tok.shape, BF16),
            vmem(small.shape, F32), vmem(shapes[0], F32), vmem(shapes[1], F32),
            vmem(shapes[2], F32), vmem(shapes[3], F32), vmem((3,) + shapes[4], F32),
            [vmem(shapes[7], F32)] * 3, dma(24),
        ],
        compiler_params=pltpu.CompilerParams(vmem_limit_bytes=60 * 2**20),
        name="outputs",
    )(ff, at, tok, small)


def on_device_full(
    tokens, cotangent, w_qkv, conv_weight, w_out, w_gate, w_up, w_down, gain_mix, gain_ffn
):
    rows, half = tokens.shape
    ffn_cols = w_gate.shape[1]
    out_ff, out_at, out_res, out_tok, small = run_layer(
        w_gate, w_up, w_down, w_qkv.T, w_out, conv_weight, gain_mix, gain_ffn,
        tokens, cotangent,
    )[:5]
    grads = outputs(out_ff, out_at, out_tok, small, ffn_cols, 8 * half * 4 * rows)
    to_tok, to_qkv, to_conv, to_out, to_gate, to_up, to_down, to_mix, to_ffn, to_rms = grads
    return (
        out_res, to_tok, to_qkv.T, to_conv, to_out, to_gate, to_up, to_down,
        to_mix, to_ffn, to_rms[:3],
    )


def on_device(tokens, cotangent, lengths, deal_order, *weights):
    total_rows = tokens.shape[1] * lax.axis_size("col")
    if (
        lengths.shape[0] * LONGEST == total_rows
        and lax.axis_size("row") == 4
        and lax.axis_size("col") == 8
        and total_rows == 4 * LONGEST
        and weights[0].shape[1] == 2 * HEADROWS
        and weights[3].shape[1] == 4 * TILE + 96
    ):
        return on_device_full(tokens, cotangent, *weights)
    return on_device_general(tokens, cotangent, lengths, deal_order, *weights)


def solution(mesh):
    in_specs = (
        P("row", "col"),
        P("row", "col"),
        P(),
        P(),
        P("row", "col"),
        P(None, "col"),
        P("col", "row"),
        P("row", "col"),
        P("row", "col"),
        P("row", "col"),
        P("row"),
        P("row"),
    )
    out_specs = (
        P("row", "col"),
        P("row", "col"),
        P("row", "col"),
        P(None, "col"),
        P("col", "row"),
        P("row", "col"),
        P("row", "col"),
        P("row", "col"),
        P("row"),
        P("row"),
        P(),
    )
    return jax.shard_map(
        on_device, mesh=mesh, in_specs=in_specs, out_specs=out_specs, check_vma=False
    )
```

```python
import functools

import jax
import jax.numpy as jnp
from jax import lax
from jax.experimental import pallas as pl
from jax.experimental.pallas import tpu as pltpu
from jax.sharding import PartitionSpec as P

D = 1792
FEAT = 16
CONV = 3
LONGEST = 1024
HDIM = 112


EPSILON = 1e-06


def dealing(lengths, deal_order, total_rows):
    seq_ids = jnp.arange(lengths.shape[0], dtype=jnp.int32)
    chosen = (deal_order[:, None] == seq_ids[None, :]).astype(jnp.int32)
    dealt_lengths = jnp.sum(chosen * lengths[None, :], 1)
    given_start = jnp.cumsum(lengths) - lengths
    dealt_start = jnp.cumsum(dealt_lengths) - dealt_lengths
    given_of_dealt = jnp.sum(chosen * given_start[None, :], 1)
    dealt_of_given = jnp.sum(chosen * dealt_start[:, None], 0)
    places = jnp.arange(total_rows, dtype=jnp.int32)
    in_dealt = (places[:, None] >= dealt_start[None, :]) & (
        places[:, None] < (dealt_start + dealt_lengths)[None, :]
    )
    in_given = (places[:, None] >= given_start[None, :]) & (
        places[:, None] < (given_start + lengths)[None, :]
    )
    source = places + jnp.sum(jnp.where(in_dealt, (given_of_dealt - dealt_start)[None, :], 0), 1)
    target = places + jnp.sum(jnp.where(in_given, (dealt_of_given - given_start)[None, :], 0), 1)
    offsets = places - jnp.sum(jnp.where(in_dealt, dealt_start[None, :], 0), 1)
    return (source, target, offsets)


def convolve(raw_values, kernel_conv, offsets):
    mixed = kernel_conv[0] * raw_values
    for delay_step in range(1, CONV):
        moved = jnp.concatenate(
            [jnp.zeros_like(raw_values[:delay_step]), raw_values[:-delay_step]], 0
        )
        mixed = mixed + kernel_conv[delay_step] * jnp.where(
            (offsets >= delay_step)[:, None, None], moved, 0.0
        )
    return mixed


def convolve_back(grad_mixed, raw_values, kernel_conv, offsets):
    grad_raw = kernel_conv[0] * grad_mixed
    sums_list = [jnp.sum(grad_mixed * raw_values, 0)]
    for delay_step in range(1, CONV):
        masked = jnp.where((offsets >= delay_step)[:, None, None], grad_mixed, 0.0)
        pulled = jnp.concatenate([masked[delay_step:], jnp.zeros_like(masked[:delay_step])], 0)
        grad_raw = grad_raw + kernel_conv[delay_step] * pulled
        moved = jnp.concatenate(
            [jnp.zeros_like(raw_values[:delay_step]), raw_values[:-delay_step]], 0
        )
        sums_list.append(jnp.sum(masked * moved, 0))
    return (grad_raw, jnp.stack(sums_list))


def bin_scores(query, keys, offsets):
    scores = jnp.einsum("thf,shf->hts", query, keys, preferred_element_type=jnp.float32) * FEAT ** (
        -0.5
    )
    positions = jnp.arange(query.shape[0], dtype=jnp.int32)
    visible = (positions[None, :] <= positions[:, None]) & (
        positions[:, None] - positions[None, :] <= offsets[:, None]
    )
    kernel = jnp.where(visible[None], 1.0 + scores + 0.5 * scores * scores, 0.0)
    return (scores, visible, kernel)


def attend_bin(pieces):
    query, keys, values, offsets = pieces
    scores, visible, kernel = bin_scores(query, keys, offsets)
    weights = (kernel / jnp.sum(kernel, -1, keepdims=True)).astype(jnp.bfloat16)
    return jnp.einsum("hts,shd->thd", weights, values, preferred_element_type=jnp.float32)


def attend_back(pieces):
    query, keys, values, offsets, grad_attend = pieces
    scores, visible, kernel = bin_scores(query, keys, offsets)
    totals = jnp.sum(kernel, -1, keepdims=True)
    weights = kernel / totals
    grad_weights = jnp.einsum(
        "thd,shd->hts", grad_attend, values, preferred_element_type=jnp.float32
    )
    grad_values = jnp.einsum(
        "hts,thd->shd",
        weights.astype(jnp.bfloat16),
        grad_attend,
        preferred_element_type=jnp.float32,
    )
    grad_kernel = (grad_weights - jnp.sum(grad_weights * weights, -1, keepdims=True)) / totals
    grad_scores = jnp.where(visible[None], grad_kernel * (1.0 + scores), 0.0).astype(jnp.bfloat16)
    grad_query = jnp.einsum(
        "hts,shf->thf", grad_scores, keys, preferred_element_type=jnp.float32
    ) * FEAT ** (-0.5)
    grad_keys = jnp.einsum(
        "hts,thf->shf", grad_scores, query, preferred_element_type=jnp.float32
    ) * FEAT ** (-0.5)
    return (grad_query, grad_keys, grad_values)


def times_transposed(left, right):
    return lax.dot_general(
        left, right, (((1,), (1,)), ((), ())), preferred_element_type=jnp.float32
    )


def tokens_product(left, right):
    return lax.dot_general(
        left, right, (((0,), (0,)), ((), ())), preferred_element_type=jnp.float32
    )


def plain_product(left, right):
    return jnp.dot(left, right, preferred_element_type=jnp.float32)


def gather_cols(values):
    return lax.all_gather(values, "col", axis=0, tiled=True)


def gather_rows(values):
    return lax.all_gather(values, "row", axis=0, tiled=True)


def grad_gather_cols(values):
    return lax.all_gather(values, "col", axis=1, tiled=True)


def grad_gather_rows(values):
    return lax.all_gather(values, "row", axis=0, tiled=True)


def width_total(values):
    return lax.psum(values, "row")


def forward_rows(gathered, row_index, weight, rows_here):

    def partial_term(row_start, row_count):
        picked = jnp.take(gathered, row_index, axis=0)
        return jnp.dot(picked, weight, preferred_element_type=jnp.float32)

    return lax.psum_scatter(
        partial_term(jnp.int32(0), rows_here * lax.axis_size("row")),
        "row",
        scatter_dimension=0,
        tiled=True,
    )


def forward_cols(gathered, row_index, weight, rows_here, product):

    def partial_term(row_start, row_count):
        picked = jnp.take(gathered, row_index, axis=0)
        return product(picked, weight)

    return lax.psum_scatter(
        partial_term(jnp.int32(0), lax.axis_size("col") * rows_here).astype(jnp.bfloat16),
        "col",
        scatter_dimension=0,
        tiled=True,
    ).astype(jnp.float32)


def backward_rows(gathered, row_index, weight, rows_here, contract):

    def partial_term(row_start, row_count):
        picked = jnp.take(gathered, row_index, axis=1)
        return lax.dot_general(
            picked, weight, (((0,), (contract,)), ((), ())), preferred_element_type=jnp.float32
        )

    return lax.psum_scatter(
        partial_term(jnp.int32(0), lax.axis_size("row") * rows_here).astype(jnp.bfloat16),
        "row",
        scatter_dimension=0,
        tiled=True,
    ).astype(jnp.float32)


def backward_cols(gathered, row_index, weight, rows_here):

    def partial_term(row_start, row_count):
        picked = jnp.take(gathered, row_index, axis=0)
        return times_transposed(picked, weight)

    return lax.psum_scatter(
        partial_term(jnp.int32(0), lax.axis_size("col") * rows_here).astype(jnp.bfloat16),
        "col",
        scatter_dimension=0,
        tiled=True,
    ).astype(jnp.float32)


def norm_forward(values, norm_gain):
    totals = width_total(jnp.sum(values * values, -1))
    inverse = lax.rsqrt(totals / D + EPSILON)
    return (values * inverse[:, None] * norm_gain, inverse)


def norm_back(values, inverse, norm_gain, grad_normed, dot_sums):
    cubed = inverse * inverse * inverse
    return grad_normed * norm_gain * inverse[:, None] - values * (cubed * dot_sums / D)[:, None]


def on_device_general(
    tokens,
    cotangent,
    lengths,
    deal_order,
    w_qkv,
    conv_weight,
    w_out,
    w_gate,
    w_up,
    w_down,
    gain_mix,
    gain_ffn,
):
    local_rows = tokens.shape[1]
    total_rows = local_rows * lax.axis_size("col")
    group_rows = total_rows // lax.axis_size("row")
    bin_count = group_rows // LONGEST
    heads_here = w_out.shape[0] // HDIM
    ffn_cols = w_gate.shape[1]
    source, target, offsets = dealing(lengths, deal_order, total_rows)
    group_offsets = lax.dynamic_slice_in_dim(
        offsets, lax.axis_index("row") * group_rows, group_rows
    )
    inputs = tokens.astype(jnp.float32).T
    gain_one = gain_mix.astype(jnp.float32)
    gain_two = gain_ffn.astype(jnp.float32)
    both_weights = jnp.concatenate([w_gate, w_up], 1)
    normed_one, inverse_one = norm_forward(inputs, gain_one)
    low_one = normed_one.astype(jnp.bfloat16)
    all_one = gather_cols(low_one)
    projected = forward_rows(all_one, source, w_qkv, group_rows)
    projected = projected.reshape(group_rows, heads_here, 2 * FEAT + HDIM)
    query = projected[:, :, :FEAT].astype(jnp.bfloat16)
    keys = projected[:, :, FEAT : 2 * FEAT].astype(jnp.bfloat16)
    raw_values = projected[:, :, 2 * FEAT :]
    kernel_conv = conv_weight.astype(jnp.float32).reshape(CONV, heads_here, HDIM)
    values = convolve(raw_values, kernel_conv, group_offsets).astype(jnp.bfloat16)
    binned = (
        query.reshape(bin_count, LONGEST, heads_here, FEAT),
        keys.reshape(bin_count, LONGEST, heads_here, FEAT),
        values.reshape(bin_count, LONGEST, heads_here, HDIM),
        group_offsets.reshape(bin_count, LONGEST),
    )
    attended = (
        lax.map(attend_bin, binned).reshape(group_rows, heads_here * HDIM).astype(jnp.bfloat16)
    )
    all_attended = gather_rows(attended)
    branch_mix = forward_cols(all_attended, target, w_out, local_rows, plain_product)
    middle = inputs + branch_mix
    normed_two, inverse_two = norm_forward(middle, gain_two)
    low_two = normed_two.astype(jnp.bfloat16)
    all_two = gather_cols(low_two)
    gate_up = forward_rows(all_two, source, both_weights, group_rows)
    gate = gate_up[:, :ffn_cols]
    up_proj = gate_up[:, ffn_cols:]
    activated = jax.nn.silu(gate)
    hidden = (activated * up_proj).astype(jnp.bfloat16)
    all_hidden = gather_rows(hidden)
    branch_ffn = forward_cols(all_hidden, target, w_down, local_rows, times_transposed)
    result_full = middle + branch_ffn
    grad_result = cotangent.astype(jnp.float32).T
    all_grad_ffn = grad_gather_cols(cotangent)
    hidden_again = gather_rows(hidden)
    grad_down = jnp.dot(
        jnp.take(all_grad_ffn, source, axis=1), hidden_again, preferred_element_type=jnp.float32
    )
    grad_hidden = backward_rows(all_grad_ffn, source, w_down, group_rows, 0)
    gate_sigmoid = jax.nn.sigmoid(gate)
    grad_gate_part = grad_hidden * up_proj * gate_sigmoid * (1.0 + gate * (1.0 - gate_sigmoid))
    grad_up_part = grad_hidden * activated
    grad_gate_up = jnp.concatenate([grad_gate_part, grad_up_part], 1).astype(jnp.bfloat16)
    all_grad_gate_up = grad_gather_rows(grad_gate_up)
    two_again = gather_cols(low_two)
    grad_both = tokens_product(jnp.take(two_again, source, axis=0), all_grad_gate_up)
    grad_normed_two = backward_cols(all_grad_gate_up, target, both_weights, local_rows)
    dots_two = width_total(jnp.sum(grad_normed_two * gain_two * middle, -1))
    grad_middle = grad_result + norm_back(middle, inverse_two, gain_two, grad_normed_two, dots_two)
    gain_part_two = jnp.sum(grad_normed_two * middle * inverse_two[:, None], 0)
    low_grad_middle = grad_middle.T.astype(jnp.bfloat16)
    all_grad_middle = grad_gather_cols(low_grad_middle)
    attended_again = gather_rows(attended)
    grad_out = lax.dot_general(
        attended_again,
        jnp.take(all_grad_middle, source, axis=1),
        (((0,), (1,)), ((), ())),
        preferred_element_type=jnp.float32,
    )
    grad_attended = backward_rows(all_grad_middle, source, w_out, group_rows, 1).astype(
        jnp.bfloat16
    )
    binned_back = binned + (grad_attended.reshape(bin_count, LONGEST, heads_here, HDIM),)
    grad_query, grad_keys, grad_values = lax.map(attend_back, binned_back)
    grad_values = grad_values.reshape(group_rows, heads_here, HDIM)
    grad_raw, conv_part = convolve_back(grad_values, raw_values, kernel_conv, group_offsets)
    grad_projected = jnp.concatenate(
        [
            grad_query.reshape(group_rows, heads_here, FEAT),
            grad_keys.reshape(group_rows, heads_here, FEAT),
            grad_raw,
        ],
        2,
    )
    grad_projected = grad_projected.reshape(group_rows, heads_here * (2 * FEAT + HDIM)).astype(
        jnp.bfloat16
    )
    all_grad_projected = grad_gather_rows(grad_projected)
    one_again = gather_cols(low_one)
    grad_qkv = tokens_product(jnp.take(one_again, source, axis=0), all_grad_projected)
    grad_normed_one = backward_cols(all_grad_projected, target, w_qkv, local_rows)
    squares = jnp.stack(
        [
            jnp.sum(branch_mix * branch_mix),
            jnp.sum(branch_ffn * branch_ffn),
            jnp.sum(result_full * result_full),
        ]
    )
    dots_one, grad_conv, squares_rows = width_total(
        (
            jnp.sum(grad_normed_one * gain_one * inputs, -1),
            conv_part.reshape(CONV, heads_here * HDIM),
            squares,
        )
    )
    grad_tokens = grad_middle + norm_back(inputs, inverse_one, gain_one, grad_normed_one, dots_one)
    gain_part_one = jnp.sum(grad_normed_one * inputs * inverse_one[:, None], 0)
    grad_gain_mix, grad_gain_ffn, squares_all = lax.psum(
        (gain_part_one, gain_part_two, squares_rows), "col"
    )
    rms_values = jnp.sqrt(squares_all / (total_rows * D))
    return (
        result_full.T.astype(jnp.bfloat16),
        grad_tokens.T,
        grad_qkv,
        grad_conv,
        grad_out,
        grad_both[:, :ffn_cols],
        grad_both[:, ffn_cols:],
        grad_down,
        grad_gain_mix,
        grad_gain_ffn,
        rms_values,
    )


HEADROWS = 2 * FEAT + HDIM
BLOCKROWS = HEADROWS + HDIM
TILE = 128
WIDE = 512
SPAN = 256
MARKS = 292
MESH = pl.DeviceIdType.MESH
ANY = pl.BlockSpec(memory_space=pl.ANY)
F32, BF16 = jnp.float32, jnp.bfloat16


def place():
    column = lax.axis_index("col")
    return lax.axis_index("row"), column // 2, column % 2


def device(chip, plane, core):
    return (chip, plane * 2 + core)


def other_chips(chip):
    y, x = chip // 2, chip % 2
    return (y * 2 + 1 - x, (1 - y) * 2 + x, (1 - y) * 2 + 1 - x)


def away(plane, step):
    if step == 1:
        return plane + 1 - 2 * (plane % 2)
    if step == 2:
        return (plane + 2) % 4
    return 3 - plane


def is_inner(plane):
    return ((plane + 1) // 2) % 2 == 1


def remote(source, target, send, receive, to):
    return pltpu.make_async_remote_copy(
        src_ref=source,
        dst_ref=target,
        send_sem=send,
        recv_sem=receive,
        device_id=to,
        device_id_type=MESH,
    )


def lanes(start, size=TILE):
    return pl.ds(pl.multiple_of(start, TILE), size)


def rows_at(start, size, step):
    return pl.ds(pl.multiple_of(start, step), size)


def no(flag):
    return jnp.logical_not(flag)


def dot(a, b, over_a, over_b):
    return lax.dot_general(
        a, b, (((over_a,), (over_b,)), ((), ())), preferred_element_type=F32
    )


class Marks:
    def __init__(self, ref):
        self.ref, self.used = ref, 0

    def one(self):
        self.used += 1
        return self.ref.at[self.used - 1]

    def many(self, count):
        base = self.used
        self.used += count
        return lambda i: self.ref.at[base + i]


class Spread:
    def __init__(self, ref, owner, chip, plane, core, marks):
        self.ref, self.spot = ref, (chip, plane, core)
        self.sends = marks.many(3)
        self.arrived = marks.one()
        inner = is_inner(plane)
        self.mine = plane == owner
        self.outer_owner = self.mine & no(inner)
        self.inner_owner = self.mine & inner
        far = (plane == away(owner, 2)) | ((plane == away(owner, 3)) & is_inner(owner))
        self.relays = inner & far

    def copy(self, step, send):
        chip, plane, core = self.spot
        return remote(
            self.ref, self.ref, self.sends(send), self.arrived,
            device(chip, away(plane, step), core),
        )

    def start(self):
        pl.when(self.outer_owner)(lambda: self.copy(2, 1).start())
        pl.when(self.inner_owner)(lambda: self.copy(3, 1).start())
        pl.when(self.mine)(lambda: self.copy(1, 0).start())

    def relay(self):
        @pl.when(self.relays)
        def _():
            self.copy(1, 2).wait_recv()
            self.copy(1, 2).start()

    def arrive(self):
        pl.when(no(self.mine | self.relays))(lambda: self.copy(1, 2).wait_recv())

    def finish(self):
        @pl.when(self.mine)
        def _():
            self.copy(1, 0).wait_send()
            self.copy(1, 1).wait_send()

        pl.when(self.relays)(lambda: self.copy(1, 2).wait_send())


class Chain:
    def __init__(self, ref, owner, chip, plane, core, marks):
        self.ref, self.spot = ref, (chip, plane, core)
        self.sends = marks.many(2)
        self.arrived = marks.one()
        inner = is_inner(plane)
        self.mine = plane == owner
        self.mine_inner, self.mine_outer = self.mine & inner, self.mine & no(inner)
        self.from_end = inner & (plane == away(owner, 1))
        self.from_inner = inner & (plane == away(owner, 3))
        self.from_far = inner & (plane == away(owner, 2))
        self.waits = no(inner) & no(self.mine)

    def copy(self, step, send):
        chip, plane, core = self.spot
        return remote(
            self.ref, self.ref, self.sends(send), self.arrived,
            device(chip, away(plane, step), core),
        )

    def start(self):
        pl.when(self.mine_outer)(lambda: self.copy(1, 0).start())

    def start_inner(self):
        @pl.when(self.mine_inner)
        def _():
            self.copy(3, 1).start()
            self.copy(1, 0).start()

    def relay(self):
        pl.when(self.from_end | self.from_inner)(lambda: self.copy(1, 0).wait_recv())
        pl.when(self.from_end)(lambda: self.copy(3, 0).start())
        pl.when(self.from_inner)(lambda: self.copy(1, 0).start())

    def relay_far(self):
        @pl.when(self.from_far)
        def _():
            self.copy(1, 0).wait_recv()
            self.copy(1, 0).start()

    def arrive(self):
        pl.when(self.waits)(lambda: self.copy(1, 0).wait_recv())

    def finish(self):
        pl.when(no(self.waits))(lambda: self.copy(1, 0).wait_send())
        pl.when(self.mine_inner)(lambda: self.copy(3, 1).wait_send())


class MainTiles:
    def __init__(self, ff, chip, plane, core, marks):
        self.ff, self.spot = ff, (chip, plane, core)
        self.sends, self.here = marks.many(5), marks.many(3)
        self.inner = is_inner(plane)

    def copy(self, slot, to_step, send, receive):
        chip, plane, core = self.spot
        tiles = self.ff.at[:, :, lanes(slot * TILE)]
        return remote(
            tiles, tiles, self.sends(send), self.here(receive),
            device(chip, away(plane, to_step), core),
        )

    def got(self, step):
        self.copy(self.spot[1], 1, 0, step - 1).wait_recv()

    def start(self):
        plane = self.spot[1]
        self.copy(plane, 1, 0, 0).start()
        pl.when(self.inner)(lambda: self.copy(plane, 3, 2, 2).start())

    def relay(self):
        plane = self.spot[1]

        @pl.when(self.inner)
        def _():
            self.got(1)
            self.copy(away(plane, 1), 3, 1, 1).start()
            self.got(3)
            self.copy(away(plane, 3), 1, 3, 1).start()

    def relay_far(self):
        plane = self.spot[1]

        @pl.when(self.inner)
        def _():
            self.got(2)
            self.copy(away(plane, 2), 1, 4, 2).start()

    def arrive(self, step):
        pl.when(no(self.inner))(lambda: self.got(step))

    def finish(self):
        self.copy(self.spot[1], 1, 0, 0).wait_send()

        @pl.when(self.inner)
        def _():
            for send in range(1, 5):
                self.copy(self.spot[1], 1, send, 0).wait_send()


class MainGrads:
    def __init__(self, gout, slots, chip, plane, core, marks):
        self.gout, self.slots, self.spot = gout, slots, (chip, plane, core)
        self.sends, self.here = marks.many(3), marks.many(5)
        self.inner = is_inner(plane)

    def copy(self, slot, to_step, send, receive):
        chip, plane, core = self.spot
        return remote(
            self.gout.at[:, :, lanes(slot * TILE)], self.slots.at[receive],
            self.sends(send), self.here(receive), device(chip, away(plane, to_step), core),
        )

    def start_rows(self, at_rows):
        chip, plane, core = self.spot
        slot = away(plane, 1)
        remote(
            self.gout.at[:, at_rows, lanes(slot * TILE)], self.slots.at[0, :, at_rows],
            self.sends(0), self.here(0), device(chip, slot, core),
        ).start()

    def start(self, step):
        receive = {1: 0, 2: 4, 3: 3}[step]
        self.copy(away(self.spot[1], step), 1, step - 1, receive).start()

    def relay(self, step, add):
        @pl.when(self.inner)
        def _():
            receive = {2: 3, 3: 4}[step]
            self.copy(self.spot[1], 1, 0, receive).wait_recv()
            slot = away(self.spot[1], step)
            add(slot, self.slots.at[receive])
            self.copy(slot, step, step - 1, step - 1).start()

    def total(self, add):
        plane = self.spot[1]
        self.copy(plane, 1, 0, 0).wait_recv()
        add(plane, self.slots.at[0])

        @pl.when(no(self.inner))
        def _():
            self.copy(plane, 1, 0, 1).wait_recv()
            add(plane, self.slots.at[1])

        @pl.when(self.inner)
        def _():
            self.copy(plane, 1, 0, 2).wait_recv()
            add(plane, self.slots.at[2])

    def finish(self):
        for send in range(3):
            self.copy(self.spot[1], 1, send, 0).wait_send()


class Collect:
    def __init__(self, ref, slots, owner, chip, plane, core, marks):
        self.ref, self.slots, self.spot = ref, slots, (chip, plane, core)
        self.send = marks.one()
        self.arrived = marks.many(3)
        inner, inner_owner = is_inner(plane), is_inner(owner)
        self.mine = plane == owner
        self.mine_outer = self.mine & no(inner)
        self.mine_inner = self.mine & inner
        self.near = plane == away(owner, 1)
        second, third = plane == away(owner, 2), plane == away(owner, 3)
        self.hands = no(inner) & (second | third) & no(self.near)
        self.adds_second = inner & second & no(inner_owner)
        self.adds_third = inner & third & inner_owner

    def copy(self, step, slot):
        chip, plane, core = self.spot
        return remote(
            self.ref, self.slots.at[slot], self.send, self.arrived(slot),
            device(chip, away(plane, step), core),
        )

    def start(self):
        pl.when(self.near)(lambda: self.copy(1, 0).start())
        pl.when(self.hands)(lambda: self.copy(1, 2).start())

    def relay(self, add):
        @pl.when(self.adds_second | self.adds_third)
        def _():
            self.copy(1, 2).wait_recv()
            add(self.slots.at[2])

        pl.when(self.adds_second)(lambda: self.copy(2, 1).start())
        pl.when(self.adds_third)(lambda: self.copy(3, 1).start())

    def total(self, add):
        @pl.when(self.mine)
        def _():
            for slot in range(2):
                self.copy(1, slot).wait_recv()
                add(self.slots.at[slot])

    def finish(self):
        pl.when(no(self.mine))(lambda: self.copy(1, 0).wait_send())


def layer_kernel(
    w_gate, w_up, w_down, w_qkv, w_out, conv, gain_mix, gain_ffn, tok, cot,
    out_ff, out_at, out_res, out_tok, out_small, main_got, extra_got, att_got, tail_got,
    ff, at, xs, gs, low2, part, acc3, gout, gat, from_mate, both, got, turned, hid, gg,
    gn, gcol, raw, qs, ks, vs, att, gatt, gproj, mid, gmid, gsum, normed, sending, inv_all,
    inv_sum, small, small_a, small_b, raw_ff, raw_qkv, raw_out, raw_conv, tapped,
    gains, gain_rows, packed, packed_back, at_tail, gat_tail, sem, free_mate, free_chips,
):
    chip, plane, core = place()
    others = other_chips(chip)
    mate = device(chip, plane, 1 - core)
    marks = Marks(sem)
    rows = tok.shape[0]
    width = 4 * rows
    half = tok.shape[1]
    seq = 2 * half
    own_half = lanes(core * half, half)
    first = core * half + chip * TILE
    peers = [device(c, plane, core) for c in others]
    line = [device(chip, away(plane, step), core) for step in (1, 2, 3)]
    sides = [device(c, plane, 1 - core) for c in others]
    line_mates = [device(chip, away(plane, step), 1 - core) for step in (1, 2, 3)]

    barrier = pltpu.get_barrier_semaphore()
    partners = peers + [mate] + sides + line + line_mates
    for partner in partners:
        pl.semaphore_signal(barrier, inc=1, device_id=partner, device_id_type=MESH)

    def block_rows(c):
        return rows_at(c * rows, rows, rows)

    ffn_weights = (w_gate, w_up, w_down)
    ffn_cols = w_gate.shape[1]
    wat, last_tile = gat.at[:, 0], packed_back.at[:, 0:rows]
    early = marks.many(6)
    loads = [
        pltpu.make_async_copy(source, target, early(i))
        for i, (source, target) in enumerate(
            (
                (w_qkv, raw_qkv), (w_out, raw_out), (conv, raw_conv),
                (gain_mix, gain_rows[0]), (gain_ffn, gain_rows[1]),
            )
        )
    ]
    for load in loads:
        load.start()
    for load in loads:
        load.wait()
    for i in range(2):
        gains[i] = gain_rows[i][...].reshape(1, rows)
    tapped[...] = jnp.zeros(tapped.shape, F32)
    tapped[0:CONV, 0 : 2 * HDIM] = raw_conv[...].astype(F32)
    tap_rows = tapped[...].T
    tail = lax.broadcasted_iota(jnp.int32, (HDIM, TILE), 1)
    spare = rows % TILE
    for h in range(2):
        wat[h, :HEADROWS, :rows] = raw_qkv[h * HEADROWS : (h + 1) * HEADROWS]
        wat[h, HEADROWS:, :rows] = raw_out[h * HDIM : (h + 1) * HDIM]
        columns = wat[h, 2 * FEAT : HEADROWS, WIDE - TILE :].astype(F32)
        for j in range(CONV):
            column = tap_rows[h * HDIM : (h + 1) * HDIM, j : j + 1]
            columns = jnp.where(tail == spare + j, column, columns)
        wat[h, 2 * FEAT : HEADROWS, WIDE - TILE :] = columns.astype(BF16)
    pl.semaphore_wait(barrier, len(partners))

    far_core = plane // 2
    holds_att = core == far_core
    holds_extra = holds_att & (chip // 2 == plane % 2)
    extra_plane = 2 * core + chip // 2
    extra_chip = (plane % 2) * 2 + core
    out_rows, in_rows = pl.ds(HEADROWS, HDIM), pl.ds(0, HEADROWS)
    whole = rows // TILE * TILE
    lead = 16
    tail_in, tail_out = pl.ds(0, lead + HEADROWS), pl.ds(lead + HEADROWS, HDIM)

    def leftover(ref, p):
        pair = [ref[c * rows + whole : (c + 1) * rows] for c in (2 * p, 2 * p + 1)]
        return jnp.concatenate(pair, 0)

    def heads_times(h, start, size, right):
        tails = slice(lead + start, lead + start + size)
        total = dot(at_tail[h, 0, tails], leftover(right, 0), 1, 0)
        total += dot(at_tail[h, 1, tails], leftover(right, 1), 1, 0)
        for c in range(4):
            total += dot(
                at[h, c, start : start + size, :whole], right[c * rows : c * rows + whole], 1, 0
            )
        return total

    def heads_spread(start, size, left, where, target):
        tails = slice(lead + start, lead + start + size)

        @pl.loop(0, 4)
        def _(c):
            total = dot(at[0, c, start : start + size, :whole], left[0, :, where], 0, 0)
            total += dot(at[1, c, start : start + size, :whole], left[1, :, where], 0, 0)
            target[rows_at(c * rows, whole, 16), where] = total.astype(BF16)

        for p in range(2):
            total = dot(at_tail[0, p, tails], left[0, :, where], 0, 0)
            total += dot(at_tail[1, p, tails], left[1, :, where], 0, 0)
            for i, c in enumerate((2 * p, 2 * p + 1)):
                size_left = rows - whole
                target[c * rows + whole : (c + 1) * rows, where] = total[
                    i * size_left : (i + 1) * size_left
                ].astype(BF16)

    lane_at = lax.broadcasted_iota(jnp.int32, (1, TILE), 1)

    def pack_heads(start, size):
        a = plane % 2
        for p in range(2):
            even, odd = [
                at[a, 2 * p + i, start : start + size, whole:].astype(F32) for i in range(2)
            ]
            tile = jnp.where(lane_at < spare, even, pltpu.roll(odd, spare, 1))
            at_tail[a, p, lead + start : lead + start + size] = tile.astype(BF16)

    def pack_taps():
        a = plane % 2
        columns = at[a, 0, 2 * FEAT : HEADROWS, whole:].astype(F32).T
        at_tail[a, 0, 0:lead, 0:HDIM] = columns[spare : spare + lead].astype(BF16)

    def unpack_heads(start, size):
        a = plane % 2
        for p in range(2):
            tile = gat_tail[a, p, lead + start : lead + start + size].astype(F32)
            for i, half_tile in enumerate((tile, pltpu.roll(tile, spare, 1))):
                gat[a, 2 * p + i, start : start + size, whole:] = half_tile.astype(BF16)

    def unpack_taps():
        a = plane % 2
        columns = gat_tail[a, 0, 0:lead, 0:HDIM].astype(F32).T
        for c in range(4):
            tile = gat[a, c, 2 * FEAT : HEADROWS, whole:].astype(F32)
            for j in range(CONV):
                tile = jnp.where(tail == spare + j, columns[:, j : j + 1], tile)
            gat[a, c, 2 * FEAT : HEADROWS, whole:] = tile.astype(BF16)

    att_self = [(2 * core + h == chip) & holds_att for h in range(2)]

    class Heads:
        def __init__(self, span):
            self.span, self.local = span, marks.one()
            self.send, self.here = marks.many(2), marks.many(4)

        def copy(self, h):
            return remote(
                wat.at[h, self.span], at.at[plane % 2, chip, self.span], self.send(h),
                self.here(chip), device(2 * core + h, plane, far_core),
            )

        def keep(self, h):
            return pltpu.make_async_copy(
                wat.at[h, self.span], at.at[plane % 2, chip, self.span], self.local
            )

        def start(self):
            for h in range(2):
                pl.when(att_self[h])(lambda: self.keep(h).start())
                pl.when(no(att_self[h]))(lambda: self.copy(h).start())

        def arrive(self):
            for h in range(2):
                pl.when(att_self[h])(lambda: self.keep(h).wait())

            for c in range(4):

                @pl.when(holds_att & no((c == chip) & (core == chip // 2)))
                def _():
                    remote(
                        wat.at[0, self.span], at.at[plane % 2, c, self.span], self.send(0),
                        self.here(c), mate,
                    ).wait_recv()

        def finish(self):
            for h in range(2):
                pl.when(no(att_self[h]))(lambda: self.copy(h).wait_send())

    heads_in, heads_out = Heads(in_rows), Heads(out_rows)
    heads_in.start()
    heads_out.start()

    class Gather:
        def __init__(self, source, target_of, earlier=None):
            self.source, self.target_of = source, target_of
            self.marks = earlier.marks if earlier else [marks.many(6), marks.many(6)] + [
                marks.many(4), marks.many(4), marks.one()
            ]
            self.send, self.here, self.mate_send, self.mate_here, kept = self.marks
            self.keep = pltpu.make_async_copy(source, target_of(chip), kept)
            mine = self.halves(source)
            there = self.halves(target_of(chip))
            self.copies = {
                mark: remote(
                    mine[half], there[half], self.send(mark), self.here(mark), peers[p]
                )
                for mark, half, p in ((0, 0, 0), (3, 1, 1), (1, 1, 0), (2, 0, 1))
            }
            for copy in self.copies.values():
                copy.start()
            self.keep.start()
            self.crossing = []
            self.cross(source, chip, 3)

        def cross(self, source, c, mark):
            copy = remote(
                source, self.target_of(c), self.mate_send(mark), self.mate_here(mark), mate
            )
            copy.start()
            self.crossing.append(copy)

        def halves(self, block):
            size = block.shape[0] // 2
            return block.at[0:size], block.at[size : 2 * size]

        def pass_on(self):
            for mark, half, p, onward in ((0, 0, 0, 4), (3, 1, 1, 5)):
                self.copies[mark].wait_recv()
                block = self.halves(self.target_of(others[p]))[half]
                self.copies[onward] = remote(
                    block, block, self.send(onward), self.here(onward), peers[1 - p]
                )
                self.copies[onward].start()
            for mark, p in ((1, 0), (2, 1)):
                self.copies[mark].wait_recv()
                self.cross(self.target_of(others[p]), others[p], p)

        def arrive(self):
            for mark in (4, 5):
                self.copies[mark].wait_recv()
            self.cross(self.target_of(others[2]), others[2], 2)
            for copy in self.crossing:
                copy.wait_recv()
            self.keep.wait()

        def finish(self):
            for copy in list(self.copies.values()) + self.crossing:
                copy.wait_send()

    tokens_in = Gather(tok, lambda c: xs.at[block_rows(c), own_half])
    gain_send, gain_here = marks.many(3), marks.many(3)
    gain_copies = [
        remote(gains, gn.at[chip], gain_send(p), gain_here(p), peers[p]) for p in range(3)
    ]
    gain_keep = pltpu.make_async_copy(gains, gn.at[chip], marks.one())
    for copy in gain_copies + [gain_keep]:
        copy.start()

    in_line, out_line = [
        [
            Spread(ref, 2 * core + a, chip, plane, core, marks)
            for a in range(2)
            for ref in (at.at[a, :, span, 0:whole], at_tail.at[a, :, tail_span])
        ]
        for span, tail_span in ((in_rows, tail_in), (out_rows, tail_out))
    ]
    heads_in.arrive()

    @pl.when(holds_att)
    def _():
        pack_heads(0, HEADROWS)
        pack_taps()

    for item in in_line:
        item.start()
    heads_out.arrive()
    pl.when(holds_att)(lambda: pack_heads(HEADROWS, HDIM))
    for item in out_line:
        item.start()
    heads_in.finish()
    heads_out.finish()

    short = ffn_cols - 4 * TILE
    for m in range(3):
        load = pltpu.make_async_copy(ffn_weights[m], raw_ff, early(5))
        load.start()
        load.wait()
        last_tile[m, :, 0:short] = raw_ff[:, 4 * TILE :]
        last_tile[m, :, short:] = jnp.zeros((rows, TILE - short), BF16)

    tokens_in.pass_on()
    main_send, main_here, main_local = marks.many(9), marks.many(9), marks.many(3)
    main_here_at = [ff.at[m, block_rows(chip), lanes(plane * TILE)] for m in range(3)]
    mains = [
        remote(
            ffn_weights[m].at[:, lanes(others[p] * TILE)], main_here_at[m],
            main_send(3 * p + m), main_here(3 * p + m), peers[p],
        )
        for p in range(3)
        for m in range(3)
    ]
    mains += [
        pltpu.make_async_copy(
            ffn_weights[m].at[:, lanes(chip * TILE)], main_here_at[m], main_local(m)
        )
        for m in range(3)
    ]
    for copy in mains:
        copy.start()

    extra_send, extra_here, extra_local = marks.one(), marks.many(4), marks.one()
    extra_self = (extra_chip == chip) & holds_att
    last = lanes(4 * TILE)

    def extra_copy():
        return remote(
            last_tile, ff.at[:, block_rows(chip), last], extra_send, extra_here(chip),
            device(extra_chip, plane, far_core),
        )

    def extra_keep():
        return pltpu.make_async_copy(
            last_tile, ff.at[:, block_rows(chip), last], extra_local
        )

    @pl.when(extra_self)
    def _():
        extra_keep().start()

    @pl.when(no(extra_self))
    def _():
        extra_copy().start()

    for item in in_line:
        item.relay()
    tokens_in.arrive()
    cot_in = Gather(cot, lambda c: gs.at[block_rows(c), own_half])
    for copy in gain_copies + [gain_keep]:
        copy.wait()

    for item in out_line:
        item.relay()
    @pl.loop(0, 4)
    def _(c):
        pair = jnp.concatenate(
            [gn[c, 0].astype(F32), gn[c, 1].astype(F32), jnp.zeros((6, rows), F32)], 0
        )
        gcol[block_rows(c), 0:8] = pair.T.astype(BF16)

    step_rows = 64

    def add_squares(i, total):
        x = xs[rows_at(i * step_rows, step_rows, step_rows)].astype(F32)
        return total + jnp.sum((x * x).reshape(step_rows // 8, 8, seq), 0)

    squares = lax.fori_loop(0, width // step_rows, add_squares, jnp.zeros((8, seq), F32))
    inv_all[...] = lax.rsqrt(jnp.sum(squares, 0, keepdims=True) / D + EPSILON)
    tokens_in.finish()
    normed[...] = xs[:, lanes(first)]

    @pl.loop(0, width // step_rows)
    def _(i):
        at_rows = rows_at(i * step_rows, step_rows, step_rows)
        xs[at_rows] = (
            xs[at_rows].astype(F32) * inv_all[...] * gcol[at_rows, 0:1].astype(F32)
        ).astype(BF16)

    for item in in_line:
        item.arrive()

    position = lax.broadcasted_iota(jnp.int32, (1, seq), 1)

    def taps(h):
        columns = at_tail[h, 0, 0:lead, 0:HDIM].astype(F32).T
        return [columns[:, j : j + 1] for j in range(CONV)]

    @pl.loop(0, 2)
    def _(h):
        projected = heads_times(h, 0, HEADROWS, xs)
        qs[h] = (projected[:FEAT].astype(BF16).astype(F32) * FEAT**-0.5).astype(BF16)
        ks[h] = projected[FEAT : 2 * FEAT].astype(BF16)
        values = projected[2 * FEAT :]
        raw[h] = values
        tap = taps(h)
        mixed = tap[0] * values
        for j in range(1, CONV):
            moved = pltpu.roll(values, j, 1)
            mixed += tap[j] * jnp.where(position >= j, moved, 0.0)
        vs[h] = mixed.astype(BF16)

    def kernel_of(h, b):
        seen = (b + 1) * SPAN
        scores = dot(ks[h, :, :seen], qs[h, :, b * SPAN : seen], 0, 0)
        kernel = 1.0 + scores + 0.5 * scores * scores
        key_at = lax.broadcasted_iota(jnp.int32, (seen, SPAN), 0)
        query_at = lax.broadcasted_iota(jnp.int32, (seen, SPAN), 1) + b * SPAN
        visible = key_at <= query_at
        return scores, jnp.where(visible, kernel, 0.0), visible

    @pl.loop(0, 2)
    def _(h):
        for b in range(seq // SPAN):
            seen = (b + 1) * SPAN
            _, kernel, _ = kernel_of(h, b)
            inverse = 1.0 / jnp.sum(kernel, 0, keepdims=True)
            inv_sum[h, :, b * SPAN : seen] = inverse
            weights = (kernel * inverse).astype(BF16)
            att[h, :, b * SPAN : seen] = dot(vs[h, :, :seen], weights, 1, 0).astype(BF16)

    for copy in mains:
        copy.wait()
    main_line = MainTiles(ff, chip, plane, core, marks)
    main_line.start()

    @pl.when(extra_self)
    def _():
        extra_keep().wait()

    @pl.when(no(extra_self))
    def _():
        extra_copy().wait_send()

    for c in range(4):

        @pl.when(holds_extra & no((c == chip) & (core == chip % 2)))
        def _():
            remote(
                last_tile, ff.at[:, block_rows(c), last], extra_send, extra_here(c), mate
            ).wait_recv()

    third = short // 3
    unit_at = lax.broadcasted_iota(jnp.int32, (rows, TILE), 1)

    def pack(source, target):
        @pl.loop(0, 3)
        def _(m):
            fourth = source[m, 3 * rows :, last].astype(F32)
            for b in range(3):
                own = source[m, b * rows : (b + 1) * rows, last].astype(F32)
                moved = pltpu.roll(fourth, (short - b * third) % TILE, 1)
                target[m, b * rows : (b + 1) * rows] = jnp.where(
                    unit_at < short, own, moved
                ).astype(BF16)

    def unpack(source, target):
        @pl.loop(0, 3)
        def _(m):
            fourth = jnp.zeros((rows, TILE), F32)
            for b in range(3):
                block = source[m, b * rows : (b + 1) * rows].astype(F32)
                target[m, b * rows : (b + 1) * rows, last] = jnp.where(
                    unit_at < short, block, 0.0
                ).astype(BF16)
                moved = pltpu.roll(block, (b * third - short) % TILE, 1)
                here = (unit_at >= b * third) & (unit_at < (b + 1) * third)
                fourth = jnp.where(here, moved, fourth)
            target[m, 3 * rows :, last] = fourth.astype(BF16)

    pl.when(holds_extra)(lambda: pack(ff, packed))
    extra_line = Chain(packed, extra_plane, chip, plane, core, marks)
    extra_line.start()

    for item in out_line:
        item.arrive()

    def default_got(i):
        return got.at[i]

    class Sum:
        def __init__(
            self, guard, earlier=None, both=both, got=None, share=True, at_once=True
        ):
            self.marks = earlier.marks if earlier else [marks.many(4), marks.many(4)] + [
                marks.many(6), marks.many(6)
            ]
            self.guard, self.both, self.share, self.at_once = guard, both, share, at_once
            self.got = got or default_got

        def begin(self, fill):
            fill((1 - core) * half)
            send, here = self.marks[:2]
            self.order = (others[2], others[0], others[1], chip)
            self.to_mate = [
                remote(
                    part.at[:, lanes((1 - core) * half + c * TILE)],
                    from_mate.at[:, lanes(c * TILE)], send(i), here(i), mate,
                )
                for i, c in enumerate(self.order)
            ]
            if self.guard:
                pl.semaphore_wait(free_mate, 1)
            for copy in self.to_mate:
                copy.start()
            fill(core * half)

        def release(self):
            pl.semaphore_signal(free_mate, inc=1, device_id=mate, device_id_type=MESH)

        def combine(self):
            self.prepare()
            for i, c in enumerate(self.order):
                self.to_mate[i].wait_recv()
                where, own = lanes(c * TILE), lanes(core * half + c * TILE)

                @pl.loop(0, 4)
                def _(b):
                    at_rows = block_rows(b)
                    self.both[at_rows, where] = (
                        part[at_rows, own].astype(F32) + from_mate[at_rows, where].astype(F32)
                    ).astype(BF16)

                if self.at_once:
                    self.send(i)
            for copy in self.to_mate:
                copy.wait_send()

        def piece(self, upper, c):
            size = width // 2
            return self.both.at[pl.ds(0 if upper else size, size), lanes(c * TILE)]

        def prepare(self):
            size = width // 2
            top, bottom = pl.ds(0, size), pl.ds(size, size)
            send, here = self.marks[2:]
            x, y, across = others
            self.across = [
                remote(self.piece(True, across), self.got(2).at[top], send(0), here(0), peers[0]),
                remote(
                    self.piece(False, across), self.got(2).at[bottom], send(1), here(1), peers[1]
                ),
            ]
            self.plain = [
                remote(self.piece(True, x), self.got(0).at[top], send(2), here(2), peers[0]),
                remote(self.piece(False, y), self.got(1).at[bottom], send(3), here(3), peers[1]),
            ]
            self.added = [
                remote(self.piece(True, y), self.got(1).at[top], send(4), here(4), peers[1]),
                remote(self.piece(False, x), self.got(0).at[bottom], send(5), here(5), peers[0]),
            ]

        def send(self, i):
            if i == 0:
                if self.guard and self.share:
                    pl.semaphore_wait(free_chips, 2)
                for copy in self.across:
                    copy.start()
            elif i < 3:
                self.plain[i - 1].start()

        def send_all(self):
            for i in range(3):
                self.send(i)

        def pass_on(self):
            size = width // 2
            quarter = size // 2
            for i, c in ((0, others[1]), (1, others[0])):
                self.across[i].wait_recv()
                for q in range(2):
                    at_rows = pl.ds(i * size + q * quarter, quarter)
                    self.both[at_rows, lanes(c * TILE)] = (
                        self.both[at_rows, lanes(c * TILE)].astype(F32) + self.got(2)[at_rows].astype(F32)
                    ).astype(BF16)
                self.added[i].start()

        def finish(self, store):
            for copy in self.plain + self.added:
                copy.wait()
            for copy in self.across:
                copy.wait_send()

            @pl.loop(0, 4)
            def _(c):
                at_rows = block_rows(c)
                total = self.both[at_rows, lanes(chip * TILE)].astype(F32)
                for p in range(2):
                    total += self.got(p)[at_rows].astype(F32)
                store(at_rows, total)

            for p in range(2 if self.share else 0):
                pl.semaphore_signal(free_chips, inc=1, device_id=peers[p], device_id_type=MESH)

    def fill_branch(start):
        heads_spread(HEADROWS, HDIM, att, lanes(start, half), part)

    small[...] = jnp.zeros(small.shape, F32)
    square_at = lax.broadcasted_iota(jnp.int32, (1, WIDE), 1)

    def note_square(index, value):
        total = jnp.sum(value * value)
        small[0, 2:3, :] += jnp.where(square_at == index, total, 0.0)

    def store_branch(at_rows, total):
        note_square(0, total)
        mid[at_rows] = normed[at_rows].astype(F32) + total

    branch_sum = Sum(guard=False)
    branch_sum.begin(fill_branch)
    cot_in.pass_on()
    branch_sum.combine()
    branch_sum.release()
    branch_sum.pass_on()
    main_line.relay()
    extra_line.start_inner()
    branch_sum.finish(store_branch)
    middle = mid[...]
    inverse_two = lax.rsqrt(jnp.sum(middle * middle, 0, keepdims=True) / D + EPSILON)

    @pl.loop(0, 4)
    def _(c):
        at_rows = block_rows(c)
        sending[0, at_rows] = (mid[at_rows] * inverse_two * gcol[at_rows, 1:2].astype(F32)).astype(BF16)

    def token_block(c):
        return low2.at[:, lanes(core * half + c * TILE)]

    low_in = Gather(sending.at[0], token_block, tokens_in)
    cot_in.arrive()
    cot_in.finish()

    @pl.loop(0, 4)
    def _(c):
        acc3[block_rows(c)] = jnp.zeros((rows, seq), F32)

    low_in.pass_on()
    low_in.arrive()
    low_in.finish()

    main_line.relay_far()
    extra_line.relay()
    def feed_units(slot):
        where = lanes(slot * TILE)
        unit_rows = rows_at(slot * TILE, TILE, TILE)
        for m in range(3):
            turned[m * TILE : (m + 1) * TILE] = ff[m, :, where].T

        @pl.loop(0, seq // SPAN)
        def _(n):
            span = lanes(n * SPAN, SPAN)
            gate_up = dot(turned[: 2 * TILE], low2[:, span], 1, 0)
            grad_hidden = dot(turned[2 * TILE :], gs[:, span], 1, 0)
            gate, up = gate_up[:TILE], gate_up[TILE:]
            sigmoid = 1.0 / (1.0 + jnp.exp(-gate))
            activated = gate * sigmoid
            hid[unit_rows, span] = (activated * up).astype(BF16)
            gg[:TILE, span] = (
                grad_hidden * up * sigmoid * (1.0 + gate * (1.0 - sigmoid))
            ).astype(BF16)
            gg[TILE:, span] = (grad_hidden * activated).astype(BF16)

    def feed_input(slot, at_rows):
        where = lanes(slot * TILE)
        pair = jnp.concatenate([ff[0, at_rows, where], ff[1, at_rows, where]], 1)
        acc3[at_rows] += dot(pair, gg[...], 1, 0)

    def feed_weights(slot, at_rows):
        where = lanes(slot * TILE)
        unit_rows = rows_at(slot * TILE, TILE, TILE)
        grads = dot(low2[at_rows], gg[...], 1, 1).astype(BF16)
        gout[0, at_rows, where] = grads[:, :TILE]
        gout[1, at_rows, where] = grads[:, TILE:]
        gout[2, at_rows, where] = dot(gs[at_rows], hid[unit_rows], 1, 1).astype(BF16)

    main_back = MainGrads(gout, main_got, chip, plane, core, marks)
    extra_back = Collect(packed_back, extra_got, extra_plane, chip, plane, core, marks)
    load_marks = marks.many(3)

    spare_lanes = [lanes((1 - core) * half + m * TILE) for m in range(3)]

    def add_tiles(slot, source):
        loads = [
            pltpu.make_async_copy(source.at[m], gs.at[:, spare_lanes[m]], load_marks(m))
            for m in range(3)
        ]
        for load in loads:
            load.start()
        for load in loads:
            load.wait()
        where = lanes(slot * TILE)

        @pl.loop(0, 4)
        def _(c):
            at_rows = block_rows(c)
            for m in range(3):
                gout[m, at_rows, where] = (
                    gout[m, at_rows, where].astype(F32)
                    + gs[at_rows, spare_lanes[m]].astype(F32)
                ).astype(BF16)

    def add_extra(source):
        packed_rows = slice(0, 3 * rows)
        loads = [
            pltpu.make_async_copy(source.at[m], gs.at[packed_rows, spare_lanes[m]], load_marks(m))
            for m in range(3)
        ]
        for load in loads:
            load.start()
        for load in loads:
            load.wait()

        @pl.loop(0, 3)
        def _(b):
            at_rows = block_rows(b)
            for m in range(3):
                packed_back[m, at_rows] = (
                    packed_back[m, at_rows].astype(F32)
                    + gs[at_rows, spare_lanes[m]].astype(F32)
                ).astype(BF16)

    slots = [away(plane, 1), plane, away(plane, 2), away(plane, 3)]
    inner = is_inner(plane)

    @pl.loop(0, 4)
    def _(turn):
        pl.when(turn == 2)(lambda: extra_line.relay_far())

        for i, step in ((0, 1), (2, 2), (3, 3)):

            @pl.when(turn == i)
            def _():
                main_line.arrive(step)

        slot = sum((turn == i).astype(jnp.int32) * slots[i] for i in range(4))
        feed_units(slot)

        @pl.loop(0, 4)
        def _(c):
            feed_input(slot, block_rows(c))
            feed_weights(slot, block_rows(c))
            pl.when((turn == 0) & no(inner))(lambda: main_back.start_rows(block_rows(c)))

        for i, step in ((2, 2), (3, 3)):

            @pl.when((turn == i) & no(inner))
            def _():
                main_back.start(step)

    extra_line.arrive()
    unpack(packed, ff)
    feed_units(4)

    @pl.loop(0, 4)
    def _(c):
        feed_input(4, block_rows(c))

    main_line.finish()

    def fill_grad_two(start):
        @pl.loop(0, 4)
        def _(c):
            where = lanes(start, half)
            part[block_rows(c), where] = acc3[block_rows(c), where].astype(BF16)

    def store_gsum(at_rows, total):
        gsum[at_rows] = total

    two_sum = Sum(True, branch_sum)
    two_sum.begin(fill_grad_two)
    two_sum.combine()
    @pl.loop(0, 4)
    def _(c):
        feed_weights(4, block_rows(c))

    two_sum.release()
    pl.when(inner)(lambda: main_back.start(1))
    pack(gout, packed_back)
    extra_back.start()
    main_back.relay(3, add_tiles)
    two_sum.pass_on()

    def fill_ffn(start):
        @pl.loop(0, 4)
        def _(c):
            where = lanes(start, half)
            part[block_rows(c), where] = dot(
                ff[2, block_rows(c)], hid[:, where], 1, 0
            ).astype(BF16)

    ffn_sum = Sum(
        guard=True, both=ff.at[1, :, lanes(0, half)],
        got=lambda i: ff.at[0, :, lanes(i * TILE)], share=False,
        at_once=False,
    )
    ffn_sum.begin(fill_ffn)
    two_sum.finish(store_gsum)

    def norm_back(source, inverse, gain_lane, base, store):
        def add_dots(c, total):
            at_rows = block_rows(c)
            gain = gcol[at_rows, gain_lane : gain_lane + 1].astype(F32)
            return total + jnp.sum(gsum[at_rows] * gain * source(at_rows), 0, keepdims=True)

        dots = lax.fori_loop(0, 4, add_dots, jnp.zeros((1, TILE), F32))
        scaled = inverse * inverse * inverse * dots / D

        @pl.loop(0, 4)
        def _(c):
            at_rows = block_rows(c)
            gain = gcol[at_rows, gain_lane : gain_lane + 1].astype(F32)
            grad, value = gsum[at_rows], source(at_rows)
            store(at_rows, base(at_rows) + (grad * gain * inverse - value * scaled))

        def gain_back():
            @pl.loop(0, 4)
            def _(c):
                at_rows = block_rows(c)
                for_gain = jnp.sum((gsum[at_rows] * source(at_rows) * inverse).T, 0, keepdims=True)
                small[c, gain_lane : gain_lane + 1, 0:rows] = for_gain

        return gain_back

    def store_middle(at_rows, value):
        gmid[at_rows] = value
        sending[1, at_rows] = value.astype(BF16)

    gain_two_back = norm_back(
        lambda r: mid[r], inverse_two, 1, lambda r: gs[r, lanes(first)].astype(F32), store_middle
    )
    mid_in = Gather(sending.at[1], token_block, tokens_in)
    gain_two_back()
    ffn_sum.combine()
    ffn_sum.release()
    mid_in.pass_on()
    ffn_sum.send_all()
    mid_in.arrive()

    @pl.loop(0, 2)
    def _(h):
        total = heads_times(h, HEADROWS, HDIM, low2)
        gatt[h] = total.astype(BF16)

    main_back.relay(2, add_tiles)

    out_back, in_back = [
        [
            Collect(ref, slots_, 2 * core + a, chip, plane, core, marks)
            for a in range(2)
            for ref, slots_ in (
                (gat.at[a, :, span, 0:whole], att_got.at[a, :, :, span]),
                (gat_tail.at[a, :, tail_span], tail_got.at[a, :, :, tail_span]),
            )
        ]
        for span, tail_span in ((out_rows, tail_out), (in_rows, tail_in))
    ]

    def head_grads(left, right, start, size):
        @pl.loop(0, 2)
        def _(h):
            for c in range(4):
                gat[h, c, start : start + size, :whole] = dot(
                    left[h], right[c * rows : c * rows + whole], 1, 1
                ).astype(BF16)
            for p in range(2):
                gat_tail[h, p, lead + start : lead + start + size] = dot(
                    left[h], leftover(right, p), 1, 1
                ).astype(BF16)

    head_grads(att, low2, HEADROWS, HDIM)
    for item in out_back:
        item.start()


    ffn_sum.pass_on()

    @pl.loop(0, 2)
    def _(h):
        grad_keys = jnp.zeros((FEAT, seq), F32)
        grad_values = jnp.zeros((HDIM, seq), F32)

        def padded(value):
            short = seq - value.shape[1]
            if not short:
                return value
            return jnp.concatenate([value, jnp.zeros((value.shape[0], short), F32)], 1)

        for b in range(seq // SPAN):
            seen = (b + 1) * SPAN
            span = slice(b * SPAN, seen)
            scores, kernel, visible = kernel_of(h, b)
            inverse = inv_sum[h, :, span]
            weights = kernel * inverse
            grad_weights = dot(vs[h, :, :seen], gatt[h, :, span], 0, 0)
            grad_values += padded(dot(gatt[h, :, span], weights.astype(BF16), 1, 1))
            dots = jnp.sum(grad_weights * weights, 0, keepdims=True)
            grad_kernel = (grad_weights - dots) * inverse
            grad_scores = jnp.where(visible, grad_kernel * (1.0 + scores), 0.0).astype(BF16)
            gproj[h, :FEAT, span] = (
                dot(ks[h, :, :seen], grad_scores, 1, 0) * FEAT**-0.5
            ).astype(BF16)
            grad_keys += padded(dot(qs[h, :, span], grad_scores, 1, 1))
        gproj[h, FEAT : 2 * FEAT] = grad_keys.astype(BF16)
        tap = taps(h)
        grad_raw = tap[0] * grad_values
        sums = [jnp.sum(grad_values * raw[h], 1, keepdims=True)]
        for j in range(1, CONV):
            masked = jnp.where(position >= j, grad_values, 0.0)
            grad_raw += tap[j] * pltpu.roll(masked, seq - j, 1)
            sums.append(jnp.sum(masked * pltpu.roll(raw[h], j, 1), 1, keepdims=True))
        gproj[h, 2 * FEAT :] = grad_raw.astype(BF16)
        columns = jnp.zeros((HDIM, TILE), F32)
        for j in range(CONV):
            columns = jnp.where(tail == j, sums[j], columns)
        gat_tail[h, 0, 0:lead, 0:HDIM] = columns.T[0:lead].astype(BF16)

    head_grads(gproj, xs, 0, HEADROWS)
    for item in in_back:
        item.start()

    mid_in.finish()

    def store_result(at_rows, total):
        note_square(1, total)
        total = mid[at_rows] + total
        note_square(2, total)
        sending[0, at_rows] = total.astype(BF16)

    def hand_out(source, target):
        send, here = marks.many(3), marks.many(3)
        copies = [
            remote(
                source.at[block_rows(others[p])], target.at[:, lanes(chip * TILE)],
                send(p), here(p), peers[p],
            )
            for p in range(3)
        ]
        copies.append(
            pltpu.make_async_copy(
                source.at[block_rows(chip)], target.at[:, lanes(chip * TILE)], marks.one()
            )
        )
        for copy in copies:
            copy.start()
        return copies

    ffn_sum.finish(store_result)
    pending = hand_out(sending.at[0], out_res)


    def fill_grad_one(start):
        heads_spread(0, HEADROWS, gproj, lanes(start, half), part)

    one_sum = Sum(True, branch_sum)
    one_sum.begin(fill_grad_one)
    one_sum.combine()
    one_sum.release()
    extra_back.relay(add_extra)

    one_sum.pass_on()

    main_back.total(add_tiles)
    back_send, back_here = marks.many(3), marks.many(3)
    mine = lanes(plane * TILE)
    back_to = out_ff.at[:, :, lanes(chip * TILE)]
    backs = [
        remote(
            gout.at[:, block_rows(others[p]), mine], back_to, back_send(p), back_here(p), peers[p]
        )
        for p in range(3)
    ]
    backs.append(
        pltpu.make_async_copy(gout.at[:, block_rows(chip), mine], back_to, marks.one())
    )
    for copy in backs:
        copy.start()
    pending += backs

    one_sum.finish(store_gsum)
    head_marks = marks.many(4)

    def add_head(i, start, size, tail_start, tail_size):
        a, is_tail = i // 2, i % 2
        target, count = (gat_tail, 2) if is_tail else (gat, 4)
        begin, extent = (tail_start, tail_size) if is_tail else (start, size)
        wide = TILE if is_tail else whole

        def add(source):
            loads = [
                pltpu.make_async_copy(
                    source.at[c], part.at[c * BLOCKROWS : c * BLOCKROWS + extent, 0:wide],
                    head_marks(c),
                )
                for c in range(count)
            ]
            for load in loads:
                load.start()
            for load in loads:
                load.wait()
            for c in range(count):
                target[a, c, begin : begin + extent, 0:wide] = (
                    target[a, c, begin : begin + extent, 0:wide].astype(F32)
                    + part[c * BLOCKROWS : c * BLOCKROWS + extent, 0:wide].astype(F32)
                ).astype(BF16)

        return add

    def add_out(i):
        return add_head(i, HEADROWS, HDIM, lead + HEADROWS, HDIM)

    def add_in(i):
        return add_head(i, 0, HEADROWS, 0, lead + HEADROWS)

    for i in range(4):
        out_back[i].relay(add_out(i))

    inverse_own = inv_all[:, lanes(first)]

    def store_tokens(at_rows, value):
        sending[1, at_rows] = value.astype(BF16)

    gain_one_back = norm_back(
        lambda r: normed[r].astype(F32), inverse_own, 0, lambda r: gmid[r], store_tokens
    )
    pending += hand_out(sending.at[1], out_tok)
    gain_one_back()

    for c in range(1, 4):
        small[c, 2:3] = small[0, 2:3]
    a_send, a_here = marks.many(3), marks.many(3)
    trio = [
        remote(small.at[others[p]], small_a.at[p], a_send(p), a_here(p), peers[p])
        for p in range(3)
    ]
    for copy in trio:
        copy.start()

    extra_back.total(add_extra)
    pl.when(holds_extra)(lambda: unpack(packed_back, gout))
    last_send, last_here, last_local = marks.many(4), marks.one(), marks.one()

    def last_copy(c):
        return remote(
            gout.at[:, block_rows(c), last], out_ff.at[:, :, last], last_send(c), last_here,
            device(c, plane, chip % 2),
        )

    def last_keep():
        return pltpu.make_async_copy(
            gout.at[:, block_rows(chip), last], out_ff.at[:, :, last], last_local
        )

    for c in range(4):
        same = (c == chip) & (core == chip % 2)

        @pl.when(holds_extra & same)
        def _():
            last_keep().start()

        @pl.when(holds_extra & no(same))
        def _():
            last_copy(c).start()

    for i in range(4):
        in_back[i].relay(add_in(i))
    class HeadsBack:
        def __init__(self, span):
            self.span, self.local = span, marks.one()
            self.send, self.here = marks.many(4), marks.many(2)

        def same(self, c):
            return (c == chip) & (core == chip // 2)

        def copy(self, c):
            return remote(
                gat.at[plane % 2, c, self.span], out_at.at[chip % 2, self.span], self.send(c),
                self.here(chip % 2), device(c, plane, chip // 2),
            )

        def keep(self):
            return pltpu.make_async_copy(
                gat.at[plane % 2, chip, self.span], out_at.at[chip % 2, self.span], self.local
            )

        def start(self):
            for c in range(4):
                pl.when(holds_att & self.same(c))(lambda: self.keep().start())
                pl.when(holds_att & no(self.same(c)))(lambda: self.copy(c).start())

        def finish(self):
            for c in range(4):
                pl.when(holds_att & self.same(c))(lambda: self.keep().wait())
                pl.when(holds_att & no(self.same(c)))(lambda: self.copy(c).wait_send())

            for h in range(2):

                @pl.when(no(att_self[h]))
                def _():
                    remote(
                        gat.at[0, 0, self.span], out_at.at[h, self.span], self.send(0),
                        self.here(h), mate,
                    ).wait_recv()

    heads_back = [HeadsBack(out_rows), HeadsBack(in_rows)]
    for i in range(4):
        out_back[i].total(add_out(i))
    pl.when(holds_att)(lambda: unpack_heads(HEADROWS, HDIM))
    heads_back[0].start()

    for i in range(4):
        in_back[i].total(add_in(i))

    @pl.when(holds_att)
    def _():
        unpack_heads(0, HEADROWS)
        unpack_taps()

    heads_back[1].start()

    for copy in trio:
        copy.wait()
    small_b[0] = small[chip] + small_a[0] + small_a[1] + small_a[2]
    b_send, b_here = marks.many(7), marks.many(7)
    seven = [
        remote(small_b.at[0], small_b.at[1 + i], b_send(i), b_here(i), to)
        for i, to in enumerate(line + [mate] + line_mates)
    ]
    for copy in seven:
        copy.start()

    for copy in seven:
        copy.wait()
    total = small_b[0]
    for i in range(7):
        total += small_b[1 + i]
    small_a[0] = total
    small_out = pltpu.make_async_copy(small_a.at[0], out_small, marks.one())
    small_out.start()
    pending.append(small_out)
    for item in in_line + out_line + [extra_line, main_back, extra_back] + out_back + in_back:
        item.finish()
    for copy in pending:
        copy.wait()
    for c in range(4):
        same = (c == chip) & (core == chip % 2)
        pl.when(holds_extra & same)(lambda: last_keep().wait())
        pl.when(holds_extra & no(same))(lambda: last_copy(c).wait_send())

    @pl.when(no(extra_self))
    def _():
        last_copy(0).wait_recv()

    for item in heads_back:
        item.finish()

    pl.semaphore_wait(free_mate, 1)
    pl.semaphore_wait(free_chips, 2)
    assert marks.used <= MARKS, marks.used


def dma(*shape):
    return pltpu.SemaphoreType.DMA(shape)


def run_layer(w_gate, w_up, w_down, w_qkv, w_out, conv, gain_mix, gain_ffn, tok, cot):
    rows, half = tok.shape
    width, seq = 4 * rows, 2 * half
    shape = jax.ShapeDtypeStruct
    vmem = pltpu.VMEM
    tiles = (3, width, TILE)
    head = (4, BLOCKROWS, WIDE)
    return pl.pallas_call(
        layer_kernel,
        out_shape=[
            shape((3, rows, 5 * TILE), BF16),
            shape((2, BLOCKROWS, WIDE), BF16),
            shape((rows, half), BF16),
            shape((rows, half), BF16),
            shape((8, WIDE), F32),
            shape((5,) + tiles, BF16),
            shape((3, 3, 3 * rows, TILE), BF16),
            shape((2, 3, 4, BLOCKROWS, rows // TILE * TILE), BF16),
            shape((2, 3, 2, 16 + BLOCKROWS, TILE), BF16),
        ],
        in_specs=[ANY] * 10,
        out_specs=[ANY] * 9,
        scratch_shapes=[
            vmem((3, width, 5 * TILE), BF16),
            vmem((2,) + head, BF16),
            vmem((width, seq), BF16),
            vmem((width, seq), BF16),
            vmem((width, seq), BF16),
            vmem((width, seq), BF16),
            vmem((width, seq), F32),
            vmem((3, width, 5 * TILE), BF16),
            vmem((2,) + head, BF16),
            vmem((width, half), BF16),
            vmem((width, half), BF16),
            vmem((3, width, TILE), BF16),
            vmem((3 * TILE, width), BF16),
            vmem((5 * TILE, seq), BF16),
            vmem((2 * TILE, seq), BF16),
            vmem((4, 2, 1, rows), BF16),
            vmem((width, TILE), BF16),
            vmem((2, HDIM, seq), F32),
            vmem((2, FEAT, seq), BF16),
            vmem((2, FEAT, seq), BF16),
            vmem((2, HDIM, seq), BF16),
            vmem((2, HDIM, seq), BF16),
            vmem((2, HDIM, seq), BF16),
            vmem((2, HEADROWS, seq), BF16),
            vmem((width, TILE), F32),
            vmem((width, TILE), F32),
            vmem((width, TILE), F32),
            vmem((width, TILE), BF16),
            vmem((2, width, TILE), BF16),
            vmem((1, seq), F32),
            vmem((2, 1, seq), F32),
            vmem((4, 8, WIDE), F32),
            vmem((3, 8, WIDE), F32),
            vmem((8, 8, WIDE), F32),
            vmem(w_gate.shape, BF16),
            vmem(w_qkv.shape, BF16),
            vmem(w_out.shape, BF16),
            vmem(conv.shape, BF16),
            vmem((8, 2 * TILE), F32),
            vmem((2, 1, rows), BF16),
            [vmem((rows,), BF16)] * 2,
            vmem((3, 3 * rows, TILE), BF16),
            vmem((3, 3 * rows, TILE), BF16),
            vmem((2, 2, 16 + BLOCKROWS, TILE), BF16),
            vmem((2, 2, 16 + BLOCKROWS, TILE), BF16),
            dma(MARKS),
            pltpu.SemaphoreType.REGULAR,
            pltpu.SemaphoreType.REGULAR,
        ],
        compiler_params=pltpu.CompilerParams(
            collective_id=0, has_side_effects=True, vmem_limit_bytes=63 * 2**20
        ),
        name="layer",
    )(w_gate, w_up, w_down, w_qkv, w_out, conv, gain_mix, gain_ffn, tok, cot)


def outputs_kernel(
    count, ff, at, res, tok, small, to_res, to_tok, to_qkv, to_conv, to_out, to_gate, to_up, to_down,
    to_mix, to_ffn, to_rms, ff_in, at_in, res_in, tok_in, small_in, tok_out, qkv_out, conv_out, out_out,
    ff_out, rms_out, sem,
):
    rows, cols = to_gate.shape
    marks = Marks(sem)
    loads = [
        pltpu.make_async_copy(source, target, marks.one())
        for source, target in (
            [(tok, tok_in), (at, at_in), (res, res_in)] + [(ff.at[m], ff_in.at[m]) for m in range(3)]
            + [(small, small_in)]
        )
    ]
    for load in loads:
        load.start()
    stores = []

    def store(source, target):
        stores.append(pltpu.make_async_copy(source, target, marks.one()))
        stores[-1].start()

    loads[0].wait()
    tok_out[...] = tok_in[...].astype(F32)
    store(tok_out, to_tok)
    loads[1].wait()
    for h in range(2):
        qkv_out[h * HEADROWS : (h + 1) * HEADROWS] = at_in[h, :HEADROWS, :rows].astype(F32)
        out_out[h * HDIM : (h + 1) * HDIM] = at_in[h, HEADROWS:, :rows].astype(F32)
    store(qkv_out, to_qkv)
    store(out_out, to_out)
    loads[2].wait()
    store(res_in, to_res)
    taps = jnp.concatenate(
        [at_in[h, 2 * FEAT : HEADROWS, WIDE - TILE :].astype(F32) for h in range(2)], 0
    )
    conv_out[...] = taps.T[rows % TILE : rows % TILE + CONV]
    store(conv_out, to_conv)
    for m, target in enumerate((to_gate, to_up, to_down)):
        loads[3 + m].wait()
        ff_out[m] = ff_in[m, :, :cols].astype(F32)
        store(ff_out.at[m], target)
    loads[6].wait()
    for i, target in enumerate((to_mix, to_ffn, to_rms)):
        row = small_in[i : i + 1, : target.shape[0]].reshape(target.shape[0])
        rms_out[i][...] = jnp.sqrt(row / count) if i == 2 else row
        store(rms_out[i], target)
    for copy in stores:
        copy.wait()


def outputs(ff, at, res, tok, small, ffn_cols, count):
    rows, half = tok.shape
    shape = jax.ShapeDtypeStruct
    shapes = [
        (rows, half), (2 * HEADROWS, rows), (CONV, 2 * HDIM), (2 * HDIM, rows),
        (rows, ffn_cols), (rows, ffn_cols), (rows, ffn_cols), (rows,), (rows,), (3,),
    ]
    vmem = pltpu.VMEM
    return pl.pallas_call(
        functools.partial(outputs_kernel, count),
        out_shape=[shape(res.shape, BF16)] + [shape(s, F32) for s in shapes],
        in_specs=[ANY] * 5,
        out_specs=[ANY] * 11,
        scratch_shapes=[
            vmem(ff.shape, BF16), vmem(at.shape, BF16), vmem(res.shape, BF16), vmem(tok.shape, BF16),
            vmem(small.shape, F32), vmem(shapes[0], F32), vmem(shapes[1], F32),
            vmem(shapes[2], F32), vmem(shapes[3], F32), vmem((3,) + shapes[4], F32),
            [vmem(s, F32) for s in shapes[7:]], dma(24),
        ],
        compiler_params=pltpu.CompilerParams(vmem_limit_bytes=60 * 2**20),
        name="outputs",
    )(ff, at, res, tok, small)


def on_device_full(
    tokens, cotangent, w_qkv, conv_weight, w_out, w_gate, w_up, w_down, gain_mix, gain_ffn
):
    rows, half = tokens.shape
    ffn_cols = w_gate.shape[1]
    out_ff, out_at, out_res, out_tok, small = run_layer(
        w_gate, w_up, w_down, w_qkv.T, w_out, conv_weight, gain_mix, gain_ffn,
        tokens, cotangent,
    )[:5]
    result, to_tok, to_qkv, *others = outputs(
        out_ff, out_at, out_res, out_tok, small, ffn_cols, 8 * half * 4 * rows
    )
    return (result, to_tok, to_qkv.T, *others)


def on_device(tokens, cotangent, lengths, deal_order, *weights):
    total_rows = tokens.shape[1] * lax.axis_size("col")
    if (
        lengths.shape[0] * LONGEST == total_rows
        and lax.axis_size("row") == 4
        and lax.axis_size("col") == 8
        and total_rows == 4 * LONGEST
        and weights[0].shape[1] == 2 * HEADROWS
        and weights[3].shape[1] == 4 * TILE + 96
    ):
        return on_device_full(tokens, cotangent, *weights)
    return on_device_general(tokens, cotangent, lengths, deal_order, *weights)


def solution(mesh):
    in_specs = (
        P("row", "col"),
        P("row", "col"),
        P(),
        P(),
        P("row", "col"),
        P(None, "col"),
        P("col", "row"),
        P("row", "col"),
        P("row", "col"),
        P("row", "col"),
        P("row"),
        P("row"),
    )
    out_specs = (
        P("row", "col"),
        P("row", "col"),
        P("row", "col"),
        P(None, "col"),
        P("col", "row"),
        P("row", "col"),
        P("row", "col"),
        P("row", "col"),
        P("row"),
        P("row"),
        P(),
    )
    return jax.shard_map(
        on_device, mesh=mesh, in_specs=in_specs, out_specs=out_specs, check_vma=False
    )
```

```python
import functools

import jax
import jax.numpy as jnp
from jax import lax
from jax.experimental import pallas as pl
from jax.experimental.pallas import tpu as pltpu
from jax.sharding import PartitionSpec as P

D = 1792
FEAT = 16
CONV = 3
LONGEST = 1024
HDIM = 112


EPSILON = 1e-06


def dealing(lengths, deal_order, total_rows):
    seq_ids = jnp.arange(lengths.shape[0], dtype=jnp.int32)
    chosen = (deal_order[:, None] == seq_ids[None, :]).astype(jnp.int32)
    dealt_lengths = jnp.sum(chosen * lengths[None, :], 1)
    given_start = jnp.cumsum(lengths) - lengths
    dealt_start = jnp.cumsum(dealt_lengths) - dealt_lengths
    given_of_dealt = jnp.sum(chosen * given_start[None, :], 1)
    dealt_of_given = jnp.sum(chosen * dealt_start[:, None], 0)
    places = jnp.arange(total_rows, dtype=jnp.int32)
    in_dealt = (places[:, None] >= dealt_start[None, :]) & (
        places[:, None] < (dealt_start + dealt_lengths)[None, :]
    )
    in_given = (places[:, None] >= given_start[None, :]) & (
        places[:, None] < (given_start + lengths)[None, :]
    )
    source = places + jnp.sum(jnp.where(in_dealt, (given_of_dealt - dealt_start)[None, :], 0), 1)
    target = places + jnp.sum(jnp.where(in_given, (dealt_of_given - given_start)[None, :], 0), 1)
    offsets = places - jnp.sum(jnp.where(in_dealt, dealt_start[None, :], 0), 1)
    return (source, target, offsets)


def convolve(raw_values, kernel_conv, offsets):
    mixed = kernel_conv[0] * raw_values
    for delay_step in range(1, CONV):
        moved = jnp.concatenate(
            [jnp.zeros_like(raw_values[:delay_step]), raw_values[:-delay_step]], 0
        )
        mixed = mixed + kernel_conv[delay_step] * jnp.where(
            (offsets >= delay_step)[:, None, None], moved, 0.0
        )
    return mixed


def convolve_back(grad_mixed, raw_values, kernel_conv, offsets):
    grad_raw = kernel_conv[0] * grad_mixed
    sums_list = [jnp.sum(grad_mixed * raw_values, 0)]
    for delay_step in range(1, CONV):
        masked = jnp.where((offsets >= delay_step)[:, None, None], grad_mixed, 0.0)
        pulled = jnp.concatenate([masked[delay_step:], jnp.zeros_like(masked[:delay_step])], 0)
        grad_raw = grad_raw + kernel_conv[delay_step] * pulled
        moved = jnp.concatenate(
            [jnp.zeros_like(raw_values[:delay_step]), raw_values[:-delay_step]], 0
        )
        sums_list.append(jnp.sum(masked * moved, 0))
    return (grad_raw, jnp.stack(sums_list))


def bin_scores(query, keys, offsets):
    scores = jnp.einsum("thf,shf->hts", query, keys, preferred_element_type=jnp.float32) * FEAT ** (
        -0.5
    )
    positions = jnp.arange(query.shape[0], dtype=jnp.int32)
    visible = (positions[None, :] <= positions[:, None]) & (
        positions[:, None] - positions[None, :] <= offsets[:, None]
    )
    kernel = jnp.where(visible[None], 1.0 + scores + 0.5 * scores * scores, 0.0)
    return (scores, visible, kernel)


def attend_bin(pieces):
    query, keys, values, offsets = pieces
    scores, visible, kernel = bin_scores(query, keys, offsets)
    weights = (kernel / jnp.sum(kernel, -1, keepdims=True)).astype(jnp.bfloat16)
    return jnp.einsum("hts,shd->thd", weights, values, preferred_element_type=jnp.float32)


def attend_back(pieces):
    query, keys, values, offsets, grad_attend = pieces
    scores, visible, kernel = bin_scores(query, keys, offsets)
    totals = jnp.sum(kernel, -1, keepdims=True)
    weights = kernel / totals
    grad_weights = jnp.einsum(
        "thd,shd->hts", grad_attend, values, preferred_element_type=jnp.float32
    )
    grad_values = jnp.einsum(
        "hts,thd->shd",
        weights.astype(jnp.bfloat16),
        grad_attend,
        preferred_element_type=jnp.float32,
    )
    grad_kernel = (grad_weights - jnp.sum(grad_weights * weights, -1, keepdims=True)) / totals
    grad_scores = jnp.where(visible[None], grad_kernel * (1.0 + scores), 0.0).astype(jnp.bfloat16)
    grad_query = jnp.einsum(
        "hts,shf->thf", grad_scores, keys, preferred_element_type=jnp.float32
    ) * FEAT ** (-0.5)
    grad_keys = jnp.einsum(
        "hts,thf->shf", grad_scores, query, preferred_element_type=jnp.float32
    ) * FEAT ** (-0.5)
    return (grad_query, grad_keys, grad_values)


def times_transposed(left, right):
    return lax.dot_general(
        left, right, (((1,), (1,)), ((), ())), preferred_element_type=jnp.float32
    )


def tokens_product(left, right):
    return lax.dot_general(
        left, right, (((0,), (0,)), ((), ())), preferred_element_type=jnp.float32
    )


def plain_product(left, right):
    return jnp.dot(left, right, preferred_element_type=jnp.float32)


def gather_cols(values):
    return lax.all_gather(values, "col", axis=0, tiled=True)


def gather_rows(values):
    return lax.all_gather(values, "row", axis=0, tiled=True)


def grad_gather_cols(values):
    return lax.all_gather(values, "col", axis=1, tiled=True)


def grad_gather_rows(values):
    return lax.all_gather(values, "row", axis=0, tiled=True)


def width_total(values):
    return lax.psum(values, "row")


def forward_rows(gathered, row_index, weight, rows_here):

    def partial_term(row_start, row_count):
        picked = jnp.take(gathered, row_index, axis=0)
        return jnp.dot(picked, weight, preferred_element_type=jnp.float32)

    return lax.psum_scatter(
        partial_term(jnp.int32(0), rows_here * lax.axis_size("row")),
        "row",
        scatter_dimension=0,
        tiled=True,
    )


def forward_cols(gathered, row_index, weight, rows_here, product):

    def partial_term(row_start, row_count):
        picked = jnp.take(gathered, row_index, axis=0)
        return product(picked, weight)

    return lax.psum_scatter(
        partial_term(jnp.int32(0), lax.axis_size("col") * rows_here).astype(jnp.bfloat16),
        "col",
        scatter_dimension=0,
        tiled=True,
    ).astype(jnp.float32)


def backward_rows(gathered, row_index, weight, rows_here, contract):

    def partial_term(row_start, row_count):
        picked = jnp.take(gathered, row_index, axis=1)
        return lax.dot_general(
            picked, weight, (((0,), (contract,)), ((), ())), preferred_element_type=jnp.float32
        )

    return lax.psum_scatter(
        partial_term(jnp.int32(0), lax.axis_size("row") * rows_here).astype(jnp.bfloat16),
        "row",
        scatter_dimension=0,
        tiled=True,
    ).astype(jnp.float32)


def backward_cols(gathered, row_index, weight, rows_here):

    def partial_term(row_start, row_count):
        picked = jnp.take(gathered, row_index, axis=0)
        return times_transposed(picked, weight)

    return lax.psum_scatter(
        partial_term(jnp.int32(0), lax.axis_size("col") * rows_here).astype(jnp.bfloat16),
        "col",
        scatter_dimension=0,
        tiled=True,
    ).astype(jnp.float32)


def norm_forward(values, norm_gain):
    totals = width_total(jnp.sum(values * values, -1))
    inverse = lax.rsqrt(totals / D + EPSILON)
    return (values * inverse[:, None] * norm_gain, inverse)


def norm_back(values, inverse, norm_gain, grad_normed, dot_sums):
    cubed = inverse * inverse * inverse
    return grad_normed * norm_gain * inverse[:, None] - values * (cubed * dot_sums / D)[:, None]


def on_device_general(
    tokens,
    cotangent,
    lengths,
    deal_order,
    w_qkv,
    conv_weight,
    w_out,
    w_gate,
    w_up,
    w_down,
    gain_mix,
    gain_ffn,
):
    local_rows = tokens.shape[1]
    total_rows = local_rows * lax.axis_size("col")
    group_rows = total_rows // lax.axis_size("row")
    bin_count = group_rows // LONGEST
    heads_here = w_out.shape[0] // HDIM
    ffn_cols = w_gate.shape[1]
    source, target, offsets = dealing(lengths, deal_order, total_rows)
    group_offsets = lax.dynamic_slice_in_dim(
        offsets, lax.axis_index("row") * group_rows, group_rows
    )
    inputs = tokens.astype(jnp.float32).T
    gain_one = gain_mix.astype(jnp.float32)
    gain_two = gain_ffn.astype(jnp.float32)
    both_weights = jnp.concatenate([w_gate, w_up], 1)
    normed_one, inverse_one = norm_forward(inputs, gain_one)
    low_one = normed_one.astype(jnp.bfloat16)
    all_one = gather_cols(low_one)
    projected = forward_rows(all_one, source, w_qkv, group_rows)
    projected = projected.reshape(group_rows, heads_here, 2 * FEAT + HDIM)
    query = projected[:, :, :FEAT].astype(jnp.bfloat16)
    keys = projected[:, :, FEAT : 2 * FEAT].astype(jnp.bfloat16)
    raw_values = projected[:, :, 2 * FEAT :]
    kernel_conv = conv_weight.astype(jnp.float32).reshape(CONV, heads_here, HDIM)
    values = convolve(raw_values, kernel_conv, group_offsets).astype(jnp.bfloat16)
    binned = (
        query.reshape(bin_count, LONGEST, heads_here, FEAT),
        keys.reshape(bin_count, LONGEST, heads_here, FEAT),
        values.reshape(bin_count, LONGEST, heads_here, HDIM),
        group_offsets.reshape(bin_count, LONGEST),
    )
    attended = (
        lax.map(attend_bin, binned).reshape(group_rows, heads_here * HDIM).astype(jnp.bfloat16)
    )
    all_attended = gather_rows(attended)
    branch_mix = forward_cols(all_attended, target, w_out, local_rows, plain_product)
    middle = inputs + branch_mix
    normed_two, inverse_two = norm_forward(middle, gain_two)
    low_two = normed_two.astype(jnp.bfloat16)
    all_two = gather_cols(low_two)
    gate_up = forward_rows(all_two, source, both_weights, group_rows)
    gate = gate_up[:, :ffn_cols]
    up_proj = gate_up[:, ffn_cols:]
    activated = jax.nn.silu(gate)
    hidden = (activated * up_proj).astype(jnp.bfloat16)
    all_hidden = gather_rows(hidden)
    branch_ffn = forward_cols(all_hidden, target, w_down, local_rows, times_transposed)
    result_full = middle + branch_ffn
    grad_result = cotangent.astype(jnp.float32).T
    all_grad_ffn = grad_gather_cols(cotangent)
    hidden_again = gather_rows(hidden)
    grad_down = jnp.dot(
        jnp.take(all_grad_ffn, source, axis=1), hidden_again, preferred_element_type=jnp.float32
    )
    grad_hidden = backward_rows(all_grad_ffn, source, w_down, group_rows, 0)
    gate_sigmoid = jax.nn.sigmoid(gate)
    grad_gate_part = grad_hidden * up_proj * gate_sigmoid * (1.0 + gate * (1.0 - gate_sigmoid))
    grad_up_part = grad_hidden * activated
    grad_gate_up = jnp.concatenate([grad_gate_part, grad_up_part], 1).astype(jnp.bfloat16)
    all_grad_gate_up = grad_gather_rows(grad_gate_up)
    two_again = gather_cols(low_two)
    grad_both = tokens_product(jnp.take(two_again, source, axis=0), all_grad_gate_up)
    grad_normed_two = backward_cols(all_grad_gate_up, target, both_weights, local_rows)
    dots_two = width_total(jnp.sum(grad_normed_two * gain_two * middle, -1))
    grad_middle = grad_result + norm_back(middle, inverse_two, gain_two, grad_normed_two, dots_two)
    gain_part_two = jnp.sum(grad_normed_two * middle * inverse_two[:, None], 0)
    low_grad_middle = grad_middle.T.astype(jnp.bfloat16)
    all_grad_middle = grad_gather_cols(low_grad_middle)
    attended_again = gather_rows(attended)
    grad_out = lax.dot_general(
        attended_again,
        jnp.take(all_grad_middle, source, axis=1),
        (((0,), (1,)), ((), ())),
        preferred_element_type=jnp.float32,
    )
    grad_attended = backward_rows(all_grad_middle, source, w_out, group_rows, 1).astype(
        jnp.bfloat16
    )
    binned_back = binned + (grad_attended.reshape(bin_count, LONGEST, heads_here, HDIM),)
    grad_query, grad_keys, grad_values = lax.map(attend_back, binned_back)
    grad_values = grad_values.reshape(group_rows, heads_here, HDIM)
    grad_raw, conv_part = convolve_back(grad_values, raw_values, kernel_conv, group_offsets)
    grad_projected = jnp.concatenate(
        [
            grad_query.reshape(group_rows, heads_here, FEAT),
            grad_keys.reshape(group_rows, heads_here, FEAT),
            grad_raw,
        ],
        2,
    )
    grad_projected = grad_projected.reshape(group_rows, heads_here * (2 * FEAT + HDIM)).astype(
        jnp.bfloat16
    )
    all_grad_projected = grad_gather_rows(grad_projected)
    one_again = gather_cols(low_one)
    grad_qkv = tokens_product(jnp.take(one_again, source, axis=0), all_grad_projected)
    grad_normed_one = backward_cols(all_grad_projected, target, w_qkv, local_rows)
    squares = jnp.stack(
        [
            jnp.sum(branch_mix * branch_mix),
            jnp.sum(branch_ffn * branch_ffn),
            jnp.sum(result_full * result_full),
        ]
    )
    dots_one, grad_conv, squares_rows = width_total(
        (
            jnp.sum(grad_normed_one * gain_one * inputs, -1),
            conv_part.reshape(CONV, heads_here * HDIM),
            squares,
        )
    )
    grad_tokens = grad_middle + norm_back(inputs, inverse_one, gain_one, grad_normed_one, dots_one)
    gain_part_one = jnp.sum(grad_normed_one * inputs * inverse_one[:, None], 0)
    grad_gain_mix, grad_gain_ffn, squares_all = lax.psum(
        (gain_part_one, gain_part_two, squares_rows), "col"
    )
    rms_values = jnp.sqrt(squares_all / (total_rows * D))
    return (
        result_full.T.astype(jnp.bfloat16),
        grad_tokens.T,
        grad_qkv,
        grad_conv,
        grad_out,
        grad_both[:, :ffn_cols],
        grad_both[:, ffn_cols:],
        grad_down,
        grad_gain_mix,
        grad_gain_ffn,
        rms_values,
    )


HEADROWS = 2 * FEAT + HDIM
BLOCKROWS = HEADROWS + HDIM
TILE = 128
WIDE = 512
SPAN = 256
MARKS = 292
MESH = pl.DeviceIdType.MESH
ANY = pl.BlockSpec(memory_space=pl.ANY)
F32, BF16 = jnp.float32, jnp.bfloat16


def place():
    column = lax.axis_index("col")
    return lax.axis_index("row"), column // 2, column % 2


def device(chip, plane, core):
    return (chip, plane * 2 + core)


def other_chips(chip):
    y, x = chip // 2, chip % 2
    return (y * 2 + 1 - x, (1 - y) * 2 + x, (1 - y) * 2 + 1 - x)


def away(plane, step):
    if step == 1:
        return plane + 1 - 2 * (plane % 2)
    if step == 2:
        return (plane + 2) % 4
    return 3 - plane


def is_inner(plane):
    return ((plane + 1) // 2) % 2 == 1


def remote(source, target, send, receive, to):
    return pltpu.make_async_remote_copy(
        src_ref=source,
        dst_ref=target,
        send_sem=send,
        recv_sem=receive,
        device_id=to,
        device_id_type=MESH,
    )


def lanes(start, size=TILE):
    return pl.ds(pl.multiple_of(start, TILE), size)


def rows_at(start, size, step):
    return pl.ds(pl.multiple_of(start, step), size)


def no(flag):
    return jnp.logical_not(flag)


def dot(a, b, over_a, over_b):
    return lax.dot_general(
        a, b, (((over_a,), (over_b,)), ((), ())), preferred_element_type=F32
    )


class Marks:
    def __init__(self, ref):
        self.ref, self.used = ref, 0

    def one(self):
        self.used += 1
        return self.ref.at[self.used - 1]

    def many(self, count):
        base = self.used
        self.used += count
        return lambda i: self.ref.at[base + i]


class Spread:
    def __init__(self, ref, owner, chip, plane, core, marks):
        self.ref, self.spot = ref, (chip, plane, core)
        self.sends = marks.many(3)
        self.arrived = marks.one()
        inner = is_inner(plane)
        self.mine = plane == owner
        self.outer_owner = self.mine & no(inner)
        self.inner_owner = self.mine & inner
        far = (plane == away(owner, 2)) | ((plane == away(owner, 3)) & is_inner(owner))
        self.relays = inner & far

    def copy(self, step, send):
        chip, plane, core = self.spot
        return remote(
            self.ref, self.ref, self.sends(send), self.arrived,
            device(chip, away(plane, step), core),
        )

    def start(self):
        pl.when(self.outer_owner)(lambda: self.copy(2, 1).start())
        pl.when(self.inner_owner)(lambda: self.copy(3, 1).start())
        pl.when(self.mine)(lambda: self.copy(1, 0).start())

    def relay(self):
        @pl.when(self.relays)
        def _():
            self.copy(1, 2).wait_recv()
            self.copy(1, 2).start()

    def arrive(self):
        pl.when(no(self.mine | self.relays))(lambda: self.copy(1, 2).wait_recv())

    def finish(self):
        @pl.when(self.mine)
        def _():
            self.copy(1, 0).wait_send()
            self.copy(1, 1).wait_send()

        pl.when(self.relays)(lambda: self.copy(1, 2).wait_send())


class Chain:
    def __init__(self, ref, owner, chip, plane, core, marks):
        self.ref, self.spot = ref, (chip, plane, core)
        self.sends = marks.many(2)
        self.arrived = marks.one()
        inner = is_inner(plane)
        self.mine = plane == owner
        self.mine_inner, self.mine_outer = self.mine & inner, self.mine & no(inner)
        self.from_end = inner & (plane == away(owner, 1))
        self.from_inner = inner & (plane == away(owner, 3))
        self.from_far = inner & (plane == away(owner, 2))
        self.waits = no(inner) & no(self.mine)

    def copy(self, step, send):
        chip, plane, core = self.spot
        return remote(
            self.ref, self.ref, self.sends(send), self.arrived,
            device(chip, away(plane, step), core),
        )

    def start(self):
        pl.when(self.mine_outer)(lambda: self.copy(1, 0).start())

    def start_inner(self):
        @pl.when(self.mine_inner)
        def _():
            self.copy(3, 1).start()
            self.copy(1, 0).start()

    def relay(self):
        pl.when(self.from_end | self.from_inner)(lambda: self.copy(1, 0).wait_recv())
        pl.when(self.from_end)(lambda: self.copy(3, 0).start())
        pl.when(self.from_inner)(lambda: self.copy(1, 0).start())

    def relay_far(self):
        @pl.when(self.from_far)
        def _():
            self.copy(1, 0).wait_recv()
            self.copy(1, 0).start()

    def arrive(self):
        pl.when(self.waits)(lambda: self.copy(1, 0).wait_recv())

    def finish(self):
        pl.when(no(self.waits))(lambda: self.copy(1, 0).wait_send())
        pl.when(self.mine_inner)(lambda: self.copy(3, 1).wait_send())


class MainTiles:
    def __init__(self, ff, chip, plane, core, marks):
        self.ff, self.spot = ff, (chip, plane, core)
        self.sends, self.here = marks.many(5), marks.many(3)
        self.inner = is_inner(plane)

    def copy(self, slot, to_step, send, receive):
        chip, plane, core = self.spot
        tiles = self.ff.at[:, :, lanes(slot * TILE)]
        return remote(
            tiles, tiles, self.sends(send), self.here(receive),
            device(chip, away(plane, to_step), core),
        )

    def got(self, step):
        self.copy(self.spot[1], 1, 0, step - 1).wait_recv()

    def start(self):
        plane = self.spot[1]
        self.copy(plane, 1, 0, 0).start()
        pl.when(self.inner)(lambda: self.copy(plane, 3, 2, 2).start())

    def relay(self):
        plane = self.spot[1]

        @pl.when(self.inner)
        def _():
            self.got(1)
            self.copy(away(plane, 1), 3, 1, 1).start()
            self.got(3)
            self.copy(away(plane, 3), 1, 3, 1).start()

    def relay_far(self):
        plane = self.spot[1]

        @pl.when(self.inner)
        def _():
            self.got(2)
            self.copy(away(plane, 2), 1, 4, 2).start()

    def arrive(self, step):
        pl.when(no(self.inner))(lambda: self.got(step))

    def finish(self):
        self.copy(self.spot[1], 1, 0, 0).wait_send()

        @pl.when(self.inner)
        def _():
            for send in range(1, 5):
                self.copy(self.spot[1], 1, send, 0).wait_send()


class MainGrads:
    def __init__(self, gout, slots, chip, plane, core, marks):
        self.gout, self.slots, self.spot = gout, slots, (chip, plane, core)
        self.sends, self.here = marks.many(3), marks.many(5)
        self.inner = is_inner(plane)

    def copy(self, slot, to_step, send, receive):
        chip, plane, core = self.spot
        return remote(
            self.gout.at[:, :, lanes(slot * TILE)], self.slots.at[receive],
            self.sends(send), self.here(receive), device(chip, away(plane, to_step), core),
        )

    def start_rows(self, at_rows):
        chip, plane, core = self.spot
        slot = away(plane, 1)
        remote(
            self.gout.at[:, at_rows, lanes(slot * TILE)], self.slots.at[0, :, at_rows],
            self.sends(0), self.here(0), device(chip, slot, core),
        ).start()

    def start(self, step):
        receive = {1: 0, 2: 4, 3: 3}[step]
        self.copy(away(self.spot[1], step), 1, step - 1, receive).start()

    def relay(self, step, add):
        @pl.when(self.inner)
        def _():
            receive = {2: 3, 3: 4}[step]
            self.copy(self.spot[1], 1, 0, receive).wait_recv()
            slot = away(self.spot[1], step)
            add(slot, self.slots.at[receive])
            self.copy(slot, step, step - 1, step - 1).start()

    def total(self, add):
        plane = self.spot[1]
        self.copy(plane, 1, 0, 0).wait_recv()
        add(plane, self.slots.at[0])

        @pl.when(no(self.inner))
        def _():
            self.copy(plane, 1, 0, 1).wait_recv()
            add(plane, self.slots.at[1])

        @pl.when(self.inner)
        def _():
            self.copy(plane, 1, 0, 2).wait_recv()
            add(plane, self.slots.at[2])

    def finish(self):
        for send in range(3):
            self.copy(self.spot[1], 1, send, 0).wait_send()


class Collect:
    def __init__(self, ref, slots, owner, chip, plane, core, marks):
        self.ref, self.slots, self.spot = ref, slots, (chip, plane, core)
        self.send = marks.one()
        self.arrived = marks.many(3)
        inner, inner_owner = is_inner(plane), is_inner(owner)
        self.mine = plane == owner
        self.mine_outer = self.mine & no(inner)
        self.mine_inner = self.mine & inner
        self.near = plane == away(owner, 1)
        second, third = plane == away(owner, 2), plane == away(owner, 3)
        self.hands = no(inner) & (second | third) & no(self.near)
        self.adds_second = inner & second & no(inner_owner)
        self.adds_third = inner & third & inner_owner

    def copy(self, step, slot):
        chip, plane, core = self.spot
        return remote(
            self.ref, self.slots.at[slot], self.send, self.arrived(slot),
            device(chip, away(plane, step), core),
        )

    def start(self):
        pl.when(self.near)(lambda: self.copy(1, 0).start())
        pl.when(self.hands)(lambda: self.copy(1, 2).start())

    def relay(self, add):
        @pl.when(self.adds_second | self.adds_third)
        def _():
            self.copy(1, 2).wait_recv()
            add(self.slots.at[2])

        pl.when(self.adds_second)(lambda: self.copy(2, 1).start())
        pl.when(self.adds_third)(lambda: self.copy(3, 1).start())

    def total(self, add):
        @pl.when(self.mine)
        def _():
            for slot in range(2):
                self.copy(1, slot).wait_recv()
                add(self.slots.at[slot])

    def finish(self):
        pl.when(no(self.mine))(lambda: self.copy(1, 0).wait_send())


def layer_kernel(
    w_gate, w_up, w_down, w_qkv, w_out, conv, gain_mix, gain_ffn, tok, cot,
    out_ff, out_at, out_res, out_tok, out_small, main_got, extra_got, att_got, tail_got,
    ff, at, xs, gs, low2, part, acc3, gout, gat, from_mate, both, got, turned, hid, gg,
    gn, gcol, raw, qs, ks, vs, att, gatt, gproj, mid, gmid, gsum, normed, sending, inv_all,
    inv_sum, small, small_a, small_b, raw_ff, raw_qkv, raw_out, raw_conv, tapped,
    gains, gain_rows, packed, packed_back, at_tail, gat_tail, sem, free_mate, free_chips,
):
    chip, plane, core = place()
    others = other_chips(chip)
    mate = device(chip, plane, 1 - core)
    marks = Marks(sem)
    rows = tok.shape[0]
    width = 4 * rows
    half = tok.shape[1]
    seq = 2 * half
    own_half = lanes(core * half, half)
    first = core * half + chip * TILE
    peers = [device(c, plane, core) for c in others]
    line = [device(chip, away(plane, step), core) for step in (1, 2, 3)]
    sides = [device(c, plane, 1 - core) for c in others]
    line_mates = [device(chip, away(plane, step), 1 - core) for step in (1, 2, 3)]

    barrier = pltpu.get_barrier_semaphore()
    partners = peers + [mate] + sides + line + line_mates
    for partner in partners:
        pl.semaphore_signal(barrier, inc=1, device_id=partner, device_id_type=MESH)

    def block_rows(c):
        return rows_at(c * rows, rows, rows)

    ffn_weights = (w_gate, w_up, w_down)
    ffn_cols = w_gate.shape[1]
    wat, last_tile = gat.at[:, 0], packed_back.at[:, 0:rows]
    early = marks.many(6)
    loads = [
        pltpu.make_async_copy(source, target, early(i))
        for i, (source, target) in enumerate(
            (
                (w_qkv, raw_qkv), (w_out, raw_out), (conv, raw_conv),
                (gain_mix, gain_rows[0]), (gain_ffn, gain_rows[1]),
            )
        )
    ]
    for load in loads:
        load.start()
    for load in loads:
        load.wait()
    for i in range(2):
        gains[i] = gain_rows[i][...].reshape(1, rows)
    tapped[...] = jnp.zeros(tapped.shape, F32)
    tapped[0:CONV, 0 : 2 * HDIM] = raw_conv[...].astype(F32)
    tap_rows = tapped[...].T
    tail = lax.broadcasted_iota(jnp.int32, (HDIM, TILE), 1)
    spare = rows % TILE
    for h in range(2):
        wat[h, :HEADROWS, :rows] = raw_qkv[h * HEADROWS : (h + 1) * HEADROWS]
        wat[h, HEADROWS:, :rows] = raw_out[h * HDIM : (h + 1) * HDIM]
        columns = wat[h, 2 * FEAT : HEADROWS, WIDE - TILE :].astype(F32)
        for j in range(CONV):
            column = tap_rows[h * HDIM : (h + 1) * HDIM, j : j + 1]
            columns = jnp.where(tail == spare + j, column, columns)
        wat[h, 2 * FEAT : HEADROWS, WIDE - TILE :] = columns.astype(BF16)
    pl.semaphore_wait(barrier, len(partners))

    far_core = plane // 2
    holds_att = core == far_core
    holds_extra = holds_att & (chip // 2 == plane % 2)
    extra_plane = 2 * core + chip // 2
    extra_chip = (plane % 2) * 2 + core
    out_rows, in_rows = pl.ds(HEADROWS, HDIM), pl.ds(0, HEADROWS)
    whole = rows // TILE * TILE
    lead = 16
    tail_in, tail_out = pl.ds(0, lead + HEADROWS), pl.ds(lead + HEADROWS, HDIM)

    def leftover(ref, p):
        pair = [ref[c * rows + whole : (c + 1) * rows] for c in (2 * p, 2 * p + 1)]
        return jnp.concatenate(pair, 0)

    def heads_times(h, start, size, right):
        tails = slice(lead + start, lead + start + size)
        total = dot(at_tail[h, 0, tails], leftover(right, 0), 1, 0)
        total += dot(at_tail[h, 1, tails], leftover(right, 1), 1, 0)
        for c in range(4):
            total += dot(
                at[h, c, start : start + size, :whole], right[c * rows : c * rows + whole], 1, 0
            )
        return total

    def heads_spread(start, size, left, where, target):
        tails = slice(lead + start, lead + start + size)

        @pl.loop(0, 4)
        def _(c):
            total = dot(at[0, c, start : start + size, :whole], left[0, :, where], 0, 0)
            total += dot(at[1, c, start : start + size, :whole], left[1, :, where], 0, 0)
            target[rows_at(c * rows, whole, 16), where] = total.astype(BF16)

        for p in range(2):
            total = dot(at_tail[0, p, tails], left[0, :, where], 0, 0)
            total += dot(at_tail[1, p, tails], left[1, :, where], 0, 0)
            for i, c in enumerate((2 * p, 2 * p + 1)):
                size_left = rows - whole
                target[c * rows + whole : (c + 1) * rows, where] = total[
                    i * size_left : (i + 1) * size_left
                ].astype(BF16)

    lane_at = lax.broadcasted_iota(jnp.int32, (1, TILE), 1)

    def pack_heads(start, size):
        a = plane % 2
        for p in range(2):
            even, odd = [
                at[a, 2 * p + i, start : start + size, whole:].astype(F32) for i in range(2)
            ]
            tile = jnp.where(lane_at < spare, even, pltpu.roll(odd, spare, 1))
            at_tail[a, p, lead + start : lead + start + size] = tile.astype(BF16)

    def pack_taps():
        a = plane % 2
        columns = at[a, 0, 2 * FEAT : HEADROWS, whole:].astype(F32).T
        at_tail[a, 0, 0:lead, 0:HDIM] = columns[spare : spare + lead].astype(BF16)

    def unpack_heads(start, size):
        a = plane % 2
        for p in range(2):
            tile = gat_tail[a, p, lead + start : lead + start + size].astype(F32)
            for i, half_tile in enumerate((tile, pltpu.roll(tile, spare, 1))):
                gat[a, 2 * p + i, start : start + size, whole:] = half_tile.astype(BF16)

    def unpack_taps():
        a = plane % 2
        columns = gat_tail[a, 0, 0:lead, 0:HDIM].astype(F32).T
        for c in range(4):
            tile = gat[a, c, 2 * FEAT : HEADROWS, whole:].astype(F32)
            for j in range(CONV):
                tile = jnp.where(tail == spare + j, columns[:, j : j + 1], tile)
            gat[a, c, 2 * FEAT : HEADROWS, whole:] = tile.astype(BF16)

    att_self = [(2 * core + h == chip) & holds_att for h in range(2)]

    class Heads:
        def __init__(self, span):
            self.span, self.local = span, marks.one()
            self.send, self.here = marks.many(2), marks.many(4)

        def copy(self, h):
            return remote(
                wat.at[h, self.span], at.at[plane % 2, chip, self.span], self.send(h),
                self.here(chip), device(2 * core + h, plane, far_core),
            )

        def keep(self, h):
            return pltpu.make_async_copy(
                wat.at[h, self.span], at.at[plane % 2, chip, self.span], self.local
            )

        def start(self):
            for h in range(2):
                pl.when(att_self[h])(lambda: self.keep(h).start())
                pl.when(no(att_self[h]))(lambda: self.copy(h).start())

        def arrive(self):
            for h in range(2):
                pl.when(att_self[h])(lambda: self.keep(h).wait())

            for c in range(4):

                @pl.when(holds_att & no((c == chip) & (core == chip // 2)))
                def _():
                    remote(
                        wat.at[0, self.span], at.at[plane % 2, c, self.span], self.send(0),
                        self.here(c), mate,
                    ).wait_recv()

        def finish(self):
            for h in range(2):
                pl.when(no(att_self[h]))(lambda: self.copy(h).wait_send())

    heads_in, heads_out = Heads(in_rows), Heads(out_rows)
    heads_in.start()
    heads_out.start()

    class Gather:
        def __init__(self, source, target_of, earlier=None):
            self.source, self.target_of = source, target_of
            self.marks = earlier.marks if earlier else [marks.many(6), marks.many(6)] + [
                marks.many(4), marks.many(4), marks.one()
            ]
            self.send, self.here, self.mate_send, self.mate_here, kept = self.marks
            self.keep = pltpu.make_async_copy(source, target_of(chip), kept)
            mine = self.halves(source)
            there = self.halves(target_of(chip))
            self.copies = {
                mark: remote(
                    mine[half], there[half], self.send(mark), self.here(mark), peers[p]
                )
                for mark, half, p in ((0, 0, 0), (3, 1, 1), (1, 1, 0), (2, 0, 1))
            }
            for copy in self.copies.values():
                copy.start()
            self.keep.start()
            self.crossing = []
            self.cross(source, chip, 3)

        def cross(self, source, c, mark):
            copy = remote(
                source, self.target_of(c), self.mate_send(mark), self.mate_here(mark), mate
            )
            copy.start()
            self.crossing.append(copy)

        def halves(self, block):
            size = block.shape[0] // 2
            return block.at[0:size], block.at[size : 2 * size]

        def pass_on(self):
            for mark, half, p, onward in ((0, 0, 0, 4), (3, 1, 1, 5)):
                self.copies[mark].wait_recv()
                block = self.halves(self.target_of(others[p]))[half]
                self.copies[onward] = remote(
                    block, block, self.send(onward), self.here(onward), peers[1 - p]
                )
                self.copies[onward].start()
            for mark, p in ((1, 0), (2, 1)):
                self.copies[mark].wait_recv()
                self.cross(self.target_of(others[p]), others[p], p)

        def arrive(self):
            for mark in (4, 5):
                self.copies[mark].wait_recv()
            self.cross(self.target_of(others[2]), others[2], 2)
            for copy in self.crossing:
                copy.wait_recv()
            self.keep.wait()

        def finish(self):
            for copy in list(self.copies.values()) + self.crossing:
                copy.wait_send()

    tokens_in = Gather(tok, lambda c: xs.at[block_rows(c), own_half])
    gain_send, gain_here = marks.many(3), marks.many(3)
    gain_copies = [
        remote(gains, gn.at[chip], gain_send(p), gain_here(p), peers[p]) for p in range(3)
    ]
    gain_keep = pltpu.make_async_copy(gains, gn.at[chip], marks.one())
    for copy in gain_copies + [gain_keep]:
        copy.start()

    in_line, out_line = [
        [
            Spread(ref, 2 * core + a, chip, plane, core, marks)
            for a in range(2)
            for ref in (at.at[a, :, span, 0:whole], at_tail.at[a, :, tail_span])
        ]
        for span, tail_span in ((in_rows, tail_in), (out_rows, tail_out))
    ]
    heads_in.arrive()

    @pl.when(holds_att)
    def _():
        pack_heads(0, HEADROWS)
        pack_taps()

    for item in in_line:
        item.start()
    heads_out.arrive()
    pl.when(holds_att)(lambda: pack_heads(HEADROWS, HDIM))
    for item in out_line:
        item.start()
    heads_in.finish()
    heads_out.finish()

    short = ffn_cols - 4 * TILE
    for m in range(3):
        load = pltpu.make_async_copy(ffn_weights[m], raw_ff, early(5))
        load.start()
        load.wait()
        last_tile[m, :, 0:short] = raw_ff[:, 4 * TILE :]
        last_tile[m, :, short:] = jnp.zeros((rows, TILE - short), BF16)

    tokens_in.pass_on()
    main_send, main_here, main_local = marks.many(9), marks.many(9), marks.many(3)
    main_here_at = [ff.at[m, block_rows(chip), lanes(plane * TILE)] for m in range(3)]
    mains = [
        remote(
            ffn_weights[m].at[:, lanes(others[p] * TILE)], main_here_at[m],
            main_send(3 * p + m), main_here(3 * p + m), peers[p],
        )
        for p in range(3)
        for m in range(3)
    ]
    mains += [
        pltpu.make_async_copy(
            ffn_weights[m].at[:, lanes(chip * TILE)], main_here_at[m], main_local(m)
        )
        for m in range(3)
    ]
    for copy in mains:
        copy.start()

    extra_send, extra_here, extra_local = marks.one(), marks.many(4), marks.one()
    extra_self = (extra_chip == chip) & holds_att
    last = lanes(4 * TILE)

    def extra_copy():
        return remote(
            last_tile, ff.at[:, block_rows(chip), last], extra_send, extra_here(chip),
            device(extra_chip, plane, far_core),
        )

    def extra_keep():
        return pltpu.make_async_copy(
            last_tile, ff.at[:, block_rows(chip), last], extra_local
        )

    @pl.when(extra_self)
    def _():
        extra_keep().start()

    @pl.when(no(extra_self))
    def _():
        extra_copy().start()

    for item in in_line:
        item.relay()
    tokens_in.arrive()
    cot_in = Gather(cot, lambda c: gs.at[block_rows(c), own_half])
    for copy in gain_copies + [gain_keep]:
        copy.wait()

    for item in out_line:
        item.relay()
    @pl.loop(0, 4)
    def _(c):
        pair = jnp.concatenate(
            [gn[c, 0].astype(F32), gn[c, 1].astype(F32), jnp.zeros((6, rows), F32)], 0
        )
        gcol[block_rows(c), 0:8] = pair.T.astype(BF16)

    step_rows = 64

    def add_squares(i, total):
        x = xs[rows_at(i * step_rows, step_rows, step_rows)].astype(F32)
        return total + jnp.sum((x * x).reshape(step_rows // 8, 8, seq), 0)

    squares = lax.fori_loop(0, width // step_rows, add_squares, jnp.zeros((8, seq), F32))
    inv_all[...] = lax.rsqrt(jnp.sum(squares, 0, keepdims=True) / D + EPSILON)
    tokens_in.finish()
    normed[...] = xs[:, lanes(first)]

    @pl.loop(0, width // step_rows)
    def _(i):
        at_rows = rows_at(i * step_rows, step_rows, step_rows)
        xs[at_rows] = (
            xs[at_rows].astype(F32) * inv_all[...] * gcol[at_rows, 0:1].astype(F32)
        ).astype(BF16)

    for item in in_line:
        item.arrive()

    position = lax.broadcasted_iota(jnp.int32, (1, seq), 1)

    def taps(h):
        columns = at_tail[h, 0, 0:lead, 0:HDIM].astype(F32).T
        return [columns[:, j : j + 1] for j in range(CONV)]

    @pl.loop(0, 2)
    def _(h):
        projected = heads_times(h, 0, HEADROWS, xs)
        qs[h] = (projected[:FEAT].astype(BF16).astype(F32) * FEAT**-0.5).astype(BF16)
        ks[h] = projected[FEAT : 2 * FEAT].astype(BF16)
        values = projected[2 * FEAT :]
        raw[h] = values
        tap = taps(h)
        mixed = tap[0] * values
        for j in range(1, CONV):
            moved = pltpu.roll(values, j, 1)
            mixed += tap[j] * jnp.where(position >= j, moved, 0.0)
        vs[h] = mixed.astype(BF16)

    def kernel_of(h, b):
        seen = (b + 1) * SPAN
        scores = dot(ks[h, :, :seen], qs[h, :, b * SPAN : seen], 0, 0)
        kernel = 1.0 + scores + 0.5 * scores * scores
        key_at = lax.broadcasted_iota(jnp.int32, (seen, SPAN), 0)
        query_at = lax.broadcasted_iota(jnp.int32, (seen, SPAN), 1) + b * SPAN
        visible = key_at <= query_at
        return scores, jnp.where(visible, kernel, 0.0), visible

    @pl.loop(0, 2)
    def _(h):
        for b in range(seq // SPAN):
            seen = (b + 1) * SPAN
            _, kernel, _ = kernel_of(h, b)
            inverse = 1.0 / jnp.sum(kernel, 0, keepdims=True)
            inv_sum[h, :, b * SPAN : seen] = inverse
            weights = (kernel * inverse).astype(BF16)
            att[h, :, b * SPAN : seen] = dot(vs[h, :, :seen], weights, 1, 0).astype(BF16)

    for copy in mains:
        copy.wait()
    main_line = MainTiles(ff, chip, plane, core, marks)
    main_line.start()

    @pl.when(extra_self)
    def _():
        extra_keep().wait()

    @pl.when(no(extra_self))
    def _():
        extra_copy().wait_send()

    for c in range(4):

        @pl.when(holds_extra & no((c == chip) & (core == chip % 2)))
        def _():
            remote(
                last_tile, ff.at[:, block_rows(c), last], extra_send, extra_here(c), mate
            ).wait_recv()

    third = short // 3
    unit_at = lax.broadcasted_iota(jnp.int32, (rows, TILE), 1)

    def pack(source, target):
        @pl.loop(0, 3)
        def _(m):
            fourth = source[m, 3 * rows :, last].astype(F32)
            for b in range(3):
                own = source[m, b * rows : (b + 1) * rows, last].astype(F32)
                moved = pltpu.roll(fourth, (short - b * third) % TILE, 1)
                target[m, b * rows : (b + 1) * rows] = jnp.where(
                    unit_at < short, own, moved
                ).astype(BF16)

    def unpack(source, target):
        @pl.loop(0, 3)
        def _(m):
            fourth = jnp.zeros((rows, TILE), F32)
            for b in range(3):
                block = source[m, b * rows : (b + 1) * rows].astype(F32)
                target[m, b * rows : (b + 1) * rows, last] = jnp.where(
                    unit_at < short, block, 0.0
                ).astype(BF16)
                moved = pltpu.roll(block, (b * third - short) % TILE, 1)
                here = (unit_at >= b * third) & (unit_at < (b + 1) * third)
                fourth = jnp.where(here, moved, fourth)
            target[m, 3 * rows :, last] = fourth.astype(BF16)

    pl.when(holds_extra)(lambda: pack(ff, packed))
    extra_line = Chain(packed, extra_plane, chip, plane, core, marks)
    extra_line.start()

    for item in out_line:
        item.arrive()

    def default_got(i):
        return got.at[i]

    class Sum:
        def __init__(
            self, guard, earlier=None, both=both, got=None, share=True, at_once=True
        ):
            self.marks = earlier.marks if earlier else [marks.many(4), marks.many(4)] + [
                marks.many(6), marks.many(6)
            ]
            self.guard, self.both, self.share, self.at_once = guard, both, share, at_once
            self.got = got or default_got

        def begin(self, fill):
            fill((1 - core) * half)
            send, here = self.marks[:2]
            self.order = (others[2], others[0], others[1], chip)
            self.to_mate = [
                remote(
                    part.at[:, lanes((1 - core) * half + c * TILE)],
                    from_mate.at[:, lanes(c * TILE)], send(i), here(i), mate,
                )
                for i, c in enumerate(self.order)
            ]
            if self.guard:
                pl.semaphore_wait(free_mate, 1)
            for copy in self.to_mate:
                copy.start()
            fill(core * half)

        def release(self):
            pl.semaphore_signal(free_mate, inc=1, device_id=mate, device_id_type=MESH)

        def combine(self):
            self.prepare()
            for i, c in enumerate(self.order):
                self.to_mate[i].wait_recv()
                where, own = lanes(c * TILE), lanes(core * half + c * TILE)

                @pl.loop(0, 4)
                def _(b):
                    at_rows = block_rows(b)
                    self.both[at_rows, where] = (
                        part[at_rows, own].astype(F32) + from_mate[at_rows, where].astype(F32)
                    ).astype(BF16)

                if self.at_once:
                    self.send(i)
            for copy in self.to_mate:
                copy.wait_send()

        def piece(self, upper, c):
            size = width // 2
            return self.both.at[pl.ds(0 if upper else size, size), lanes(c * TILE)]

        def prepare(self):
            size = width // 2
            top, bottom = pl.ds(0, size), pl.ds(size, size)
            send, here = self.marks[2:]
            x, y, across = others
            self.across = [
                remote(self.piece(True, across), self.got(2).at[top], send(0), here(0), peers[0]),
                remote(
                    self.piece(False, across), self.got(2).at[bottom], send(1), here(1), peers[1]
                ),
            ]
            self.plain = [
                remote(self.piece(True, x), self.got(0).at[top], send(2), here(2), peers[0]),
                remote(self.piece(False, y), self.got(1).at[bottom], send(3), here(3), peers[1]),
            ]
            self.added = [
                remote(self.piece(True, y), self.got(1).at[top], send(4), here(4), peers[1]),
                remote(self.piece(False, x), self.got(0).at[bottom], send(5), here(5), peers[0]),
            ]

        def send(self, i):
            if i == 0:
                if self.guard and self.share:
                    pl.semaphore_wait(free_chips, 2)
                for copy in self.across:
                    copy.start()
            elif i < 3:
                self.plain[i - 1].start()

        def send_all(self):
            for i in range(3):
                self.send(i)

        def pass_on(self):
            size = width // 2
            quarter = size // 2
            for i, c in ((0, others[1]), (1, others[0])):
                self.across[i].wait_recv()
                for q in range(2):
                    at_rows = pl.ds(i * size + q * quarter, quarter)
                    self.both[at_rows, lanes(c * TILE)] = (
                        self.both[at_rows, lanes(c * TILE)].astype(F32) + self.got(2)[at_rows].astype(F32)
                    ).astype(BF16)
                self.added[i].start()

        def finish(self, store):
            for copy in self.plain + self.added:
                copy.wait()
            for copy in self.across:
                copy.wait_send()

            @pl.loop(0, 4)
            def _(c):
                at_rows = block_rows(c)
                total = self.both[at_rows, lanes(chip * TILE)].astype(F32)
                for p in range(2):
                    total += self.got(p)[at_rows].astype(F32)
                store(at_rows, total)

            for p in range(2 if self.share else 0):
                pl.semaphore_signal(free_chips, inc=1, device_id=peers[p], device_id_type=MESH)

    def fill_branch(start):
        heads_spread(HEADROWS, HDIM, att, lanes(start, half), part)

    small[...] = jnp.zeros(small.shape, F32)
    square_at = lax.broadcasted_iota(jnp.int32, (1, WIDE), 1)

    def note_square(index, value):
        total = jnp.sum(value * value)
        small[0, 2:3, :] += jnp.where(square_at == index, total, 0.0)

    def store_branch(at_rows, total):
        note_square(0, total)
        mid[at_rows] = normed[at_rows].astype(F32) + total

    branch_sum = Sum(guard=False)
    branch_sum.begin(fill_branch)
    cot_in.pass_on()
    branch_sum.combine()
    branch_sum.release()
    branch_sum.pass_on()
    main_line.relay()
    extra_line.start_inner()
    branch_sum.finish(store_branch)
    middle = mid[...]
    inverse_two = lax.rsqrt(jnp.sum(middle * middle, 0, keepdims=True) / D + EPSILON)

    @pl.loop(0, 4)
    def _(c):
        at_rows = block_rows(c)
        sending[0, at_rows] = (mid[at_rows] * inverse_two * gcol[at_rows, 1:2].astype(F32)).astype(BF16)

    def token_block(c):
        return low2.at[:, lanes(core * half + c * TILE)]

    low_in = Gather(sending.at[0], token_block, tokens_in)
    cot_in.arrive()
    cot_in.finish()

    @pl.loop(0, 4)
    def _(c):
        acc3[block_rows(c)] = jnp.zeros((rows, seq), F32)

    low_in.pass_on()
    low_in.arrive()
    low_in.finish()

    main_line.relay_far()
    extra_line.relay()
    def feed_units(slot):
        where = lanes(slot * TILE)
        unit_rows = rows_at(slot * TILE, TILE, TILE)
        for m in range(3):
            turned[m * TILE : (m + 1) * TILE] = ff[m, :, where].T

        @pl.loop(0, seq // SPAN)
        def _(n):
            span = lanes(n * SPAN, SPAN)
            gate_up = dot(turned[: 2 * TILE], low2[:, span], 1, 0)
            grad_hidden = dot(turned[2 * TILE :], gs[:, span], 1, 0)
            gate, up = gate_up[:TILE], gate_up[TILE:]
            sigmoid = 1.0 / (1.0 + jnp.exp(-gate))
            activated = gate * sigmoid
            hid[unit_rows, span] = (activated * up).astype(BF16)
            gg[:TILE, span] = (
                grad_hidden * up * sigmoid * (1.0 + gate * (1.0 - sigmoid))
            ).astype(BF16)
            gg[TILE:, span] = (grad_hidden * activated).astype(BF16)

    def feed_input(slot, at_rows):
        where = lanes(slot * TILE)
        pair = jnp.concatenate([ff[0, at_rows, where], ff[1, at_rows, where]], 1)
        acc3[at_rows] += dot(pair, gg[...], 1, 0)

    def feed_weights(slot, at_rows):
        where = lanes(slot * TILE)
        unit_rows = rows_at(slot * TILE, TILE, TILE)
        grads = dot(low2[at_rows], gg[...], 1, 1).astype(BF16)
        gout[0, at_rows, where] = grads[:, :TILE]
        gout[1, at_rows, where] = grads[:, TILE:]
        gout[2, at_rows, where] = dot(gs[at_rows], hid[unit_rows], 1, 1).astype(BF16)

    main_back = MainGrads(gout, main_got, chip, plane, core, marks)
    extra_back = Collect(packed_back, extra_got, extra_plane, chip, plane, core, marks)
    load_marks = marks.many(3)

    spare_lanes = [lanes((1 - core) * half + m * TILE) for m in range(3)]

    def add_tiles(slot, source):
        loads = [
            pltpu.make_async_copy(source.at[m], gs.at[:, spare_lanes[m]], load_marks(m))
            for m in range(3)
        ]
        for load in loads:
            load.start()
        for load in loads:
            load.wait()
        where = lanes(slot * TILE)

        @pl.loop(0, 4)
        def _(c):
            at_rows = block_rows(c)
            for m in range(3):
                gout[m, at_rows, where] = (
                    gout[m, at_rows, where].astype(F32)
                    + gs[at_rows, spare_lanes[m]].astype(F32)
                ).astype(BF16)

    def add_extra(source):
        packed_rows = slice(0, 3 * rows)
        loads = [
            pltpu.make_async_copy(source.at[m], gs.at[packed_rows, spare_lanes[m]], load_marks(m))
            for m in range(3)
        ]
        for load in loads:
            load.start()
        for load in loads:
            load.wait()

        @pl.loop(0, 3)
        def _(b):
            at_rows = block_rows(b)
            for m in range(3):
                packed_back[m, at_rows] = (
                    packed_back[m, at_rows].astype(F32)
                    + gs[at_rows, spare_lanes[m]].astype(F32)
                ).astype(BF16)

    slots = [away(plane, 1), plane, away(plane, 2), away(plane, 3)]
    inner = is_inner(plane)

    @pl.loop(0, 4)
    def _(turn):
        pl.when(turn == 2)(lambda: extra_line.relay_far())

        for i, step in ((0, 1), (2, 2), (3, 3)):

            @pl.when(turn == i)
            def _():
                main_line.arrive(step)

        slot = sum((turn == i).astype(jnp.int32) * slots[i] for i in range(4))
        feed_units(slot)

        @pl.loop(0, 4)
        def _(c):
            feed_input(slot, block_rows(c))
            feed_weights(slot, block_rows(c))
            pl.when((turn == 0) & no(inner))(lambda: main_back.start_rows(block_rows(c)))

        for i, step in ((2, 2), (3, 3)):

            @pl.when((turn == i) & no(inner))
            def _():
                main_back.start(step)

    extra_line.arrive()
    unpack(packed, ff)
    feed_units(4)

    @pl.loop(0, 4)
    def _(c):
        feed_input(4, block_rows(c))

    main_line.finish()

    def fill_grad_two(start):
        @pl.loop(0, 4)
        def _(c):
            where = lanes(start, half)
            part[block_rows(c), where] = acc3[block_rows(c), where].astype(BF16)

    def store_gsum(at_rows, total):
        gsum[at_rows] = total

    two_sum = Sum(True, branch_sum)
    two_sum.begin(fill_grad_two)
    two_sum.combine()
    @pl.loop(0, 4)
    def _(c):
        feed_weights(4, block_rows(c))

    two_sum.release()
    pl.when(inner)(lambda: main_back.start(1))
    pack(gout, packed_back)
    extra_back.start()
    main_back.relay(3, add_tiles)
    two_sum.pass_on()

    def fill_ffn(start):
        @pl.loop(0, 4)
        def _(c):
            where = lanes(start, half)
            part[block_rows(c), where] = dot(
                ff[2, block_rows(c)], hid[:, where], 1, 0
            ).astype(BF16)

    ffn_sum = Sum(
        guard=True, both=ff.at[1, :, lanes(0, half)],
        got=lambda i: ff.at[0, :, lanes(i * TILE)], share=False,
        at_once=False,
    )
    ffn_sum.begin(fill_ffn)
    two_sum.finish(store_gsum)

    def norm_back(source, inverse, gain_lane, base, store):
        def add_dots(c, total):
            at_rows = block_rows(c)
            gain = gcol[at_rows, gain_lane : gain_lane + 1].astype(F32)
            return total + jnp.sum(gsum[at_rows] * gain * source(at_rows), 0, keepdims=True)

        dots = lax.fori_loop(0, 4, add_dots, jnp.zeros((1, TILE), F32))
        scaled = inverse * inverse * inverse * dots / D

        @pl.loop(0, 4)
        def _(c):
            at_rows = block_rows(c)
            gain = gcol[at_rows, gain_lane : gain_lane + 1].astype(F32)
            grad, value = gsum[at_rows], source(at_rows)
            store(at_rows, base(at_rows) + (grad * gain * inverse - value * scaled))

        def gain_back():
            @pl.loop(0, 4)
            def _(c):
                at_rows = block_rows(c)
                for_gain = jnp.sum((gsum[at_rows] * source(at_rows) * inverse).T, 0, keepdims=True)
                small[c, gain_lane : gain_lane + 1, 0:rows] = for_gain

        return gain_back

    def store_middle(at_rows, value):
        gmid[at_rows] = value
        sending[1, at_rows] = value.astype(BF16)

    gain_two_back = norm_back(
        lambda r: mid[r], inverse_two, 1, lambda r: gs[r, lanes(first)].astype(F32), store_middle
    )
    mid_in = Gather(sending.at[1], token_block, tokens_in)
    gain_two_back()
    ffn_sum.combine()
    ffn_sum.release()
    mid_in.pass_on()
    ffn_sum.send_all()
    mid_in.arrive()

    @pl.loop(0, 2)
    def _(h):
        total = heads_times(h, HEADROWS, HDIM, low2)
        gatt[h] = total.astype(BF16)

    main_back.relay(2, add_tiles)

    out_back, in_back = [
        [
            Collect(ref, slots_, 2 * core + a, chip, plane, core, marks)
            for a in range(2)
            for ref, slots_ in (
                (gat.at[a, :, span, 0:whole], att_got.at[a, :, :, span]),
                (gat_tail.at[a, :, tail_span], tail_got.at[a, :, :, tail_span]),
            )
        ]
        for span, tail_span in ((out_rows, tail_out), (in_rows, tail_in))
    ]

    def head_grads(left, right, start, size):
        @pl.loop(0, 2)
        def _(h):
            for c in range(4):
                gat[h, c, start : start + size, :whole] = dot(
                    left[h], right[c * rows : c * rows + whole], 1, 1
                ).astype(BF16)
            for p in range(2):
                gat_tail[h, p, lead + start : lead + start + size] = dot(
                    left[h], leftover(right, p), 1, 1
                ).astype(BF16)

    head_grads(att, low2, HEADROWS, HDIM)
    for item in out_back:
        item.start()


    ffn_sum.pass_on()

    @pl.loop(0, 2)
    def _(h):
        grad_keys = jnp.zeros((FEAT, seq), F32)
        grad_values = jnp.zeros((HDIM, seq), F32)

        def padded(value):
            short = seq - value.shape[1]
            if not short:
                return value
            return jnp.concatenate([value, jnp.zeros((value.shape[0], short), F32)], 1)

        for b in range(seq // SPAN):
            seen = (b + 1) * SPAN
            span = slice(b * SPAN, seen)
            scores, kernel, visible = kernel_of(h, b)
            inverse = inv_sum[h, :, span]
            weights = kernel * inverse
            grad_weights = dot(vs[h, :, :seen], gatt[h, :, span], 0, 0)
            grad_values += padded(dot(gatt[h, :, span], weights.astype(BF16), 1, 1))
            dots = jnp.sum(grad_weights * weights, 0, keepdims=True)
            grad_kernel = (grad_weights - dots) * inverse
            grad_scores = jnp.where(visible, grad_kernel * (1.0 + scores), 0.0).astype(BF16)
            gproj[h, :FEAT, span] = (
                dot(ks[h, :, :seen], grad_scores, 1, 0) * FEAT**-0.5
            ).astype(BF16)
            grad_keys += padded(dot(qs[h, :, span], grad_scores, 1, 1))
        gproj[h, FEAT : 2 * FEAT] = grad_keys.astype(BF16)
        tap = taps(h)
        grad_raw = tap[0] * grad_values
        sums = [jnp.sum(grad_values * raw[h], 1, keepdims=True)]
        for j in range(1, CONV):
            masked = jnp.where(position >= j, grad_values, 0.0)
            grad_raw += tap[j] * pltpu.roll(masked, seq - j, 1)
            sums.append(jnp.sum(masked * pltpu.roll(raw[h], j, 1), 1, keepdims=True))
        gproj[h, 2 * FEAT :] = grad_raw.astype(BF16)
        columns = jnp.zeros((HDIM, TILE), F32)
        for j in range(CONV):
            columns = jnp.where(tail == j, sums[j], columns)
        gat_tail[h, 0, 0:lead, 0:HDIM] = columns.T[0:lead].astype(BF16)

    mid_in.finish()

    def store_result(at_rows, total):
        note_square(1, total)
        total = mid[at_rows] + total
        note_square(2, total)
        sending[0, at_rows] = total.astype(BF16)

    def hand_out(source, target):
        send, here = marks.many(3), marks.many(3)
        copies = [
            remote(
                source.at[block_rows(others[p])], target.at[:, lanes(chip * TILE)],
                send(p), here(p), peers[p],
            )
            for p in range(3)
        ]
        copies.append(
            pltpu.make_async_copy(
                source.at[block_rows(chip)], target.at[:, lanes(chip * TILE)], marks.one()
            )
        )
        for copy in copies:
            copy.start()
        return copies

    ffn_sum.finish(store_result)
    pending = hand_out(sending.at[0], out_res)


    def fill_grad_one(start):
        heads_spread(0, HEADROWS, gproj, lanes(start, half), part)

    one_sum = Sum(True, branch_sum)
    one_sum.begin(fill_grad_one)
    one_sum.combine()
    one_sum.release()
    head_grads(gproj, xs, 0, HEADROWS)
    for item in in_back:
        item.start()

    extra_back.relay(add_extra)

    one_sum.pass_on()

    main_back.total(add_tiles)
    back_send, back_here = marks.many(3), marks.many(3)
    mine = lanes(plane * TILE)
    back_to = out_ff.at[:, :, lanes(chip * TILE)]
    backs = [
        remote(
            gout.at[:, block_rows(others[p]), mine], back_to, back_send(p), back_here(p), peers[p]
        )
        for p in range(3)
    ]
    backs.append(
        pltpu.make_async_copy(gout.at[:, block_rows(chip), mine], back_to, marks.one())
    )
    for copy in backs:
        copy.start()
    pending += backs

    one_sum.finish(store_gsum)
    head_marks = marks.many(4)

    def add_head(i, start, size, tail_start, tail_size):
        a, is_tail = i // 2, i % 2
        target, count = (gat_tail, 2) if is_tail else (gat, 4)
        begin, extent = (tail_start, tail_size) if is_tail else (start, size)
        wide = TILE if is_tail else whole

        def add(source):
            loads = [
                pltpu.make_async_copy(
                    source.at[c], part.at[c * BLOCKROWS : c * BLOCKROWS + extent, 0:wide],
                    head_marks(c),
                )
                for c in range(count)
            ]
            for load in loads:
                load.start()
            for load in loads:
                load.wait()
            for c in range(count):
                target[a, c, begin : begin + extent, 0:wide] = (
                    target[a, c, begin : begin + extent, 0:wide].astype(F32)
                    + part[c * BLOCKROWS : c * BLOCKROWS + extent, 0:wide].astype(F32)
                ).astype(BF16)

        return add

    def add_out(i):
        return add_head(i, HEADROWS, HDIM, lead + HEADROWS, HDIM)

    def add_in(i):
        return add_head(i, 0, HEADROWS, 0, lead + HEADROWS)

    for i in range(4):
        out_back[i].relay(add_out(i))

    inverse_own = inv_all[:, lanes(first)]

    def store_tokens(at_rows, value):
        sending[1, at_rows] = value.astype(BF16)

    gain_one_back = norm_back(
        lambda r: normed[r].astype(F32), inverse_own, 0, lambda r: gmid[r], store_tokens
    )
    pending += hand_out(sending.at[1], out_tok)
    gain_one_back()

    for c in range(1, 4):
        small[c, 2:3] = small[0, 2:3]
    a_send, a_here = marks.many(3), marks.many(3)
    trio = [
        remote(small.at[others[p]], small_a.at[p], a_send(p), a_here(p), peers[p])
        for p in range(3)
    ]
    for copy in trio:
        copy.start()

    extra_back.total(add_extra)
    pl.when(holds_extra)(lambda: unpack(packed_back, gout))
    last_send, last_here, last_local = marks.many(4), marks.one(), marks.one()

    def last_copy(c):
        return remote(
            gout.at[:, block_rows(c), last], out_ff.at[:, :, last], last_send(c), last_here,
            device(c, plane, chip % 2),
        )

    def last_keep():
        return pltpu.make_async_copy(
            gout.at[:, block_rows(chip), last], out_ff.at[:, :, last], last_local
        )

    for c in range(4):
        same = (c == chip) & (core == chip % 2)

        @pl.when(holds_extra & same)
        def _():
            last_keep().start()

        @pl.when(holds_extra & no(same))
        def _():
            last_copy(c).start()

    for i in range(4):
        in_back[i].relay(add_in(i))
    class HeadsBack:
        def __init__(self, span):
            self.span, self.local = span, marks.one()
            self.send, self.here = marks.many(4), marks.many(2)

        def same(self, c):
            return (c == chip) & (core == chip // 2)

        def copy(self, c):
            return remote(
                gat.at[plane % 2, c, self.span], out_at.at[chip % 2, self.span], self.send(c),
                self.here(chip % 2), device(c, plane, chip // 2),
            )

        def keep(self):
            return pltpu.make_async_copy(
                gat.at[plane % 2, chip, self.span], out_at.at[chip % 2, self.span], self.local
            )

        def start(self):
            for c in range(4):
                pl.when(holds_att & self.same(c))(lambda: self.keep().start())
                pl.when(holds_att & no(self.same(c)))(lambda: self.copy(c).start())

        def finish(self):
            for c in range(4):
                pl.when(holds_att & self.same(c))(lambda: self.keep().wait())
                pl.when(holds_att & no(self.same(c)))(lambda: self.copy(c).wait_send())

            for h in range(2):

                @pl.when(no(att_self[h]))
                def _():
                    remote(
                        gat.at[0, 0, self.span], out_at.at[h, self.span], self.send(0),
                        self.here(h), mate,
                    ).wait_recv()

    heads_back = [HeadsBack(out_rows), HeadsBack(in_rows)]
    for i in range(4):
        out_back[i].total(add_out(i))
    pl.when(holds_att)(lambda: unpack_heads(HEADROWS, HDIM))
    heads_back[0].start()

    for i in range(4):
        in_back[i].total(add_in(i))

    @pl.when(holds_att)
    def _():
        unpack_heads(0, HEADROWS)
        unpack_taps()

    heads_back[1].start()

    for copy in trio:
        copy.wait()
    small_b[0] = small[chip] + small_a[0] + small_a[1] + small_a[2]
    b_send, b_here = marks.many(7), marks.many(7)
    seven = [
        remote(small_b.at[0], small_b.at[1 + i], b_send(i), b_here(i), to)
        for i, to in enumerate(line + [mate] + line_mates)
    ]
    for copy in seven:
        copy.start()

    for copy in seven:
        copy.wait()
    total = small_b[0]
    for i in range(7):
        total += small_b[1 + i]
    small_a[0] = total
    small_out = pltpu.make_async_copy(small_a.at[0], out_small, marks.one())
    small_out.start()
    pending.append(small_out)
    for item in in_line + out_line + [extra_line, main_back, extra_back] + out_back + in_back:
        item.finish()
    for copy in pending:
        copy.wait()
    for c in range(4):
        same = (c == chip) & (core == chip % 2)
        pl.when(holds_extra & same)(lambda: last_keep().wait())
        pl.when(holds_extra & no(same))(lambda: last_copy(c).wait_send())

    @pl.when(no(extra_self))
    def _():
        last_copy(0).wait_recv()

    for item in heads_back:
        item.finish()

    pl.semaphore_wait(free_mate, 1)
    pl.semaphore_wait(free_chips, 2)
    assert marks.used <= MARKS, marks.used


def dma(*shape):
    return pltpu.SemaphoreType.DMA(shape)


def run_layer(w_gate, w_up, w_down, w_qkv, w_out, conv, gain_mix, gain_ffn, tok, cot):
    rows, half = tok.shape
    width, seq = 4 * rows, 2 * half
    shape = jax.ShapeDtypeStruct
    vmem = pltpu.VMEM
    tiles = (3, width, TILE)
    head = (4, BLOCKROWS, WIDE)
    return pl.pallas_call(
        layer_kernel,
        out_shape=[
            shape((3, rows, 5 * TILE), BF16),
            shape((2, BLOCKROWS, WIDE), BF16),
            shape((rows, half), BF16),
            shape((rows, half), BF16),
            shape((8, WIDE), F32),
            shape((5,) + tiles, BF16),
            shape((3, 3, 3 * rows, TILE), BF16),
            shape((2, 3, 4, BLOCKROWS, rows // TILE * TILE), BF16),
            shape((2, 3, 2, 16 + BLOCKROWS, TILE), BF16),
        ],
        in_specs=[ANY] * 10,
        out_specs=[ANY] * 9,
        scratch_shapes=[
            vmem((3, width, 5 * TILE), BF16),
            vmem((2,) + head, BF16),
            vmem((width, seq), BF16),
            vmem((width, seq), BF16),
            vmem((width, seq), BF16),
            vmem((width, seq), BF16),
            vmem((width, seq), F32),
            vmem((3, width, 5 * TILE), BF16),
            vmem((2,) + head, BF16),
            vmem((width, half), BF16),
            vmem((width, half), BF16),
            vmem((3, width, TILE), BF16),
            vmem((3 * TILE, width), BF16),
            vmem((5 * TILE, seq), BF16),
            vmem((2 * TILE, seq), BF16),
            vmem((4, 2, 1, rows), BF16),
            vmem((width, TILE), BF16),
            vmem((2, HDIM, seq), F32),
            vmem((2, FEAT, seq), BF16),
            vmem((2, FEAT, seq), BF16),
            vmem((2, HDIM, seq), BF16),
            vmem((2, HDIM, seq), BF16),
            vmem((2, HDIM, seq), BF16),
            vmem((2, HEADROWS, seq), BF16),
            vmem((width, TILE), F32),
            vmem((width, TILE), F32),
            vmem((width, TILE), F32),
            vmem((width, TILE), BF16),
            vmem((2, width, TILE), BF16),
            vmem((1, seq), F32),
            vmem((2, 1, seq), F32),
            vmem((4, 8, WIDE), F32),
            vmem((3, 8, WIDE), F32),
            vmem((8, 8, WIDE), F32),
            vmem(w_gate.shape, BF16),
            vmem(w_qkv.shape, BF16),
            vmem(w_out.shape, BF16),
            vmem(conv.shape, BF16),
            vmem((8, 2 * TILE), F32),
            vmem((2, 1, rows), BF16),
            [vmem((rows,), BF16)] * 2,
            vmem((3, 3 * rows, TILE), BF16),
            vmem((3, 3 * rows, TILE), BF16),
            vmem((2, 2, 16 + BLOCKROWS, TILE), BF16),
            vmem((2, 2, 16 + BLOCKROWS, TILE), BF16),
            dma(MARKS),
            pltpu.SemaphoreType.REGULAR,
            pltpu.SemaphoreType.REGULAR,
        ],
        compiler_params=pltpu.CompilerParams(
            collective_id=0, has_side_effects=True, vmem_limit_bytes=63 * 2**20
        ),
        name="layer",
    )(w_gate, w_up, w_down, w_qkv, w_out, conv, gain_mix, gain_ffn, tok, cot)


def outputs_kernel(
    count, ff, at, res, tok, small, to_res, to_tok, to_qkv, to_conv, to_out, to_gate, to_up, to_down,
    to_mix, to_ffn, to_rms, ff_in, at_in, res_in, tok_in, small_in, tok_out, qkv_out, conv_out, out_out,
    ff_out, rms_out, sem,
):
    rows, cols = to_gate.shape
    marks = Marks(sem)
    loads = [
        pltpu.make_async_copy(source, target, marks.one())
        for source, target in (
            [(tok, tok_in), (at, at_in), (res, res_in)] + [(ff.at[m], ff_in.at[m]) for m in range(3)]
            + [(small, small_in)]
        )
    ]
    for load in loads:
        load.start()
    stores = []

    def store(source, target):
        stores.append(pltpu.make_async_copy(source, target, marks.one()))
        stores[-1].start()

    loads[0].wait()
    tok_out[...] = tok_in[...].astype(F32)
    store(tok_out, to_tok)
    loads[1].wait()
    for h in range(2):
        qkv_out[h * HEADROWS : (h + 1) * HEADROWS] = at_in[h, :HEADROWS, :rows].astype(F32)
        out_out[h * HDIM : (h + 1) * HDIM] = at_in[h, HEADROWS:, :rows].astype(F32)
    store(qkv_out, to_qkv)
    store(out_out, to_out)
    loads[2].wait()
    store(res_in, to_res)
    taps = jnp.concatenate(
        [at_in[h, 2 * FEAT : HEADROWS, WIDE - TILE :].astype(F32) for h in range(2)], 0
    )
    conv_out[...] = taps.T[rows % TILE : rows % TILE + CONV]
    store(conv_out, to_conv)
    for m, target in enumerate((to_gate, to_up, to_down)):
        loads[3 + m].wait()
        ff_out[m] = ff_in[m, :, :cols].astype(F32)
        store(ff_out.at[m], target)
    loads[6].wait()
    for i, target in enumerate((to_mix, to_ffn, to_rms)):
        row = small_in[i : i + 1, : target.shape[0]].reshape(target.shape[0])
        rms_out[i][...] = jnp.sqrt(row / count) if i == 2 else row
        store(rms_out[i], target)
    for copy in stores:
        copy.wait()


def outputs(ff, at, res, tok, small, ffn_cols, count):
    rows, half = tok.shape
    shape = jax.ShapeDtypeStruct
    shapes = [
        (rows, half), (2 * HEADROWS, rows), (CONV, 2 * HDIM), (2 * HDIM, rows),
        (rows, ffn_cols), (rows, ffn_cols), (rows, ffn_cols), (rows,), (rows,), (3,),
    ]
    vmem = pltpu.VMEM
    return pl.pallas_call(
        functools.partial(outputs_kernel, count),
        out_shape=[shape(res.shape, BF16)] + [shape(s, F32) for s in shapes],
        in_specs=[ANY] * 5,
        out_specs=[ANY] * 11,
        scratch_shapes=[
            vmem(ff.shape, BF16), vmem(at.shape, BF16), vmem(res.shape, BF16), vmem(tok.shape, BF16),
            vmem(small.shape, F32), vmem(shapes[0], F32), vmem(shapes[1], F32),
            vmem(shapes[2], F32), vmem(shapes[3], F32), vmem((3,) + shapes[4], F32),
            [vmem(s, F32) for s in shapes[7:]], dma(24),
        ],
        compiler_params=pltpu.CompilerParams(vmem_limit_bytes=60 * 2**20),
        name="outputs",
    )(ff, at, res, tok, small)


def on_device_full(
    tokens, cotangent, w_qkv, conv_weight, w_out, w_gate, w_up, w_down, gain_mix, gain_ffn
):
    rows, half = tokens.shape
    ffn_cols = w_gate.shape[1]
    out_ff, out_at, out_res, out_tok, small = run_layer(
        w_gate, w_up, w_down, w_qkv.T, w_out, conv_weight, gain_mix, gain_ffn,
        tokens, cotangent,
    )[:5]
    result, to_tok, to_qkv, *others = outputs(
        out_ff, out_at, out_res, out_tok, small, ffn_cols, 8 * half * 4 * rows
    )
    return (result, to_tok, to_qkv.T, *others)


def on_device(tokens, cotangent, lengths, deal_order, *weights):
    total_rows = tokens.shape[1] * lax.axis_size("col")
    if (
        lengths.shape[0] * LONGEST == total_rows
        and lax.axis_size("row") == 4
        and lax.axis_size("col") == 8
        and total_rows == 4 * LONGEST
        and weights[0].shape[1] == 2 * HEADROWS
        and weights[3].shape[1] == 4 * TILE + 96
    ):
        return on_device_full(tokens, cotangent, *weights)
    return on_device_general(tokens, cotangent, lengths, deal_order, *weights)


def solution(mesh):
    in_specs = (
        P("row", "col"),
        P("row", "col"),
        P(),
        P(),
        P("row", "col"),
        P(None, "col"),
        P("col", "row"),
        P("row", "col"),
        P("row", "col"),
        P("row", "col"),
        P("row"),
        P("row"),
    )
    out_specs = (
        P("row", "col"),
        P("row", "col"),
        P("row", "col"),
        P(None, "col"),
        P("col", "row"),
        P("row", "col"),
        P("row", "col"),
        P("row", "col"),
        P("row"),
        P("row"),
        P(),
    )
    return jax.shard_map(
        on_device, mesh=mesh, in_specs=in_specs, out_specs=out_specs, check_vma=False
    )
```
